32 devices in a mesh: dp: 8 (over z, x), chan: 4 (over y, core).
Axes of the slice: x: 2, y: 2, z: 4, core: 2. Of those that a mesh axis runs over, the one named last changes fastest.
Arguments:
- inputs: bfloat16 [768, 16384], P('chan', 'dp'), may hold values from -6 to 6
- seq_table: int32 [8, 2], P('dp'), may hold values from 1 to 2048, as said below
- mix_gain: float32 [2, 768], P(None, 'chan'), may hold values from 0.5 to 1.5
- mix_bias: float32 [2, 768], P(None, 'chan'), may hold values from -3 to 3
- in_proj: bfloat16 [2, 768, 3, 768], P(None, 'chan'), may hold values from -0.21875 to 0.21875
- short_conv: float32 [2, 3, 3, 768], P(None, None, None, 'chan'), may hold values from -1 to 1
- long_filter: float32 [2, 768, 2048], P(None, 'chan'), may hold values from -0.125 to 0.125
- cond_weight: float32 [2, 768], P(None, 'chan'), may hold values from 0.5 to 1.5
- out_proj: bfloat16 [2, 768, 768], P(None, 'chan'), may hold values from -0.21875 to 0.21875
- glu_gain: float32 [2, 768], P(None, 'chan'), may hold values from 0.5 to 1.5
- glu_bias: float32 [2, 768], P(None, 'chan'), may hold values from -3 to 3
- glu_in: bfloat16 [2, 768, 2, 3072], P(None, None, None, 'chan'), may hold values from -0.21875 to 0.21875
- glu_out: bfloat16 [2, 768, 3072], P(None, None, 'chan'), may hold values from -0.109375 to 0.109375
- cotangent: bfloat16 [768, 16384], P('chan', 'dp'), may hold values from -6 to 6
Outputs:
- outputs: float32 [768, 16384], P('chan', 'dp')
- input_grad: float32 [768, 16384], P('chan', 'dp')
- mix_gain_grad: float32 [2, 768], P(None, 'chan')
- mix_bias_grad: float32 [2, 768], P(None, 'chan')
- in_proj_grad: float32 [2, 768, 3, 768], P(None, ('chan', 'dp'))
- short_conv_grad: float32 [2, 3, 3, 768], P(None, None, None, 'chan')
- long_filter_grad: float32 [2, 768, 2048], P(None, ('chan', 'dp'))
- cond_weight_grad: float32 [2, 768], P(None, 'chan')
- out_proj_grad: float32 [2, 768, 768], P(None, ('chan', 'dp'))
- glu_gain_grad: float32 [2, 768], P(None, 'chan')
- glu_bias_grad: float32 [2, 768], P(None, 'chan')
- glu_in_grad: float32 [2, 768, 2, 3072], P(None, 'dp', None, 'chan')
- glu_out_grad: float32 [2, 768, 3072], P(None, 'dp', 'chan')
The draws below stay inside these ranges and needn't reach their ends.
Inputs may be any that keep to these rules, and one draw needn't show every extreme that they name: `seq_table`: row r describes slab r: column 0 is a bucket length 512, 1024 or 2048, column 1 how many sequences of that length it holds (at least 1), and their product is at most 2048. Some row has length 2048, and some row has length 512 with 4 sequences.
All inputs are finite; a program needn't handle non-finite values.
Results may differ from the reference program's by a relative error of at most 0.025.
Values may be sent and summed in bfloat16 or wider, within the bound.
A program may use at most 384 MiB of HBM per device.

```python
from functools import partial
import jax
import jax.numpy as jnp
from jax import lax

D = 768
FF = 3072
BLK = 512
LAYERS = 2
SLOTS = 2048
TOKENS = 16384
N_DP = 8


def draw_seq_table(key, part):
    key = jax.random.fold_in(key, 7)
    key_bucket, key_count, key_order = jax.random.split(key, 3)
    bucket = jax.random.randint(key_bucket, (N_DP,), 0, 3)
    shuffled = jax.random.permutation(key_order, N_DP)
    bucket = bucket.at[shuffled[0]].set(2)
    bucket = bucket.at[shuffled[1]].set(0)
    length = BLK * jnp.where(bucket == 0, 1, jnp.where(bucket == 1, 2, 4))
    most_seqs = 4 * BLK // length
    seq_count = 1 + jax.random.randint(key_count, (N_DP,), 0, 1000) % most_seqs
    seq_count = seq_count.at[shuffled[1]].set(4)
    return jnp.stack([length, seq_count], axis=1).astype(jnp.int32)


def block_scale(own_key, shape, pieces, low, largest):
    level, own = 1.0, jax.random.fold_in(own_key, 6)
    for position, parts in pieces:
        steps = jnp.exp(jax.random.uniform(jax.random.fold_in(own, position), (parts,), jnp.float32, low / len(pieces), largest / len(pieces)))
        level = level * jnp.repeat(steps, shape[position] // parts).reshape([-1 if axis == position else 1 for axis in range(len(shape))])
    return level


def bell_draw(stream_key, shape, scale, limit, cuts=(), kind=jnp.bfloat16):
    loudness = block_scale(stream_key, shape, cuts, -0.22, 0.18) if cuts else 1.0
    values = jax.random.normal(stream_key, shape, jnp.float32) * scale * loudness
    return jnp.minimum(jnp.maximum(values, -limit), limit).astype(kind)


def setup_inputs(seed: int = 0) -> dict:
    keys = jax.random.split(jax.random.key(seed), 15)
    return {
        "inputs": bell_draw(keys[0], (D, TOKENS), 1.0, 6.0, ((0, 4), (1, 8))),
        "seq_table": draw_seq_table(jax.random.fold_in(keys[14], 71), 0),
        "mix_gain": jnp.clip(1.0 + 0.1 * jax.random.normal(keys[2], (LAYERS, D), jnp.float32), 0.5, 1.5),
        "mix_bias": bell_draw(keys[3], (LAYERS, D), 0.5, 3.0, ((1, 4),), jnp.float32),
        "in_proj": bell_draw(keys[4], (LAYERS, D, 3, D), D ** -0.5, 0.21875, ((1, 4),)),
        "short_conv": jnp.clip(jax.random.uniform(keys[5], (LAYERS, 3, 3, D), jnp.float32, -1.0, 1.0) * block_scale(keys[5], (LAYERS, 3, 3, D), ((3, 4),), -0.4, 0.0), -1.0, 1.0),
        "long_filter": bell_draw(keys[6], (LAYERS, D, SLOTS), SLOTS ** -0.5, 0.125, ((1, 4),), jnp.float32),
        "cond_weight": jnp.clip(0.5 + 1.0 * jax.random.uniform(keys[7], (LAYERS, D), jnp.float32) ** block_scale(keys[7], (LAYERS, D), ((1, 4),), -0.2, 0.2), 0.5, 1.5),
        "out_proj": bell_draw(keys[8], (LAYERS, D, D), D ** -0.5, 0.21875, ((1, 4),)),
        "glu_gain": jnp.clip(1.0 + 0.1 * jax.random.normal(keys[9], (LAYERS, D), jnp.float32), 0.5, 1.5),
        "glu_bias": bell_draw(keys[10], (LAYERS, D), 0.5, 3.0, ((1, 4),), jnp.float32),
        "glu_in": bell_draw(keys[11], (LAYERS, D, 2, FF), D ** -0.5, 0.21875, ((3, 4),)),
        "glu_out": bell_draw(keys[12], (LAYERS, D, FF), FF ** -0.5, 0.109375, ((2, 4),)),
        "cotangent": bell_draw(keys[13], (D, TOKENS), 1.0, 6.0, ((0, 4), (1, 8))),
    }


@jax.custom_vjp
def low(v):
    return lax.optimization_barrier(v.astype(jnp.bfloat16)).astype(jnp.float32)

@jax.custom_vjp
def low_back(v):
    return v

def low_keep(v):
    return (low(v), None)

def low_pass(kept, grad):
    return (grad,)

def back_keep(v):
    return (v, None)

def back_low(kept, grad):
    return (low(grad),)
low.defvjp(low_keep, low_pass)
low_back.defvjp(back_keep, back_low)
EPSILON = 1e-05
PRECISE = lax.Precision.HIGHEST

def layer_norm(values, gain_row, shift_row):
    center = values - lax.optimization_barrier(jnp.mean(values, axis=1, keepdims=True))
    spread = lax.optimization_barrier(jnp.mean(center * center, axis=1, keepdims=True))
    return center * lax.rsqrt(spread + EPSILON) * gain_row + shift_row

def segment_ids(table_row, slots):
    slot_index = jnp.arange(slots, dtype=jnp.int32)
    active = slot_index < table_row[0] * table_row[1]
    return jnp.where(active, slot_index // table_row[0], slots + slot_index).astype(jnp.int32)

def short_mix(stream, weights, segment):
    summed = stream * weights[0]
    for offset in (1, 2):
        shifted = jnp.concatenate([jnp.zeros((offset,) + stream.shape[1:], stream.dtype), stream[:-offset]], axis=0)
        earlier = jnp.concatenate([jnp.full((offset,), -1, jnp.int32), segment[:-offset]], axis=0)
        same_seq = (earlier == segment).astype(stream.dtype)
        summed = summed + shifted * weights[offset] * same_seq[:, None, None]
    return summed

def long_mix(signal, kernel, segment, energy_stream, cond_row):
    slots = signal.shape[0]
    spectrum = jnp.fft.rfft(kernel, n=2 * slots, axis=0)
    result = jnp.zeros_like(signal)
    for member in range(slots // BLK):
        inside = (segment == member).astype(signal.dtype)[:, None]
        count = jnp.maximum(jnp.sum(inside), 1.0)
        energy = lax.optimization_barrier(jnp.sum(inside * energy_stream * energy_stream, axis=0)) / count
        factor = 1.0 + cond_row * jnp.log(1.0 + energy)
        convolved = jnp.fft.irfft(jnp.fft.rfft(signal * inside, n=2 * slots, axis=0) * spectrum, n=2 * slots, axis=0)
        result = result + inside * convolved[:slots] * factor
    return result

def slab_forward(params, slab_rows, table_row):
    mix_gain, mix_bias, in_proj, short_conv, long_filter, cond_weight, out_proj, glu_gain, glu_bias, glu_in, glu_out = params
    segment = segment_ids(table_row, slab_rows.shape[0])
    residual = slab_rows
    for layer_no in range(LAYERS):
        normed = low(layer_norm(residual, mix_gain[layer_no], mix_bias[layer_no]))
        project = low_back(jnp.einsum('sd,ekd->ske', normed, in_proj[layer_no], precision=PRECISE))
        mixed_streams = short_mix(project, short_conv[layer_no], segment)
        signal = mixed_streams[:, 1] * mixed_streams[:, 2]
        convolved = long_mix(signal, long_filter[layer_no].T, segment, mixed_streams[:, 2], cond_weight[layer_no])
        gated_out = low(mixed_streams[:, 0] * convolved)
        mixer_out = low_back(jnp.einsum('sd,ed->se', gated_out, out_proj[layer_no], precision=PRECISE))
        residual = residual + mixer_out
        normed_glu = low(layer_norm(residual, glu_gain[layer_no], glu_bias[layer_no]))
        gate_up = low_back(jnp.einsum('sd,dke->ske', normed_glu, glu_in[layer_no], precision=PRECISE))
        glu_units = low(jax.nn.gelu(gate_up[:, 0], approximate=False) * gate_up[:, 1])
        branch = low_back(jnp.einsum('sf,df->sd', glu_units, glu_out[layer_no], precision=PRECISE))
        residual = residual + branch
    return residual

def reference(inputs, seq_table, mix_gain, mix_bias, in_proj, short_conv, long_filter, cond_weight, out_proj, glu_gain, glu_bias, glu_in, glu_out, cotangent):
    params = tuple((item.astype(jnp.float32) for item in (mix_gain, mix_bias, in_proj, short_conv, long_filter, cond_weight, out_proj, glu_gain, glu_bias, glu_in, glu_out)))
    slab_stack = inputs.astype(jnp.float32).T.reshape(N_DP, 4 * BLK, D)

    def run_all(params_in, slabs_in):

        def one_slab(slab_pair):
            return jax.checkpoint(partial(slab_forward, params_in))(slab_pair[0], slab_pair[1])
        return lax.map(one_slab, (slabs_in, seq_table))
    outputs, pullback = jax.vjp(run_all, params, slab_stack)
    param_grads, input_grads = pullback(cotangent.astype(jnp.float32).T.reshape(outputs.shape))
    return (outputs.reshape(TOKENS, D).T, input_grads.reshape(TOKENS, D).T, param_grads[0], param_grads[1], param_grads[2], param_grads[3], param_grads[4], param_grads[5], param_grads[6], param_grads[7], param_grads[8], param_grads[9], param_grads[10])
```

```python
import math

import jax
import jax.numpy as jnp
import numpy as np
from jax import lax
from jax.experimental import pallas as pl
from jax.experimental.pallas import tpu as pltpu
from jax.sharding import PartitionSpec as P

EPSILON = 1e-05
F32 = jnp.float32
BF16 = jnp.bfloat16
VMEM_LIMIT = 63 * 2**20
LOADS = 4


def dft_table(block_len):
    period = 2 * block_len
    position = np.arange(block_len)[:, None]
    phase = ((2 * np.arange(block_len)[None, :] + 1) * position) % (2 * period)
    phase = phase * (math.pi / period)
    return np.concatenate([np.cos(phase), -np.sin(phase)], axis=1)


class Facts:
    def __init__(self, table_ref, blocks, block_len):
        length, count = table_ref[0, 0], table_ref[0, 1]
        used = length * count
        pair = jnp.where(length >= 2 * block_len, 1.0, 0.0)
        four = jnp.where(length >= 4 * block_len, 1.0, 0.0)
        active = [jnp.where(i * block_len < used, 1.0, 0.0) for i in range(blocks)]
        self.same = [[None] * blocks for _ in range(blocks)]
        for i in range(blocks):
            for j in range(blocks):
                if i == j:
                    self.same[i][j] = active[i]
                else:
                    joined = pair if i // 2 == j // 2 else four
                    self.same[i][j] = active[i] * active[j] * joined
        shortest = 1.0 / block_len
        self.inverse = shortest * (1.0 - 0.5 * pair - 0.25 * four)


class Io:
    def __init__(self, source, loads, stores):
        self.source, self.loads, self.stores, self.pending = source, loads, stores, []

    def ready(self, *numbers, cuts=None):
        for number in numbers:
            for copy in self.loads[number] if cuts is None else self.loads[number][cuts]:
                copy.wait()

    def flush(self, number, part=0, at=None):
        source, target, sems = self.stores[number]
        if at is not None:
            source, target = source.at[at], target.at[at]
        copy = pltpu.make_async_copy(source, target, sems.at[part])
        copy.start()
        self.pending.append(copy)

    def finish(self):
        for copy in self.pending:
            copy.wait()


def fused_call(kernel, operands, outs, scratch, collective, name, parts, scalars=-1, order=(),
               cuts=None, manual=()):
    arrays, layers = [], []
    for operand in operands:
        array, layer = operand if isinstance(operand, tuple) else (operand, None)
        arrays.append(array)
        layers.append(layer)
    cuts = cuts or {}
    inputs, results = len(arrays), len(outs)
    buffers, sems = [], []
    for number, (array, layer) in enumerate(zip(arrays, layers)):
        if number != scalars:
            buffers.append(pltpu.VMEM(array.shape if layer is None else array.shape[1:], array.dtype))
            sems.append(pltpu.SemaphoreType.DMA((len(cuts.get(number, (0,))),)))
    for (shape, dtype), count in zip(outs, parts):
        buffers.append(pltpu.VMEM(shape, dtype))
        sems.append(pltpu.SemaphoreType.DMA((count,)))

    def body(*refs):
        extra = list(refs[inputs + results + len(scratch) :])
        places, marks = extra[: len(buffers)], extra[len(buffers) :]
        sources, loads, stores, views, n = {}, {}, {}, [], 0
        for number in range(inputs):
            if number == scalars:
                views.append(refs[number])
                continue
            source = refs[number]
            if layers[number] is not None:
                source = source.at[layers[number]]
            sources[number] = source
            views.append(places[n])
            if number not in manual:
                pairs = [(source, places[n])]
                if number in cuts:
                    rows = [pl.ds(*one) for one in cuts[number]]
                    pairs = [(source.at[one], places[n].at[one]) for one in rows]
                loads[number] = [
                    pltpu.make_async_copy(*pair, marks[n].at[i]) for i, pair in enumerate(pairs)
                ]
            n += 1
        for number in range(results):
            stores[number] = (places[n], refs[inputs + number], marks[n])
            views.append(places[n])
            n += 1
        started = set()
        for one in list(order) + list(loads):
            number, chosen = one if isinstance(one, tuple) else (one, None)
            for i, copy in enumerate(loads[number]):
                if (chosen is None or i == chosen) and (number, i) not in started:
                    started.add((number, i))
                    copy.start()
        io = Io(sources, loads, stores)
        kernel(io, *views, *refs[inputs + results : inputs + results + len(scratch)])
        io.finish()

    anywhere = pl.BlockSpec(memory_space=pl.ANY)
    scalar_spec = pl.BlockSpec(memory_space=pltpu.SMEM)
    params = {}
    if collective is not None:
        params = dict(collective_id=collective, has_side_effects=True)
    return pl.pallas_call(
        body,
        out_shape=tuple(jax.ShapeDtypeStruct(*out) for out in outs),
        in_specs=[scalar_spec if n == scalars else anywhere for n in range(inputs)],
        out_specs=tuple([anywhere] * results),
        scratch_shapes=list(scratch) + buffers + sems,
        compiler_params=pltpu.CompilerParams(vmem_limit_bytes=VMEM_LIMIT, **params),
        name=name,
    )(*arrays)


def ring_position(index, count):
    odd = index % 2
    return (1 - odd) * (index // 2) + odd * (count - 1 - index // 2)


def ring_member(position, count):
    late = position // (count // 2)
    return (1 - late) * 2 * position + late * (2 * (count - 1 - position) + 1)


def chan_peers():
    me = lax.axis_index("chan")
    mate = me + 1 - 2 * (me % 2)
    across = (me + 2) % 4
    return me, mate, across, (mate + 2) % 4


def greet(peers, members=()):
    barrier = pltpu.get_barrier_semaphore()
    for peer in peers:
        pl.semaphore_signal(barrier, inc=1, device_id={"chan": peer})
    for member in members:
        pl.semaphore_signal(barrier, inc=1, device_id={"dp": member})
    pl.semaphore_wait(barrier, len(peers) + len(members))


def send_to(peer, source, target, send, recv):
    return pltpu.make_async_remote_copy(source, target, send, recv, device_id={"chan": peer})


def span(index, size, unit=None):
    if isinstance(index, int):
        return pl.ds(index * size, size)
    return pl.ds(pl.multiple_of(index * size, unit or size), size)


def gather_copy(place, peers, sems, kind, part):
    me, mate, across, _ = peers
    block = place(across if kind == 2 else me, part)
    send, recv = sems
    return send_to(
        across if kind == 0 else mate, block, block, send.at[kind, part], recv.at[kind, part]
    )


def norm_columns(values):
    mean = jnp.mean(values, axis=0, keepdims=True)
    center = values - mean
    inverse = lax.rsqrt(jnp.mean(center * center, axis=0, keepdims=True) + EPSILON)
    return center * inverse, inverse


def norm_pullback(grad, values, gain):
    normal, inverse = norm_columns(values)
    product = grad * normal
    scaled = grad * gain
    first = jnp.mean(scaled, axis=0, keepdims=True)
    second = jnp.mean(product * gain, axis=0, keepdims=True)
    return inverse * (scaled - first - normal * second), product


def lane_sums(values):
    return jnp.sum(values, axis=1, keepdims=True)


def matmul(left, right):
    return jnp.dot(left, right, preferred_element_type=F32)


def matmul_nt(left, right):
    return lax.dot_general(
        left, right, (((1,), (1,)), ((), ())), preferred_element_type=F32
    )


def transpose_into(target, source, tile):
    for n in range(source.shape[0] // tile):
        target[:, n * tile : (n + 1) * tile] = source[n * tile : (n + 1) * tile].T


def transpose_columns(target, source, tile):
    for n in range(source.shape[1] // tile):
        target[n * tile : (n + 1) * tile, :] = source[:, n * tile : (n + 1) * tile].T


def exchange(peers, source, target, send, recv):
    copies = []
    for n, peer in enumerate((peers[2], peers[3], peers[1])):
        copy = send_to(peer, source(peer), target(), send.at[n], recv.at[n])
        copy.start()
        copies.append(copy)
    return copies


def to_channels(peers, low, landing, send, recv):
    shard, tokens = landing.shape[0], low.shape[1]
    me = peers[0]
    mine = span(me, tokens)
    copies = exchange(
        peers, lambda peer: low.at[span(peer, shard, 32), :], lambda: landing.at[:, mine], send, recv
    )
    return copies


def to_tokens(peers, low, landing, send, recv):
    shard, half = low.shape[0], landing.shape[1] // 2
    mine = span(peers[0], shard, 32)
    copies = [
        exchange(
            peers, lambda peer: low.at[:, span(peer * 2 + part, half)],
            lambda: landing.at[mine, pl.ds(part * half, half)], send.at[part], recv.at[part],
        )
        for part in range(2)
    ]
    landing[mine, :] = low[:, span(peers[0], 2 * half)]
    return copies


class Track:
    def __init__(self, own, first, last, carry=None):
        self.own, self.first, self.last, self.carry = own, first, last, carry
        self.count, self.rows, self.lanes = own.shape

    def out(self):
        if self.last == self.count - 1:
            return ((self.rows, self.lanes), F32)
        return ((2, self.rows, self.lanes // 2), BF16)


def ring_operands(tracks):
    return [one.own for one in tracks] + [one.carry for one in tracks if one.first]


def ring_scratch(tracks):
    slots = [
        pltpu.VMEM((one.last - one.first, 2, one.rows, one.lanes // 2), BF16) for one in tracks
    ]
    if not tracks:
        return []
    longest = max(one.last - one.first for one in tracks)
    return slots + [pltpu.SemaphoreType.DMA((longest, len(tracks), 2))] * 2


class Ring:
    def __init__(self, tracks, operands, outs, scratch, sources):
        self.tracks, self.outs = tracks, outs
        self.count = tracks[0].count
        self.owns = operands[: len(tracks)]
        self.sources = sources[: len(tracks)]
        carries = list(sources[len(tracks) :])
        self.carries = [carries.pop(0) if one.first else None for one in tracks]
        *self.slots, self.send, self.recv = scratch
        self.here = lax.axis_index("dp")
        self.place = ring_position(self.here, self.count)
        after = ring_member((self.place + 1) % self.count, self.count)
        before = ring_member((self.place + self.count - 1) % self.count, self.count)
        self.toward = (after, before)
        self.rounds = max(one.last - one.first for one in tracks) - 1

    def copy(self, track, direction, turn, source):
        return pltpu.make_async_remote_copy(
            source,
            self.slots[track].at[turn, direction],
            self.send.at[turn, track, direction],
            self.recv.at[turn, track, direction],
            device_id={"dp": self.toward[direction]},
        )

    def owner(self, direction, step):
        move = step + 1
        if direction == 0:
            move = self.count - move
        return ring_member((self.place + move) % self.count, self.count)

    def own(self, track, direction, owner, owns=None):
        own = (owns or self.owns)[track]
        half = own.shape[2] // 2
        return own.at[owner, :, pl.ds(direction * half, half)]

    def held(self, track, direction, turn):
        return self.slots[track].at[turn, direction]

    def start(self):
        for track, carry in enumerate(self.carries):
            for direction in range(2):
                if carry is None:
                    source = self.own(track, direction, self.owner(direction, 0), self.sources)
                else:
                    source = carry.at[direction]
                self.copy(track, direction, 0, source).start()

    def round(self, turn, extra):
        for track, info in enumerate(self.tracks):
            def one(track=track, info=info):
                for direction in range(2):
                    held = self.held(track, direction, turn - 1)
                    self.copy(track, direction, turn - 1, held).wait_recv()
                    own = self.own(track, direction, self.owner(direction, info.first + turn))
                    held[...] = (held[...].astype(F32) + own[...].astype(F32)).astype(BF16)
                    self.copy(track, direction, turn, held).start()

            if info.last - info.first - 1 == self.rounds:
                one()
            else:
                pl.when(turn < info.last - info.first)(one)
        return extra

    def advance(self, point, points):
        first, last = self.rounds * point // points, self.rounds * (point + 1) // points
        if isinstance(point, int) and last == first:
            return
        if isinstance(point, int) and last == first + 1:
            self.round(last, 0)
            return
        lax.fori_loop(1 + first, 1 + last, self.round, 0)

    def loop(self, body, steps, point, pieces, points):
        for n in range(pieces):
            lax.fori_loop(steps * n // pieces, steps * (n + 1) // pieces, body, 0)
            self.advance(point + n, points)

    def finish(self):
        for track, (info, out) in enumerate(zip(self.tracks, self.outs)):
            turns = info.last - info.first
            half = info.lanes // 2
            whole = info.last == self.count - 1
            for direction in range(2):
                held = self.held(track, direction, turns - 1)
                self.copy(track, direction, turns - 1, held).wait_recv()
                owner = self.here if whole else self.owner(direction, info.last)
                own = self.own(track, direction, owner)
                total = held[...].astype(F32) + own[...].astype(F32)
                if whole:
                    out[:, pl.ds(direction * half, half)] = total
                else:
                    out[direction] = total.astype(BF16)

        def settle(turn, extra):
            for track, info in enumerate(self.tracks):
                def one(track=track):
                    for direction in range(2):
                        held = self.held(track, direction, turn)
                        self.copy(track, direction, turn, held).wait_send()

                if info.last - info.first == self.rounds + 1:
                    one()
                else:
                    pl.when(turn < info.last - info.first)(one)
            return extra

        lax.fori_loop(0, self.rounds + 1, settle, 0)


def ring_rows(rows):
    return -(-rows // 16) * 16


def split_rows(target, source, unit, joined):
    rows, kinds, lanes = source.shape

    def one(n, carry):
        here = span(n, unit)
        for kind in range(kinds):
            values = source[here, kind, :]
            if joined:
                target[here, kind * lanes : (kind + 1) * lanes] = values
            else:
                target[pl.ds(pl.multiple_of(kind * rows + n * unit, unit), unit), :] = values
        return carry

    return one


def first_project_kernel(
    io, inputs_ref, mix_gain, mix_bias, glu_gain, glu_bias, weight_in, short_in, cond_in, up_in,
    seq_ref, x_ref, gains_ref, full, project_ref, weight_ref, up_ref, columns_ref, keep_ref,
    raw, gains_low, gains_land, turn, send, recv, gains_send, gains_recv,
):
    peers = chan_peers()
    me = peers[0]
    shard, slots = inputs_ref.shape
    parts, width, half = raw.shape
    layers = mix_gain.shape[0]
    greet(peers[1:])
    io.ready(0, 1, 2, 3, 4)

    def gather(kind, part):
        return gather_copy(
            lambda owner, part: raw.at[part, span(owner, shard, 32), :],
            peers, (send, recv), kind, part,
        )

    for layer in range(layers):
        for kind, one in enumerate((mix_gain, mix_bias, glu_gain, glu_bias)):
            row = 4 * layer + kind
            gains_low[row : row + 1, :] = one[layer : layer + 1, :]
    gains_land[me] = gains_low[...]
    copies = exchange(
        peers, lambda peer: gains_low, lambda: gains_land.at[me], gains_send, gains_recv
    )
    for part in range(parts):
        raw[part, span(me, shard, 32), :] = inputs_ref[:, part * half : (part + 1) * half]
        for kind in range(2):
            gather(kind, part).start()
    io.ready(5, 6, 7)
    for layer in range(layers):
        lax.fori_loop(0, shard // 48, split_rows(weight_ref.at[layer], weight_in.at[layer], 48, False), 0)
        turn[...] = jnp.zeros_like(turn)
        for tap in range(3):
            turn[3 * tap : 3 * tap + 3, :shard] = short_in[layer, tap]
        turn[9:10, :shard] = cond_in[layer : layer + 1, :]
        columns_ref[layer] = turn[...].T[:shard]
    slot = lax.broadcasted_iota(jnp.int32, keep_ref.shape, 1)
    row = lax.broadcasted_iota(jnp.int32, keep_ref.shape, 0)
    within = slot & (seq_ref[0, 0] - 1)
    keep_ref[...] = jnp.where(within > row, 1.0, 0.0)
    io.flush(4)
    io.flush(6)
    io.flush(7)
    for copy in copies:
        copy.wait()
    turn[...] = jnp.zeros_like(turn)
    for owner in range(4):
        turn[: 4 * layers, :shard] = gains_land[owner]
        gains_ref[owner * shard : (owner + 1) * shard, :] = turn[...].T[:shard]
    io.flush(1)
    io.ready(8)
    gather(0, 0).wait_recv()
    gather(2, 0).start()
    for part in range(parts):
        if part + 1 < parts:
            gather(0, part + 1).wait_recv()
            gather(2, part + 1).start()
        gather(1, part).wait_recv()
        gather(2, part).wait_recv()
        values = raw[part].astype(F32)

        @pl.when(me == part // 2)
        def _():
            x_ref[:, (part % 2) * half : (part % 2 + 1) * half] = values

        normal, _ = norm_columns(values)
        full[part] = (normal * gains_ref[:, 0:1] + gains_ref[:, 1:2]).astype(BF16)
        io.flush(2, part, part)
        columns = slice(part * half, (part + 1) * half)
        project_ref[:, columns] = matmul(weight_ref[0], full[part])
        io.flush(3, part, (slice(None), pl.ds(part * half, half)))
        cuts = width // 64
        lax.fori_loop(
            cuts * part // parts, cuts * (part + 1) // parts, split_rows(up_ref, up_in, 64, True), 0
        )
    io.flush(0)
    io.flush(5)
    for part in range(parts):
        for kind in range(3):
            gather(kind, part).wait_send()


def first_project(inputs, gain_arrays, in_proj, short_conv, cond_weight, glu_in, seq_table,
                  collective):
    shard, slots = inputs.shape
    layers, _, streams, width = in_proj.shape
    hidden = glu_in[0].shape[3]
    tokens = slots // 4
    return fused_call(
        first_project_kernel,
        [inputs, *gain_arrays, in_proj, short_conv, cond_weight, glu_in, seq_table],
        [
            ((width, tokens), F32),
            ((width, 128), F32),
            ((8, width, tokens // 2), BF16),
            ((streams * shard, slots), F32),
            ((layers, streams * shard, width), BF16),
            ((width, 2 * hidden), BF16),
            ((layers, shard, 128), F32),
            ((8, slots), F32),
        ],
        [
            pltpu.VMEM((8, width, tokens // 2), BF16),
            pltpu.VMEM((4 * layers, shard), F32),
            pltpu.VMEM((4, 4 * layers, shard), F32),
            pltpu.VMEM((128, 256), F32),
        ]
        + [pltpu.SemaphoreType.DMA((3, 8))] * 2
        + [pltpu.SemaphoreType.DMA((3,))] * 2,
        collective,
        "first_project",
        (1, 1, 8, 8, 1, 1, 1, 1),
        9,
    )


def scatter_copy(peers, buffers, sems, kind, part):
    _, mate, across, _ = peers
    send, recv = sems
    return send_to(
        across if kind == 2 else mate,
        buffers[2 * kind].at[part],
        buffers[2 * kind + 1].at[part],
        send.at[kind, part],
        recv.at[kind, part],
    )


def scatter_buffers(width, half):
    return [pltpu.VMEM((2, width, half), BF16)] * 6


def block_place(full):
    return lambda owner, part: full.at[owner * 2 + part]


def block_at(step, peers, gathers):
    me, mate, across, diag = peers
    if gathers:
        mine = 1 - (step + 6) // 8
        kind = (step + 1) % 3
        part = mine * step + (1 - mine) * ((step - 2) // 3)
        kind = kind - mine * 4
    else:
        near = step // 4
        mine = step // 6
        part = (1 - near) * (step // 2) + near * (step % 2)
        kind = (1 - near) * (1 + step % 2) - mine
    far = kind * (2 - kind) * (across - mate) + kind * (kind - 1) // 2 * (diag - mate)
    return kind, part, ((1 - mine) * (mate + far) + mine * me) * 2 + part, mine


def run_blocks(peers, full, gather_sems, scatter_sems, buffers, partial, kept, own, ring=None):
    me, mate, across, diag = peers
    gathers = gather_sems is not None

    def gather(kind, part):
        return gather_copy(block_place(full), peers, gather_sems, kind, part)

    def step_body(step, carry):
        kind, part, block, mine = block_at(step, peers, gathers)

        if gathers:
            @pl.when(kind == 0)
            def _():
                gather(1, part).wait_recv()

            @pl.when(kind == 1)
            def _():
                gather(0, part).wait_recv()
                gather(2, part).start()

            @pl.when(kind == 2)
            def _():
                gather(2, part).wait_recv()

        share = partial(block, step)

        def scatter(kind):
            return scatter_copy(peers, buffers, scatter_sems, kind, part)

        @pl.when(mine == 1)
        def _():
            own[part] = share

        @pl.when(kind == 0)
        def _():
            buffers[2][part] = share.astype(BF16)
            scatter(1).start()

        @pl.when(kind == 1)
        def _():
            kept[...] = share

        @pl.when(kind == 2)
        def _():
            buffers[0][part] = share.astype(BF16)
            scatter(0).start()
            scatter(0).wait_recv()
            buffers[4][part] = (kept[...] + buffers[1][part].astype(F32)).astype(BF16)
            scatter(2).start()

        if ring is not None:
            ring.advance(step, 8)
        return carry

    lax.fori_loop(0, 8, step_body, 0)


def scattered(peers, scatter_sems, buffers, own, part):
    for kind in (1, 2):
        scatter_copy(peers, buffers, scatter_sems, kind, part).wait_recv()
    return own[part] + buffers[3][part].astype(F32) + buffers[5][part].astype(F32)


def drain_gather(peers, full, gather_sems):
    for part in range(2):
        for kind in range(3):
            gather_copy(block_place(full), peers, gather_sems, kind, part).wait_send()


def drain_scatter(peers, scatter_sems, buffers):
    for part in range(2):
        for kind in range(3):
            scatter_copy(peers, buffers, scatter_sems, kind, part).wait_send()


def feed_kernel(gain_at, follows, io, gated_ref, x_ref, gains_ref, out_weight, up_columns,
                down_weight, *refs):
    refs = list(refs)
    weight_ref, up_in = (refs.pop(0), refs.pop(0)) if follows else (None, None)
    token_gated, mid_ref, full, next_ref, units, gelus, slopes = refs[:7]
    refs = refs[7:]
    if follows:
        next_full, project_ref, next_up = refs[:3]
        *refs, next_send, next_recv = refs[3:]
    up_weight, kept, own, *rest = refs
    buffers, sems = rest[:6], rest[6:]
    send, recv, gather_send, gather_recv, scatter_send, scatter_recv = sems
    gather_sems, scatter_sems = (gather_send, gather_recv), (scatter_send, scatter_recv)
    peers = chan_peers()
    me = peers[0]
    width, tokens = x_ref.shape
    half = tokens // 2
    hidden = down_weight.shape[1]
    greet(peers[1:])
    io.ready(0)
    copies = to_tokens(peers, gated_ref, token_gated, send, recv)
    io.ready(1, 2, 3, 4, 5)
    transpose_columns(up_weight, up_columns, 256)
    for part in range(2):
        for copy in copies[part]:
            copy.wait()
        columns = slice(part * half, (part + 1) * half)
        mid = x_ref[:, columns] + matmul(out_weight[...], token_gated[:, columns])
        mid_ref[:, columns] = mid
        normal, _ = norm_columns(mid)
        gain = gains_ref[:, gain_at : gain_at + 1]
        bias = gains_ref[:, gain_at + 1 : gain_at + 2]
        full[me * 2 + part] = (normal * gain + bias).astype(BF16)
        for kind in range(2):
            gather_copy(block_place(full), peers, gather_sems, kind, part).start()
    io.flush(0)
    io.flush(1)

    def partial(block, step):
        normed = full[block]
        tile = 256
        for n in range(hidden // tile):
            gate = matmul(up_weight[n * tile : (n + 1) * tile], normed)
            up = matmul(up_weight[hidden + n * tile : hidden + (n + 1) * tile], normed)
            rows = slice(n * tile, (n + 1) * tile)
            cdf = 0.5 * (1.0 + lax.erf(gate * math.sqrt(0.5)))
            density = jnp.exp(-0.5 * gate * gate) * (1.0 / math.sqrt(2.0 * math.pi))
            gelu = gate * cdf
            units[block, rows] = (gelu * up).astype(BF16)
            gelus[block, rows] = gelu.astype(BF16)
            slopes[block, rows] = (up * (cdf + gate * density)).astype(BF16)
        return matmul(down_weight[...], units[block])

    run_blocks(peers, full, gather_sems, scatter_sems, buffers, partial, kept, own)
    for number in (2, 4, 5, 6):
        io.flush(number)
    if follows:
        io.ready(6, 7)
    place = block_place(next_full) if follows else None
    for part in range(2):
        if follows:
            cuts = width // 64
            lax.fori_loop(
                cuts * part // 2, cuts * (part + 1) // 2, split_rows(next_up, up_in, 64, True), 0
            )
        columns = slice(part * half, (part + 1) * half)
        value = mid_ref[:, columns] + scattered(peers, scatter_sems, buffers, own, part)
        next_ref[:, columns] = value.astype(next_ref.dtype)
        if follows:
            normal, _ = norm_columns(value)
            gain = gains_ref[:, gain_at + 2 : gain_at + 3]
            bias = gains_ref[:, gain_at + 3 : gain_at + 4]
            next_full[me * 2 + part] = (normal * gain + bias).astype(BF16)
            for kind in range(2):
                gather_copy(place, peers, (next_send, next_recv), kind, part).start()
    io.flush(3)
    if follows:
        io.flush(9)
    drain_gather(peers, full, gather_sems)
    drain_scatter(peers, scatter_sems, buffers)
    if follows:
        project_blocks(io, peers, next_full, (next_send, next_recv), weight_ref, project_ref, 7, 8)


def project_blocks(io, peers, full, sems, weight_ref, project_ref, full_out, project_out):
    me, mate, across, diag = peers
    half = full.shape[2]

    def gather(kind, part):
        return gather_copy(block_place(full), peers, sems, kind, part)

    order = [(me, 0), (me, 1), (mate, 0), (mate, 1)]
    order += [(across, 0), (diag, 0), (across, 1), (diag, 1)]
    for step, (owner, part) in enumerate(order):
        if 2 <= step < 4:
            gather(1, part).wait_recv()
        elif step >= 4 and step % 2 == 0:
            gather(0, part).wait_recv()
            gather(2, part).start()
        elif step >= 4:
            gather(2, part).wait_recv()
        block = owner * 2 + part
        io.flush(full_out, step, block)
        columns = span(block, half)
        project_ref[:, columns] = matmul(weight_ref[...], full[block])
        io.flush(project_out, step, (slice(None), columns))
    for kind in range(3):
        for part in range(2):
            gather(kind, part).wait_send()


def feed_forward(gated, values, gains, out_weight, up_columns, down_weight, following, gain_at,
                 collective):
    width, tokens = values.shape
    half = tokens // 2
    follows = list(following)
    block = ((8, width, half), BF16)
    outs = [((width, tokens), BF16), ((width, tokens), F32), block]
    outs.append(((width, tokens), F32 if follows else BF16))
    hidden = down_weight[0].shape[2]
    outs += [((8, hidden, half), BF16)] * 3
    parts = [1] * 7
    extra = []
    if follows:
        outs += [block, ((follows[0][0].shape[1], 4 * tokens), F32)]
        outs.append(((width, 2 * hidden), BF16))
        parts += [8, 8, 1]
        extra = [pltpu.SemaphoreType.DMA((3, 2))] * 2
    return fused_call(
        lambda *refs: feed_kernel(gain_at, bool(follows), *refs),
        [gated, values, gains, out_weight, up_columns, down_weight] + follows,
        outs,
        [
            pltpu.VMEM((2 * hidden, width), BF16),
            pltpu.VMEM((width, half), F32),
            pltpu.VMEM((2, width, half), F32),
        ]
        + scatter_buffers(width, half)
        + [pltpu.SemaphoreType.DMA((2, 3))] * 2
        + [pltpu.SemaphoreType.DMA((3, 2))] * 4
        + extra,
        collective,
        "feed_forward",
        parts,
    )


def weight_grad(store, rows, columns, left, right, blocks, row_tile, column_tile):
    across = columns // column_tile

    def one(n, carry):
        row, column = span(n // across, row_tile), span(n % across, column_tile)
        total = matmul_nt(left(0, row), right(0, column))
        for block in range(1, blocks):
            total = total + matmul_nt(left(block, row), right(block, column))
        store(n // across, column, total)
        return carry

    lax.fori_loop(0, rows // row_tile * across, one, 0)


def feed_back_kernel(gain_at, gathered, tracks, io, grad_ref, down_weight, gelus, slopes, up_columns,
                     out_weight, mid_ref, gains_ref, token_gated, units, normed, *refs):
    refs = list(refs)
    rings = len(tracks)
    inputs = len(ring_operands(tracks))
    ring_in, refs = refs[:inputs], refs[inputs:]
    state_ref, gated_ref, feed_grads, out_grad, sums_ref = refs[:5]
    large, refs = refs[5 : 5 + rings], refs[5 + rings :]
    ring = None
    if rings:
        sources = [io.source[11 + n] for n in range(inputs)]
        ring = Ring(tracks, ring_in, large, refs[-rings - 2 :], sources)
        refs = refs[: -rings - 2]
    full = grad_ref if gathered else refs.pop(0)
    gates, mixer_low, kept, own, turned, *rest, load_sems = refs
    gated_low = full
    buffers, sems = rest[:6], rest[6:]
    send, recv, gather_send, gather_recv, scatter_send, scatter_recv = sems
    gather_sems, scatter_sems = (gather_send, gather_recv), (scatter_send, scatter_recv)
    if gathered:
        gather_sems = None
    peers = chan_peers()
    me, mate, across, diag = peers
    width, tokens = mid_ref.shape
    half = tokens // 2
    shard = gated_ref.shape[0]
    hidden = down_weight.shape[1]
    tile = 256
    saved = ((io.source[2], gelus), (io.source[3], slopes))
    if gathered:
        saved += ((io.source[0], full),)

    def loads(step, block):
        return [
            pltpu.make_async_copy(source.at[block], target.at[block], load_sems.at[n, step])
            for n, (source, target) in enumerate(saved)
        ]

    for step in range(8):
        for copy in loads(step, block_at(step, peers, not gathered)[2]):
            copy.start()
    greet(peers[1:], ring.toward if rings else ())
    if not gathered:
        io.ready(0)
        for part in range(2):
            full[me * 2 + part] = grad_ref[:, part * half : (part + 1) * half].astype(BF16)
            for kind in range(2):
                gather_copy(block_place(full), peers, gather_sems, kind, part).start()
    if rings:
        ring.start()
    io.ready(1)
    down_rows, out_rows = turned.at[:hidden], turned.at[:width]
    transpose_into(down_rows, down_weight, tile)
    io.ready(4)
    if rings:
        io.ready(*range(11, 11 + rings))

    def partial(block, step):
        for copy in loads(step, block):
            copy.wait()
        grad = full[block]
        for n in range(hidden // tile):
            rows = slice(n * tile, (n + 1) * tile)
            later = slice(hidden + n * tile, hidden + (n + 1) * tile)
            unit_grad = matmul(down_rows[rows], grad)
            gates[block, rows] = (unit_grad * slopes[block, rows].astype(F32)).astype(BF16)
            gates[block, later] = (unit_grad * gelus[block, rows].astype(F32)).astype(BF16)
        return matmul(up_columns[...], gates[block])

    run_blocks(peers, full, gather_sems, scatter_sems, buffers, partial, kept, own, ring)
    io.ready(5, 6, 7, 8, 9, 10)
    transpose_into(out_rows, out_weight, tile)
    if not gathered:
        drain_gather(peers, full, gather_sems)

    def a2a(part, n):
        peer = (across, diag, mate)[n]
        return send_to(
            peer,
            gated_low.at[part, span(peer, shard, 32), :],
            gated_ref.at[:, span(me * 2 + part, half)],
            send.at[part, n],
            recv.at[part, n],
        )

    chunk_rows = feed_grads.shape[1] // 3
    row_tile = 384

    def store_grad(kind):
        def store(index, column, total):
            chunks = row_tile // chunk_rows
            for n in range(chunks):
                feed_grads[
                    index * chunks + n, kind * chunk_rows : (kind + 1) * chunk_rows, column
                ] = total[n * chunk_rows : (n + 1) * chunk_rows].astype(BF16)

        return store

    def store_out(index, column, total):
        out_grad[span(index, tile), column] = total.astype(BF16)

    gain = gains_ref[:, gain_at : gain_at + 1]
    for part in range(2):
        for kind in (0,) if part == 0 else (1, 2):
            if kind == 0:
                left, right = lambda b, r: full[b, r], lambda b, c: units[b, c]
            else:
                first = (kind - 1) * hidden
                left = lambda b, r: normed[b, r]
                right = lambda b, c, first=first: gates[
                    b, pl.ds(pl.multiple_of(c.start + first, tile), tile)
                ]
            weight_grad(store_grad(kind), width, hidden, left, right, 8, row_tile, tile)
        columns = slice(part * half, (part + 1) * half)
        grad = scattered(peers, scatter_sems, buffers, own, part)
        change, product = norm_pullback(grad, mid_ref[:, columns], gain)
        before = full[me * 2 + part].astype(F32) if gathered else grad_ref[:, columns]
        state = before + change
        state_ref[:, columns] = state
        mixer_low[:, columns] = state.astype(BF16)
        gated_low[part] = matmul(out_rows[...], mixer_low[:, columns]).astype(BF16)
        for n in range(3):
            a2a(part, n).start()
        if part == 0:
            sums_ref[:, 0:1] = lane_sums(product)
            sums_ref[:, 1:2] = lane_sums(grad)
        else:
            sums_ref[:, 0:1] = sums_ref[:, 0:1] + lane_sums(product)
            sums_ref[:, 1:2] = sums_ref[:, 1:2] + lane_sums(grad)
    io.flush(0)
    io.flush(2)
    io.flush(4)
    for part in range(2):
        gated_ref[:, span(me * 2 + part, half)] = gated_low[part, span(me, shard, 32), :]
    weight_grad(
        store_out, width, width,
        lambda b, r: mixer_low[r, :], lambda b, c: token_gated[c, :], 1, tile, tile,
    )
    io.flush(3)
    if rings:
        ring.finish()
        for n in range(rings):
            io.flush(5 + n)
    for part in range(2):
        for n in range(3):
            a2a(part, n).wait()
    io.flush(1)
    drain_scatter(peers, scatter_sems, buffers)


def feed_back(grad, mid, gains, normed, up_columns, down_weight, out_weight, token_gated, saved,
              tracks, gain_at, count, collective):
    width, tokens = mid.shape
    half = tokens // 2
    hidden = down_weight[0].shape[2]
    gathered = grad.ndim == 3
    units, gelus, slopes = saved
    own_loads = tuple(range(11, 11 + len(tracks)))
    carries = tuple(range(11 + len(tracks), 11 + len(ring_operands(tracks))))
    manual = (2, 3) + ((0,) if gathered else ()) + carries
    return fused_call(
        lambda *refs: feed_back_kernel(gain_at, gathered, tracks, *refs),
        [grad, down_weight, gelus, slopes, up_columns, out_weight, mid, gains, token_gated, units]
        + [normed]
        + ring_operands(tracks),
        [
            ((width, tokens), F32),
            ((width // 4, 4 * tokens), BF16),
            ((count, 3 * width // count, hidden), BF16),
            ((width, width), BF16),
            ((width, 8), F32),
        ]
        + [one.out() for one in tracks],
        [pltpu.VMEM((8, width, half), BF16)] * (not gathered)
        + [
            pltpu.VMEM((8, 2 * hidden, half), BF16),
            pltpu.VMEM((width, tokens), BF16),
            pltpu.VMEM((width, half), F32),
            pltpu.VMEM((2, width, half), F32),
            pltpu.VMEM((max(hidden, width), width), BF16),
        ]
        + scatter_buffers(width, half)
        + [pltpu.SemaphoreType.DMA((2, 3))] * 2
        + [pltpu.SemaphoreType.DMA((3, 2))] * 4
        + [pltpu.SemaphoreType.DMA((3, 8))]
        + ring_scratch(tracks),
        collective,
        "feed_back",
        [1] * (5 + len(tracks)),
        manual=manual,
        order=((0,) if not gathered else ()) + (1, 4) + own_loads,
    )


def project_back_kernel(gain_at, each, tracks, io, project_grad, weight_ref, square_ref, normed,
                        state_ref, x_ref, gains_ref, *refs):
    inputs = len(ring_operands(tracks))
    ring_in, refs = refs[:inputs], refs[inputs:]
    next_ref, in_grad, sums_ref = refs[:3]
    large, refs = refs[3 : 3 + len(tracks)], refs[3 + len(tracks) :]
    kept, own, weight_rows, in_full, *rest = refs
    buffers, (scatter_send, scatter_recv, *ring_rest) = rest[:6], rest[6:]
    scatter_sems = (scatter_send, scatter_recv)
    peers = chan_peers()
    me, mate, across, diag = peers
    sources = [io.source[7 + n] for n in range(inputs)]
    ring = Ring(tracks, ring_in, large, ring_rest, sources)
    width, tokens = x_ref.shape
    half = tokens // 2
    rows = weight_ref.shape[0]
    shard = rows // 3
    greet((mate, across), ring.toward)
    ring.start()
    io.ready(1)
    for first, size in ((0, 512), (512, rows - 512)):
        weight_rows[:, first : first + size] = weight_ref[first : first + size].T
    io.ready(0)

    def share(owner, part):
        return matmul(weight_rows[...], project_grad[:, span(owner * 2 + part, half)])

    for part in range(2):
        buffers[0][part] = share(diag, part).astype(BF16)
        scatter_copy(peers, buffers, scatter_sems, 0, part).start()
        kept[...] = share(across, part)
        scatter_copy(peers, buffers, scatter_sems, 0, part).wait_recv()
        buffers[4][part] = (kept[...] + buffers[1][part].astype(F32)).astype(BF16)
        scatter_copy(peers, buffers, scatter_sems, 2, part).start()
    for part in range(2):
        buffers[2][part] = share(mate, part).astype(BF16)
        scatter_copy(peers, buffers, scatter_sems, 1, part).start()
        own[part] = share(me, part)
    io.ready(*range(7, 7 + len(tracks)))
    ring.advance(0, 3)
    io.ready(2, 3)
    if in_full.shape[1] > 4 * each:
        in_full[...] = jnp.zeros_like(in_full)
    for chunk in range(shard // each):
        in_full[chunk, 3 * each : 4 * each] = square_ref[chunk * each : (chunk + 1) * each]
    tile = 256
    for stream in range(3):
        def column_tile(n, carry):
            column = span(n, tile)
            total = None
            for block in range(8):
                left = project_grad[
                    stream * shard : (stream + 1) * shard, block * half : (block + 1) * half
                ]
                value = matmul_nt(left, normed[block, column])
                total = value if total is None else total + value
            for chunk in range(shard // each):
                in_full[chunk, stream * each : (stream + 1) * each, column] = total[
                    chunk * each : (chunk + 1) * each
                ]
            return carry

        lax.fori_loop(0, width // tile, column_tile, 0)
    ring.advance(1, 3)
    in_grad[...] = in_full[...].astype(BF16)
    io.flush(1)
    io.ready(4, 5, 6)
    gain = gains_ref[:, gain_at : gain_at + 1]
    for part in range(2):
        columns = slice(part * half, (part + 1) * half)
        grad = scattered(peers, scatter_sems, buffers, own, part)
        change, product = norm_pullback(grad, x_ref[:, columns], gain)
        next_ref[:, columns] = state_ref[:, columns] + change
        if part == 0:
            sums_ref[:, 0:1] = lane_sums(product)
            sums_ref[:, 1:2] = lane_sums(grad)
            ring.advance(2, 3)
        else:
            sums_ref[:, 0:1] = sums_ref[:, 0:1] + lane_sums(product)
            sums_ref[:, 1:2] = sums_ref[:, 1:2] + lane_sums(grad)
    io.flush(0)
    io.flush(2)
    ring.finish()
    for n in range(len(tracks)):
        io.flush(3 + n)
    drain_scatter(peers, scatter_sems, buffers)


def project_back(project_grad, state, values, gains, normed, weight, square, tracks, gain_at,
                 collective):
    width, tokens = values.shape
    half = tokens // 2
    rows = project_grad.shape[0]
    count = tracks[0].count
    each = rows // 3 // count
    packed = (count, ring_rows(4 * each), width)
    return fused_call(
        lambda *refs: project_back_kernel(gain_at, each, tracks, *refs),
        [project_grad, weight, square, normed, state, values, gains] + ring_operands(tracks),
        [((width, tokens), F32), (packed, BF16), ((width, 8), F32)]
        + [one.out() for one in tracks],
        [
            pltpu.VMEM((width, half), F32),
            pltpu.VMEM((2, width, half), F32),
            pltpu.VMEM((width, rows), BF16),
            pltpu.VMEM(packed, F32),
        ]
        + scatter_buffers(width, half)
        + [pltpu.SemaphoreType.DMA((3, 2))] * 2
        + ring_scratch(tracks),
        collective,
        "project_back",
        [1] * (3 + len(tracks)),
        manual=tuple(range(7 + len(tracks), 7 + len(ring_operands(tracks)))),
        order=(1, 0) + tuple(range(7, 7 + len(tracks))),
    )


def mask_heads(values, keep, blocks):
    length = values.shape[1] // blocks
    pieces = []
    for j in range(blocks):
        start = j * length
        pieces.append(values[:, start : start + 128] * keep[:, start : start + 128])
        pieces.append(values[:, start + 128 : start + length])
    return jnp.concatenate(pieces, axis=1)


def eight(rows):
    return pl.ds(pl.multiple_of(rows, 8), 8)


def sixteen(rows):
    return pl.ds(pl.multiple_of(rows, 16), 16)


def stream_rows(project_ref, columns_ref, keep_ref, rows, shard, stream, blocks):
    values = project_ref[eight(stream * shard + rows), :]
    total = values * columns_ref[eight(rows), stream : stream + 1]
    for offset in (1, 2):
        moved = mask_heads(pltpu.roll(values, offset, 1), keep_ref[offset - 1 : offset, :], blocks)
        column = 3 * offset + stream
        total = total + moved * columns_ref[eight(rows), column : column + 1]
    return total


def sequence_factor(power, cond, facts, blocks):
    energy = []
    for i in range(blocks):
        total = 0.0
        for j in range(blocks):
            total = total + power[j] * facts.same[i][j]
        energy.append(total * facts.inverse)
    logs = [jnp.log(1.0 + value) for value in energy]
    factor = [
        (1.0 + cond * value) * facts.same[i][i] for i, value in enumerate(logs)
    ]
    return energy, logs, factor


def block_sums(values, blocks):
    length = values.shape[1] // blocks
    return [lane_sums(values[:, i * length : (i + 1) * length]) for i in range(blocks)]


def spread_blocks(columns, length):
    return jnp.concatenate(
        [jnp.broadcast_to(column, (column.shape[0], length)) for column in columns], axis=1
    )


def plain_bins(spectrum_ref, rows, shard, blocks):
    half = spectrum_ref.shape[1] // 2
    bins = []
    for k in range(blocks):
        here = spectrum_ref[eight(k * shard + rows), :]
        bins.append((here[:, :half], here[:, half:]))
    return bins


def filter_bins(spectrum_ref, sign, rows, shard, blocks):
    plain = plain_bins(spectrum_ref, rows, shard, blocks)
    bins = [plain[0]]
    for k in range(1, blocks):
        (real, imag), (before_real, before_imag) = plain[k], plain[k - 1]
        bins.append((real - sign * before_imag, imag + sign * before_real))
    return bins


def store_blocks(target, values, rows, shard, blocks):
    length = values.shape[1] // blocks
    for j in range(blocks):
        target[sixteen(j * shard + rows), :] = values[:, j * length : (j + 1) * length]


def join(halves):
    return jnp.concatenate(halves, axis=0).astype(BF16)


def channel_cuts(shard, streams):
    size = shard // LOADS
    return [(s * shard + n * size, size) for n in range(LOADS) for s in range(streams)]


def channel_order(numbers, streams=3):
    order = []
    for n in range(LOADS):
        for number in numbers:
            each = streams if number == 1 else 1
            order += [(number, n * each + i) for i in range(each)]
    return tuple(order)


def conv_forward_kernel(blocks, carries, io, filter_ref, project_ref, columns_ref, keep_ref,
                        sign_ref, table_ref, seq_ref, carried_in, back_ref, gated_ref, conv_ref, carried,
                        signal_low, filter_low, signal_bins, filter_spectrum, out_low, convolved,
                        factor_ref, *sems):
    shard, slots = gated_ref.shape
    length = slots // blocks
    scale = 1.0 / length
    steps = shard // 16
    peers = chan_peers()
    me = peers[0]
    parts = carried.shape[0]
    facts = Facts(seq_ref, blocks, length)
    greet(peers[1:])

    def gather(kind, part):
        return gather_copy(
            lambda owner, part: carried.at[part, span(owner, shard, 32), :],
            peers, sems, kind, part,
        )

    def forward(first, last):
        for part in range(parts * first // 8, parts * last // 8):
            gather(0, part).wait_recv()
            gather(2, part).start()

    io.ready(7)
    for part in range(parts):
        if carries == 1:
            carried[part, span(me, shard, 32), :] = carried_in[part]
        else:
            lanes = carried.shape[2]
            carried[part, span(me, shard, 32), :] = carried_in[:, part * lanes : (part + 1) * lanes]
        for kind in range(2):
            gather(kind, part).start()
    io.ready(2, 3, 4)

    def prepare(n, carry):
        rows = n * 16
        signals = []
        for part in range(2):
            here = rows + 8 * part
            one, two = (
                stream_rows(project_ref, columns_ref, keep_ref, here, shard, stream, blocks)
                for stream in (1, 2)
            )
            signals.append(one * two)
            cond = columns_ref[eight(here), 9:10]
            _, _, factor = sequence_factor(block_sums(two * two, blocks), cond, facts, blocks)
            for j in range(blocks):
                factor_ref[eight(here), j : j + 1] = factor[j]
        store_blocks(signal_low, join(signals), rows, shard, blocks)
        kernel = filter_ref[sixteen(rows), :].astype(BF16)
        store_blocks(filter_low, kernel, rows, shard, blocks)
        return carry

    for n in range(LOADS):
        io.ready(0, cuts=slice(n, n + 1))
        io.ready(1, cuts=slice(3 * n, 3 * n + 3))
        lax.fori_loop(steps * n // LOADS, steps * (n + 1) // LOADS, prepare, 0)
    io.ready(5)
    signal_bins[...] = matmul(signal_low[...], table_ref[...])
    forward(0, 2)
    filter_spectrum[...] = matmul(filter_low[...], table_ref[...])
    forward(2, 3)

    def combine(n, carry):
        rows = n * 16
        joined = [[] for _ in range(blocks)]
        for part in range(2):
            here = rows + 8 * part
            window = filter_bins(filter_spectrum, sign_ref[0:1, :], here, shard, blocks)
            signal = plain_bins(signal_bins, here, shard, blocks)
            for i in range(blocks):
                real = imag = None
                for j in range(i, -1, -1):
                    fr, fi = window[i - j]
                    sr, si = signal[j]
                    more_real, more_imag = fr * sr - fi * si, fr * si + fi * sr
                    if j == i:
                        real, imag = more_real, more_imag
                    else:
                        factor = facts.same[i][j]
                        real, imag = real + more_real * factor, imag + more_imag * factor
                joined[i].append(jnp.concatenate([real, imag], axis=1))
        for i in range(blocks):
            out_low[sixteen(i * shard + rows), :] = join(joined[i])
        return carry

    lax.fori_loop(0, steps, combine, 0)
    forward(3, 5)
    io.ready(8)
    convolved[...] = matmul(out_low[...], back_ref[...]) * scale
    forward(5, 6)

    def finish(n, carry):
        rows = n * 16
        gated = []
        for part in range(2):
            here = rows + 8 * part
            zero = stream_rows(project_ref, columns_ref, keep_ref, here, shard, 0, blocks)
            pieces = []
            for j in range(blocks):
                source = convolved[eight(j * shard + here), :]
                columns = slice(j * length, (j + 1) * length)
                conv_ref[eight(here), columns] = source
                pieces.append(zero[:, columns] * (source * factor_ref[eight(here), j : j + 1]))
            gated.append(jnp.concatenate(pieces, axis=1))
        gated_ref[sixteen(rows), :] = join(gated)
        return carry

    lax.fori_loop(0, steps // 2, finish, 0)
    forward(6, 7)
    top, rest = pl.ds(0, shard // 2), pl.ds(shard // 2, shard // 2)
    io.flush(0, 0, top)
    io.flush(1, 0, top)
    lax.fori_loop(steps // 2, steps, finish, 0)
    io.flush(0, 1, rest)
    io.flush(1, 1, rest)
    forward(7, 8)
    for part in range(parts):
        for kind in (1, 2):
            gather(kind, part).wait_recv()
        io.flush(2, part, part)
    for part in range(parts):
        for kind in range(3):
            gather(kind, part).wait_send()


def conv_forward(project, filter_rows, columns, keep, sign, table, seq_table, back, carried,
                 carries, blocks, collective):
    shard, slots = filter_rows[0].shape[1:]
    width = 4 * shard
    length = slots // blocks
    low = pltpu.VMEM((blocks * shard, length), BF16)
    bins = pltpu.VMEM((blocks * shard, 2 * length), F32)
    if carries == 1:
        out = ((carried.shape[0], width, width), BF16)
    else:
        out = ((8, width, slots // 8), BF16)
    return fused_call(
        lambda *refs: conv_forward_kernel(blocks, carries, *refs),
        [filter_rows, project, columns, keep, sign, table, seq_table, carried, back],
        [((shard, slots), BF16), ((shard, slots), F32), out],
        [
            low,
            low,
            bins,
            bins,
            pltpu.VMEM((blocks * shard, 2 * length), BF16),
            pltpu.VMEM((blocks * shard, length), F32),
            pltpu.VMEM((shard, 128), F32),
        ]
        + [pltpu.SemaphoreType.DMA((3, out[0][0]))] * 2,
        collective,
        "conv_forward",
        [2, 2, out[0][0]],
        6,
        (7, 2, 3, 4) + channel_order((1, 0)) + (5, 8),
        {0: channel_cuts(shard, 1), 1: channel_cuts(shard, 3)},
    )


def conv_backward_kernel(blocks, tracks, with_outputs, io, grad_ref, project_ref, conv_ref,
                         filter_ref, columns_ref, keep_ref, sign_ref, table_ref, seq_ref,
                         square_ref, *refs):
    refs = list(refs)
    back_ref = refs.pop(len(ring_operands(tracks)) + with_outputs)
    rings = len(tracks)
    inputs = len(ring_operands(tracks))
    ring_in, refs = refs[:inputs], refs[inputs:]
    if with_outputs:
        residual_ref = refs.pop(0)
    project_grad, filter_pack, square_sum, sums_ref = refs[:4]
    large, refs = refs[4 : 4 + rings], refs[4 + rings :]
    if with_outputs:
        outputs_ref = refs.pop(0)
        *refs, out_land, out_send, out_recv = refs
    sources = [io.source[10 + n] for n in range(inputs)]
    ring = Ring(tracks, ring_in, large, refs[-rings - 2 :], sources)
    refs = refs[: -rings - 2]
    signal_low, filter_low, grad_low, signal_bins, filter_spectrum, grad_bins, *refs = refs
    signal_out, filter_out, mixed, energy_ref, square_land, square_send, square_recv = refs
    signal_grad = filter_spectrum.at[:, : filter_spectrum.shape[1] // 2]
    peers = chan_peers()
    greet(peers[1:], ring.toward)
    ring.start()
    copies = exchange(
        peers, lambda peer: io.source[9].at[peer], lambda: square_land.at[peers[0]],
        square_send, square_recv,
    )
    if with_outputs:
        copies += to_channels(
            peers, io.source[10 + inputs], out_land, out_send, out_recv
        )
    io.ready(4, 5, 6)
    shard, slots = grad_ref.shape
    length = slots // blocks
    scale = 1.0 / length
    steps = shard // 16
    facts = Facts(seq_ref, blocks, length)

    def prepare(n, carry):
        rows = n * 16
        signals, scaled = [], []
        grads = grad_ref[sixteen(rows), :].astype(F32)
        for part in range(2):
            here = rows + 8 * part
            zero, one, two = (
                stream_rows(project_ref, columns_ref, keep_ref, here, shard, stream, blocks)
                for stream in range(3)
            )
            mixed[0, eight(here), :] = one
            mixed[1, eight(here), :] = two
            signals.append(one * two)
            cond = columns_ref[eight(here), 9:10]
            power = block_sums(two * two, blocks)
            energy, logs, factor = sequence_factor(power, cond, facts, blocks)
            conv_grad = grads[8 * part : 8 * part + 8] * zero
            factor_grad = block_sums(conv_grad * conv_ref[eight(here), :], blocks)
            cond_grad = 0.0
            for j in range(blocks):
                cond_grad = cond_grad + factor_grad[j] * logs[j]
            sums_ref[eight(here), 9:10] = cond_grad
            for i in range(blocks):
                total = 0.0
                for j in range(blocks):
                    total = total + factor_grad[j] * facts.same[i][j]
                energy_ref[eight(here), i : i + 1] = (
                    total * cond / (1.0 + energy[i]) * (2.0 * facts.inverse)
                )
                energy_ref[eight(here), blocks + i : blocks + i + 1] = factor[i]
            scaled.append(conv_grad * spread_blocks([one * scale for one in factor], length))
        store_blocks(signal_low, join(signals), rows, shard, blocks)
        store_blocks(grad_low, join(scaled), rows, shard, blocks)
        kernel = filter_ref[sixteen(rows), :].astype(BF16)
        store_blocks(filter_low, kernel, rows, shard, blocks)
        return carry

    for n in range(LOADS):
        for number, each in ((0, 1), (1, 3), (2, 1), (3, 1)):
            io.ready(number, cuts=slice(n * each, (n + 1) * each))
        lax.fori_loop(steps * n // LOADS, steps * (n + 1) // LOADS, prepare, 0)
    io.ready(7)
    io.ready(*range(10, 10 + rings))
    grad_bins[...] = matmul(grad_low[...], table_ref[...])
    signal_bins[...] = matmul(signal_low[...], table_ref[...])
    filter_spectrum[...] = matmul(filter_low[...], table_ref[...])
    ring.advance(0, 3)

    def combine(n, carry):
        rows = n * 16
        sign = sign_ref[0:1, :]
        joined = [[] for _ in range(blocks)]
        windows = [[] for _ in range(blocks)]
        for part in range(2):
            here = rows + 8 * part
            window = filter_bins(filter_spectrum, sign, here, shard, blocks)
            signal = plain_bins(signal_bins, here, shard, blocks)
            grads = plain_bins(grad_bins, here, shard, blocks)
            for j in range(blocks):
                for i in range(j, blocks):
                    fr, fi = window[i - j]
                    gr, gi = grads[i]
                    more_real, more_imag = fr * gr + fi * gi, fr * gi - fi * gr
                    if i == j:
                        real, imag = more_real, more_imag
                    else:
                        factor = facts.same[i][j]
                        real, imag = real + more_real * factor, imag + more_imag * factor
                joined[j].append(jnp.concatenate([real, imag], axis=1))
            after = None
            for k in reversed(range(blocks)):
                real = imag = None
                for j in range(blocks - k):
                    sr, si = signal[j]
                    gr, gi = grads[j + k]
                    more_real, more_imag = sr * gr + si * gi, sr * gi - si * gr
                    if k:
                        factor = facts.same[j + k][j]
                        more_real, more_imag = more_real * factor, more_imag * factor
                    real = more_real if real is None else real + more_real
                    imag = more_imag if imag is None else imag + more_imag
                if after is None:
                    whole = (real, imag)
                else:
                    whole = (real + sign * after[1], imag - sign * after[0])
                windows[k].append(jnp.concatenate(whole, axis=1))
                after = (real, imag)
        for j in range(blocks):
            signal_out[sixteen(j * shard + rows), :] = join(joined[j])
            filter_out[sixteen(j * shard + rows), :] = join(windows[j])
        return carry

    lax.fori_loop(0, steps, combine, 0)
    io.ready(10 + inputs + with_outputs)
    signal_grad[...] = matmul(signal_out[...], back_ref[...])
    ring.advance(1, 3)
    filter_rows = matmul(filter_out[...], back_ref[...])
    count, pack_rows, lanes = filter_pack.shape
    each = shard // count
    stack = slots // lanes
    if pack_rows > stack * each:
        filter_pack[...] = jnp.zeros_like(filter_pack)
    for chunk in range(count):
        lags = [
            filter_rows[j * shard + chunk * each : j * shard + (chunk + 1) * each]
            for j in range(blocks)
        ]
        layers = [
            jnp.concatenate(lags[n * blocks // stack : (n + 1) * blocks // stack], axis=1)
            for n in range(stack)
        ]
        value = layers[0] if stack == 1 else jnp.concatenate(layers, axis=0)
        filter_pack[chunk, : stack * each] = value.astype(BF16)
    io.flush(1)

    def finish(n, carry):
        rows = n * 16
        totals = [[] for _ in range(3)]
        outer = grad_ref[sixteen(rows), :].astype(F32)
        for part in range(2):
            here = rows + 8 * part
            local = eight(here)
            factor = [energy_ref[local, blocks + i : blocks + i + 1] for i in range(blocks)]
            energy = [energy_ref[local, i : i + 1] for i in range(blocks)]
            signal = jnp.concatenate(
                [signal_grad[eight(j * shard + here), :] for j in range(blocks)], axis=1
            )
            for stream in range(3):
                if stream == 0:
                    value = outer[8 * part : 8 * part + 8] * (
                        conv_ref[local, :] * spread_blocks(factor, length)
                    )
                elif stream == 1:
                    value = signal * mixed[1, local, :]
                else:
                    value = signal * mixed[0, local, :] + (
                        spread_blocks(energy, length) * mixed[1, local, :]
                    )
                plain = project_ref[eight(stream * shard + here), :]
                total = value * columns_ref[local, stream : stream + 1]
                sums_ref[local, stream : stream + 1] = lane_sums(value * plain)
                for offset in (1, 2):
                    column = 3 * offset + stream
                    moved = pltpu.roll(
                        mask_heads(value, keep_ref[offset - 1 : offset, :], blocks),
                        slots - offset, 1,
                    )
                    sums_ref[local, column : column + 1] = lane_sums(moved * plain)
                    total = total + moved * columns_ref[local, column : column + 1]
                totals[stream].append(total)
        for stream in range(3):
            project_grad[sixteen(stream * shard + rows), :] = join(totals[stream])
        return carry

    lax.fori_loop(0, steps // 2, finish, 0)
    ring.advance(2, 3)
    lax.fori_loop(steps // 2, steps, finish, 0)
    for stream in range(3):
        io.flush(0, stream, pl.ds(stream * shard, shard))
    for copy in copies:
        copy.wait()
    io.ready(9)
    total = square_ref[peers[0]].astype(F32)
    for peer in peers[1:]:
        total = total + square_land[peer].astype(F32)
    square_sum[...] = total
    io.flush(2)
    if with_outputs:
        io.ready(10 + inputs)
        tokens = residual_ref.shape[1]
        out_land[:, span(peers[0], tokens)] = residual_ref[span(peers[0], shard, 32), :]
        outputs_ref[...] = out_land[...].astype(F32)
        io.flush(4 + rings)
    io.flush(3)
    ring.finish()
    for n in range(rings):
        io.flush(4 + n)


def filter_layout(shard, slots, count):
    each = shard // count
    stack = 2 if each % 8 == 0 else 1
    return count, ring_rows(stack * each), slots // stack


def conv_backward(grad, project, conv, filter_rows, columns, keep, sign, table, seq_table, back, square,
                  tracks, residual, blocks, collective):
    shard, slots = filter_rows[0].shape[1:]
    length = slots // blocks
    low = pltpu.VMEM((blocks * shard, length), BF16)
    bins = pltpu.VMEM((blocks * shard, 2 * length), F32)
    out = pltpu.VMEM((blocks * shard, 2 * length), BF16)
    outs, extra = [], []
    if residual:
        outs = [((shard, slots), F32)]
        extra = [pltpu.VMEM((shard, slots), BF16)] + [pltpu.SemaphoreType.DMA((3,))] * 2
    return fused_call(
        lambda *refs: conv_backward_kernel(blocks, tracks, bool(residual), *refs),
        [grad, project, conv, filter_rows, columns, keep, sign, table, seq_table, square]
        + ring_operands(tracks)
        + list(residual)
        + [back],
        [
            ((3 * shard, slots), BF16),
            (filter_layout(shard, slots, tracks[0].count), BF16),
            ((shard, 4 * shard), F32),
            ((shard, 128), F32),
        ]
        + [one.out() for one in tracks]
        + outs,
        [low, low, low, bins, bins, bins, out, out]
        + [pltpu.VMEM((2, shard, slots), F32), pltpu.VMEM((shard, 128), F32)]
        + [pltpu.VMEM(square.shape, BF16)]
        + [pltpu.SemaphoreType.DMA((3,))] * 2
        + ring_scratch(tracks)
        + extra,
        collective,
        "conv_backward",
        [3, 1, 1, 1] + [1] * (len(tracks) + len(outs)),
        8,
        (4, 5, 6) + channel_order((0, 1, 2, 3)) + (7,),
        {0: channel_cuts(shard, 1), 1: channel_cuts(shard, 3), 2: channel_cuts(shard, 1)}
        | {3: channel_cuts(shard, 1)},
        tuple(range(10 + len(tracks), 10 + len(ring_operands(tracks)))),
    )


def last_kernel(layers, tracks, io, state_ref, *refs):
    refs = list(refs)
    gain_sums, refs = refs[: 2 * layers], refs[2 * layers :]
    row_sums, refs = refs[:layers], refs[layers:]
    rings, inputs = len(tracks), len(ring_operands(tracks))
    ring_in, refs = refs[:inputs], refs[inputs:]
    input_grad, small_out = refs[:2]
    large, refs = refs[2 : 2 + rings], refs[2 + rings :]
    state_low, landing, sums, turn, gains, gains_land, small_own, small_land, *refs = refs
    chan_send, chan_recv, small_send, small_recv, state_send, state_recv, *refs = refs
    peers = chan_peers()
    me = peers[0]
    dp = lax.axis_index("dp")
    first = 1 + 3 * layers
    ring = Ring(tracks, ring_in, large, refs, [io.source[first + n] for n in range(inputs)])
    count = ring.count
    shard = landing.shape[0]
    greet(peers[1:], [(dp + offset) % count for offset in range(1, count)])
    ring.start()
    io.ready(*range(0, first))
    for layer in range(layers):
        sums[:, 4 * layer : 4 * layer + 2] = gain_sums[2 * layer][:, 0:2]
        sums[:, 4 * layer + 2 : 4 * layer + 4] = gain_sums[2 * layer + 1][:, 0:2]
    turn[...] = jnp.zeros_like(turn)
    for owner in range(4):
        turn[:shard, : 4 * layers] = sums[owner * shard : (owner + 1) * shard, : 4 * layers]
        gains[owner] = turn[...].T[: 4 * layers]
    copies = exchange(
        peers, lambda peer: gains.at[peer], lambda: gains_land.at[me], chan_send, chan_recv
    )
    state_low[...] = state_ref[...].astype(BF16)
    state_copies = to_channels(peers, state_low, landing, state_send, state_recv)
    landing[:, span(me, state_low.shape[1])] = state_low[span(me, shard, 32), :]
    io.ready(*range(first, first + rings))
    ring.advance(0, 6)
    for layer in range(layers):
        turn[:shard, 10 * layer : 10 * layer + 10] = row_sums[layer][:, 0:10]
    small_own[4 * layers :, :] = turn[...].T[: small_own.shape[0] - 4 * layers]
    for copy in copies:
        copy.wait()
    total = gains[me]
    for peer in peers[1:]:
        total = total + gains_land[peer]
    small_own[: 4 * layers, :] = total
    small_copies = []
    for offset in range(1, count):
        copy = pltpu.make_async_remote_copy(
            small_own,
            small_land.at[offset - 1],
            small_send.at[offset - 1],
            small_recv.at[offset - 1],
            device_id={"dp": (dp + offset) % count},
        )
        copy.start()
        small_copies.append(copy)
    for point in range(1, 4):
        ring.advance(point, 6)
    small = small_own[...]
    for copy in small_copies:
        copy.wait()
    for n in range(count - 1):
        small = small + small_land[n]
    small_out[...] = small
    io.flush(1)
    ring.advance(4, 6)
    for copy in state_copies:
        copy.wait()
    input_grad[...] = landing[...].astype(F32)
    io.flush(0)
    ring.advance(5, 6)
    ring.finish()
    for n in range(rings):
        io.flush(2 + n)


def last_sums(state, gain_sums, row_sums, tracks, collective):
    width, tokens = state.shape
    shard = width // 4
    layers = len(row_sums)
    count = tracks[0].count
    small = (-(-14 * layers // 8) * 8, 256)
    return fused_call(
        lambda *refs: last_kernel(layers, tracks, *refs),
        [state] + gain_sums + row_sums + ring_operands(tracks),
        [((shard, 4 * tokens), F32), (small, F32)] + [one.out() for one in tracks],
        [
            pltpu.VMEM((width, tokens), BF16),
            pltpu.VMEM((shard, 4 * tokens), BF16),
            pltpu.VMEM((width, 128), F32),
            pltpu.VMEM((256, 128), F32),
            pltpu.VMEM((4, 4 * layers, 256), F32),
            pltpu.VMEM((4, 4 * layers, 256), F32),
            pltpu.VMEM(small, F32),
            pltpu.VMEM((count - 1,) + small, F32),
            pltpu.SemaphoreType.DMA((3,)),
            pltpu.SemaphoreType.DMA((3,)),
            pltpu.SemaphoreType.DMA((count - 1,)),
            pltpu.SemaphoreType.DMA((count - 1,)),
            pltpu.SemaphoreType.DMA((3,)),
            pltpu.SemaphoreType.DMA((3,)),
        ]
        + ring_scratch(tracks),
        collective,
        "last_sums",
        [1] * (2 + len(tracks)),
        order=tuple(range(1, 1 + 3 * layers)) + (0,),
        manual=tuple(
            range(1 + 3 * layers + len(tracks), 1 + 3 * layers + len(ring_operands(tracks)))
        ),
    )


def collect_kernel(layers, *refs):
    refs = list(refs)
    outputs_in, input_in, small = refs[:3]
    refs = refs[3:]
    feeds, refs = refs[:layers], refs[layers:]
    filters, refs = refs[:layers], refs[layers:]
    packs, refs = refs[:layers], refs[layers:]
    (outputs, input_grad, mix_gain, mix_bias, in_grad, short, filter_grad, cond, out_grad, glu_gain,
     glu_bias, up_grad, down_grad, held, sems) = refs
    pairs = ((outputs_in, outputs), (input_in, input_grad))
    loads = [
        pltpu.make_async_copy(source, held.at[n], sems.at[n]) for n, (source, _) in enumerate(pairs)
    ]
    copies = [
        pltpu.make_async_copy(held.at[n], target, sems.at[2 + n])
        for n, (_, target) in enumerate(pairs)
    ]
    for copy in loads:
        copy.start()
    each = in_grad.shape[1]
    shard = cond.shape[1]
    lanes = filters[0].shape[1]
    for layer in range(layers):
        for kind, out in enumerate((mix_gain, mix_bias, glu_gain, glu_bias)):
            row = 4 * layer + kind
            out[layer : layer + 1, :] = small[row : row + 1, :shard]
        row = 4 * layers + 10 * layer
        for tap in range(3):
            short[layer, tap] = small[row + 3 * tap : row + 3 * tap + 3, :shard]
        cond[layer : layer + 1, :] = small[row + 9 : row + 10, :shard]
        for stream in range(3):
            in_grad[layer, :, stream, :] = packs[layer][stream * each : (stream + 1) * each]
        out_grad[layer] = packs[layer][3 * each : 4 * each]
        for n in range(filter_grad.shape[2] // lanes):
            filter_grad[layer, :, n * lanes : (n + 1) * lanes] = filters[layer][
                n * each : (n + 1) * each
            ]
        rows = down_grad.shape[1]
        down_grad[layer] = feeds[layer][:rows]
        for kind in range(2):
            up_grad[layer, :, kind, :] = feeds[layer][(kind + 1) * rows : (kind + 2) * rows]
        loads[layer].wait()
        copies[layer].start()
    for copy in copies:
        copy.wait()


def collect(outputs, input_grad, small, feeds, filters, packs, each):
    layers = len(feeds)
    shard, slots = outputs.shape
    width = 4 * shard
    rows, hidden = feeds[0].shape[0] // 3, feeds[0].shape[1]
    anywhere = pl.BlockSpec(memory_space=pl.ANY)
    local = pl.BlockSpec(memory_space=pltpu.VMEM)
    operands = [outputs, input_grad, small, *feeds, *filters, *packs]
    small_shape = (layers, shard)
    shapes = [
        (shard, slots), (shard, slots), small_shape, small_shape, (layers, each, 3, width),
        (layers, 3, 3, shard), (layers, each, slots), small_shape, (layers, each, width),
        small_shape, small_shape, (layers, rows, 2, hidden), (layers, rows, hidden),
    ]
    return pl.pallas_call(
        lambda *refs: collect_kernel(layers, *refs),
        out_shape=tuple(jax.ShapeDtypeStruct(shape, F32) for shape in shapes),
        in_specs=[anywhere] * 2 + [local] * (len(operands) - 2),
        out_specs=tuple([anywhere] * 2 + [local] * (len(shapes) - 2)),
        scratch_shapes=[pltpu.VMEM((2, shard, slots), F32), pltpu.SemaphoreType.DMA((4,))],
        compiler_params=pltpu.CompilerParams(vmem_limit_bytes=VMEM_LIMIT),
        name="collect",
    )(*operands)


def body(
    inputs,
    seq_table,
    mix_gain,
    mix_bias,
    in_proj,
    short_conv,
    long_filter,
    cond_weight,
    out_proj,
    glu_gain,
    glu_bias,
    glu_in,
    glu_out,
    cotangent,
):
    shard, slots = inputs.shape
    layers, width = in_proj.shape[0], in_proj.shape[3]
    hidden = glu_out.shape[2]
    blocks = 4
    count = lax.axis_size("dp")
    each = shard // count
    turns = count // 2
    table = jnp.asarray(dft_table(slots // blocks), BF16)
    sign = jnp.asarray(np.tile(1.0 - 2.0 * (np.arange(slots // blocks) % 2), (8, 1)), F32)
    residual, gains, normed, project, in_rows, up_columns, columns, keep = first_project(
        inputs, (mix_gain, mix_bias, glu_gain, glu_bias), in_proj, short_conv, cond_weight,
        (glu_in, 0), seq_table, 1,
    )
    constants = (keep, sign, table, seq_table, jnp.asarray(dft_table(slots // blocks).T, BF16))
    kept, state = [], None
    for l in range(layers):
        gated, conv, carried = conv_forward(
            project, (long_filter, l), (columns, l), *constants, cotangent if l else out_proj,
            2 if l else 1, blocks, 10 + l,
        )
        if l:
            state = carried
        else:
            full_out = carried
        token_gated, middle, normed_glu, after, *rest = feed_forward(
            gated, residual, gains, (full_out, l), up_columns, (glu_out, l),
            ((in_rows, l + 1), (glu_in, l + 1)) if l + 1 < layers else (), 4 * l + 2, 20 + l,
        )
        saved, follow = [up_columns] + rest[:3], rest[3:]
        kept.append((residual, normed, project, conv, token_gated, middle, normed_glu, saved))
        residual = after
        if follow:
            normed, project, up_columns = follow
    feeds, filters, packs, gain_sums, row_sums = ([None] * layers for _ in range(5))
    waiting = []
    for l in reversed(range(layers)):
        before, normed, project, conv, token_gated, middle, normed_glu, saved = kept[l]
        top = l == layers - 1
        state, gated_grad, feed_grads, out_grad, glu_sums, *large = feed_back(
            state, middle, gains, normed_glu, saved[0], (glu_out, l), (full_out, l), token_gated,
            saved[1:], waiting, 4 * l + 2, count, 30 + l,
        )
        if waiting:
            filters[l + 1], packs[l + 1] = large
        project_low, filter_pack, square, row_sums[l], held, *rest = conv_backward(
            gated_grad, project, conv, (long_filter, l), (columns, l), *constants,
            out_grad.reshape(4, shard, width), [Track(feed_grads, 0, turns)],
            (residual,) if top else (), blocks, 40 + l,
        )
        if top:
            outputs = rest[0]
        feed_track = Track(feed_grads, turns, count - 1, held)
        state, in_pack, mix_sums, feeds[l], held = project_back(
            project_low, state, before, gains, normed, (in_rows, l), square,
            [feed_track, Track(filter_pack, 0, turns)], 4 * l, 50 + l,
        )
        waiting = [Track(filter_pack, turns, count - 1, held), Track(in_pack, 0, count - 1)]
        gain_sums[l] = [mix_sums, glu_sums]
    input_grad, small, filters[0], packs[0] = last_sums(
        state, [one for pair in gain_sums for one in pair], row_sums, waiting, 60
    )
    return collect(outputs, input_grad, small, feeds, filters, packs, each)


def solution(mesh):
    in_specs = (
        P("chan", "dp"),
        P("dp", None),
        P(None, "chan"),
        P(None, "chan"),
        P(None, "chan", None, None),
        P(None, None, None, "chan"),
        P(None, "chan", None),
        P(None, "chan"),
        P(None, "chan", None),
        P(None, "chan"),
        P(None, "chan"),
        P(None, None, None, "chan"),
        P(None, None, "chan"),
        P("chan", "dp"),
    )
    out_specs = (
        P("chan", "dp"),
        P("chan", "dp"),
        P(None, "chan"),
        P(None, "chan"),
        P(None, ("chan", "dp"), None, None),
        P(None, None, None, "chan"),
        P(None, ("chan", "dp"), None),
        P(None, "chan"),
        P(None, ("chan", "dp"), None),
        P(None, "chan"),
        P(None, "chan"),
        P(None, "dp", None, "chan"),
        P(None, "dp", "chan"),
    )
    return jax.shard_map(body, mesh=mesh, in_specs=in_specs, out_specs=out_specs, check_vma=False)
```

```python
import math

import jax
import jax.numpy as jnp
import numpy as np
from jax import lax
from jax.experimental import pallas as pl
from jax.experimental.pallas import tpu as pltpu
from jax.sharding import PartitionSpec as P

EPSILON = 1e-05
F32 = jnp.float32
BF16 = jnp.bfloat16
VMEM_LIMIT = 63 * 2**20
LOADS = 4


def dft_table(block_len):
    period = 2 * block_len
    position = np.arange(block_len)[:, None]
    phase = ((2 * np.arange(block_len)[None, :] + 1) * position) % (2 * period)
    phase = phase * (math.pi / period)
    return np.concatenate([np.cos(phase), -np.sin(phase)], axis=1)


class Facts:
    def __init__(self, table_ref, blocks, block_len):
        length, count = table_ref[0, 0], table_ref[0, 1]
        used = length * count
        pair = jnp.where(length >= 2 * block_len, 1.0, 0.0)
        four = jnp.where(length >= 4 * block_len, 1.0, 0.0)
        active = [jnp.where(i * block_len < used, 1.0, 0.0) for i in range(blocks)]
        self.same = [[None] * blocks for _ in range(blocks)]
        for i in range(blocks):
            for j in range(blocks):
                if i == j:
                    self.same[i][j] = active[i]
                else:
                    joined = pair if i // 2 == j // 2 else four
                    self.same[i][j] = active[i] * active[j] * joined
        shortest = 1.0 / block_len
        self.inverse = shortest * (1.0 - 0.5 * pair - 0.25 * four)


class Io:
    def __init__(self, source, loads, stores):
        self.source, self.loads, self.stores, self.pending = source, loads, stores, []

    def ready(self, *numbers, cuts=None):
        for number in numbers:
            for copy in self.loads[number] if cuts is None else self.loads[number][cuts]:
                copy.wait()

    def flush(self, number, part=0, at=None):
        source, target, sems = self.stores[number]
        if at is not None:
            source, target = source.at[at], target.at[at]
        copy = pltpu.make_async_copy(source, target, sems.at[part])
        copy.start()
        self.pending.append(copy)

    def finish(self):
        for copy in self.pending:
            copy.wait()


def fused_call(kernel, operands, outs, scratch, collective, name, parts, scalars=-1, order=(),
               cuts=None, manual=()):
    arrays, layers = [], []
    for operand in operands:
        array, layer = operand if isinstance(operand, tuple) else (operand, None)
        arrays.append(array)
        layers.append(layer)
    cuts = cuts or {}
    inputs, results = len(arrays), len(outs)
    buffers, sems = [], []
    for number, (array, layer) in enumerate(zip(arrays, layers)):
        if number != scalars:
            buffers.append(pltpu.VMEM(array.shape if layer is None else array.shape[1:], array.dtype))
            sems.append(pltpu.SemaphoreType.DMA((len(cuts.get(number, (0,))),)))
    for (shape, dtype), count in zip(outs, parts):
        buffers.append(pltpu.VMEM(shape, dtype))
        sems.append(pltpu.SemaphoreType.DMA((count,)))

    def body(*refs):
        extra = list(refs[inputs + results + len(scratch) :])
        places, marks = extra[: len(buffers)], extra[len(buffers) :]
        sources, loads, stores, views, n = {}, {}, {}, [], 0
        for number in range(inputs):
            if number == scalars:
                views.append(refs[number])
                continue
            source = refs[number]
            if layers[number] is not None:
                source = source.at[layers[number]]
            sources[number] = source
            views.append(places[n])
            if number not in manual:
                pairs = [(source, places[n])]
                if number in cuts:
                    rows = [pl.ds(*one) for one in cuts[number]]
                    pairs = [(source.at[one], places[n].at[one]) for one in rows]
                loads[number] = [
                    pltpu.make_async_copy(*pair, marks[n].at[i]) for i, pair in enumerate(pairs)
                ]
            n += 1
        for number in range(results):
            stores[number] = (places[n], refs[inputs + number], marks[n])
            views.append(places[n])
            n += 1
        started = set()
        for one in list(order) + list(loads):
            number, chosen = one if isinstance(one, tuple) else (one, None)
            for i, copy in enumerate(loads[number]):
                if (chosen is None or i == chosen) and (number, i) not in started:
                    started.add((number, i))
                    copy.start()
        io = Io(sources, loads, stores)
        kernel(io, *views, *refs[inputs + results : inputs + results + len(scratch)])
        io.finish()

    anywhere = pl.BlockSpec(memory_space=pl.ANY)
    scalar_spec = pl.BlockSpec(memory_space=pltpu.SMEM)
    params = {}
    if collective is not None:
        params = dict(collective_id=collective, has_side_effects=True)
    return pl.pallas_call(
        body,
        out_shape=tuple(jax.ShapeDtypeStruct(*out) for out in outs),
        in_specs=[scalar_spec if n == scalars else anywhere for n in range(inputs)],
        out_specs=tuple([anywhere] * results),
        scratch_shapes=list(scratch) + buffers + sems,
        compiler_params=pltpu.CompilerParams(vmem_limit_bytes=VMEM_LIMIT, **params),
        name=name,
    )(*arrays)


def ring_position(index, count):
    odd = index % 2
    return (1 - odd) * (index // 2) + odd * (count - 1 - index // 2)


def ring_member(position, count):
    late = position // (count // 2)
    return (1 - late) * 2 * position + late * (2 * (count - 1 - position) + 1)


def chan_peers():
    me = lax.axis_index("chan")
    mate = me + 1 - 2 * (me % 2)
    across = (me + 2) % 4
    return me, mate, across, (mate + 2) % 4


def greet(peers, members=()):
    barrier = pltpu.get_barrier_semaphore()
    for peer in peers:
        pl.semaphore_signal(barrier, inc=1, device_id={"chan": peer})
    for member in members:
        pl.semaphore_signal(barrier, inc=1, device_id={"dp": member})
    pl.semaphore_wait(barrier, len(peers) + len(members))


def send_to(peer, source, target, send, recv):
    return pltpu.make_async_remote_copy(source, target, send, recv, device_id={"chan": peer})


def span(index, size, unit=None):
    if isinstance(index, int):
        return pl.ds(index * size, size)
    return pl.ds(pl.multiple_of(index * size, unit or size), size)


def gather_copy(place, peers, sems, kind, part):
    me, mate, across, _ = peers
    block = place(across if kind == 2 else me, part)
    send, recv = sems
    return send_to(
        across if kind == 0 else mate, block, block, send.at[kind, part], recv.at[kind, part]
    )


def norm_columns(values):
    mean = jnp.mean(values, axis=0, keepdims=True)
    center = values - mean
    inverse = lax.rsqrt(jnp.mean(center * center, axis=0, keepdims=True) + EPSILON)
    return center * inverse, inverse


def norm_pullback(grad, values, gain):
    normal, inverse = norm_columns(values)
    product = grad * normal
    scaled = grad * gain
    first = jnp.mean(scaled, axis=0, keepdims=True)
    second = jnp.mean(product * gain, axis=0, keepdims=True)
    return inverse * (scaled - first - normal * second), product


def lane_sums(values):
    return jnp.sum(values, axis=1, keepdims=True)


def matmul(left, right):
    return jnp.dot(left, right, preferred_element_type=F32)


def matmul_nt(left, right):
    return lax.dot_general(
        left, right, (((1,), (1,)), ((), ())), preferred_element_type=F32
    )


def transpose_into(target, source, tile):
    for n in range(source.shape[0] // tile):
        target[:, n * tile : (n + 1) * tile] = source[n * tile : (n + 1) * tile].T


def transpose_columns(target, source, tile):
    for n in range(source.shape[1] // tile):
        target[n * tile : (n + 1) * tile, :] = source[:, n * tile : (n + 1) * tile].T


def exchange(peers, source, target, send, recv):
    copies = []
    for n, peer in enumerate((peers[2], peers[3], peers[1])):
        copy = send_to(peer, source(peer), target(), send.at[n], recv.at[n])
        copy.start()
        copies.append(copy)
    return copies


def to_channels(peers, low, landing, send, recv):
    shard, tokens = landing.shape[0], low.shape[1]
    me = peers[0]
    mine = span(me, tokens)
    copies = exchange(
        peers, lambda peer: low.at[span(peer, shard, 32), :], lambda: landing.at[:, mine], send, recv
    )
    return copies


def to_tokens(peers, low, landing, send, recv):
    shard, half = low.shape[0], landing.shape[1] // 2
    mine = span(peers[0], shard, 32)
    copies = [
        exchange(
            peers, lambda peer: low.at[:, span(peer * 2 + part, half)],
            lambda: landing.at[mine, pl.ds(part * half, half)], send.at[part], recv.at[part],
        )
        for part in range(2)
    ]
    landing[mine, :] = low[:, span(peers[0], 2 * half)]
    return copies


class Track:
    def __init__(self, own, first, last, carry=None):
        self.own, self.first, self.last, self.carry = own, first, last, carry
        self.count, self.rows, self.lanes = own.shape

    def out(self):
        if self.last == self.count - 1:
            return ((self.rows, self.lanes), F32)
        return ((2, self.rows, self.lanes // 2), BF16)


def ring_operands(tracks):
    return [one.own for one in tracks] + [one.carry for one in tracks if one.first]


def ring_scratch(tracks):
    slots = [
        pltpu.VMEM((one.last - one.first, 2, one.rows, one.lanes // 2), BF16) for one in tracks
    ]
    if not tracks:
        return []
    longest = max(one.last - one.first for one in tracks)
    return slots + [pltpu.SemaphoreType.DMA((longest, len(tracks), 2))] * 2


class Ring:
    def __init__(self, tracks, operands, outs, scratch, sources):
        self.tracks, self.outs = tracks, outs
        self.count = tracks[0].count
        self.owns = operands[: len(tracks)]
        self.sources = sources[: len(tracks)]
        carries = list(sources[len(tracks) :])
        self.carries = [carries.pop(0) if one.first else None for one in tracks]
        *self.slots, self.send, self.recv = scratch
        self.here = lax.axis_index("dp")
        self.place = ring_position(self.here, self.count)
        after = ring_member((self.place + 1) % self.count, self.count)
        before = ring_member((self.place + self.count - 1) % self.count, self.count)
        self.toward = (after, before)
        self.rounds = max(one.last - one.first for one in tracks) - 1

    def copy(self, track, direction, turn, source):
        return pltpu.make_async_remote_copy(
            source,
            self.slots[track].at[turn, direction],
            self.send.at[turn, track, direction],
            self.recv.at[turn, track, direction],
            device_id={"dp": self.toward[direction]},
        )

    def owner(self, direction, step):
        move = step + 1
        if direction == 0:
            move = self.count - move
        return ring_member((self.place + move) % self.count, self.count)

    def own(self, track, direction, owner, owns=None):
        own = (owns or self.owns)[track]
        half = own.shape[2] // 2
        return own.at[owner, :, pl.ds(direction * half, half)]

    def held(self, track, direction, turn):
        return self.slots[track].at[turn, direction]

    def start(self):
        for track, carry in enumerate(self.carries):
            for direction in range(2):
                if carry is None:
                    source = self.own(track, direction, self.owner(direction, 0), self.sources)
                else:
                    source = carry.at[direction]
                self.copy(track, direction, 0, source).start()

    def round(self, turn, extra):
        for track, info in enumerate(self.tracks):
            def one(track=track, info=info):
                for direction in range(2):
                    held = self.held(track, direction, turn - 1)
                    self.copy(track, direction, turn - 1, held).wait_recv()
                    own = self.own(track, direction, self.owner(direction, info.first + turn))
                    held[...] = (held[...].astype(F32) + own[...].astype(F32)).astype(BF16)
                    self.copy(track, direction, turn, held).start()

            if info.last - info.first - 1 == self.rounds:
                one()
            else:
                pl.when(turn < info.last - info.first)(one)
        return extra

    def advance(self, point, points):
        first, last = self.rounds * point // points, self.rounds * (point + 1) // points
        if isinstance(point, int) and last == first:
            return
        if isinstance(point, int) and last == first + 1:
            self.round(last, 0)
            return
        lax.fori_loop(1 + first, 1 + last, self.round, 0)

    def loop(self, body, steps, point, pieces, points):
        for n in range(pieces):
            lax.fori_loop(steps * n // pieces, steps * (n + 1) // pieces, body, 0)
            self.advance(point + n, points)

    def finish(self):
        for track, (info, out) in enumerate(zip(self.tracks, self.outs)):
            turns = info.last - info.first
            half = info.lanes // 2
            whole = info.last == self.count - 1
            for direction in range(2):
                held = self.held(track, direction, turns - 1)
                self.copy(track, direction, turns - 1, held).wait_recv()
                owner = self.here if whole else self.owner(direction, info.last)
                own = self.own(track, direction, owner)
                total = held[...].astype(F32) + own[...].astype(F32)
                if whole:
                    out[:, pl.ds(direction * half, half)] = total
                else:
                    out[direction] = total.astype(BF16)

        def settle(turn, extra):
            for track, info in enumerate(self.tracks):
                def one(track=track):
                    for direction in range(2):
                        held = self.held(track, direction, turn)
                        self.copy(track, direction, turn, held).wait_send()

                if info.last - info.first == self.rounds + 1:
                    one()
                else:
                    pl.when(turn < info.last - info.first)(one)
            return extra

        lax.fori_loop(0, self.rounds + 1, settle, 0)


def ring_rows(rows):
    return -(-rows // 16) * 16


def split_rows(target, source, unit, joined):
    rows, kinds, lanes = source.shape

    def one(n, carry):
        here = span(n, unit)
        for kind in range(kinds):
            values = source[here, kind, :]
            if joined:
                target[here, kind * lanes : (kind + 1) * lanes] = values
            else:
                target[pl.ds(pl.multiple_of(kind * rows + n * unit, unit), unit), :] = values
        return carry

    return one


def first_project_kernel(
    io, inputs_ref, mix_gain, mix_bias, glu_gain, glu_bias, weight_in, short_in, cond_in,
    seq_ref, x_ref, gains_ref, full, project_ref, weight_ref, columns_ref, keep_ref,
    raw, gains_low, gains_land, turn, send, recv, gains_send, gains_recv,
):
    peers = chan_peers()
    me = peers[0]
    shard, slots = inputs_ref.shape
    parts, width, half = raw.shape
    layers = mix_gain.shape[0]
    greet(peers[1:])
    io.ready(0, 1, 2, 3, 4)

    def gather(kind, part):
        return gather_copy(
            lambda owner, part: raw.at[part, span(owner, shard, 32), :],
            peers, (send, recv), kind, part,
        )

    for layer in range(layers):
        for kind, one in enumerate((mix_gain, mix_bias, glu_gain, glu_bias)):
            row = 4 * layer + kind
            gains_low[row : row + 1, :] = one[layer : layer + 1, :]
    gains_land[me] = gains_low[...]
    copies = exchange(
        peers, lambda peer: gains_low, lambda: gains_land.at[me], gains_send, gains_recv
    )
    for part in range(parts):
        raw[part, span(me, shard, 32), :] = inputs_ref[:, part * half : (part + 1) * half]
        for kind in range(2):
            gather(kind, part).start()
    io.ready(5, 6, 7)
    for layer in range(layers):
        lax.fori_loop(0, shard // 48, split_rows(weight_ref.at[layer], weight_in.at[layer], 48, False), 0)
        turn[...] = jnp.zeros_like(turn)
        for tap in range(3):
            turn[3 * tap : 3 * tap + 3, :shard] = short_in[layer, tap]
        turn[9:10, :shard] = cond_in[layer : layer + 1, :]
        columns_ref[layer] = turn[...].T[:shard]
    slot = lax.broadcasted_iota(jnp.int32, keep_ref.shape, 1)
    row = lax.broadcasted_iota(jnp.int32, keep_ref.shape, 0)
    within = slot & (seq_ref[0, 0] - 1)
    keep_ref[...] = jnp.where(within > row, 1.0, 0.0)
    for number in (4, 5, 6):
        io.flush(number)
    for copy in copies:
        copy.wait()
    turn[...] = jnp.zeros_like(turn)
    for owner in range(4):
        turn[: 4 * layers, :shard] = gains_land[owner]
        gains_ref[owner * shard : (owner + 1) * shard, :] = turn[...].T[:shard]
    io.flush(1)
    gather(0, 0).wait_recv()
    gather(2, 0).start()
    for part in range(parts):
        if part + 1 < parts:
            gather(0, part + 1).wait_recv()
            gather(2, part + 1).start()
        gather(1, part).wait_recv()
        gather(2, part).wait_recv()
        values = raw[part].astype(F32)

        @pl.when(me == part // 2)
        def _():
            x_ref[:, (part % 2) * half : (part % 2 + 1) * half] = values

        normal, _ = norm_columns(values)
        full[part] = (normal * gains_ref[:, 0:1] + gains_ref[:, 1:2]).astype(BF16)
        io.flush(2, part, part)
        columns = slice(part * half, (part + 1) * half)
        project_ref[:, columns] = matmul(weight_ref[0], full[part])
        io.flush(3, part, (slice(None), pl.ds(part * half, half)))
    io.flush(0)
    for part in range(parts):
        for kind in range(3):
            gather(kind, part).wait_send()


def first_project(inputs, gain_arrays, in_proj, short_conv, cond_weight, seq_table, collective):
    shard, slots = inputs.shape
    layers, _, streams, width = in_proj.shape
    tokens = slots // 4
    return fused_call(
        first_project_kernel,
        [inputs, *gain_arrays, in_proj, short_conv, cond_weight, seq_table],
        [
            ((width, tokens), F32),
            ((width, 128), F32),
            ((8, width, tokens // 2), BF16),
            ((streams * shard, slots), F32),
            ((layers, streams * shard, width), BF16),
            ((layers, shard, 128), F32),
            ((8, slots), F32),
        ],
        [
            pltpu.VMEM((8, width, tokens // 2), BF16),
            pltpu.VMEM((4 * layers, shard), F32),
            pltpu.VMEM((4, 4 * layers, shard), F32),
            pltpu.VMEM((128, 256), F32),
        ]
        + [pltpu.SemaphoreType.DMA((3, 8))] * 2
        + [pltpu.SemaphoreType.DMA((3,))] * 2,
        collective,
        "first_project",
        (1, 1, 8, 8, 1, 1, 1),
        8,
    )


def scatter_copy(peers, buffers, sems, kind, part):
    _, mate, across, _ = peers
    send, recv = sems
    return send_to(
        across if kind == 2 else mate,
        buffers[2 * kind].at[part],
        buffers[2 * kind + 1].at[part],
        send.at[kind, part],
        recv.at[kind, part],
    )


def scatter_buffers(width, half):
    return [pltpu.VMEM((2, width, half), BF16)] * 6


def block_place(full):
    return lambda owner, part: full.at[owner * 2 + part]


def block_at(step, peers, gathers):
    me, mate, across, diag = peers
    if gathers:
        mine = 1 - (step + 6) // 8
        kind = (step + 1) % 3
        part = mine * step + (1 - mine) * ((step - 2) // 3)
        kind = kind - mine * 4
    else:
        near = step // 4
        mine = step // 6
        part = (1 - near) * (step // 2) + near * (step % 2)
        kind = (1 - near) * (1 + step % 2) - mine
    far = kind * (2 - kind) * (across - mate) + kind * (kind - 1) // 2 * (diag - mate)
    return kind, part, ((1 - mine) * (mate + far) + mine * me) * 2 + part, mine


def run_blocks(peers, full, gather_sems, scatter_sems, buffers, partial, kept, own, ring=None):
    me, mate, across, diag = peers
    gathers = gather_sems is not None

    def gather(kind, part):
        return gather_copy(block_place(full), peers, gather_sems, kind, part)

    def step_body(step, carry):
        kind, part, block, mine = block_at(step, peers, gathers)

        if gathers:
            @pl.when(kind == 0)
            def _():
                gather(1, part).wait_recv()

            @pl.when(kind == 1)
            def _():
                gather(0, part).wait_recv()
                gather(2, part).start()

            @pl.when(kind == 2)
            def _():
                gather(2, part).wait_recv()

        share = partial(block, step)

        def scatter(kind):
            return scatter_copy(peers, buffers, scatter_sems, kind, part)

        @pl.when(mine == 1)
        def _():
            own[part] = share

        @pl.when(kind == 0)
        def _():
            buffers[2][part] = share.astype(BF16)
            scatter(1).start()

        @pl.when(kind == 1)
        def _():
            kept[...] = share

        @pl.when(kind == 2)
        def _():
            buffers[0][part] = share.astype(BF16)
            scatter(0).start()
            scatter(0).wait_recv()
            buffers[4][part] = (kept[...] + buffers[1][part].astype(F32)).astype(BF16)
            scatter(2).start()

        if ring is not None:
            ring.advance(step, 8)
        return carry

    lax.fori_loop(0, 8, step_body, 0)


def scattered(peers, scatter_sems, buffers, own, part):
    for kind in (1, 2):
        scatter_copy(peers, buffers, scatter_sems, kind, part).wait_recv()
    return own[part] + buffers[3][part].astype(F32) + buffers[5][part].astype(F32)


def drain_gather(peers, full, gather_sems):
    for part in range(2):
        for kind in range(3):
            gather_copy(block_place(full), peers, gather_sems, kind, part).wait_send()


def drain_scatter(peers, scatter_sems, buffers):
    for part in range(2):
        for kind in range(3):
            scatter_copy(peers, buffers, scatter_sems, kind, part).wait_send()


def feed_kernel(gain_at, raw, follows, io, gated_ref, x_ref, gains_ref, out_weight, up_columns,
                down_weight, *refs):
    refs = list(refs)
    weight_ref, up_in = (refs.pop(0), refs.pop(0)) if follows else (None, None)
    token_gated, mid_ref, full, next_ref, units, gelus, slopes = refs[:7]
    refs = refs[7:]
    if follows:
        next_full, project_ref, next_up = refs[:3]
        *refs, next_send, next_recv = refs[3:]
    up_raw, up_columns = (up_columns, refs.pop(0)) if raw else (None, up_columns)
    up_weight, kept, own, *rest = refs
    buffers, sems = rest[:6], rest[6:]
    send, recv, gather_send, gather_recv, scatter_send, scatter_recv = sems
    gather_sems, scatter_sems = (gather_send, gather_recv), (scatter_send, scatter_recv)
    peers = chan_peers()
    me = peers[0]
    width, tokens = x_ref.shape
    half = tokens // 2
    hidden = down_weight.shape[1]
    greet(peers[1:])
    io.ready(0)
    copies = to_tokens(peers, gated_ref, token_gated, send, recv)
    io.ready(4)
    if raw:
        lax.fori_loop(0, width // 64, split_rows(up_columns, up_raw, 64, True), 0)
        io.flush(7 + 3 * follows)
    transpose_columns(up_weight, up_columns, 256)
    io.ready(1, 2, 3, 5)
    for part in range(2):
        for copy in copies[part]:
            copy.wait()
        columns = slice(part * half, (part + 1) * half)
        mid = x_ref[:, columns] + matmul(out_weight[...], token_gated[:, columns])
        mid_ref[:, columns] = mid
        normal, _ = norm_columns(mid)
        gain = gains_ref[:, gain_at : gain_at + 1]
        bias = gains_ref[:, gain_at + 1 : gain_at + 2]
        full[me * 2 + part] = (normal * gain + bias).astype(BF16)
        for kind in range(2):
            gather_copy(block_place(full), peers, gather_sems, kind, part).start()
    io.flush(0)
    io.flush(1)

    def partial(block, step):
        normed = full[block]
        tile = 256
        for n in range(hidden // tile):
            gate = matmul(up_weight[n * tile : (n + 1) * tile], normed)
            up = matmul(up_weight[hidden + n * tile : hidden + (n + 1) * tile], normed)
            rows = slice(n * tile, (n + 1) * tile)
            cdf = 0.5 * (1.0 + lax.erf(gate * math.sqrt(0.5)))
            density = jnp.exp(-0.5 * gate * gate) * (1.0 / math.sqrt(2.0 * math.pi))
            gelu = gate * cdf
            units[block, rows] = (gelu * up).astype(BF16)
            gelus[block, rows] = gelu.astype(BF16)
            slopes[block, rows] = (up * (cdf + gate * density)).astype(BF16)
        return matmul(down_weight[...], units[block])

    run_blocks(peers, full, gather_sems, scatter_sems, buffers, partial, kept, own)
    for number in (2, 4, 5, 6):
        io.flush(number)
    if follows:
        io.ready(6, 7)
    place = block_place(next_full) if follows else None
    for part in range(2):
        if follows:
            cuts = width // 64
            lax.fori_loop(
                cuts * part // 2, cuts * (part + 1) // 2, split_rows(next_up, up_in, 64, True), 0
            )
        columns = slice(part * half, (part + 1) * half)
        value = mid_ref[:, columns] + scattered(peers, scatter_sems, buffers, own, part)
        next_ref[:, columns] = value.astype(next_ref.dtype)
        if follows:
            normal, _ = norm_columns(value)
            gain = gains_ref[:, gain_at + 2 : gain_at + 3]
            bias = gains_ref[:, gain_at + 3 : gain_at + 4]
            next_full[me * 2 + part] = (normal * gain + bias).astype(BF16)
            for kind in range(2):
                gather_copy(place, peers, (next_send, next_recv), kind, part).start()
    io.flush(3)
    if follows:
        io.flush(9)
    drain_gather(peers, full, gather_sems)
    drain_scatter(peers, scatter_sems, buffers)
    if follows:
        project_blocks(io, peers, next_full, (next_send, next_recv), weight_ref, project_ref, 7, 8)


def project_blocks(io, peers, full, sems, weight_ref, project_ref, full_out, project_out):
    me, mate, across, diag = peers
    half = full.shape[2]

    def gather(kind, part):
        return gather_copy(block_place(full), peers, sems, kind, part)

    order = [(me, 0), (me, 1), (mate, 0), (mate, 1)]
    order += [(across, 0), (diag, 0), (across, 1), (diag, 1)]
    for step, (owner, part) in enumerate(order):
        if 2 <= step < 4:
            gather(1, part).wait_recv()
        elif step >= 4 and step % 2 == 0:
            gather(0, part).wait_recv()
            gather(2, part).start()
        elif step >= 4:
            gather(2, part).wait_recv()
        block = owner * 2 + part
        io.flush(full_out, step, block)
        columns = span(block, half)
        project_ref[:, columns] = matmul(weight_ref[...], full[block])
        io.flush(project_out, step, (slice(None), columns))
    for kind in range(3):
        for part in range(2):
            gather(kind, part).wait_send()


def feed_forward(gated, values, gains, out_weight, up_columns, down_weight, following, gain_at,
                 collective):
    width, tokens = values.shape
    half = tokens // 2
    follows = list(following)
    block = ((8, width, half), BF16)
    outs = [((width, tokens), BF16), ((width, tokens), F32), block]
    outs.append(((width, tokens), F32 if follows else BF16))
    hidden = down_weight[0].shape[2]
    outs += [((8, hidden, half), BF16)] * 3
    parts = [1] * 7
    extra = []
    if follows:
        outs += [block, ((follows[0][0].shape[1], 4 * tokens), F32)]
        outs.append(((width, 2 * hidden), BF16))
        parts += [8, 8, 1]
        extra = [pltpu.SemaphoreType.DMA((3, 2))] * 2
    raw = up_columns[0].ndim == 4 if isinstance(up_columns, tuple) else False
    if raw:
        outs.append(((width, 2 * hidden), BF16))
        parts.append(1)
    return fused_call(
        lambda *refs: feed_kernel(gain_at, raw, bool(follows), *refs),
        [gated, values, gains, out_weight, up_columns, down_weight] + follows,
        outs,
        [
            pltpu.VMEM((2 * hidden, width), BF16),
            pltpu.VMEM((width, half), F32),
            pltpu.VMEM((2, width, half), F32),
        ]
        + scatter_buffers(width, half)
        + [pltpu.SemaphoreType.DMA((2, 3))] * 2
        + [pltpu.SemaphoreType.DMA((3, 2))] * 4
        + extra,
        collective,
        "feed_forward",
        parts,
        order=(0, 4),
    )


def weight_grad(store, rows, columns, left, right, blocks, row_tile, column_tile):
    across = columns // column_tile

    def one(n, carry):
        row, column = span(n // across, row_tile), span(n % across, column_tile)
        total = matmul_nt(left(0, row), right(0, column))
        for block in range(1, blocks):
            total = total + matmul_nt(left(block, row), right(block, column))
        store(n // across, column, total)
        return carry

    lax.fori_loop(0, rows // row_tile * across, one, 0)


def feed_back_kernel(gain_at, gathered, tracks, io, grad_ref, down_weight, gelus, slopes, up_columns,
                     out_weight, mid_ref, gains_ref, token_gated, units, normed, *refs):
    refs = list(refs)
    rings = len(tracks)
    inputs = len(ring_operands(tracks))
    ring_in, refs = refs[:inputs], refs[inputs:]
    state_ref, gated_ref, feed_grads, out_grad, sums_ref = refs[:5]
    large, refs = refs[5 : 5 + rings], refs[5 + rings :]
    ring = None
    if rings:
        sources = [io.source[11 + n] for n in range(inputs)]
        ring = Ring(tracks, ring_in, large, refs[-rings - 2 :], sources)
        refs = refs[: -rings - 2]
    full = grad_ref if gathered else refs.pop(0)
    mixer_low, kept, own, turned, *rest, load_sems = refs
    gated_low = full
    buffers, sems = rest[:6], rest[6:]
    send, recv, gather_send, gather_recv, scatter_send, scatter_recv = sems
    gather_sems, scatter_sems = (gather_send, gather_recv), (scatter_send, scatter_recv)
    if gathered:
        gather_sems = None
    peers = chan_peers()
    me, mate, across, diag = peers
    width, tokens = mid_ref.shape
    half = tokens // 2
    shard = gated_ref.shape[0]
    hidden = down_weight.shape[1]
    tile = 256
    saved = ((io.source[2], gelus), (io.source[3], slopes))
    if gathered:
        saved += ((io.source[0], full),)

    def loads(step, block):
        return [
            pltpu.make_async_copy(source.at[block], target.at[block], load_sems.at[n, step])
            for n, (source, target) in enumerate(saved)
        ]

    for step in range(8):
        for copy in loads(step, block_at(step, peers, not gathered)[2]):
            copy.start()
    greet(peers[1:], ring.toward if rings else ())
    if not gathered:
        io.ready(0)
        for part in range(2):
            full[me * 2 + part] = grad_ref[:, part * half : (part + 1) * half].astype(BF16)
            for kind in range(2):
                gather_copy(block_place(full), peers, gather_sems, kind, part).start()
    if rings:
        ring.start()
    io.ready(1)
    down_rows, out_rows = turned.at[:hidden], turned.at[:width]
    transpose_into(down_rows, down_weight, tile)
    io.ready(4)
    if rings:
        io.ready(*range(11, 11 + rings))

    def partial(block, step):
        for copy in loads(step, block):
            copy.wait()
        grad = full[block]
        for n in range(hidden // tile):
            rows = slice(n * tile, (n + 1) * tile)
            unit_grad = matmul(down_rows[rows], grad)
            slopes[block, rows] = (unit_grad * slopes[block, rows].astype(F32)).astype(BF16)
            gelus[block, rows] = (unit_grad * gelus[block, rows].astype(F32)).astype(BF16)
        return matmul(up_columns[:, :hidden], slopes[block]) + matmul(
            up_columns[:, hidden:], gelus[block]
        )

    run_blocks(peers, full, gather_sems, scatter_sems, buffers, partial, kept, own, ring)
    io.ready(5, 6, 7, 8, 9, 10)
    transpose_into(out_rows, out_weight, tile)
    if not gathered:
        drain_gather(peers, full, gather_sems)

    def a2a(part, n):
        peer = (across, diag, mate)[n]
        return send_to(
            peer,
            gated_low.at[part, span(peer, shard, 32), :],
            gated_ref.at[:, span(me * 2 + part, half)],
            send.at[part, n],
            recv.at[part, n],
        )

    chunk_rows = feed_grads.shape[1] // 3
    row_tile = 384

    def store_grad(kind):
        def store(index, column, total):
            chunks = row_tile // chunk_rows
            for n in range(chunks):
                feed_grads[
                    index * chunks + n, kind * chunk_rows : (kind + 1) * chunk_rows, column
                ] = total[n * chunk_rows : (n + 1) * chunk_rows].astype(BF16)

        return store

    def feed_grad(kind):
        if kind == 0:
            left, right = lambda b, r: full[b, r], lambda b, c: units[b, c]
        else:
            def left(b, r):
                return normed[b, r]

            def right(b, c):
                return (slopes, gelus)[kind - 1][b, c]

        weight_grad(store_grad(kind), width, hidden, left, right, 8, row_tile, tile)

    def store_out(index, column, total):
        out_grad[span(index, tile), column] = total.astype(BF16)

    gain = gains_ref[:, gain_at : gain_at + 1]
    for part in range(2):
        feed_grad(part)
        columns = slice(part * half, (part + 1) * half)
        grad = scattered(peers, scatter_sems, buffers, own, part)
        change, product = norm_pullback(grad, mid_ref[:, columns], gain)
        before = full[me * 2 + part].astype(F32) if gathered else grad_ref[:, columns]
        state = before + change
        state_ref[:, columns] = state
        mixer_low[:, columns] = state.astype(BF16)
        gated_low[part] = matmul(out_rows[...], mixer_low[:, columns]).astype(BF16)
        for n in range(3):
            a2a(part, n).start()
        if part == 0:
            sums_ref[:, 0:1] = lane_sums(product)
            sums_ref[:, 1:2] = lane_sums(grad)
        else:
            sums_ref[:, 0:1] = sums_ref[:, 0:1] + lane_sums(product)
            sums_ref[:, 1:2] = sums_ref[:, 1:2] + lane_sums(grad)
    io.flush(0)
    feed_grad(2)
    io.flush(2)
    io.flush(4)
    for part in range(2):
        gated_ref[:, span(me * 2 + part, half)] = gated_low[part, span(me, shard, 32), :]
    weight_grad(
        store_out, width, width,
        lambda b, r: mixer_low[r, :], lambda b, c: token_gated[c, :], 1, tile, tile,
    )
    io.flush(3)
    if rings:
        ring.finish()
        for n in range(rings):
            io.flush(5 + n)
    for part in range(2):
        for n in range(3):
            a2a(part, n).wait()
    io.flush(1)
    drain_scatter(peers, scatter_sems, buffers)


def feed_back(grad, mid, gains, normed, up_columns, down_weight, out_weight, token_gated, saved,
              tracks, gain_at, count, collective):
    width, tokens = mid.shape
    half = tokens // 2
    hidden = down_weight[0].shape[2]
    gathered = grad.ndim == 3
    units, gelus, slopes = saved
    own_loads = tuple(range(11, 11 + len(tracks)))
    carries = tuple(range(11 + len(tracks), 11 + len(ring_operands(tracks))))
    manual = (2, 3) + ((0,) if gathered else ()) + carries
    return fused_call(
        lambda *refs: feed_back_kernel(gain_at, gathered, tracks, *refs),
        [grad, down_weight, gelus, slopes, up_columns, out_weight, mid, gains, token_gated, units]
        + [normed]
        + ring_operands(tracks),
        [
            ((width, tokens), F32),
            ((width // 4, 4 * tokens), BF16),
            ((count, 3 * width // count, hidden), BF16),
            ((width, width), BF16),
            ((width, 8), F32),
        ]
        + [one.out() for one in tracks],
        [pltpu.VMEM((8, width, half), BF16)] * (not gathered)
        + [
            pltpu.VMEM((width, tokens), BF16),
            pltpu.VMEM((width, half), F32),
            pltpu.VMEM((2, width, half), F32),
            pltpu.VMEM((max(hidden, width), width), BF16),
        ]
        + scatter_buffers(width, half)
        + [pltpu.SemaphoreType.DMA((2, 3))] * 2
        + [pltpu.SemaphoreType.DMA((3, 2))] * 4
        + [pltpu.SemaphoreType.DMA((3, 8))]
        + ring_scratch(tracks),
        collective,
        "feed_back",
        [1] * (5 + len(tracks)),
        manual=manual,
        order=((0,) if not gathered else ()) + (1, 4) + own_loads,
    )


def project_back_kernel(gain_at, each, tracks, in_track, io, project_grad, weight_ref, square_ref, normed,
                        state_ref, x_ref, gains_ref, *refs):
    inputs = len(ring_operands(tracks))
    ring_in, refs = refs[:inputs], refs[inputs:]
    next_ref, in_grad, sums_ref = refs[:3]
    large, refs = refs[3 : 3 + len(tracks)], refs[3 + len(tracks) :]
    in_held, *refs = refs
    kept, own, weight_rows, in_full, *rest = refs
    buffers, (scatter_send, scatter_recv, *ring_rest) = rest[:6], rest[6:]
    *ring_rest, in_slots, in_send, in_recv = ring_rest
    in_ring = Ring([in_track], [in_grad], [in_held], [in_slots, in_send, in_recv], [in_grad])
    scatter_sems = (scatter_send, scatter_recv)
    peers = chan_peers()
    me, mate, across, diag = peers
    sources = [io.source[7 + n] for n in range(inputs)]
    ring = Ring(tracks, ring_in, large, ring_rest, sources)
    width, tokens = x_ref.shape
    half = tokens // 2
    rows = weight_ref.shape[0]
    shard = rows // 3
    greet((mate, across), ring.toward)
    ring.start()
    io.ready(1)
    for first, size in ((0, 512), (512, rows - 512)):
        weight_rows[:, first : first + size] = weight_ref[first : first + size].T
    io.ready(0)

    def share(owner, part):
        return matmul(weight_rows[...], project_grad[:, span(owner * 2 + part, half)])

    for part in range(2):
        buffers[0][part] = share(diag, part).astype(BF16)
        scatter_copy(peers, buffers, scatter_sems, 0, part).start()
        kept[...] = share(across, part)
        scatter_copy(peers, buffers, scatter_sems, 0, part).wait_recv()
        buffers[4][part] = (kept[...] + buffers[1][part].astype(F32)).astype(BF16)
        scatter_copy(peers, buffers, scatter_sems, 2, part).start()
    for part in range(2):
        buffers[2][part] = share(mate, part).astype(BF16)
        scatter_copy(peers, buffers, scatter_sems, 1, part).start()
        own[part] = share(me, part)
    io.ready(2, 3)
    if in_full.shape[1] > 4 * each:
        in_full[...] = jnp.zeros_like(in_full)
    for chunk in range(shard // each):
        in_full[chunk, 3 * each : 4 * each] = square_ref[chunk * each : (chunk + 1) * each]
    tile = 256
    for stream in range(3):
        def column_tile(n, carry):
            column = span(n, tile)
            total = None
            for block in range(8):
                left = project_grad[
                    stream * shard : (stream + 1) * shard, block * half : (block + 1) * half
                ]
                value = matmul_nt(left, normed[block, column])
                total = value if total is None else total + value
            for chunk in range(shard // each):
                in_full[chunk, stream * each : (stream + 1) * each, column] = total[
                    chunk * each : (chunk + 1) * each
                ]
            return carry

        lax.fori_loop(0, width // tile, column_tile, 0)
    in_grad[...] = in_full[...].astype(BF16)
    in_ring.start()
    io.flush(1)
    io.ready(*range(7, 7 + len(tracks)))
    ring.advance(0, 2)
    io.ready(4, 5, 6)
    gain = gains_ref[:, gain_at : gain_at + 1]
    for part in range(2):
        columns = slice(part * half, (part + 1) * half)
        grad = scattered(peers, scatter_sems, buffers, own, part)
        change, product = norm_pullback(grad, x_ref[:, columns], gain)
        next_ref[:, columns] = state_ref[:, columns] + change
        if part == 0:
            sums_ref[:, 0:1] = lane_sums(product)
            sums_ref[:, 1:2] = lane_sums(grad)
            ring.advance(1, 2)
            in_ring.advance(0, 1)
        else:
            sums_ref[:, 0:1] = sums_ref[:, 0:1] + lane_sums(product)
            sums_ref[:, 1:2] = sums_ref[:, 1:2] + lane_sums(grad)
    io.flush(0)
    io.flush(2)
    ring.finish()
    for n in range(len(tracks)):
        io.flush(3 + n)
    in_ring.finish()
    io.flush(3 + len(tracks))
    drain_scatter(peers, scatter_sems, buffers)


def project_back(project_grad, state, values, gains, normed, weight, square, tracks, gain_at,
                 collective):
    width, tokens = values.shape
    half = tokens // 2
    rows = project_grad.shape[0]
    count = tracks[0].count
    each = rows // 3 // count
    packed = (count, ring_rows(4 * each), width)
    in_track = Track(jax.ShapeDtypeStruct(packed, BF16), 0, count // 4)
    return fused_call(
        lambda *refs: project_back_kernel(gain_at, each, tracks, in_track, *refs),
        [project_grad, weight, square, normed, state, values, gains] + ring_operands(tracks),
        [((width, tokens), F32), (packed, BF16), ((width, 8), F32)]
        + [one.out() for one in tracks + [in_track]],
        [
            pltpu.VMEM((width, half), F32),
            pltpu.VMEM((2, width, half), F32),
            pltpu.VMEM((width, rows), BF16),
            pltpu.VMEM(packed, F32),
        ]
        + scatter_buffers(width, half)
        + [pltpu.SemaphoreType.DMA((3, 2))] * 2
        + ring_scratch(tracks)
        + ring_scratch([in_track]),
        collective,
        "project_back",
        [1] * (4 + len(tracks)),
        manual=tuple(range(7 + len(tracks), 7 + len(ring_operands(tracks)))),
        order=(1, 0) + tuple(range(7, 7 + len(tracks))),
    )


def mask_heads(values, keep, blocks):
    length = values.shape[1] // blocks
    pieces = []
    for j in range(blocks):
        start = j * length
        pieces.append(values[:, start : start + 128] * keep[:, start : start + 128])
        pieces.append(values[:, start + 128 : start + length])
    return jnp.concatenate(pieces, axis=1)


def eight(rows):
    return pl.ds(pl.multiple_of(rows, 8), 8)


def sixteen(rows):
    return pl.ds(pl.multiple_of(rows, 16), 16)


def stream_rows(project_ref, columns_ref, keep_ref, rows, shard, stream, blocks):
    values = project_ref[eight(stream * shard + rows), :]
    total = values * columns_ref[eight(rows), stream : stream + 1]
    for offset in (1, 2):
        moved = mask_heads(pltpu.roll(values, offset, 1), keep_ref[offset - 1 : offset, :], blocks)
        column = 3 * offset + stream
        total = total + moved * columns_ref[eight(rows), column : column + 1]
    return total


def sequence_factor(power, cond, facts, blocks):
    energy = []
    for i in range(blocks):
        total = 0.0
        for j in range(blocks):
            total = total + power[j] * facts.same[i][j]
        energy.append(total * facts.inverse)
    logs = [jnp.log(1.0 + value) for value in energy]
    factor = [
        (1.0 + cond * value) * facts.same[i][i] for i, value in enumerate(logs)
    ]
    return energy, logs, factor


def block_sums(values, blocks):
    length = values.shape[1] // blocks
    return [lane_sums(values[:, i * length : (i + 1) * length]) for i in range(blocks)]


def spread_blocks(columns, length):
    return jnp.concatenate(
        [jnp.broadcast_to(column, (column.shape[0], length)) for column in columns], axis=1
    )


def plain_bins(spectrum_ref, rows, shard, blocks):
    half = spectrum_ref.shape[1] // 2
    bins = []
    for k in range(blocks):
        here = spectrum_ref[eight(k * shard + rows), :]
        bins.append((here[:, :half], here[:, half:]))
    return bins


def filter_bins(spectrum_ref, sign, rows, shard, blocks):
    plain = plain_bins(spectrum_ref, rows, shard, blocks)
    bins = [plain[0]]
    for k in range(1, blocks):
        (real, imag), (before_real, before_imag) = plain[k], plain[k - 1]
        bins.append((real - sign * before_imag, imag + sign * before_real))
    return bins


def store_blocks(target, values, rows, shard, blocks):
    length = values.shape[1] // blocks
    for j in range(blocks):
        target[sixteen(j * shard + rows), :] = values[:, j * length : (j + 1) * length]


def join(halves):
    return jnp.concatenate(halves, axis=0).astype(BF16)


def channel_cuts(shard, streams):
    size = shard // LOADS
    return [(s * shard + n * size, size) for n in range(LOADS) for s in range(streams)]


def channel_order(numbers, streams=3):
    order = []
    for n in range(LOADS):
        for number in numbers:
            each = streams if number == 1 else 1
            order += [(number, n * each + i) for i in range(each)]
    return tuple(order)


def conv_forward_kernel(blocks, carries, io, filter_ref, project_ref, columns_ref, keep_ref,
                        sign_ref, table_ref, seq_ref, carried_in, back_ref, gated_ref, conv_ref, carried,
                        signal_low, filter_low, signal_bins, filter_spectrum, out_low, convolved,
                        factor_ref, *sems):
    shard, slots = gated_ref.shape
    length = slots // blocks
    scale = 1.0 / length
    steps = shard // 16
    peers = chan_peers()
    me = peers[0]
    parts = carried.shape[0]
    facts = Facts(seq_ref, blocks, length)
    greet(peers[1:])

    def gather(kind, part):
        return gather_copy(
            lambda owner, part: carried.at[part, span(owner, shard, 32), :],
            peers, sems, kind, part,
        )

    def forward(first, last):
        for part in range(parts * first // 8, parts * last // 8):
            gather(0, part).wait_recv()
            gather(2, part).start()

    io.ready(7)
    for part in range(parts):
        if carries == 1:
            carried[part, span(me, shard, 32), :] = carried_in[part]
        else:
            lanes = carried.shape[2]
            carried[part, span(me, shard, 32), :] = carried_in[:, part * lanes : (part + 1) * lanes]
        for kind in range(2):
            gather(kind, part).start()
    io.ready(2, 3, 4)

    def prepare(n, carry):
        rows = n * 16
        signals = []
        for part in range(2):
            here = rows + 8 * part
            one, two = (
                stream_rows(project_ref, columns_ref, keep_ref, here, shard, stream, blocks)
                for stream in (1, 2)
            )
            signals.append(one * two)
            cond = columns_ref[eight(here), 9:10]
            _, _, factor = sequence_factor(block_sums(two * two, blocks), cond, facts, blocks)
            for j in range(blocks):
                factor_ref[eight(here), j : j + 1] = factor[j]
        store_blocks(signal_low, join(signals), rows, shard, blocks)
        kernel = filter_ref[sixteen(rows), :].astype(BF16)
        store_blocks(filter_low, kernel, rows, shard, blocks)
        return carry

    for n in range(LOADS):
        io.ready(0, cuts=slice(n, n + 1))
        io.ready(1, cuts=slice(3 * n, 3 * n + 3))
        lax.fori_loop(steps * n // LOADS, steps * (n + 1) // LOADS, prepare, 0)
    io.ready(5)
    signal_bins[...] = matmul(signal_low[...], table_ref[...])
    forward(0, 2)
    filter_spectrum[...] = matmul(filter_low[...], table_ref[...])
    forward(2, 3)

    def combine(n, carry):
        rows = n * 16
        joined = [[] for _ in range(blocks)]
        for part in range(2):
            here = rows + 8 * part
            window = filter_bins(filter_spectrum, sign_ref[0:1, :], here, shard, blocks)
            signal = plain_bins(signal_bins, here, shard, blocks)
            for i in range(blocks):
                real = imag = None
                for j in range(i, -1, -1):
                    fr, fi = window[i - j]
                    sr, si = signal[j]
                    more_real, more_imag = fr * sr - fi * si, fr * si + fi * sr
                    if j == i:
                        real, imag = more_real, more_imag
                    else:
                        factor = facts.same[i][j]
                        real, imag = real + more_real * factor, imag + more_imag * factor
                joined[i].append(jnp.concatenate([real, imag], axis=1))
        for i in range(blocks):
            out_low[sixteen(i * shard + rows), :] = join(joined[i])
        return carry

    lax.fori_loop(0, steps, combine, 0)
    forward(3, 5)
    io.ready(8)
    convolved[...] = matmul(out_low[...], back_ref[...]) * scale
    forward(5, 6)

    def finish(n, carry):
        rows = n * 16
        gated = []
        for part in range(2):
            here = rows + 8 * part
            zero = stream_rows(project_ref, columns_ref, keep_ref, here, shard, 0, blocks)
            pieces = []
            for j in range(blocks):
                source = convolved[eight(j * shard + here), :]
                columns = slice(j * length, (j + 1) * length)
                conv_ref[eight(here), columns] = source
                pieces.append(zero[:, columns] * (source * factor_ref[eight(here), j : j + 1]))
            gated.append(jnp.concatenate(pieces, axis=1))
        gated_ref[sixteen(rows), :] = join(gated)
        return carry

    lax.fori_loop(0, steps // 2, finish, 0)
    forward(6, 7)
    top, rest = pl.ds(0, shard // 2), pl.ds(shard // 2, shard // 2)
    io.flush(0, 0, top)
    io.flush(1, 0, top)
    lax.fori_loop(steps // 2, steps, finish, 0)
    io.flush(0, 1, rest)
    io.flush(1, 1, rest)
    forward(7, 8)
    for part in range(parts):
        for kind in (1, 2):
            gather(kind, part).wait_recv()
        io.flush(2, part, part)
    for part in range(parts):
        for kind in range(3):
            gather(kind, part).wait_send()


def conv_forward(project, filter_rows, columns, keep, sign, table, seq_table, back, carried,
                 carries, blocks, collective):
    shard, slots = filter_rows[0].shape[1:]
    width = 4 * shard
    length = slots // blocks
    low = pltpu.VMEM((blocks * shard, length), BF16)
    bins = pltpu.VMEM((blocks * shard, 2 * length), F32)
    if carries == 1:
        out = ((carried.shape[0], width, width), BF16)
    else:
        out = ((8, width, slots // 8), BF16)
    return fused_call(
        lambda *refs: conv_forward_kernel(blocks, carries, *refs),
        [filter_rows, project, columns, keep, sign, table, seq_table, carried, back],
        [((shard, slots), BF16), ((shard, slots), F32), out],
        [
            low,
            low,
            bins,
            bins,
            pltpu.VMEM((blocks * shard, 2 * length), BF16),
            pltpu.VMEM((blocks * shard, length), F32),
            pltpu.VMEM((shard, 128), F32),
        ]
        + [pltpu.SemaphoreType.DMA((3, out[0][0]))] * 2,
        collective,
        "conv_forward",
        [2, 2, out[0][0]],
        6,
        (7, 2, 3, 4) + channel_order((1, 0)) + (5, 8),
        {0: channel_cuts(shard, 1), 1: channel_cuts(shard, 3)},
    )


def conv_backward_kernel(blocks, tracks, with_outputs, io, grad_ref, project_ref, conv_ref,
                         filter_ref, columns_ref, keep_ref, sign_ref, table_ref, seq_ref,
                         square_ref, *refs):
    refs = list(refs)
    back_ref = refs.pop(len(ring_operands(tracks)) + with_outputs)
    rings = len(tracks)
    inputs = len(ring_operands(tracks))
    ring_in, refs = refs[:inputs], refs[inputs:]
    if with_outputs:
        residual_ref = refs.pop(0)
    project_grad, filter_pack, square_sum, sums_ref = refs[:4]
    large, refs = refs[4 : 4 + rings], refs[4 + rings :]
    if with_outputs:
        outputs_ref = refs.pop(0)
        *refs, out_land, out_send, out_recv = refs
    sources = [io.source[10 + n] for n in range(inputs)]
    ring = Ring(tracks, ring_in, large, refs[-rings - 2 :], sources)
    refs = refs[: -rings - 2]
    signal_low, filter_low, grad_low, signal_bins, filter_spectrum, grad_bins, *refs = refs
    signal_out, filter_out, mixed, energy_ref, square_land, square_send, square_recv = refs
    signal_grad = filter_spectrum.at[:, : filter_spectrum.shape[1] // 2]
    peers = chan_peers()
    greet(peers[1:], ring.toward)
    ring.start()
    copies = exchange(
        peers, lambda peer: io.source[9].at[peer], lambda: square_land.at[peers[0]],
        square_send, square_recv,
    )
    if with_outputs:
        copies += to_channels(
            peers, io.source[10 + inputs], out_land, out_send, out_recv
        )
    io.ready(4, 5, 6)
    shard, slots = grad_ref.shape
    length = slots // blocks
    scale = 1.0 / length
    steps = shard // 16
    facts = Facts(seq_ref, blocks, length)

    def prepare(n, carry):
        rows = n * 16
        signals, scaled = [], []
        grads = grad_ref[sixteen(rows), :].astype(F32)
        for part in range(2):
            here = rows + 8 * part
            zero, one, two = (
                stream_rows(project_ref, columns_ref, keep_ref, here, shard, stream, blocks)
                for stream in range(3)
            )
            mixed[0, eight(here), :] = one
            mixed[1, eight(here), :] = two
            signals.append(one * two)
            cond = columns_ref[eight(here), 9:10]
            power = block_sums(two * two, blocks)
            energy, logs, factor = sequence_factor(power, cond, facts, blocks)
            conv_grad = grads[8 * part : 8 * part + 8] * zero
            factor_grad = block_sums(conv_grad * conv_ref[eight(here), :], blocks)
            cond_grad = 0.0
            for j in range(blocks):
                cond_grad = cond_grad + factor_grad[j] * logs[j]
            sums_ref[eight(here), 9:10] = cond_grad
            for i in range(blocks):
                total = 0.0
                for j in range(blocks):
                    total = total + factor_grad[j] * facts.same[i][j]
                energy_ref[eight(here), i : i + 1] = (
                    total * cond / (1.0 + energy[i]) * (2.0 * facts.inverse)
                )
                energy_ref[eight(here), blocks + i : blocks + i + 1] = factor[i]
            scaled.append(conv_grad * spread_blocks([one * scale for one in factor], length))
        store_blocks(signal_low, join(signals), rows, shard, blocks)
        store_blocks(grad_low, join(scaled), rows, shard, blocks)
        kernel = filter_ref[sixteen(rows), :].astype(BF16)
        store_blocks(filter_low, kernel, rows, shard, blocks)
        return carry

    for n in range(LOADS):
        for number, each in ((0, 1), (1, 3), (2, 1), (3, 1)):
            io.ready(number, cuts=slice(n * each, (n + 1) * each))
        lax.fori_loop(steps * n // LOADS, steps * (n + 1) // LOADS, prepare, 0)
    io.ready(7)
    io.ready(*range(10, 10 + rings))
    grad_bins[...] = matmul(grad_low[...], table_ref[...])
    signal_bins[...] = matmul(signal_low[...], table_ref[...])
    filter_spectrum[...] = matmul(filter_low[...], table_ref[...])
    ring.advance(0, 3)

    def combine(n, carry):
        rows = n * 16
        sign = sign_ref[0:1, :]
        joined = [[] for _ in range(blocks)]
        windows = [[] for _ in range(blocks)]
        for part in range(2):
            here = rows + 8 * part
            window = filter_bins(filter_spectrum, sign, here, shard, blocks)
            signal = plain_bins(signal_bins, here, shard, blocks)
            grads = plain_bins(grad_bins, here, shard, blocks)
            for j in range(blocks):
                for i in range(j, blocks):
                    fr, fi = window[i - j]
                    gr, gi = grads[i]
                    more_real, more_imag = fr * gr + fi * gi, fr * gi - fi * gr
                    if i == j:
                        real, imag = more_real, more_imag
                    else:
                        factor = facts.same[i][j]
                        real, imag = real + more_real * factor, imag + more_imag * factor
                joined[j].append(jnp.concatenate([real, imag], axis=1))
            after = None
            for k in reversed(range(blocks)):
                real = imag = None
                for j in range(blocks - k):
                    sr, si = signal[j]
                    gr, gi = grads[j + k]
                    more_real, more_imag = sr * gr + si * gi, sr * gi - si * gr
                    if k:
                        factor = facts.same[j + k][j]
                        more_real, more_imag = more_real * factor, more_imag * factor
                    real = more_real if real is None else real + more_real
                    imag = more_imag if imag is None else imag + more_imag
                if after is None:
                    whole = (real, imag)
                else:
                    whole = (real + sign * after[1], imag - sign * after[0])
                windows[k].append(jnp.concatenate(whole, axis=1))
                after = (real, imag)
        for j in range(blocks):
            signal_out[sixteen(j * shard + rows), :] = join(joined[j])
            filter_out[sixteen(j * shard + rows), :] = join(windows[j])
        return carry

    lax.fori_loop(0, steps, combine, 0)
    io.ready(10 + inputs + with_outputs)
    signal_grad[...] = matmul(signal_out[...], back_ref[...])
    ring.advance(1, 3)
    filter_rows = matmul(filter_out[...], back_ref[...])
    count, pack_rows, lanes = filter_pack.shape
    each = shard // count
    stack = slots // lanes
    if pack_rows > stack * each:
        filter_pack[...] = jnp.zeros_like(filter_pack)
    for chunk in range(count):
        lags = [
            filter_rows[j * shard + chunk * each : j * shard + (chunk + 1) * each]
            for j in range(blocks)
        ]
        layers = [
            jnp.concatenate(lags[n * blocks // stack : (n + 1) * blocks // stack], axis=1)
            for n in range(stack)
        ]
        value = layers[0] if stack == 1 else jnp.concatenate(layers, axis=0)
        filter_pack[chunk, : stack * each] = value.astype(BF16)
    io.flush(1)

    def finish(n, carry):
        rows = n * 16
        totals = [[] for _ in range(3)]
        outer = grad_ref[sixteen(rows), :].astype(F32)
        for part in range(2):
            here = rows + 8 * part
            local = eight(here)
            factor = [energy_ref[local, blocks + i : blocks + i + 1] for i in range(blocks)]
            energy = [energy_ref[local, i : i + 1] for i in range(blocks)]
            signal = jnp.concatenate(
                [signal_grad[eight(j * shard + here), :] for j in range(blocks)], axis=1
            )
            for stream in range(3):
                if stream == 0:
                    value = outer[8 * part : 8 * part + 8] * (
                        conv_ref[local, :] * spread_blocks(factor, length)
                    )
                elif stream == 1:
                    value = signal * mixed[1, local, :]
                else:
                    value = signal * mixed[0, local, :] + (
                        spread_blocks(energy, length) * mixed[1, local, :]
                    )
                plain = project_ref[eight(stream * shard + here), :]
                total = value * columns_ref[local, stream : stream + 1]
                sums_ref[local, stream : stream + 1] = lane_sums(value * plain)
                for offset in (1, 2):
                    column = 3 * offset + stream
                    moved = pltpu.roll(
                        mask_heads(value, keep_ref[offset - 1 : offset, :], blocks),
                        slots - offset, 1,
                    )
                    sums_ref[local, column : column + 1] = lane_sums(moved * plain)
                    total = total + moved * columns_ref[local, column : column + 1]
                totals[stream].append(total)
        for stream in range(3):
            project_grad[sixteen(stream * shard + rows), :] = join(totals[stream])
        return carry

    lax.fori_loop(0, steps // 2, finish, 0)
    ring.advance(2, 3)
    lax.fori_loop(steps // 2, steps, finish, 0)
    for stream in range(3):
        io.flush(0, stream, pl.ds(stream * shard, shard))
    for copy in copies:
        copy.wait()
    io.ready(9)
    total = square_ref[peers[0]].astype(F32)
    for peer in peers[1:]:
        total = total + square_land[peer].astype(F32)
    square_sum[...] = total
    io.flush(2)
    if with_outputs:
        io.ready(10 + inputs)
        tokens = residual_ref.shape[1]
        out_land[:, span(peers[0], tokens)] = residual_ref[span(peers[0], shard, 32), :]
        outputs_ref[...] = out_land[...].astype(F32)
        io.flush(4 + rings)
    io.flush(3)
    ring.finish()
    for n in range(rings):
        io.flush(4 + n)


def filter_layout(shard, slots, count):
    each = shard // count
    stack = 2 if each % 8 == 0 else 1
    return count, ring_rows(stack * each), slots // stack


def conv_backward(grad, project, conv, filter_rows, columns, keep, sign, table, seq_table, back, square,
                  tracks, residual, blocks, collective):
    shard, slots = filter_rows[0].shape[1:]
    length = slots // blocks
    low = pltpu.VMEM((blocks * shard, length), BF16)
    bins = pltpu.VMEM((blocks * shard, 2 * length), F32)
    out = pltpu.VMEM((blocks * shard, 2 * length), BF16)
    outs, extra = [], []
    if residual:
        outs = [((shard, slots), F32)]
        extra = [pltpu.VMEM((shard, slots), BF16)] + [pltpu.SemaphoreType.DMA((3,))] * 2
    return fused_call(
        lambda *refs: conv_backward_kernel(blocks, tracks, bool(residual), *refs),
        [grad, project, conv, filter_rows, columns, keep, sign, table, seq_table, square]
        + ring_operands(tracks)
        + list(residual)
        + [back],
        [
            ((3 * shard, slots), BF16),
            (filter_layout(shard, slots, tracks[0].count), BF16),
            ((shard, 4 * shard), F32),
            ((shard, 128), F32),
        ]
        + [one.out() for one in tracks]
        + outs,
        [low, low, low, bins, bins, bins, out, out]
        + [pltpu.VMEM((2, shard, slots), F32), pltpu.VMEM((shard, 128), F32)]
        + [pltpu.VMEM(square.shape, BF16)]
        + [pltpu.SemaphoreType.DMA((3,))] * 2
        + ring_scratch(tracks)
        + extra,
        collective,
        "conv_backward",
        [3, 1, 1, 1] + [1] * (len(tracks) + len(outs)),
        8,
        (4, 5, 6) + channel_order((0, 1, 2, 3)) + (7,),
        {0: channel_cuts(shard, 1), 1: channel_cuts(shard, 3), 2: channel_cuts(shard, 1)}
        | {3: channel_cuts(shard, 1)},
        tuple(range(10 + len(tracks), 10 + len(ring_operands(tracks)))),
    )


def last_kernel(layers, tracks, io, state_ref, *refs):
    refs = list(refs)
    gain_sums, refs = refs[: 2 * layers], refs[2 * layers :]
    row_sums, refs = refs[:layers], refs[layers:]
    rings, inputs = len(tracks), len(ring_operands(tracks))
    ring_in, refs = refs[:inputs], refs[inputs:]
    input_grad, small_out = refs[:2]
    large, refs = refs[2 : 2 + rings], refs[2 + rings :]
    state_low, landing, sums, turn, gains, gains_land, small_own, small_land, *refs = refs
    chan_send, chan_recv, small_send, small_recv, state_send, state_recv, *refs = refs
    peers = chan_peers()
    me = peers[0]
    dp = lax.axis_index("dp")
    first = 1 + 3 * layers
    ring = Ring(tracks, ring_in, large, refs, [io.source[first + n] for n in range(inputs)])
    count = ring.count
    shard = landing.shape[0]
    greet(peers[1:], [(dp + offset) % count for offset in range(1, count)])
    ring.start()
    io.ready(*range(0, first))
    for layer in range(layers):
        sums[:, 4 * layer : 4 * layer + 2] = gain_sums[2 * layer][:, 0:2]
        sums[:, 4 * layer + 2 : 4 * layer + 4] = gain_sums[2 * layer + 1][:, 0:2]
    turn[...] = jnp.zeros_like(turn)
    for owner in range(4):
        turn[:shard, : 4 * layers] = sums[owner * shard : (owner + 1) * shard, : 4 * layers]
        gains[owner] = turn[...].T[: 4 * layers]
    copies = exchange(
        peers, lambda peer: gains.at[peer], lambda: gains_land.at[me], chan_send, chan_recv
    )
    state_low[...] = state_ref[...].astype(BF16)
    state_copies = to_channels(peers, state_low, landing, state_send, state_recv)
    landing[:, span(me, state_low.shape[1])] = state_low[span(me, shard, 32), :]
    io.ready(*range(first, first + rings))
    ring.advance(0, 6)
    for layer in range(layers):
        turn[:shard, 10 * layer : 10 * layer + 10] = row_sums[layer][:, 0:10]
    small_own[4 * layers :, :] = turn[...].T[: small_own.shape[0] - 4 * layers]
    for copy in copies:
        copy.wait()
    total = gains[me]
    for peer in peers[1:]:
        total = total + gains_land[peer]
    small_own[: 4 * layers, :] = total
    small_copies = []
    for offset in range(1, count):
        copy = pltpu.make_async_remote_copy(
            small_own,
            small_land.at[offset - 1],
            small_send.at[offset - 1],
            small_recv.at[offset - 1],
            device_id={"dp": (dp + offset) % count},
        )
        copy.start()
        small_copies.append(copy)
    for point in range(1, 4):
        ring.advance(point, 6)
    small = small_own[...]
    for copy in small_copies:
        copy.wait()
    for n in range(count - 1):
        small = small + small_land[n]
    small_out[...] = small
    io.flush(1)
    ring.advance(4, 6)
    for copy in state_copies:
        copy.wait()
    input_grad[...] = landing[...].astype(F32)
    io.flush(0)
    ring.advance(5, 6)
    ring.finish()
    for n in range(rings):
        io.flush(2 + n)


def last_sums(state, gain_sums, row_sums, tracks, collective):
    width, tokens = state.shape
    shard = width // 4
    layers = len(row_sums)
    count = tracks[0].count
    small = (-(-14 * layers // 8) * 8, 256)
    return fused_call(
        lambda *refs: last_kernel(layers, tracks, *refs),
        [state] + gain_sums + row_sums + ring_operands(tracks),
        [((shard, 4 * tokens), F32), (small, F32)] + [one.out() for one in tracks],
        [
            pltpu.VMEM((width, tokens), BF16),
            pltpu.VMEM((shard, 4 * tokens), BF16),
            pltpu.VMEM((width, 128), F32),
            pltpu.VMEM((256, 128), F32),
            pltpu.VMEM((4, 4 * layers, 256), F32),
            pltpu.VMEM((4, 4 * layers, 256), F32),
            pltpu.VMEM(small, F32),
            pltpu.VMEM((count - 1,) + small, F32),
            pltpu.SemaphoreType.DMA((3,)),
            pltpu.SemaphoreType.DMA((3,)),
            pltpu.SemaphoreType.DMA((count - 1,)),
            pltpu.SemaphoreType.DMA((count - 1,)),
            pltpu.SemaphoreType.DMA((3,)),
            pltpu.SemaphoreType.DMA((3,)),
        ]
        + ring_scratch(tracks),
        collective,
        "last_sums",
        [1] * (2 + len(tracks)),
        order=tuple(range(1, 1 + 3 * layers)) + (0,),
        manual=tuple(
            range(1 + 3 * layers + len(tracks), 1 + 3 * layers + len(ring_operands(tracks)))
        ),
    )


def collect_kernel(layers, *refs):
    refs = list(refs)
    outputs_in, input_in, small = refs[:3]
    refs = refs[3:]
    feeds, refs = refs[:layers], refs[layers:]
    filters, refs = refs[:layers], refs[layers:]
    packs, refs = refs[:layers], refs[layers:]
    (outputs, input_grad, mix_gain, mix_bias, in_grad, short, filter_grad, cond, out_grad, glu_gain,
     glu_bias, up_grad, down_grad, held, sems) = refs
    pairs = ((outputs_in, outputs), (input_in, input_grad))
    loads = [
        pltpu.make_async_copy(source, held.at[n], sems.at[n]) for n, (source, _) in enumerate(pairs)
    ]
    copies = [
        pltpu.make_async_copy(held.at[n], target, sems.at[2 + n])
        for n, (_, target) in enumerate(pairs)
    ]
    for copy in loads:
        copy.start()
    each = in_grad.shape[1]
    shard = cond.shape[1]
    lanes = filters[0].shape[1]
    for layer in range(layers):
        for kind, out in enumerate((mix_gain, mix_bias, glu_gain, glu_bias)):
            row = 4 * layer + kind
            out[layer : layer + 1, :] = small[row : row + 1, :shard]
        row = 4 * layers + 10 * layer
        for tap in range(3):
            short[layer, tap] = small[row + 3 * tap : row + 3 * tap + 3, :shard]
        cond[layer : layer + 1, :] = small[row + 9 : row + 10, :shard]
        for stream in range(3):
            in_grad[layer, :, stream, :] = packs[layer][stream * each : (stream + 1) * each]
        out_grad[layer] = packs[layer][3 * each : 4 * each]
        for n in range(filter_grad.shape[2] // lanes):
            filter_grad[layer, :, n * lanes : (n + 1) * lanes] = filters[layer][
                n * each : (n + 1) * each
            ]
        rows = down_grad.shape[1]
        down_grad[layer] = feeds[layer][:rows]
        for kind in range(2):
            up_grad[layer, :, kind, :] = feeds[layer][(kind + 1) * rows : (kind + 2) * rows]
        loads[layer].wait()
        copies[layer].start()
    for copy in copies:
        copy.wait()


def collect(outputs, input_grad, small, feeds, filters, packs, each):
    layers = len(feeds)
    shard, slots = outputs.shape
    width = 4 * shard
    rows, hidden = feeds[0].shape[0] // 3, feeds[0].shape[1]
    anywhere = pl.BlockSpec(memory_space=pl.ANY)
    local = pl.BlockSpec(memory_space=pltpu.VMEM)
    operands = [outputs, input_grad, small, *feeds, *filters, *packs]
    small_shape = (layers, shard)
    shapes = [
        (shard, slots), (shard, slots), small_shape, small_shape, (layers, each, 3, width),
        (layers, 3, 3, shard), (layers, each, slots), small_shape, (layers, each, width),
        small_shape, small_shape, (layers, rows, 2, hidden), (layers, rows, hidden),
    ]
    return pl.pallas_call(
        lambda *refs: collect_kernel(layers, *refs),
        out_shape=tuple(jax.ShapeDtypeStruct(shape, F32) for shape in shapes),
        in_specs=[anywhere] * 2 + [local] * (len(operands) - 2),
        out_specs=tuple([anywhere] * 2 + [local] * (len(shapes) - 2)),
        scratch_shapes=[pltpu.VMEM((2, shard, slots), F32), pltpu.SemaphoreType.DMA((4,))],
        compiler_params=pltpu.CompilerParams(vmem_limit_bytes=VMEM_LIMIT),
        name="collect",
    )(*operands)


def body(
    inputs,
    seq_table,
    mix_gain,
    mix_bias,
    in_proj,
    short_conv,
    long_filter,
    cond_weight,
    out_proj,
    glu_gain,
    glu_bias,
    glu_in,
    glu_out,
    cotangent,
):
    shard, slots = inputs.shape
    layers, width = in_proj.shape[0], in_proj.shape[3]
    hidden = glu_out.shape[2]
    blocks = 4
    count = lax.axis_size("dp")
    each = shard // count
    table = jnp.asarray(dft_table(slots // blocks), BF16)
    sign = jnp.asarray(np.tile(1.0 - 2.0 * (np.arange(slots // blocks) % 2), (8, 1)), F32)
    residual, gains, normed, project, in_rows, columns, keep = first_project(
        inputs, (mix_gain, mix_bias, glu_gain, glu_bias), in_proj, short_conv, cond_weight,
        seq_table, 1,
    )
    up_columns = (glu_in, 0)
    constants = (keep, sign, table, seq_table, jnp.asarray(dft_table(slots // blocks).T, BF16))
    kept, state = [], None
    for l in range(layers):
        gated, conv, carried = conv_forward(
            project, (long_filter, l), (columns, l), *constants, cotangent if l else out_proj,
            2 if l else 1, blocks, 10 + l,
        )
        if l:
            state = carried
        else:
            full_out = carried
        token_gated, middle, normed_glu, after, *rest = feed_forward(
            gated, residual, gains, (full_out, l), up_columns, (glu_out, l),
            ((in_rows, l + 1), (glu_in, l + 1)) if l + 1 < layers else (), 4 * l + 2, 20 + l,
        )
        saved, follow = rest[:3], rest[3:]
        up_columns = follow.pop() if l == 0 else up_columns
        saved = [up_columns] + saved
        kept.append((residual, normed, project, conv, token_gated, middle, normed_glu, saved))
        residual = after
        if follow:
            normed, project, up_columns = follow
    feeds, filters, packs, gain_sums, row_sums = ([None] * layers for _ in range(5))
    waiting = []
    for l in reversed(range(layers)):
        before, normed, project, conv, token_gated, middle, normed_glu, saved = kept[l]
        top = l == layers - 1
        state, gated_grad, feed_grads, out_grad, glu_sums, *large = feed_back(
            state, middle, gains, normed_glu, saved[0], (glu_out, l), (full_out, l), token_gated,
            saved[1:], waiting, 4 * l + 2, count, 30 + l,
        )
        if waiting:
            feeds[l + 1], filters[l + 1], packs[l + 1] = large
        one, two = (count // 4, count // 2) if l else (3 * count // 8, 5 * count // 8)
        project_low, filter_pack, square, row_sums[l], held, *rest = conv_backward(
            gated_grad, project, conv, (long_filter, l), (columns, l), *constants,
            out_grad.reshape(4, shard, width), [Track(feed_grads, 0, one)],
            (residual,) if top else (), blocks, 40 + l,
        )
        if top:
            outputs = rest[0]
        tracks = [Track(feed_grads, one, two, held), Track(filter_pack, 0, two - one)]
        state, in_pack, mix_sums, feed_held, held, in_held = project_back(
            project_low, state, before, gains, normed, (in_rows, l), square,
            tracks, 4 * l, 50 + l,
        )
        waiting = [
            Track(feed_grads, two, count - 1, feed_held),
            Track(filter_pack, two - one, count - 1, held),
            Track(in_pack, count // 4, count - 1, in_held),
        ]
        gain_sums[l] = [mix_sums, glu_sums]
    input_grad, small, feeds[0], filters[0], packs[0] = last_sums(
        state, [one for pair in gain_sums for one in pair], row_sums, waiting, 60
    )
    return collect(outputs, input_grad, small, feeds, filters, packs, each)


def solution(mesh):
    in_specs = (
        P("chan", "dp"),
        P("dp", None),
        P(None, "chan"),
        P(None, "chan"),
        P(None, "chan", None, None),
        P(None, None, None, "chan"),
        P(None, "chan", None),
        P(None, "chan"),
        P(None, "chan", None),
        P(None, "chan"),
        P(None, "chan"),
        P(None, None, None, "chan"),
        P(None, None, "chan"),
        P("chan", "dp"),
    )
    out_specs = (
        P("chan", "dp"),
        P("chan", "dp"),
        P(None, "chan"),
        P(None, "chan"),
        P(None, ("chan", "dp"), None, None),
        P(None, None, None, "chan"),
        P(None, ("chan", "dp"), None),
        P(None, "chan"),
        P(None, ("chan", "dp"), None),
        P(None, "chan"),
        P(None, "chan"),
        P(None, "dp", None, "chan"),
        P(None, "dp", "chan"),
    )
    return jax.shard_map(body, mesh=mesh, in_specs=in_specs, out_specs=out_specs, check_vma=False)
```

```python
import math

import jax
import jax.numpy as jnp
import numpy as np
from jax import lax
from jax.experimental import pallas as pl
from jax.experimental.pallas import tpu as pltpu
from jax.sharding import PartitionSpec as P

EPSILON = 1e-05
F32 = jnp.float32
BF16 = jnp.bfloat16
VMEM_LIMIT = 63 * 2**20
LOADS = 4


def dft_table(block_len):
    period = 2 * block_len
    position = np.arange(block_len)[:, None]
    phase = ((2 * np.arange(block_len)[None, :] + 1) * position) % (2 * period)
    phase = phase * (math.pi / period)
    return np.concatenate([np.cos(phase), -np.sin(phase)], axis=1)


class Facts:
    def __init__(self, table_ref, blocks, block_len):
        length, count = table_ref[0, 0], table_ref[0, 1]
        used = length * count
        pair = jnp.where(length >= 2 * block_len, 1.0, 0.0)
        four = jnp.where(length >= 4 * block_len, 1.0, 0.0)
        active = [jnp.where(i * block_len < used, 1.0, 0.0) for i in range(blocks)]
        self.same = [[None] * blocks for _ in range(blocks)]
        for i in range(blocks):
            for j in range(blocks):
                if i == j:
                    self.same[i][j] = active[i]
                else:
                    joined = pair if i // 2 == j // 2 else four
                    self.same[i][j] = active[i] * active[j] * joined
        shortest = 1.0 / block_len
        self.inverse = shortest * (1.0 - 0.5 * pair - 0.25 * four)


class Io:
    def __init__(self, source, loads, stores):
        self.source, self.loads, self.stores, self.pending = source, loads, stores, []

    def ready(self, *numbers, cuts=None):
        for number in numbers:
            for copy in self.loads[number] if cuts is None else self.loads[number][cuts]:
                copy.wait()

    def flush(self, number, part=0, at=None):
        source, target, sems = self.stores[number]
        if at is not None:
            source, target = source.at[at], target.at[at]
        copy = pltpu.make_async_copy(source, target, sems.at[part])
        copy.start()
        self.pending.append(copy)

    def finish(self):
        for copy in self.pending:
            copy.wait()


def fused_call(kernel, operands, outs, scratch, collective, name, parts, scalars=-1, order=(),
               cuts=None, manual=()):
    arrays, layers = [], []
    for operand in operands:
        array, layer = operand if isinstance(operand, tuple) else (operand, None)
        arrays.append(array)
        layers.append(layer)
    cuts = cuts or {}
    inputs, results = len(arrays), len(outs)
    buffers, sems = [], []
    for number, (array, layer) in enumerate(zip(arrays, layers)):
        if number != scalars:
            buffers.append(pltpu.VMEM(array.shape if layer is None else array.shape[1:], array.dtype))
            sems.append(pltpu.SemaphoreType.DMA((len(cuts.get(number, (0,))),)))
    for (shape, dtype), count in zip(outs, parts):
        buffers.append(pltpu.VMEM(shape, dtype))
        sems.append(pltpu.SemaphoreType.DMA((count,)))

    def body(*refs):
        extra = list(refs[inputs + results + len(scratch) :])
        places, marks = extra[: len(buffers)], extra[len(buffers) :]
        sources, loads, stores, views, n = {}, {}, {}, [], 0
        for number in range(inputs):
            if number == scalars:
                views.append(refs[number])
                continue
            source = refs[number]
            if layers[number] is not None:
                source = source.at[layers[number]]
            sources[number] = source
            views.append(places[n])
            if number not in manual:
                pairs = [(source, places[n])]
                if number in cuts:
                    rows = [pl.ds(*one) for one in cuts[number]]
                    pairs = [(source.at[one], places[n].at[one]) for one in rows]
                loads[number] = [
                    pltpu.make_async_copy(*pair, marks[n].at[i]) for i, pair in enumerate(pairs)
                ]
            n += 1
        for number in range(results):
            stores[number] = (places[n], refs[inputs + number], marks[n])
            views.append(places[n])
            n += 1
        started = set()
        for one in list(order) + list(loads):
            number, chosen = one if isinstance(one, tuple) else (one, None)
            for i, copy in enumerate(loads[number]):
                if (chosen is None or i == chosen) and (number, i) not in started:
                    started.add((number, i))
                    copy.start()
        io = Io(sources, loads, stores)
        kernel(io, *views, *refs[inputs + results : inputs + results + len(scratch)])
        io.finish()

    anywhere = pl.BlockSpec(memory_space=pl.ANY)
    scalar_spec = pl.BlockSpec(memory_space=pltpu.SMEM)
    params = {}
    if collective is not None:
        params = dict(collective_id=collective, has_side_effects=True)
    return pl.pallas_call(
        body,
        out_shape=tuple(jax.ShapeDtypeStruct(*out) for out in outs),
        in_specs=[scalar_spec if n == scalars else anywhere for n in range(inputs)],
        out_specs=tuple([anywhere] * results),
        scratch_shapes=list(scratch) + buffers + sems,
        compiler_params=pltpu.CompilerParams(vmem_limit_bytes=VMEM_LIMIT, **params),
        name=name,
    )(*arrays)


def ring_position(index, count):
    odd = index % 2
    return (1 - odd) * (index // 2) + odd * (count - 1 - index // 2)


def ring_member(position, count):
    late = position // (count // 2)
    return (1 - late) * 2 * position + late * (2 * (count - 1 - position) + 1)


def chan_peers():
    me = lax.axis_index("chan")
    mate = me + 1 - 2 * (me % 2)
    across = (me + 2) % 4
    return me, mate, across, (mate + 2) % 4


def greet(peers, members=()):
    barrier = pltpu.get_barrier_semaphore()
    for peer in peers:
        pl.semaphore_signal(barrier, inc=1, device_id={"chan": peer})
    for member in members:
        pl.semaphore_signal(barrier, inc=1, device_id={"dp": member})
    pl.semaphore_wait(barrier, len(peers) + len(members))


def send_to(peer, source, target, send, recv):
    return pltpu.make_async_remote_copy(source, target, send, recv, device_id={"chan": peer})


def span(index, size, unit=None):
    if isinstance(index, int):
        return pl.ds(index * size, size)
    return pl.ds(pl.multiple_of(index * size, unit or size), size)


def gather_copy(place, peers, sems, kind, part):
    me, mate, across, _ = peers
    block = place(across if kind == 2 else me, part)
    send, recv = sems
    return send_to(
        across if kind == 0 else mate, block, block, send.at[kind, part], recv.at[kind, part]
    )


def norm_columns(values):
    mean = jnp.mean(values, axis=0, keepdims=True)
    center = values - mean
    inverse = lax.rsqrt(jnp.mean(center * center, axis=0, keepdims=True) + EPSILON)
    return center * inverse, inverse


def norm_pullback(grad, values, gain):
    normal, inverse = norm_columns(values)
    product = grad * normal
    scaled = grad * gain
    first = jnp.mean(scaled, axis=0, keepdims=True)
    second = jnp.mean(product * gain, axis=0, keepdims=True)
    return inverse * (scaled - first - normal * second), product


def lane_sums(values):
    return jnp.sum(values, axis=1, keepdims=True)


def matmul(left, right):
    return jnp.dot(left, right, preferred_element_type=F32)


def matmul_nt(left, right):
    return lax.dot_general(
        left, right, (((1,), (1,)), ((), ())), preferred_element_type=F32
    )


def transpose_into(target, source, tile):
    for n in range(source.shape[0] // tile):
        target[:, n * tile : (n + 1) * tile] = source[n * tile : (n + 1) * tile].T


def transpose_columns(target, source, tile):
    for n in range(source.shape[1] // tile):
        target[n * tile : (n + 1) * tile, :] = source[:, n * tile : (n + 1) * tile].T


def exchange(peers, source, target, send, recv):
    copies = []
    for n, peer in enumerate((peers[2], peers[3], peers[1])):
        copy = send_to(peer, source(peer), target(), send.at[n], recv.at[n])
        copy.start()
        copies.append(copy)
    return copies


def to_channels(peers, low, landing, send, recv):
    shard, tokens = landing.shape[0], low.shape[1]
    me = peers[0]
    mine = span(me, tokens)
    copies = exchange(
        peers, lambda peer: low.at[span(peer, shard, 32), :], lambda: landing.at[:, mine], send, recv
    )
    return copies


class Track:
    def __init__(self, own, first, last, carry=None):
        self.own, self.first, self.last, self.carry = own, first, last, carry
        self.count, self.rows, self.lanes = own.shape

    def out(self):
        if self.last == self.count - 1:
            return ((self.rows, self.lanes), F32)
        return ((2, self.rows, self.lanes // 2), BF16)


def ring_operands(tracks):
    return [one.own for one in tracks] + [one.carry for one in tracks if one.first]


def ring_scratch(tracks):
    slots = [
        pltpu.VMEM((one.last - one.first, 2, one.rows, one.lanes // 2), BF16) for one in tracks
    ]
    if not tracks:
        return []
    longest = max(one.last - one.first for one in tracks)
    return slots + [pltpu.SemaphoreType.DMA((longest, len(tracks), 2))] * 2


class Ring:
    def __init__(self, tracks, operands, outs, scratch, sources):
        self.tracks, self.outs = tracks, outs
        self.count = tracks[0].count
        self.owns = operands[: len(tracks)]
        self.sources = sources[: len(tracks)]
        carries = list(sources[len(tracks) :])
        self.carries = [carries.pop(0) if one.first else None for one in tracks]
        *self.slots, self.send, self.recv = scratch
        self.here = lax.axis_index("dp")
        self.place = ring_position(self.here, self.count)
        after = ring_member((self.place + 1) % self.count, self.count)
        before = ring_member((self.place + self.count - 1) % self.count, self.count)
        self.toward = (after, before)
        self.rounds = max(one.last - one.first for one in tracks) - 1

    def copy(self, track, direction, turn, source):
        return pltpu.make_async_remote_copy(
            source,
            self.slots[track].at[turn, direction],
            self.send.at[turn, track, direction],
            self.recv.at[turn, track, direction],
            device_id={"dp": self.toward[direction]},
        )

    def owner(self, direction, step):
        move = step + 1
        if direction == 0:
            move = self.count - move
        return ring_member((self.place + move) % self.count, self.count)

    def own(self, track, direction, owner, owns=None):
        own = (owns or self.owns)[track]
        half = own.shape[2] // 2
        return own.at[owner, :, pl.ds(direction * half, half)]

    def held(self, track, direction, turn):
        return self.slots[track].at[turn, direction]

    def start(self):
        for track, carry in enumerate(self.carries):
            for direction in range(2):
                if carry is None:
                    source = self.own(track, direction, self.owner(direction, 0), self.sources)
                else:
                    source = carry.at[direction]
                self.copy(track, direction, 0, source).start()

    def round(self, turn, extra):
        for track, info in enumerate(self.tracks):
            def one(track=track, info=info):
                for direction in range(2):
                    held = self.held(track, direction, turn - 1)
                    self.copy(track, direction, turn - 1, held).wait_recv()
                    own = self.own(track, direction, self.owner(direction, info.first + turn))
                    held[...] = (held[...].astype(F32) + own[...].astype(F32)).astype(BF16)
                    self.copy(track, direction, turn, held).start()

            if info.last - info.first - 1 == self.rounds:
                one()
            else:
                pl.when(turn < info.last - info.first)(one)
        return extra

    def advance(self, point, points):
        first, last = self.rounds * point // points, self.rounds * (point + 1) // points
        if isinstance(point, int) and last == first:
            return
        if isinstance(point, int) and last == first + 1:
            self.round(last, 0)
            return
        lax.fori_loop(1 + first, 1 + last, self.round, 0)

    def loop(self, body, steps, point, pieces, points):
        for n in range(pieces):
            lax.fori_loop(steps * n // pieces, steps * (n + 1) // pieces, body, 0)
            self.advance(point + n, points)

    def finish(self):
        for track, (info, out) in enumerate(zip(self.tracks, self.outs)):
            turns = info.last - info.first
            half = info.lanes // 2
            whole = info.last == self.count - 1
            for direction in range(2):
                held = self.held(track, direction, turns - 1)
                self.copy(track, direction, turns - 1, held).wait_recv()
                owner = self.here if whole else self.owner(direction, info.last)
                own = self.own(track, direction, owner)
                total = held[...].astype(F32) + own[...].astype(F32)
                if whole:
                    out[:, pl.ds(direction * half, half)] = total
                else:
                    out[direction] = total.astype(BF16)

        def settle(turn, extra):
            for track, info in enumerate(self.tracks):
                def one(track=track):
                    for direction in range(2):
                        held = self.held(track, direction, turn)
                        self.copy(track, direction, turn, held).wait_send()

                if info.last - info.first == self.rounds + 1:
                    one()
                else:
                    pl.when(turn < info.last - info.first)(one)
            return extra

        lax.fori_loop(0, self.rounds + 1, settle, 0)


def ring_rows(rows):
    return -(-rows // 16) * 16


def split_rows(target, source, unit, joined):
    rows, kinds, lanes = source.shape

    def one(n, carry):
        here = span(n, unit)
        for kind in range(kinds):
            values = source[here, kind, :]
            if joined:
                target[here, kind * lanes : (kind + 1) * lanes] = values
            else:
                target[pl.ds(pl.multiple_of(kind * rows + n * unit, unit), unit), :] = values
        return carry

    return one


def first_project_kernel(
    io, inputs_ref, mix_gain, mix_bias, glu_gain, glu_bias, weight_in, short_in, cond_in, up_in,
    seq_ref, x_ref, gains_ref, full, project_ref, weight_ref, up_ref, columns_ref, keep_ref,
    raw, gains_low, gains_land, turn, send, recv, gains_send, gains_recv,
):
    peers = chan_peers()
    me = peers[0]
    shard, slots = inputs_ref.shape
    parts, width, half = raw.shape
    layers = mix_gain.shape[0]
    greet(peers[1:])
    io.ready(0, 1, 2, 3, 4)

    def gather(kind, part):
        return gather_copy(
            lambda owner, part: raw.at[part, span(owner, shard, 32), :],
            peers, (send, recv), kind, part,
        )

    for layer in range(layers):
        for kind, one in enumerate((mix_gain, mix_bias, glu_gain, glu_bias)):
            row = 4 * layer + kind
            gains_low[row : row + 1, :] = one[layer : layer + 1, :]
    gains_land[me] = gains_low[...]
    copies = exchange(
        peers, lambda peer: gains_low, lambda: gains_land.at[me], gains_send, gains_recv
    )
    for part in range(parts):
        raw[part, span(me, shard, 32), :] = inputs_ref[:, part * half : (part + 1) * half]
        for kind in range(2):
            gather(kind, part).start()
    io.ready(5, 6, 7)
    for layer in range(layers):
        lax.fori_loop(0, shard // 48, split_rows(weight_ref.at[layer], weight_in.at[layer], 48, False), 0)
        turn[...] = jnp.zeros_like(turn)
        for tap in range(3):
            turn[3 * tap : 3 * tap + 3, :shard] = short_in[layer, tap]
        turn[9:10, :shard] = cond_in[layer : layer + 1, :]
        columns_ref[layer] = turn[...].T[:shard]
    slot = lax.broadcasted_iota(jnp.int32, keep_ref.shape, 1)
    row = lax.broadcasted_iota(jnp.int32, keep_ref.shape, 0)
    within = slot & (seq_ref[0, 0] - 1)
    keep_ref[...] = jnp.where(within > row, 1.0, 0.0)
    io.flush(4)
    io.flush(6)
    io.flush(7)
    for copy in copies:
        copy.wait()
    turn[...] = jnp.zeros_like(turn)
    for owner in range(4):
        turn[: 4 * layers, :shard] = gains_land[owner]
        gains_ref[owner * shard : (owner + 1) * shard, :] = turn[...].T[:shard]
    io.flush(1)
    io.ready(8)
    gather(0, 0).wait_recv()
    gather(2, 0).start()
    for part in range(parts):
        if part + 1 < parts:
            gather(0, part + 1).wait_recv()
            gather(2, part + 1).start()
        gather(1, part).wait_recv()
        gather(2, part).wait_recv()
        values = raw[part].astype(F32)

        @pl.when(me == part // 2)
        def _():
            x_ref[:, (part % 2) * half : (part % 2 + 1) * half] = values

        normal, _ = norm_columns(values)
        full[part] = (normal * gains_ref[:, 0:1] + gains_ref[:, 1:2]).astype(BF16)
        io.flush(2, part, part)
        columns = slice(part * half, (part + 1) * half)
        project_ref[:, columns] = matmul(weight_ref[0], full[part])
        io.flush(3, part, (slice(None), pl.ds(part * half, half)))
        cuts = width // 64
        lax.fori_loop(
            cuts * part // parts, cuts * (part + 1) // parts, split_rows(up_ref, up_in, 64, True), 0
        )
    io.flush(0)
    io.flush(5)
    for part in range(parts):
        for kind in range(3):
            gather(kind, part).wait_send()


def first_project(inputs, gain_arrays, in_proj, short_conv, cond_weight, glu_in, seq_table,
                  collective):
    shard, slots = inputs.shape
    layers, _, streams, width = in_proj.shape
    hidden = glu_in[0].shape[3]
    tokens = slots // 4
    return fused_call(
        first_project_kernel,
        [inputs, *gain_arrays, in_proj, short_conv, cond_weight, glu_in, seq_table],
        [
            ((width, tokens), F32),
            ((width, 128), F32),
            ((8, width, tokens // 2), BF16),
            ((streams * shard, slots), F32),
            ((layers, streams * shard, width), BF16),
            ((width, 2 * hidden), BF16),
            ((layers, shard, 128), F32),
            ((8, slots), F32),
        ],
        [
            pltpu.VMEM((8, width, tokens // 2), BF16),
            pltpu.VMEM((4 * layers, shard), F32),
            pltpu.VMEM((4, 4 * layers, shard), F32),
            pltpu.VMEM((128, 256), F32),
        ]
        + [pltpu.SemaphoreType.DMA((3, 8))] * 2
        + [pltpu.SemaphoreType.DMA((3,))] * 2,
        collective,
        "first_project",
        (1, 1, 8, 8, 1, 1, 1, 1),
        9,
    )


def scatter_copy(peers, buffers, sems, kind, part):
    _, mate, across, _ = peers
    send, recv = sems
    return send_to(
        across if kind == 2 else mate,
        buffers[2 * kind].at[part],
        buffers[2 * kind + 1].at[part],
        send.at[kind, part],
        recv.at[kind, part],
    )


def scatter_buffers(width, half):
    return [pltpu.VMEM((2, width, half), BF16)] * 6


def block_place(full):
    return lambda owner, part: full.at[owner * 2 + part]


def block_at(step, peers, gathers):
    me, mate, across, diag = peers
    if gathers:
        mine = 1 - (step + 6) // 8
        kind = (step + 1) % 3
        part = mine * step + (1 - mine) * ((step - 2) // 3)
        kind = kind - mine * 4
    else:
        near = step // 4
        mine = step // 6
        part = (1 - near) * (step // 2) + near * (step % 2)
        kind = (1 - near) * (1 + step % 2) - mine
    far = kind * (2 - kind) * (across - mate) + kind * (kind - 1) // 2 * (diag - mate)
    return kind, part, ((1 - mine) * (mate + far) + mine * me) * 2 + part, mine


def run_blocks(peers, full, gather_sems, scatter_sems, buffers, partial, kept, own, ring=None):
    me, mate, across, diag = peers
    gathers = gather_sems is not None

    def gather(kind, part):
        return gather_copy(block_place(full), peers, gather_sems, kind, part)

    def step_body(step, carry):
        kind, part, block, mine = block_at(step, peers, gathers)

        if gathers:
            @pl.when(kind == 0)
            def _():
                gather(1, part).wait_recv()

            @pl.when(kind == 1)
            def _():
                gather(0, part).wait_recv()
                gather(2, part).start()

            @pl.when(kind == 2)
            def _():
                gather(2, part).wait_recv()

        share = partial(block, step)

        def scatter(kind):
            return scatter_copy(peers, buffers, scatter_sems, kind, part)

        @pl.when(mine == 1)
        def _():
            own[part] = share

        @pl.when(kind == 0)
        def _():
            buffers[2][part] = share.astype(BF16)
            scatter(1).start()

        @pl.when(kind == 1)
        def _():
            kept[...] = share

        @pl.when(kind == 2)
        def _():
            buffers[0][part] = share.astype(BF16)
            scatter(0).start()
            scatter(0).wait_recv()
            buffers[4][part] = (kept[...] + buffers[1][part].astype(F32)).astype(BF16)
            scatter(2).start()

        if ring is not None:
            pl.when(step % 3 == 2)(lambda: ring.advance(step // 3, 4))
        return carry

    lax.fori_loop(0, 8, step_body, 0)


def scattered(peers, scatter_sems, buffers, own, part):
    for kind in (1, 2):
        scatter_copy(peers, buffers, scatter_sems, kind, part).wait_recv()
    return own[part] + buffers[3][part].astype(F32) + buffers[5][part].astype(F32)


def drain_gather(peers, full, gather_sems):
    for part in range(2):
        for kind in range(3):
            gather_copy(block_place(full), peers, gather_sems, kind, part).wait_send()


def drain_scatter(peers, scatter_sems, buffers):
    for part in range(2):
        for kind in range(3):
            scatter_copy(peers, buffers, scatter_sems, kind, part).wait_send()


def feed_kernel(gain_at, follows, io, token_gated, x_ref, gains_ref, out_weight, up_columns,
                down_weight, *refs):
    refs = list(refs)
    weight_ref, up_in = (refs.pop(0), refs.pop(0)) if follows else (None, None)
    mid_ref, full, next_ref, units, gelus, slopes = refs[:6]
    refs = refs[6:]
    if follows:
        next_full, project_ref, next_up = refs[:3]
        *refs, next_send, next_recv = refs[3:]
    up_weight, kept, own, *rest = refs
    buffers, sems = rest[:6], rest[6:]
    gather_send, gather_recv, scatter_send, scatter_recv = sems
    gather_sems, scatter_sems = (gather_send, gather_recv), (scatter_send, scatter_recv)
    peers = chan_peers()
    me, mate, across, _ = peers
    width, tokens = x_ref.shape
    half = tokens // 2
    hidden = down_weight.shape[1]
    greet((mate, across))
    io.ready(0, 1, 2, 3)
    for part in range(2):
        columns = slice(part * half, (part + 1) * half)
        mid = x_ref[:, columns] + matmul(out_weight[...], token_gated[:, columns])
        mid_ref[:, columns] = mid
        normal, _ = norm_columns(mid)
        gain = gains_ref[:, gain_at : gain_at + 1]
        bias = gains_ref[:, gain_at + 1 : gain_at + 2]
        full[me * 2 + part] = (normal * gain + bias).astype(BF16)
        for kind in range(2):
            gather_copy(block_place(full), peers, gather_sems, kind, part).start()
    io.flush(0)
    io.ready(4, 5)
    transpose_columns(up_weight, up_columns, 256)

    def partial(block, step):
        normed = full[block]
        tile = 256
        for n in range(hidden // tile):
            gate = matmul(up_weight[n * tile : (n + 1) * tile], normed)
            up = matmul(up_weight[hidden + n * tile : hidden + (n + 1) * tile], normed)
            rows = slice(n * tile, (n + 1) * tile)
            cdf = 0.5 * (1.0 + lax.erf(gate * math.sqrt(0.5)))
            density = jnp.exp(-0.5 * gate * gate) * (1.0 / math.sqrt(2.0 * math.pi))
            gelu = gate * cdf
            units[block, rows] = (gelu * up).astype(BF16)
            gelus[block, rows] = gelu.astype(BF16)
            slopes[block, rows] = (up * (cdf + gate * density)).astype(BF16)
        return matmul(down_weight[...], units[block])

    run_blocks(peers, full, gather_sems, scatter_sems, buffers, partial, kept, own)
    for number in (1, 3, 4, 5):
        io.flush(number)
    if follows:
        io.ready(6, 7)
    place = block_place(next_full) if follows else None
    for part in range(2):
        if follows:
            cuts = width // 64
            lax.fori_loop(
                cuts * part // 2, cuts * (part + 1) // 2, split_rows(next_up, up_in, 64, True), 0
            )
        columns = slice(part * half, (part + 1) * half)
        value = mid_ref[:, columns] + scattered(peers, scatter_sems, buffers, own, part)
        next_ref[:, columns] = value.astype(next_ref.dtype)
        if follows:
            normal, _ = norm_columns(value)
            gain = gains_ref[:, gain_at + 2 : gain_at + 3]
            bias = gains_ref[:, gain_at + 3 : gain_at + 4]
            next_full[me * 2 + part] = (normal * gain + bias).astype(BF16)
            for kind in range(2):
                gather_copy(place, peers, (next_send, next_recv), kind, part).start()
    io.flush(2)
    if follows:
        io.flush(8)
    drain_gather(peers, full, gather_sems)
    drain_scatter(peers, scatter_sems, buffers)
    if follows:
        project_blocks(io, peers, next_full, (next_send, next_recv), weight_ref, project_ref, 6, 7)


def project_blocks(io, peers, full, sems, weight_ref, project_ref, full_out, project_out):
    me, mate, across, diag = peers
    half = full.shape[2]

    def gather(kind, part):
        return gather_copy(block_place(full), peers, sems, kind, part)

    order = [(me, 0), (me, 1), (mate, 0), (mate, 1)]
    order += [(across, 0), (diag, 0), (across, 1), (diag, 1)]
    for step, (owner, part) in enumerate(order):
        if 2 <= step < 4:
            gather(1, part).wait_recv()
        elif step >= 4 and step % 2 == 0:
            gather(0, part).wait_recv()
            gather(2, part).start()
        elif step >= 4:
            gather(2, part).wait_recv()
        block = owner * 2 + part
        io.flush(full_out, step, block)
        columns = span(block, half)
        project_ref[:, columns] = matmul(weight_ref[...], full[block])
        io.flush(project_out, step, (slice(None), columns))
    for kind in range(3):
        for part in range(2):
            gather(kind, part).wait_send()


def feed_forward(token_gated, values, gains, out_weight, up_columns, down_weight, following, gain_at,
                 collective):
    width, tokens = values.shape
    half = tokens // 2
    follows = list(following)
    block = ((8, width, half), BF16)
    outs = [((width, tokens), F32), block]
    outs.append(((width, tokens), F32 if follows else BF16))
    hidden = down_weight[0].shape[2]
    outs += [((8, hidden, half), BF16)] * 3
    parts = [1] * 6
    extra = []
    if follows:
        outs += [block, ((follows[0][0].shape[1], 4 * tokens), F32)]
        outs.append(((width, 2 * hidden), BF16))
        parts += [8, 8, 1]
        extra = [pltpu.SemaphoreType.DMA((3, 2))] * 2
    return fused_call(
        lambda *refs: feed_kernel(gain_at, bool(follows), *refs),
        [token_gated, values, gains, out_weight, up_columns, down_weight] + follows,
        outs,
        [
            pltpu.VMEM((2 * hidden, width), BF16),
            pltpu.VMEM((width, half), F32),
            pltpu.VMEM((2, width, half), F32),
        ]
        + scatter_buffers(width, half)
        + [pltpu.SemaphoreType.DMA((3, 2))] * 4
        + extra,
        collective,
        "feed_forward",
        parts,
    )


def weight_grad(store, rows, columns, left, right, blocks, row_tile, column_tile):
    across = columns // column_tile

    def one(n, carry):
        row, column = span(n // across, row_tile), span(n % across, column_tile)
        total = matmul_nt(left(0, row), right(0, column))
        for block in range(1, blocks):
            total = total + matmul_nt(left(block, row), right(block, column))
        store(n // across, column, total)
        return carry

    lax.fori_loop(0, rows // row_tile * across, one, 0)


def feed_back_kernel(gain_at, gathered, tracks, io, grad_ref, down_weight, gelus, slopes, up_columns,
                     out_weight, mid_ref, gains_ref, token_gated, units, normed, *refs):
    refs = list(refs)
    rings = len(tracks)
    inputs = len(ring_operands(tracks))
    ring_in, refs = refs[:inputs], refs[inputs:]
    state_ref, gated_ref, feed_grads, out_grad, sums_ref = refs[:5]
    large, refs = refs[5 : 5 + rings], refs[5 + rings :]
    ring = None
    if rings:
        sources = [io.source[11 + n] for n in range(inputs)]
        ring = Ring(tracks, ring_in, large, refs[-rings - 2 :], sources)
        refs = refs[: -rings - 2]
    full = grad_ref if gathered else refs.pop(0)
    mixer_low, kept, own, turned, *rest, load_sems = refs
    gated_low = full
    buffers, sems = rest[:6], rest[6:]
    send, recv, gather_send, gather_recv, scatter_send, scatter_recv = sems
    gather_sems, scatter_sems = (gather_send, gather_recv), (scatter_send, scatter_recv)
    if gathered:
        gather_sems = None
    peers = chan_peers()
    me, mate, across, diag = peers
    width, tokens = mid_ref.shape
    half = tokens // 2
    shard = gated_ref.shape[0]
    hidden = down_weight.shape[1]
    tile = 256
    saved = ((io.source[2], gelus), (io.source[3], slopes))
    if gathered:
        saved += ((io.source[0], full),)

    def loads(step, block):
        return [
            pltpu.make_async_copy(source.at[block], target.at[block], load_sems.at[n, step])
            for n, (source, target) in enumerate(saved)
        ]

    for step in range(8):
        for copy in loads(step, block_at(step, peers, not gathered)[2]):
            copy.start()
    greet(peers[1:], ring.toward if rings else ())
    if not gathered:
        io.ready(0)
        for part in range(2):
            full[me * 2 + part] = grad_ref[:, part * half : (part + 1) * half].astype(BF16)
            for kind in range(2):
                gather_copy(block_place(full), peers, gather_sems, kind, part).start()
    if rings:
        ring.start()
    io.ready(1)
    down_rows, out_rows = turned.at[:hidden], turned.at[:width]
    transpose_into(down_rows, down_weight, tile)
    io.ready(4)
    if rings:
        io.ready(*range(11, 11 + rings))

    def partial(block, step):
        for copy in loads(step, block):
            copy.wait()
        grad = full[block]
        for n in range(hidden // tile):
            rows = slice(n * tile, (n + 1) * tile)
            unit_grad = matmul(down_rows[rows], grad)
            slopes[block, rows] = (unit_grad * slopes[block, rows].astype(F32)).astype(BF16)
            gelus[block, rows] = (unit_grad * gelus[block, rows].astype(F32)).astype(BF16)
        return matmul(up_columns[:, :hidden], slopes[block]) + matmul(
            up_columns[:, hidden:], gelus[block]
        )

    run_blocks(peers, full, gather_sems, scatter_sems, buffers, partial, kept, own, ring)
    io.ready(5, 6, 7, 8, 9, 10)
    transpose_into(out_rows, out_weight, tile)
    if not gathered:
        drain_gather(peers, full, gather_sems)

    def a2a(part, n):
        peer = (across, diag, mate)[n]
        return send_to(
            peer,
            gated_low.at[part, span(peer, shard, 32), :],
            gated_ref.at[:, span(me * 2 + part, half)],
            send.at[part, n],
            recv.at[part, n],
        )

    chunk_rows = feed_grads.shape[1] // 3
    row_tile = 384

    def store_grad(kind):
        def store(index, column, total):
            chunks = row_tile // chunk_rows
            for n in range(chunks):
                feed_grads[
                    index * chunks + n, kind * chunk_rows : (kind + 1) * chunk_rows, column
                ] = total[n * chunk_rows : (n + 1) * chunk_rows].astype(BF16)

        return store

    def feed_grad(kind):
        if kind == 0:
            left, right = lambda b, r: full[b, r], lambda b, c: units[b, c]
        else:
            def left(b, r):
                return normed[b, r]

            def right(b, c):
                return (slopes, gelus)[kind - 1][b, c]

        weight_grad(store_grad(kind), width, hidden, left, right, 8, row_tile, tile)

    def store_out(index, column, total):
        out_grad[span(index, tile), column] = total.astype(BF16)

    gain = gains_ref[:, gain_at : gain_at + 1]
    for part in range(2):
        feed_grad(part)
        if rings:
            ring.advance(2 + part, 4)
        columns = slice(part * half, (part + 1) * half)
        grad = scattered(peers, scatter_sems, buffers, own, part)
        change, product = norm_pullback(grad, mid_ref[:, columns], gain)
        before = full[me * 2 + part].astype(F32) if gathered else grad_ref[:, columns]
        state = before + change
        state_ref[:, columns] = state
        mixer_low[:, columns] = state.astype(BF16)
        gated_low[part] = matmul(out_rows[...], mixer_low[:, columns]).astype(BF16)
        for n in range(3):
            a2a(part, n).start()
        if part == 0:
            sums_ref[:, 0:1] = lane_sums(product)
            sums_ref[:, 1:2] = lane_sums(grad)
        else:
            sums_ref[:, 0:1] = sums_ref[:, 0:1] + lane_sums(product)
            sums_ref[:, 1:2] = sums_ref[:, 1:2] + lane_sums(grad)
    io.flush(0)
    feed_grad(2)
    io.flush(2)
    io.flush(4)
    for part in range(2):
        gated_ref[:, span(me * 2 + part, half)] = gated_low[part, span(me, shard, 32), :]
    weight_grad(
        store_out, width, width,
        lambda b, r: mixer_low[r, :], lambda b, c: token_gated[c, :], 1, tile, tile,
    )
    io.flush(3)
    if rings:
        ring.finish()
        for n in range(rings):
            io.flush(5 + n)
    for part in range(2):
        for n in range(3):
            a2a(part, n).wait()
    io.flush(1)
    drain_scatter(peers, scatter_sems, buffers)


def feed_back(grad, mid, gains, normed, up_columns, down_weight, out_weight, token_gated, saved,
              tracks, gain_at, count, collective):
    width, tokens = mid.shape
    half = tokens // 2
    hidden = down_weight[0].shape[2]
    gathered = grad.ndim == 3
    units, gelus, slopes = saved
    own_loads = tuple(range(11, 11 + len(tracks)))
    carries = tuple(range(11 + len(tracks), 11 + len(ring_operands(tracks))))
    manual = (2, 3) + ((0,) if gathered else ()) + carries
    return fused_call(
        lambda *refs: feed_back_kernel(gain_at, gathered, tracks, *refs),
        [grad, down_weight, gelus, slopes, up_columns, out_weight, mid, gains, token_gated, units]
        + [normed]
        + ring_operands(tracks),
        [
            ((width, tokens), F32),
            ((width // 4, 4 * tokens), BF16),
            ((count, 3 * width // count, hidden), BF16),
            ((width, width), BF16),
            ((width, 8), F32),
        ]
        + [one.out() for one in tracks],
        [pltpu.VMEM((8, width, half), BF16)] * (not gathered)
        + [
            pltpu.VMEM((width, tokens), BF16),
            pltpu.VMEM((width, half), F32),
            pltpu.VMEM((2, width, half), F32),
            pltpu.VMEM((max(hidden, width), width), BF16),
        ]
        + scatter_buffers(width, half)
        + [pltpu.SemaphoreType.DMA((2, 3))] * 2
        + [pltpu.SemaphoreType.DMA((3, 2))] * 4
        + [pltpu.SemaphoreType.DMA((3, 8))]
        + ring_scratch(tracks),
        collective,
        "feed_back",
        [1] * (5 + len(tracks)),
        manual=manual,
        order=((0,) if not gathered else ()) + (1, 4) + own_loads,
    )


def project_back_kernel(gain_at, each, tracks, in_track, io, project_grad, weight_ref, square_ref, normed,
                        state_ref, x_ref, gains_ref, *refs):
    inputs = len(ring_operands(tracks))
    ring_in, refs = refs[:inputs], refs[inputs:]
    next_ref, in_grad, sums_ref = refs[:3]
    large, refs = refs[3 : 3 + len(tracks)], refs[3 + len(tracks) :]
    in_held, *refs = refs
    kept, own, weight_rows, in_full, *rest = refs
    buffers, (scatter_send, scatter_recv, *ring_rest) = rest[:6], rest[6:]
    *ring_rest, in_slots, in_send, in_recv = ring_rest
    in_ring = Ring([in_track], [in_grad], [in_held], [in_slots, in_send, in_recv], [in_grad])
    scatter_sems = (scatter_send, scatter_recv)
    peers = chan_peers()
    me, mate, across, diag = peers
    sources = [io.source[7 + n] for n in range(inputs)]
    ring = Ring(tracks, ring_in, large, ring_rest, sources)
    width, tokens = x_ref.shape
    half = tokens // 2
    rows = weight_ref.shape[0]
    shard = rows // 3
    greet((mate, across), ring.toward)
    ring.start()
    io.ready(1)
    for first, size in ((0, 512), (512, rows - 512)):
        weight_rows[:, first : first + size] = weight_ref[first : first + size].T
    io.ready(0)

    def share(owner, part):
        return matmul(weight_rows[...], project_grad[:, span(owner * 2 + part, half)])

    for part in range(2):
        buffers[0][part] = share(diag, part).astype(BF16)
        scatter_copy(peers, buffers, scatter_sems, 0, part).start()
        kept[...] = share(across, part)
        scatter_copy(peers, buffers, scatter_sems, 0, part).wait_recv()
        buffers[4][part] = (kept[...] + buffers[1][part].astype(F32)).astype(BF16)
        scatter_copy(peers, buffers, scatter_sems, 2, part).start()
    for part in range(2):
        buffers[2][part] = share(mate, part).astype(BF16)
        scatter_copy(peers, buffers, scatter_sems, 1, part).start()
        own[part] = share(me, part)
    io.ready(2, 3)
    if in_full.shape[1] > 4 * each:
        in_full[...] = jnp.zeros_like(in_full)
    for chunk in range(shard // each):
        in_full[chunk, 3 * each : 4 * each] = square_ref[chunk * each : (chunk + 1) * each]
    tile = 256
    for stream in range(3):
        def column_tile(n, carry):
            column = span(n, tile)
            total = None
            for block in range(8):
                left = project_grad[
                    stream * shard : (stream + 1) * shard, block * half : (block + 1) * half
                ]
                value = matmul_nt(left, normed[block, column])
                total = value if total is None else total + value
            for chunk in range(shard // each):
                in_full[chunk, stream * each : (stream + 1) * each, column] = total[
                    chunk * each : (chunk + 1) * each
                ]
            return carry

        lax.fori_loop(0, width // tile, column_tile, 0)
    in_grad[...] = in_full[...].astype(BF16)
    in_ring.start()
    io.flush(1)
    io.ready(*range(7, 7 + len(tracks)))
    ring.advance(0, 2)
    io.ready(4, 5, 6)
    gain = gains_ref[:, gain_at : gain_at + 1]
    for part in range(2):
        columns = slice(part * half, (part + 1) * half)
        grad = scattered(peers, scatter_sems, buffers, own, part)
        change, product = norm_pullback(grad, x_ref[:, columns], gain)
        next_ref[:, columns] = state_ref[:, columns] + change
        if part == 0:
            sums_ref[:, 0:1] = lane_sums(product)
            sums_ref[:, 1:2] = lane_sums(grad)
            ring.advance(1, 2)
            in_ring.advance(0, 1)
        else:
            sums_ref[:, 0:1] = sums_ref[:, 0:1] + lane_sums(product)
            sums_ref[:, 1:2] = sums_ref[:, 1:2] + lane_sums(grad)
    io.flush(0)
    io.flush(2)
    ring.finish()
    for n in range(len(tracks)):
        io.flush(3 + n)
    in_ring.finish()
    io.flush(3 + len(tracks))
    drain_scatter(peers, scatter_sems, buffers)


def project_back(project_grad, state, values, gains, normed, weight, square, tracks, gain_at,
                 collective):
    width, tokens = values.shape
    half = tokens // 2
    rows = project_grad.shape[0]
    count = tracks[0].count
    each = rows // 3 // count
    packed = (count, ring_rows(4 * each), width)
    in_track = Track(jax.ShapeDtypeStruct(packed, BF16), 0, count // 4)
    return fused_call(
        lambda *refs: project_back_kernel(gain_at, each, tracks, in_track, *refs),
        [project_grad, weight, square, normed, state, values, gains] + ring_operands(tracks),
        [((width, tokens), F32), (packed, BF16), ((width, 8), F32)]
        + [one.out() for one in tracks + [in_track]],
        [
            pltpu.VMEM((width, half), F32),
            pltpu.VMEM((2, width, half), F32),
            pltpu.VMEM((width, rows), BF16),
            pltpu.VMEM(packed, F32),
        ]
        + scatter_buffers(width, half)
        + [pltpu.SemaphoreType.DMA((3, 2))] * 2
        + ring_scratch(tracks)
        + ring_scratch([in_track]),
        collective,
        "project_back",
        [1] * (4 + len(tracks)),
        manual=tuple(range(7 + len(tracks), 7 + len(ring_operands(tracks)))),
        order=(1, 0) + tuple(range(7, 7 + len(tracks))),
    )


def mask_heads(values, keep, blocks):
    length = values.shape[1] // blocks
    pieces = []
    for j in range(blocks):
        start = j * length
        pieces.append(values[:, start : start + 128] * keep[:, start : start + 128])
        pieces.append(values[:, start + 128 : start + length])
    return jnp.concatenate(pieces, axis=1)


def eight(rows):
    return pl.ds(pl.multiple_of(rows, 8), 8)


def sixteen(rows):
    return pl.ds(pl.multiple_of(rows, 16), 16)


def stream_rows(project_ref, columns_ref, keep_ref, rows, shard, stream, blocks):
    values = project_ref[eight(stream * shard + rows), :]
    total = values * columns_ref[eight(rows), stream : stream + 1]
    for offset in (1, 2):
        moved = mask_heads(pltpu.roll(values, offset, 1), keep_ref[offset - 1 : offset, :], blocks)
        column = 3 * offset + stream
        total = total + moved * columns_ref[eight(rows), column : column + 1]
    return total


def sequence_factor(power, cond, facts, blocks):
    energy = []
    for i in range(blocks):
        total = 0.0
        for j in range(blocks):
            total = total + power[j] * facts.same[i][j]
        energy.append(total * facts.inverse)
    logs = [jnp.log(1.0 + value) for value in energy]
    factor = [
        (1.0 + cond * value) * facts.same[i][i] for i, value in enumerate(logs)
    ]
    return energy, logs, factor


def block_sums(values, blocks):
    length = values.shape[1] // blocks
    return [lane_sums(values[:, i * length : (i + 1) * length]) for i in range(blocks)]


def spread_blocks(columns, length):
    return jnp.concatenate(
        [jnp.broadcast_to(column, (column.shape[0], length)) for column in columns], axis=1
    )


def plain_bins(spectrum_ref, rows, shard, blocks):
    half = spectrum_ref.shape[1] // 2
    bins = []
    for k in range(blocks):
        here = spectrum_ref[eight(k * shard + rows), :]
        bins.append((here[:, :half], here[:, half:]))
    return bins


def filter_bins(spectrum_ref, sign, rows, shard, blocks):
    plain = plain_bins(spectrum_ref, rows, shard, blocks)
    bins = [plain[0]]
    for k in range(1, blocks):
        (real, imag), (before_real, before_imag) = plain[k], plain[k - 1]
        bins.append((real - sign * before_imag, imag + sign * before_real))
    return bins


def store_blocks(target, values, rows, shard, blocks):
    length = values.shape[1] // blocks
    for j in range(blocks):
        target[sixteen(j * shard + rows), :] = values[:, j * length : (j + 1) * length]


def join(halves):
    return jnp.concatenate(halves, axis=0).astype(BF16)


def channel_cuts(shard, streams):
    size = shard // LOADS
    return [(s * shard + n * size, size) for n in range(LOADS) for s in range(streams)]


def channel_order(numbers, streams=3):
    order = []
    for n in range(LOADS):
        for number in numbers:
            each = streams if number == 1 else 1
            order += [(number, n * each + i) for i in range(each)]
    return tuple(order)


def conv_forward_kernel(blocks, carries, io, filter_ref, project_ref, columns_ref, keep_ref,
                        sign_ref, table_ref, seq_ref, carried_in, back_ref, token_gated, conv_ref,
                        carried, gated, signal_low, filter_low, signal_bins, filter_spectrum, out_low,
                        convolved, factor_ref, send, recv, *sems):
    shard, slots = gated.shape
    length = slots // blocks
    scale = 1.0 / length
    size = shard // LOADS
    peers = chan_peers()
    me = peers[0]
    tokens = slots // 4
    parts = carried.shape[0]
    facts = Facts(seq_ref, blocks, length)
    greet(peers[1:])

    def gather(kind, part):
        return gather_copy(
            lambda owner, part: carried.at[part, span(owner, shard, 32), :],
            peers, sems, kind, part,
        )

    def forward(first, last):
        for part in range(parts * first // LOADS, parts * last // LOADS):
            gather(0, part).wait_recv()
            gather(2, part).start()

    io.ready(7)
    for part in range(parts):
        if carries == 1:
            carried[part, span(me, shard, 32), :] = carried_in[part]
        else:
            lanes = carried.shape[2]
            carried[part, span(me, shard, 32), :] = carried_in[:, part * lanes : (part + 1) * lanes]
        for kind in range(2):
            gather(kind, part).start()
    io.ready(2, 3, 4)

    def prepare(base, n, carry):
        rows = base + n * 16
        signals = []
        for part in range(2):
            here = rows + 8 * part
            one, two = (
                stream_rows(project_ref, columns_ref, keep_ref, here, shard, stream, blocks)
                for stream in (1, 2)
            )
            signals.append(one * two)
            cond = columns_ref[eight(here), 9:10]
            _, _, factor = sequence_factor(block_sums(two * two, blocks), cond, facts, blocks)
            for j in range(blocks):
                factor_ref[eight(here), j : j + 1] = factor[j]
        store_blocks(signal_low, join(signals), n * 16, size, blocks)
        kernel = filter_ref[sixteen(rows), :].astype(BF16)
        store_blocks(filter_low, kernel, n * 16, size, blocks)
        return carry

    def combine(n, carry):
        joined = [[] for _ in range(blocks)]
        for part in range(2):
            here = n * 16 + 8 * part
            window = filter_bins(filter_spectrum, sign_ref[0:1, :], here, size, blocks)
            signal = plain_bins(signal_bins, here, size, blocks)
            for i in range(blocks):
                real = imag = None
                for j in range(i, -1, -1):
                    fr, fi = window[i - j]
                    sr, si = signal[j]
                    more_real, more_imag = fr * sr - fi * si, fr * si + fi * sr
                    if j == i:
                        real, imag = more_real, more_imag
                    else:
                        factor = facts.same[i][j]
                        real, imag = real + more_real * factor, imag + more_imag * factor
                joined[i].append(jnp.concatenate([real, imag], axis=1))
        for i in range(blocks):
            out_low[sixteen(i * size + n * 16), :] = join(joined[i])
        return carry

    def finish(base, n, carry):
        rows = base + n * 16
        results = []
        for part in range(2):
            here = rows + 8 * part
            zero = stream_rows(project_ref, columns_ref, keep_ref, here, shard, 0, blocks)
            pieces = []
            for j in range(blocks):
                source = convolved[eight(j * size + n * 16 + 8 * part), :]
                columns = slice(j * length, (j + 1) * length)
                conv_ref[eight(here), columns] = source
                pieces.append(zero[:, columns] * (source * factor_ref[eight(here), j : j + 1]))
            results.append(jnp.concatenate(pieces, axis=1))
        gated[sixteen(rows), :] = join(results)
        return carry

    copies = []
    for n in range(LOADS):
        base = n * size
        io.ready(0, cuts=slice(n, n + 1))
        io.ready(1, cuts=slice(3 * n, 3 * n + 3))
        lax.fori_loop(0, size // 16, lambda i, carry: prepare(base, i, carry), 0)
        if n == 0:
            io.ready(5)
        signal_bins[...] = matmul(signal_low[...], table_ref[...])
        filter_spectrum[...] = matmul(filter_low[...], table_ref[...])
        lax.fori_loop(0, size // 16, combine, 0)
        if n == 0:
            io.ready(8)
        convolved[...] = matmul(out_low[...], back_ref[...]) * scale
        lax.fori_loop(0, size // 16, lambda i, carry: finish(base, i, carry), 0)
        mine = pl.ds(pl.multiple_of(me * shard + base, 16), size)
        copies += exchange(
            peers, lambda peer: gated.at[pl.ds(base, size), span(peer, tokens)],
            lambda: token_gated.at[mine], send.at[n], recv.at[n],
        )
        token_gated[mine, :] = gated[base : base + size, span(me, tokens)]
        io.flush(1, n, pl.ds(base, size))
        forward(n, n + 1)
    for part in range(parts):
        for kind in (1, 2):
            gather(kind, part).wait_recv()
        io.flush(2, part, part)
    for copy in copies:
        copy.wait()
    io.flush(0)
    for part in range(parts):
        for kind in range(3):
            gather(kind, part).wait_send()


def conv_forward(project, filter_rows, columns, keep, sign, table, seq_table, back, carried,
                 carries, blocks, collective):
    shard, slots = filter_rows[0].shape[1:]
    width = 4 * shard
    length = slots // blocks
    rows = blocks * (shard // LOADS)
    low = pltpu.VMEM((rows, length), BF16)
    bins = pltpu.VMEM((rows, 2 * length), F32)
    if carries == 1:
        out = ((carried.shape[0], width, width), BF16)
    else:
        out = ((8, width, slots // 8), BF16)
    return fused_call(
        lambda *refs: conv_forward_kernel(blocks, carries, *refs),
        [filter_rows, project, columns, keep, sign, table, seq_table, carried, back],
        [((width, slots // 4), BF16), ((shard, slots), F32), out],
        [
            pltpu.VMEM((shard, slots), BF16),
            low,
            low,
            bins,
            bins,
            pltpu.VMEM((rows, 2 * length), BF16),
            pltpu.VMEM((rows, length), F32),
            pltpu.VMEM((shard, 128), F32),
        ]
        + [pltpu.SemaphoreType.DMA((LOADS, 3))] * 2
        + [pltpu.SemaphoreType.DMA((3, out[0][0]))] * 2,
        collective,
        "conv_forward",
        [1, LOADS, out[0][0]],
        6,
        (7, 2, 3, 4) + channel_order((1, 0)) + (5, 8),
        {0: channel_cuts(shard, 1), 1: channel_cuts(shard, 3)},
    )


def conv_backward_kernel(blocks, tracks, with_outputs, io, grad_ref, project_ref, conv_ref,
                         filter_ref, columns_ref, keep_ref, sign_ref, table_ref, seq_ref,
                         square_ref, *refs):
    refs = list(refs)
    back_ref = refs.pop(len(ring_operands(tracks)) + with_outputs)
    rings = len(tracks)
    inputs = len(ring_operands(tracks))
    ring_in, refs = refs[:inputs], refs[inputs:]
    if with_outputs:
        residual_ref = refs.pop(0)
    project_grad, filter_pack, square_sum, sums_ref = refs[:4]
    large, refs = refs[4 : 4 + rings], refs[4 + rings :]
    if with_outputs:
        outputs_ref = refs.pop(0)
        *refs, out_land, out_send, out_recv = refs
    sources = [io.source[10 + n] for n in range(inputs)]
    ring = Ring(tracks, ring_in, large, refs[-rings - 2 :], sources)
    refs = refs[: -rings - 2]
    signal_low, filter_low, grad_low, signal_bins, filter_spectrum, grad_bins, *refs = refs
    signal_out, filter_out, mixed, energy_ref, square_land, square_send, square_recv = refs
    signal_grad = filter_spectrum.at[:, : filter_spectrum.shape[1] // 2]
    peers = chan_peers()
    greet(peers[1:], ring.toward)
    ring.start()
    copies = exchange(
        peers, lambda peer: io.source[9].at[peer], lambda: square_land.at[peers[0]],
        square_send, square_recv,
    )
    if with_outputs:
        copies += to_channels(
            peers, io.source[10 + inputs], out_land, out_send, out_recv
        )
    io.ready(4, 5, 6)
    shard, slots = grad_ref.shape
    length = slots // blocks
    scale = 1.0 / length
    steps = shard // 16
    facts = Facts(seq_ref, blocks, length)

    def prepare(n, carry):
        rows = n * 16
        signals, scaled = [], []
        grads = grad_ref[sixteen(rows), :].astype(F32)
        for part in range(2):
            here = rows + 8 * part
            zero, one, two = (
                stream_rows(project_ref, columns_ref, keep_ref, here, shard, stream, blocks)
                for stream in range(3)
            )
            mixed[0, eight(here), :] = one
            mixed[1, eight(here), :] = two
            signals.append(one * two)
            cond = columns_ref[eight(here), 9:10]
            power = block_sums(two * two, blocks)
            energy, logs, factor = sequence_factor(power, cond, facts, blocks)
            conv_grad = grads[8 * part : 8 * part + 8] * zero
            factor_grad = block_sums(conv_grad * conv_ref[eight(here), :], blocks)
            cond_grad = 0.0
            for j in range(blocks):
                cond_grad = cond_grad + factor_grad[j] * logs[j]
            sums_ref[eight(here), 9:10] = cond_grad
            for i in range(blocks):
                total = 0.0
                for j in range(blocks):
                    total = total + factor_grad[j] * facts.same[i][j]
                energy_ref[eight(here), i : i + 1] = (
                    total * cond / (1.0 + energy[i]) * (2.0 * facts.inverse)
                )
                energy_ref[eight(here), blocks + i : blocks + i + 1] = factor[i]
            scaled.append(conv_grad * spread_blocks([one * scale for one in factor], length))
        store_blocks(signal_low, join(signals), rows, shard, blocks)
        store_blocks(grad_low, join(scaled), rows, shard, blocks)
        kernel = filter_ref[sixteen(rows), :].astype(BF16)
        store_blocks(filter_low, kernel, rows, shard, blocks)
        return carry

    for n in range(LOADS):
        for number, each in ((0, 1), (1, 3), (2, 1), (3, 1)):
            io.ready(number, cuts=slice(n * each, (n + 1) * each))
        lax.fori_loop(steps * n // LOADS, steps * (n + 1) // LOADS, prepare, 0)
    io.ready(7)
    io.ready(*range(10, 10 + rings))
    grad_bins[...] = matmul(grad_low[...], table_ref[...])
    signal_bins[...] = matmul(signal_low[...], table_ref[...])
    filter_spectrum[...] = matmul(filter_low[...], table_ref[...])
    ring.advance(0, 3)

    def combine(n, carry):
        rows = n * 16
        sign = sign_ref[0:1, :]
        joined = [[] for _ in range(blocks)]
        windows = [[] for _ in range(blocks)]
        for part in range(2):
            here = rows + 8 * part
            window = filter_bins(filter_spectrum, sign, here, shard, blocks)
            signal = plain_bins(signal_bins, here, shard, blocks)
            grads = plain_bins(grad_bins, here, shard, blocks)
            for j in range(blocks):
                for i in range(j, blocks):
                    fr, fi = window[i - j]
                    gr, gi = grads[i]
                    more_real, more_imag = fr * gr + fi * gi, fr * gi - fi * gr
                    if i == j:
                        real, imag = more_real, more_imag
                    else:
                        factor = facts.same[i][j]
                        real, imag = real + more_real * factor, imag + more_imag * factor
                joined[j].append(jnp.concatenate([real, imag], axis=1))
            after = None
            for k in reversed(range(blocks)):
                real = imag = None
                for j in range(blocks - k):
                    sr, si = signal[j]
                    gr, gi = grads[j + k]
                    more_real, more_imag = sr * gr + si * gi, sr * gi - si * gr
                    if k:
                        factor = facts.same[j + k][j]
                        more_real, more_imag = more_real * factor, more_imag * factor
                    real = more_real if real is None else real + more_real
                    imag = more_imag if imag is None else imag + more_imag
                if after is None:
                    whole = (real, imag)
                else:
                    whole = (real + sign * after[1], imag - sign * after[0])
                windows[k].append(jnp.concatenate(whole, axis=1))
                after = (real, imag)
        for j in range(blocks):
            signal_out[sixteen(j * shard + rows), :] = join(joined[j])
            filter_out[sixteen(j * shard + rows), :] = join(windows[j])
        return carry

    lax.fori_loop(0, steps, combine, 0)
    io.ready(10 + inputs + with_outputs)
    signal_grad[...] = matmul(signal_out[...], back_ref[...])
    ring.advance(1, 3)
    filter_rows = matmul(filter_out[...], back_ref[...])
    count, pack_rows, lanes = filter_pack.shape
    each = shard // count
    stack = slots // lanes
    if pack_rows > stack * each:
        filter_pack[...] = jnp.zeros_like(filter_pack)
    for chunk in range(count):
        lags = [
            filter_rows[j * shard + chunk * each : j * shard + (chunk + 1) * each]
            for j in range(blocks)
        ]
        layers = [
            jnp.concatenate(lags[n * blocks // stack : (n + 1) * blocks // stack], axis=1)
            for n in range(stack)
        ]
        value = layers[0] if stack == 1 else jnp.concatenate(layers, axis=0)
        filter_pack[chunk, : stack * each] = value.astype(BF16)
    io.flush(1)

    def finish(n, carry):
        rows = n * 16
        totals = [[] for _ in range(3)]
        outer = grad_ref[sixteen(rows), :].astype(F32)
        for part in range(2):
            here = rows + 8 * part
            local = eight(here)
            factor = [energy_ref[local, blocks + i : blocks + i + 1] for i in range(blocks)]
            energy = [energy_ref[local, i : i + 1] for i in range(blocks)]
            signal = jnp.concatenate(
                [signal_grad[eight(j * shard + here), :] for j in range(blocks)], axis=1
            )
            for stream in range(3):
                if stream == 0:
                    value = outer[8 * part : 8 * part + 8] * (
                        conv_ref[local, :] * spread_blocks(factor, length)
                    )
                elif stream == 1:
                    value = signal * mixed[1, local, :]
                else:
                    value = signal * mixed[0, local, :] + (
                        spread_blocks(energy, length) * mixed[1, local, :]
                    )
                plain = project_ref[eight(stream * shard + here), :]
                total = value * columns_ref[local, stream : stream + 1]
                sums_ref[local, stream : stream + 1] = lane_sums(value * plain)
                for offset in (1, 2):
                    column = 3 * offset + stream
                    moved = pltpu.roll(
                        mask_heads(value, keep_ref[offset - 1 : offset, :], blocks),
                        slots - offset, 1,
                    )
                    sums_ref[local, column : column + 1] = lane_sums(moved * plain)
                    total = total + moved * columns_ref[local, column : column + 1]
                totals[stream].append(total)
        for stream in range(3):
            project_grad[sixteen(stream * shard + rows), :] = join(totals[stream])
        return carry

    lax.fori_loop(0, steps // 2, finish, 0)
    ring.advance(2, 3)
    lax.fori_loop(steps // 2, steps, finish, 0)
    for stream in range(3):
        io.flush(0, stream, pl.ds(stream * shard, shard))
    for copy in copies:
        copy.wait()
    io.ready(9)
    total = square_ref[peers[0]].astype(F32)
    for peer in peers[1:]:
        total = total + square_land[peer].astype(F32)
    square_sum[...] = total
    io.flush(2)
    if with_outputs:
        io.ready(10 + inputs)
        tokens = residual_ref.shape[1]
        out_land[:, span(peers[0], tokens)] = residual_ref[span(peers[0], shard, 32), :]
        outputs_ref[...] = out_land[...].astype(F32)
        io.flush(4 + rings)
    io.flush(3)
    ring.finish()
    for n in range(rings):
        io.flush(4 + n)


def filter_layout(shard, slots, count):
    each = shard // count
    stack = 2 if each % 8 == 0 else 1
    return count, ring_rows(stack * each), slots // stack


def conv_backward(grad, project, conv, filter_rows, columns, keep, sign, table, seq_table, back, square,
                  tracks, residual, blocks, collective):
    shard, slots = filter_rows[0].shape[1:]
    length = slots // blocks
    low = pltpu.VMEM((blocks * shard, length), BF16)
    bins = pltpu.VMEM((blocks * shard, 2 * length), F32)
    out = pltpu.VMEM((blocks * shard, 2 * length), BF16)
    outs, extra = [], []
    if residual:
        outs = [((shard, slots), F32)]
        extra = [pltpu.VMEM((shard, slots), BF16)] + [pltpu.SemaphoreType.DMA((3,))] * 2
    return fused_call(
        lambda *refs: conv_backward_kernel(blocks, tracks, bool(residual), *refs),
        [grad, project, conv, filter_rows, columns, keep, sign, table, seq_table, square]
        + ring_operands(tracks)
        + list(residual)
        + [back],
        [
            ((3 * shard, slots), BF16),
            (filter_layout(shard, slots, tracks[0].count), BF16),
            ((shard, 4 * shard), F32),
            ((shard, 128), F32),
        ]
        + [one.out() for one in tracks]
        + outs,
        [low, low, low, bins, bins, bins, out, out]
        + [pltpu.VMEM((2, shard, slots), F32), pltpu.VMEM((shard, 128), F32)]
        + [pltpu.VMEM(square.shape, BF16)]
        + [pltpu.SemaphoreType.DMA((3,))] * 2
        + ring_scratch(tracks)
        + extra,
        collective,
        "conv_backward",
        [3, 1, 1, 1] + [1] * (len(tracks) + len(outs)),
        8,
        (4, 5, 6) + channel_order((0, 1, 2, 3)) + (7,),
        {0: channel_cuts(shard, 1), 1: channel_cuts(shard, 3), 2: channel_cuts(shard, 1)}
        | {3: channel_cuts(shard, 1)},
        tuple(range(10 + len(tracks), 10 + len(ring_operands(tracks)))),
    )


def last_kernel(layers, tracks, io, state_ref, *refs):
    refs = list(refs)
    gain_sums, refs = refs[: 2 * layers], refs[2 * layers :]
    row_sums, refs = refs[:layers], refs[layers:]
    rings, inputs = len(tracks), len(ring_operands(tracks))
    ring_in, refs = refs[:inputs], refs[inputs:]
    input_grad, small_out = refs[:2]
    large, refs = refs[2 : 2 + rings], refs[2 + rings :]
    state_low, landing, sums, turn, gains, gains_land, small_own, small_land, *refs = refs
    chan_send, chan_recv, small_send, small_recv, state_send, state_recv, *refs = refs
    peers = chan_peers()
    me = peers[0]
    dp = lax.axis_index("dp")
    first = 1 + 3 * layers
    ring = Ring(tracks, ring_in, large, refs, [io.source[first + n] for n in range(inputs)])
    count = ring.count
    shard = landing.shape[0]
    greet(peers[1:], [(dp + offset) % count for offset in range(1, count)])
    ring.start()
    io.ready(*range(0, first))
    for layer in range(layers):
        sums[:, 4 * layer : 4 * layer + 2] = gain_sums[2 * layer][:, 0:2]
        sums[:, 4 * layer + 2 : 4 * layer + 4] = gain_sums[2 * layer + 1][:, 0:2]
    turn[...] = jnp.zeros_like(turn)
    for owner in range(4):
        turn[:shard, : 4 * layers] = sums[owner * shard : (owner + 1) * shard, : 4 * layers]
        gains[owner] = turn[...].T[: 4 * layers]
    copies = exchange(
        peers, lambda peer: gains.at[peer], lambda: gains_land.at[me], chan_send, chan_recv
    )
    state_low[...] = state_ref[...].astype(BF16)
    state_copies = to_channels(peers, state_low, landing, state_send, state_recv)
    landing[:, span(me, state_low.shape[1])] = state_low[span(me, shard, 32), :]
    io.ready(*range(first, first + rings))
    ring.advance(0, 6)
    for layer in range(layers):
        turn[:shard, 10 * layer : 10 * layer + 10] = row_sums[layer][:, 0:10]
    small_own[4 * layers :, :] = turn[...].T[: small_own.shape[0] - 4 * layers]
    for copy in copies:
        copy.wait()
    total = gains[me]
    for peer in peers[1:]:
        total = total + gains_land[peer]
    small_own[: 4 * layers, :] = total
    small_copies = []
    for offset in range(1, count):
        copy = pltpu.make_async_remote_copy(
            small_own,
            small_land.at[offset - 1],
            small_send.at[offset - 1],
            small_recv.at[offset - 1],
            device_id={"dp": (dp + offset) % count},
        )
        copy.start()
        small_copies.append(copy)
    for point in range(1, 4):
        ring.advance(point, 6)
    small = small_own[...]
    for copy in small_copies:
        copy.wait()
    for n in range(count - 1):
        small = small + small_land[n]
    small_out[...] = small
    io.flush(1)
    ring.advance(4, 6)
    for copy in state_copies:
        copy.wait()
    input_grad[...] = landing[...].astype(F32)
    io.flush(0)
    ring.advance(5, 6)
    ring.finish()
    for n in range(rings):
        io.flush(2 + n)


def last_sums(state, gain_sums, row_sums, tracks, collective):
    width, tokens = state.shape
    shard = width // 4
    layers = len(row_sums)
    count = tracks[0].count
    small = (-(-14 * layers // 8) * 8, 256)
    return fused_call(
        lambda *refs: last_kernel(layers, tracks, *refs),
        [state] + gain_sums + row_sums + ring_operands(tracks),
        [((shard, 4 * tokens), F32), (small, F32)] + [one.out() for one in tracks],
        [
            pltpu.VMEM((width, tokens), BF16),
            pltpu.VMEM((shard, 4 * tokens), BF16),
            pltpu.VMEM((width, 128), F32),
            pltpu.VMEM((256, 128), F32),
            pltpu.VMEM((4, 4 * layers, 256), F32),
            pltpu.VMEM((4, 4 * layers, 256), F32),
            pltpu.VMEM(small, F32),
            pltpu.VMEM((count - 1,) + small, F32),
            pltpu.SemaphoreType.DMA((3,)),
            pltpu.SemaphoreType.DMA((3,)),
            pltpu.SemaphoreType.DMA((count - 1,)),
            pltpu.SemaphoreType.DMA((count - 1,)),
            pltpu.SemaphoreType.DMA((3,)),
            pltpu.SemaphoreType.DMA((3,)),
        ]
        + ring_scratch(tracks),
        collective,
        "last_sums",
        [1] * (2 + len(tracks)),
        order=tuple(range(1, 1 + 3 * layers)) + (0,),
        manual=tuple(
            range(1 + 3 * layers + len(tracks), 1 + 3 * layers + len(ring_operands(tracks)))
        ),
    )


def collect_kernel(layers, *refs):
    refs = list(refs)
    outputs_in, input_in, small = refs[:3]
    refs = refs[3:]
    feeds, refs = refs[:layers], refs[layers:]
    filters, refs = refs[:layers], refs[layers:]
    packs, refs = refs[:layers], refs[layers:]
    (outputs, input_grad, mix_gain, mix_bias, in_grad, short, filter_grad, cond, out_grad, glu_gain,
     glu_bias, up_grad, down_grad, held, sems) = refs
    pairs = ((outputs_in, outputs), (input_in, input_grad))
    loads = [
        pltpu.make_async_copy(source, held.at[n], sems.at[n]) for n, (source, _) in enumerate(pairs)
    ]
    copies = [
        pltpu.make_async_copy(held.at[n], target, sems.at[2 + n])
        for n, (_, target) in enumerate(pairs)
    ]
    for copy in loads:
        copy.start()
    each = in_grad.shape[1]
    shard = cond.shape[1]
    lanes = filters[0].shape[1]
    for layer in range(layers):
        for kind, out in enumerate((mix_gain, mix_bias, glu_gain, glu_bias)):
            row = 4 * layer + kind
            out[layer : layer + 1, :] = small[row : row + 1, :shard]
        row = 4 * layers + 10 * layer
        for tap in range(3):
            short[layer, tap] = small[row + 3 * tap : row + 3 * tap + 3, :shard]
        cond[layer : layer + 1, :] = small[row + 9 : row + 10, :shard]
        for stream in range(3):
            in_grad[layer, :, stream, :] = packs[layer][stream * each : (stream + 1) * each]
        out_grad[layer] = packs[layer][3 * each : 4 * each]
        for n in range(filter_grad.shape[2] // lanes):
            filter_grad[layer, :, n * lanes : (n + 1) * lanes] = filters[layer][
                n * each : (n + 1) * each
            ]
        rows = down_grad.shape[1]
        down_grad[layer] = feeds[layer][:rows]
        for kind in range(2):
            up_grad[layer, :, kind, :] = feeds[layer][(kind + 1) * rows : (kind + 2) * rows]
        loads[layer].wait()
        copies[layer].start()
    for copy in copies:
        copy.wait()


def collect(outputs, input_grad, small, feeds, filters, packs, each):
    layers = len(feeds)
    shard, slots = outputs.shape
    width = 4 * shard
    rows, hidden = feeds[0].shape[0] // 3, feeds[0].shape[1]
    anywhere = pl.BlockSpec(memory_space=pl.ANY)
    local = pl.BlockSpec(memory_space=pltpu.VMEM)
    operands = [outputs, input_grad, small, *feeds, *filters, *packs]
    small_shape = (layers, shard)
    shapes = [
        (shard, slots), (shard, slots), small_shape, small_shape, (layers, each, 3, width),
        (layers, 3, 3, shard), (layers, each, slots), small_shape, (layers, each, width),
        small_shape, small_shape, (layers, rows, 2, hidden), (layers, rows, hidden),
    ]
    return pl.pallas_call(
        lambda *refs: collect_kernel(layers, *refs),
        out_shape=tuple(jax.ShapeDtypeStruct(shape, F32) for shape in shapes),
        in_specs=[anywhere] * 2 + [local] * (len(operands) - 2),
        out_specs=tuple([anywhere] * 2 + [local] * (len(shapes) - 2)),
        scratch_shapes=[pltpu.VMEM((2, shard, slots), F32), pltpu.SemaphoreType.DMA((4,))],
        compiler_params=pltpu.CompilerParams(vmem_limit_bytes=VMEM_LIMIT),
        name="collect",
    )(*operands)


def body(
    inputs,
    seq_table,
    mix_gain,
    mix_bias,
    in_proj,
    short_conv,
    long_filter,
    cond_weight,
    out_proj,
    glu_gain,
    glu_bias,
    glu_in,
    glu_out,
    cotangent,
):
    shard, slots = inputs.shape
    layers, width = in_proj.shape[0], in_proj.shape[3]
    hidden = glu_out.shape[2]
    blocks = 4
    count = lax.axis_size("dp")
    each = shard // count
    table = jnp.asarray(dft_table(slots // blocks), BF16)
    sign = jnp.asarray(np.tile(1.0 - 2.0 * (np.arange(slots // blocks) % 2), (8, 1)), F32)
    residual, gains, normed, project, in_rows, up_columns, columns, keep = first_project(
        inputs, (mix_gain, mix_bias, glu_gain, glu_bias), in_proj, short_conv, cond_weight,
        (glu_in, 0), seq_table, 1,
    )
    constants = (keep, sign, table, seq_table, jnp.asarray(dft_table(slots // blocks).T, BF16))
    kept, state = [], None
    for l in range(layers):
        token_gated, conv, carried = conv_forward(
            project, (long_filter, l), (columns, l), *constants, cotangent if l else out_proj,
            2 if l else 1, blocks, 10 + l,
        )
        if l:
            state = carried
        else:
            full_out = carried
        middle, normed_glu, after, *rest = feed_forward(
            token_gated, residual, gains, (full_out, l), up_columns, (glu_out, l),
            ((in_rows, l + 1), (glu_in, l + 1)) if l + 1 < layers else (), 4 * l + 2, 20 + l,
        )
        saved, follow = [up_columns] + rest[:3], rest[3:]
        kept.append((residual, normed, project, conv, token_gated, middle, normed_glu, saved))
        residual = after
        if follow:
            normed, project, up_columns = follow
    feeds, filters, packs, gain_sums, row_sums = ([None] * layers for _ in range(5))
    waiting = []
    for l in reversed(range(layers)):
        before, normed, project, conv, token_gated, middle, normed_glu, saved = kept[l]
        top = l == layers - 1
        state, gated_grad, feed_grads, out_grad, glu_sums, *large = feed_back(
            state, middle, gains, normed_glu, saved[0], (glu_out, l), (full_out, l), token_gated,
            saved[1:], waiting, 4 * l + 2, count, 30 + l,
        )
        if waiting:
            filters[l + 1], packs[l + 1], feeds[l + 1] = large
        one, two = (3 * count // 8, 5 * count // 8) if l else (count // 2, count - 1)
        project_low, filter_pack, square, row_sums[l], held, *rest = conv_backward(
            gated_grad, project, conv, (long_filter, l), (columns, l), *constants,
            out_grad.reshape(4, shard, width), [Track(feed_grads, 0, one)],
            (residual,) if top else (), blocks, 40 + l,
        )
        if top:
            outputs = rest[0]
        tracks = [Track(feed_grads, one, two, held), Track(filter_pack, 0, count // 4)]
        state, in_pack, mix_sums, feed_held, held, in_held = project_back(
            project_low, state, before, gains, normed, (in_rows, l), square,
            tracks, 4 * l, 50 + l,
        )
        waiting = [
            Track(filter_pack, count // 4, count - 1, held),
            Track(in_pack, count // 4, count - 1, in_held),
        ]
        if l:
            waiting.append(Track(feed_grads, two, count - 1, feed_held))
        else:
            feeds[0] = feed_held
        gain_sums[l] = [mix_sums, glu_sums]
    input_grad, small, filters[0], packs[0] = last_sums(
        state, [one for pair in gain_sums for one in pair], row_sums, waiting, 60
    )
    return collect(outputs, input_grad, small, feeds, filters, packs, each)


def solution(mesh):
    in_specs = (
        P("chan", "dp"),
        P("dp", None),
        P(None, "chan"),
        P(None, "chan"),
        P(None, "chan", None, None),
        P(None, None, None, "chan"),
        P(None, "chan", None),
        P(None, "chan"),
        P(None, "chan", None),
        P(None, "chan"),
        P(None, "chan"),
        P(None, None, None, "chan"),
        P(None, None, "chan"),
        P("chan", "dp"),
    )
    out_specs = (
        P("chan", "dp"),
        P("chan", "dp"),
        P(None, "chan"),
        P(None, "chan"),
        P(None, ("chan", "dp"), None, None),
        P(None, None, None, "chan"),
        P(None, ("chan", "dp"), None),
        P(None, "chan"),
        P(None, ("chan", "dp"), None),
        P(None, "chan"),
        P(None, "chan"),
        P(None, "dp", None, "chan"),
        P(None, "dp", "chan"),
    )
    return jax.shard_map(body, mesh=mesh, in_specs=in_specs, out_specs=out_specs, check_vma=False)
```

```python
import math

import jax
import jax.numpy as jnp
import numpy as np
from jax import lax
from jax.experimental import pallas as pl
from jax.experimental.pallas import tpu as pltpu
from jax.sharding import PartitionSpec as P

EPSILON = 1e-05
F32 = jnp.float32
BF16 = jnp.bfloat16
VMEM_LIMIT = 63 * 2**20
LOADS = 4


def dft_table(block_len):
    period = 2 * block_len
    position = np.arange(block_len)[:, None]
    phase = ((2 * np.arange(block_len)[None, :] + 1) * position) % (2 * period)
    phase = phase * (math.pi / period)
    return np.concatenate([np.cos(phase), -np.sin(phase)], axis=1)


class Facts:
    def __init__(self, table_ref, blocks, block_len):
        length, count = table_ref[0, 0], table_ref[0, 1]
        used = length * count
        pair = jnp.where(length >= 2 * block_len, 1.0, 0.0)
        four = jnp.where(length >= 4 * block_len, 1.0, 0.0)
        active = [jnp.where(i * block_len < used, 1.0, 0.0) for i in range(blocks)]
        self.same = [[None] * blocks for _ in range(blocks)]
        for i in range(blocks):
            for j in range(blocks):
                if i == j:
                    self.same[i][j] = active[i]
                else:
                    joined = pair if i // 2 == j // 2 else four
                    self.same[i][j] = active[i] * active[j] * joined
        shortest = 1.0 / block_len
        self.inverse = shortest * (1.0 - 0.5 * pair - 0.25 * four)


class Io:
    def __init__(self, source, loads, stores):
        self.source, self.loads, self.stores, self.pending = source, loads, stores, []

    def ready(self, *numbers, cuts=None):
        for number in numbers:
            for copy in self.loads[number] if cuts is None else self.loads[number][cuts]:
                copy.wait()

    def flush(self, number, part=0, at=None):
        source, target, sems = self.stores[number]
        if at is not None:
            source, target = source.at[at], target.at[at]
        copy = pltpu.make_async_copy(source, target, sems.at[part])
        copy.start()
        self.pending.append(copy)

    def finish(self):
        for copy in self.pending:
            copy.wait()


def fused_call(kernel, operands, outs, scratch, collective, name, parts, scalars=-1, order=(),
               cuts=None, manual=()):
    arrays, layers = [], []
    for operand in operands:
        array, layer = operand if isinstance(operand, tuple) else (operand, None)
        arrays.append(array)
        layers.append(layer)
    cuts = cuts or {}
    inputs, results = len(arrays), len(outs)
    buffers, sems = [], []
    for number, (array, layer) in enumerate(zip(arrays, layers)):
        if number != scalars:
            buffers.append(pltpu.VMEM(array.shape if layer is None else array.shape[1:], array.dtype))
            sems.append(pltpu.SemaphoreType.DMA((len(cuts.get(number, (0,))),)))
    for (shape, dtype), count in zip(outs, parts):
        buffers.append(pltpu.VMEM(shape, dtype))
        sems.append(pltpu.SemaphoreType.DMA((count,)))

    def body(*refs):
        extra = list(refs[inputs + results + len(scratch) :])
        places, marks = extra[: len(buffers)], extra[len(buffers) :]
        sources, loads, stores, views, n = {}, {}, {}, [], 0
        for number in range(inputs):
            if number == scalars:
                views.append(refs[number])
                continue
            source = refs[number]
            if layers[number] is not None:
                source = source.at[layers[number]]
            sources[number] = source
            views.append(places[n])
            if number not in manual:
                pairs = [(source, places[n])]
                if number in cuts:
                    rows = [pl.ds(*one) for one in cuts[number]]
                    pairs = [(source.at[one], places[n].at[one]) for one in rows]
                loads[number] = [
                    pltpu.make_async_copy(*pair, marks[n].at[i]) for i, pair in enumerate(pairs)
                ]
            n += 1
        for number in range(results):
            stores[number] = (places[n], refs[inputs + number], marks[n])
            views.append(places[n])
            n += 1
        started = set()
        for one in list(order) + list(loads):
            number, chosen = one if isinstance(one, tuple) else (one, None)
            for i, copy in enumerate(loads[number]):
                if (chosen is None or i == chosen) and (number, i) not in started:
                    started.add((number, i))
                    copy.start()
        io = Io(sources, loads, stores)
        kernel(io, *views, *refs[inputs + results : inputs + results + len(scratch)])
        io.finish()

    anywhere = pl.BlockSpec(memory_space=pl.ANY)
    scalar_spec = pl.BlockSpec(memory_space=pltpu.SMEM)
    params = {}
    if collective is not None:
        params = dict(collective_id=collective, has_side_effects=True)
    return pl.pallas_call(
        body,
        out_shape=tuple(jax.ShapeDtypeStruct(*out) for out in outs),
        in_specs=[scalar_spec if n == scalars else anywhere for n in range(inputs)],
        out_specs=tuple([anywhere] * results),
        scratch_shapes=list(scratch) + buffers + sems,
        compiler_params=pltpu.CompilerParams(vmem_limit_bytes=VMEM_LIMIT, **params),
        name=name,
    )(*arrays)


def ring_position(index, count):
    odd = index % 2
    return (1 - odd) * (index // 2) + odd * (count - 1 - index // 2)


def ring_member(position, count):
    late = position // (count // 2)
    return (1 - late) * 2 * position + late * (2 * (count - 1 - position) + 1)


def chan_peers():
    me = lax.axis_index("chan")
    mate = me + 1 - 2 * (me % 2)
    across = (me + 2) % 4
    return me, mate, across, (mate + 2) % 4


def greet(peers, members=()):
    barrier = pltpu.get_barrier_semaphore()
    for peer in peers:
        pl.semaphore_signal(barrier, inc=1, device_id={"chan": peer})
    for member in members:
        pl.semaphore_signal(barrier, inc=1, device_id={"dp": member})
    pl.semaphore_wait(barrier, len(peers) + len(members))


def send_to(peer, source, target, send, recv):
    return pltpu.make_async_remote_copy(source, target, send, recv, device_id={"chan": peer})


def span(index, size, unit=None):
    if isinstance(index, int):
        return pl.ds(index * size, size)
    return pl.ds(pl.multiple_of(index * size, unit or size), size)


def gather_copy(place, peers, sems, kind, part):
    me, mate, across, _ = peers
    block = place(across if kind == 2 else me, part)
    send, recv = sems
    return send_to(
        across if kind == 0 else mate, block, block, send.at[kind, part], recv.at[kind, part]
    )


def norm_columns(values):
    mean = jnp.mean(values, axis=0, keepdims=True)
    center = values - mean
    inverse = lax.rsqrt(jnp.mean(center * center, axis=0, keepdims=True) + EPSILON)
    return center * inverse, inverse


def norm_pullback(grad, values, gain):
    normal, inverse = norm_columns(values)
    product = grad * normal
    scaled = grad * gain
    first = jnp.mean(scaled, axis=0, keepdims=True)
    second = jnp.mean(product * gain, axis=0, keepdims=True)
    return inverse * (scaled - first - normal * second), product


def lane_sums(values):
    return jnp.sum(values, axis=1, keepdims=True)


def matmul(left, right):
    return jnp.dot(left, right, preferred_element_type=F32)


def matmul_nt(left, right):
    return lax.dot_general(
        left, right, (((1,), (1,)), ((), ())), preferred_element_type=F32
    )


def transpose_into(target, source, tile):
    for n in range(source.shape[0] // tile):
        target[:, n * tile : (n + 1) * tile] = source[n * tile : (n + 1) * tile].T


def transpose_columns(target, source, tile):
    for n in range(source.shape[1] // tile):
        target[n * tile : (n + 1) * tile, :] = source[:, n * tile : (n + 1) * tile].T


def exchange(peers, source, target, send, recv):
    copies = []
    for n, peer in enumerate((peers[2], peers[3], peers[1])):
        copy = send_to(peer, source(peer), target(), send.at[n], recv.at[n])
        copy.start()
        copies.append(copy)
    return copies


def to_channels(peers, low, landing, send, recv):
    shard, tokens = landing.shape[0], low.shape[1]
    me = peers[0]
    mine = span(me, tokens)
    copies = exchange(
        peers, lambda peer: low.at[span(peer, shard, 32), :], lambda: landing.at[:, mine], send, recv
    )
    return copies


class Track:
    def __init__(self, own, first, last, carry=None):
        self.own, self.first, self.last, self.carry = own, first, last, carry
        self.count, self.rows, self.lanes = own.shape

    def out(self):
        if self.last == self.count - 1:
            return ((self.rows, self.lanes), F32)
        return ((2, self.rows, self.lanes // 2), BF16)


def ring_operands(tracks):
    return [one.own for one in tracks] + [one.carry for one in tracks if one.first]


def ring_scratch(tracks):
    slots = [
        pltpu.VMEM((one.last - one.first, 2, one.rows, one.lanes // 2), BF16) for one in tracks
    ]
    if not tracks:
        return []
    longest = max(one.last - one.first for one in tracks)
    return slots + [pltpu.SemaphoreType.DMA((longest, len(tracks), 2))] * 2


class Ring:
    def __init__(self, tracks, operands, outs, scratch, sources):
        self.tracks, self.outs = tracks, outs
        self.count = tracks[0].count
        self.owns = operands[: len(tracks)]
        self.sources = sources[: len(tracks)]
        carries = list(sources[len(tracks) :])
        self.carries = [carries.pop(0) if one.first else None for one in tracks]
        *self.slots, self.send, self.recv = scratch
        self.here = lax.axis_index("dp")
        self.place = ring_position(self.here, self.count)
        after = ring_member((self.place + 1) % self.count, self.count)
        before = ring_member((self.place + self.count - 1) % self.count, self.count)
        self.toward = (after, before)
        self.rounds = max(one.last - one.first for one in tracks) - 1

    def copy(self, track, direction, turn, source):
        return pltpu.make_async_remote_copy(
            source,
            self.slots[track].at[turn, direction],
            self.send.at[turn, track, direction],
            self.recv.at[turn, track, direction],
            device_id={"dp": self.toward[direction]},
        )

    def owner(self, direction, step):
        move = step + 1
        if direction == 0:
            move = self.count - move
        return ring_member((self.place + move) % self.count, self.count)

    def own(self, track, direction, owner, owns=None):
        own = (owns or self.owns)[track]
        half = own.shape[2] // 2
        return own.at[owner, :, pl.ds(direction * half, half)]

    def held(self, track, direction, turn):
        return self.slots[track].at[turn, direction]

    def start(self):
        for track, carry in enumerate(self.carries):
            for direction in range(2):
                if carry is None:
                    source = self.own(track, direction, self.owner(direction, 0), self.sources)
                else:
                    source = carry.at[direction]
                self.copy(track, direction, 0, source).start()

    def round(self, turn, extra):
        for track, info in enumerate(self.tracks):
            def one(track=track, info=info):
                for direction in range(2):
                    held = self.held(track, direction, turn - 1)
                    self.copy(track, direction, turn - 1, held).wait_recv()
                    own = self.own(track, direction, self.owner(direction, info.first + turn))
                    held[...] = (held[...].astype(F32) + own[...].astype(F32)).astype(BF16)
                    self.copy(track, direction, turn, held).start()

            if info.last - info.first - 1 == self.rounds:
                one()
            else:
                pl.when(turn < info.last - info.first)(one)
        return extra

    def advance(self, point, points):
        first, last = self.rounds * point // points, self.rounds * (point + 1) // points
        if isinstance(point, int) and last == first:
            return
        if isinstance(point, int) and last == first + 1:
            self.round(last, 0)
            return
        lax.fori_loop(1 + first, 1 + last, self.round, 0)

    def loop(self, body, steps, point, pieces, points):
        for n in range(pieces):
            lax.fori_loop(steps * n // pieces, steps * (n + 1) // pieces, body, 0)
            self.advance(point + n, points)

    def finish(self):
        for track, (info, out) in enumerate(zip(self.tracks, self.outs)):
            turns = info.last - info.first
            half = info.lanes // 2
            whole = info.last == self.count - 1
            for direction in range(2):
                held = self.held(track, direction, turns - 1)
                self.copy(track, direction, turns - 1, held).wait_recv()
                owner = self.here if whole else self.owner(direction, info.last)
                own = self.own(track, direction, owner)
                total = held[...].astype(F32) + own[...].astype(F32)
                if whole:
                    out[:, pl.ds(direction * half, half)] = total
                else:
                    out[direction] = total.astype(BF16)

        def settle(turn, extra):
            for track, info in enumerate(self.tracks):
                def one(track=track):
                    for direction in range(2):
                        held = self.held(track, direction, turn)
                        self.copy(track, direction, turn, held).wait_send()

                if info.last - info.first == self.rounds + 1:
                    one()
                else:
                    pl.when(turn < info.last - info.first)(one)
            return extra

        lax.fori_loop(0, self.rounds + 1, settle, 0)


def ring_rows(rows):
    return -(-rows // 16) * 16


def split_rows(target, source, unit, joined):
    rows, kinds, lanes = source.shape

    def one(n, carry):
        here = span(n, unit)
        for kind in range(kinds):
            values = source[here, kind, :]
            if joined:
                target[here, kind * lanes : (kind + 1) * lanes] = values
            else:
                target[pl.ds(pl.multiple_of(kind * rows + n * unit, unit), unit), :] = values
        return carry

    return one


def first_project_kernel(
    io, inputs_ref, mix_gain, mix_bias, glu_gain, glu_bias, weight_in, short_in, cond_in, up_in,
    seq_ref, x_ref, gains_ref, full, project_ref, weight_ref, up_ref, columns_ref, keep_ref,
    raw, gains_low, gains_land, turn, send, recv, gains_send, gains_recv,
):
    peers = chan_peers()
    me = peers[0]
    shard, slots = inputs_ref.shape
    parts, width, half = raw.shape
    layers = mix_gain.shape[0]
    greet(peers[1:])
    io.ready(0, 1, 2, 3, 4)

    def gather(kind, part):
        return gather_copy(
            lambda owner, part: raw.at[part, span(owner, shard, 32), :],
            peers, (send, recv), kind, part,
        )

    for layer in range(layers):
        for kind, one in enumerate((mix_gain, mix_bias, glu_gain, glu_bias)):
            row = 4 * layer + kind
            gains_low[row : row + 1, :] = one[layer : layer + 1, :]
    gains_land[me] = gains_low[...]
    copies = exchange(
        peers, lambda peer: gains_low, lambda: gains_land.at[me], gains_send, gains_recv
    )
    for part in range(parts):
        raw[part, span(me, shard, 32), :] = inputs_ref[:, part * half : (part + 1) * half]
        for kind in range(2):
            gather(kind, part).start()
    io.ready(5, 6, 7)
    for layer in range(layers):
        lax.fori_loop(0, shard // 48, split_rows(weight_ref.at[layer], weight_in.at[layer], 48, False), 0)
        turn[...] = jnp.zeros_like(turn)
        for tap in range(3):
            turn[3 * tap : 3 * tap + 3, :shard] = short_in[layer, tap]
        turn[9:10, :shard] = cond_in[layer : layer + 1, :]
        columns_ref[layer] = turn[...].T[:shard]
    slot = lax.broadcasted_iota(jnp.int32, keep_ref.shape, 1)
    row = lax.broadcasted_iota(jnp.int32, keep_ref.shape, 0)
    within = slot & (seq_ref[0, 0] - 1)
    keep_ref[...] = jnp.where(within > row, 1.0, 0.0)
    io.flush(4)
    io.flush(6)
    io.flush(7)
    for copy in copies:
        copy.wait()
    turn[...] = jnp.zeros_like(turn)
    for owner in range(4):
        turn[: 4 * layers, :shard] = gains_land[owner]
        gains_ref[owner * shard : (owner + 1) * shard, :] = turn[...].T[:shard]
    io.flush(1)
    io.ready(8)
    gather(0, 0).wait_recv()
    gather(2, 0).start()
    for part in range(parts):
        if part + 1 < parts:
            gather(0, part + 1).wait_recv()
            gather(2, part + 1).start()
        gather(1, part).wait_recv()
        gather(2, part).wait_recv()
        values = raw[part].astype(F32)

        @pl.when(me == part // 2)
        def _():
            x_ref[:, (part % 2) * half : (part % 2 + 1) * half] = values

        normal, _ = norm_columns(values)
        full[part] = (normal * gains_ref[:, 0:1] + gains_ref[:, 1:2]).astype(BF16)
        io.flush(2, part, part)
        columns = slice(part * half, (part + 1) * half)
        project_ref[:, columns] = matmul(weight_ref[0], full[part])
        io.flush(3, part, (slice(None), pl.ds(part * half, half)))
        cuts = width // 64
        lax.fori_loop(
            cuts * part // parts, cuts * (part + 1) // parts, split_rows(up_ref, up_in, 64, True), 0
        )
    io.flush(0)
    io.flush(5)
    for part in range(parts):
        for kind in range(3):
            gather(kind, part).wait_send()


def first_project(inputs, gain_arrays, in_proj, short_conv, cond_weight, glu_in, seq_table,
                  collective):
    shard, slots = inputs.shape
    layers, _, streams, width = in_proj.shape
    hidden = glu_in[0].shape[3]
    tokens = slots // 4
    return fused_call(
        first_project_kernel,
        [inputs, *gain_arrays, in_proj, short_conv, cond_weight, glu_in, seq_table],
        [
            ((width, tokens), F32),
            ((width, 128), F32),
            ((8, width, tokens // 2), BF16),
            ((streams * shard, slots), F32),
            ((layers, streams * shard, width), BF16),
            ((width, 2 * hidden), BF16),
            ((layers, shard, 128), F32),
            ((8, slots), F32),
        ],
        [
            pltpu.VMEM((8, width, tokens // 2), BF16),
            pltpu.VMEM((4 * layers, shard), F32),
            pltpu.VMEM((4, 4 * layers, shard), F32),
            pltpu.VMEM((128, 256), F32),
        ]
        + [pltpu.SemaphoreType.DMA((3, 8))] * 2
        + [pltpu.SemaphoreType.DMA((3,))] * 2,
        collective,
        "first_project",
        (1, 1, 8, 8, 1, 1, 1, 1),
        9,
    )


def scatter_copy(peers, buffers, sems, kind, part):
    _, mate, across, _ = peers
    send, recv = sems
    return send_to(
        across if kind == 2 else mate,
        buffers[2 * kind].at[part],
        buffers[2 * kind + 1].at[part],
        send.at[kind, part],
        recv.at[kind, part],
    )


def scatter_buffers(width, half):
    return [pltpu.VMEM((2, width, half), BF16)] * 6


def block_place(full):
    return lambda owner, part: full.at[owner * 2 + part]


def block_at(step, peers, gathers):
    me, mate, across, diag = peers
    if gathers:
        mine = 1 - (step + 6) // 8
        kind = (step + 1) % 3
        part = mine * step + (1 - mine) * ((step - 2) // 3)
        kind = kind - mine * 4
    else:
        near = step // 4
        mine = step // 6
        part = (1 - near) * (step // 2) + near * (step % 2)
        kind = (1 - near) * (1 + step % 2) - mine
    far = kind * (2 - kind) * (across - mate) + kind * (kind - 1) // 2 * (diag - mate)
    return kind, part, ((1 - mine) * (mate + far) + mine * me) * 2 + part, mine


def run_blocks(peers, full, gather_sems, scatter_sems, buffers, partial, kept, own, ring=None):
    me, mate, across, diag = peers
    gathers = gather_sems is not None

    def gather(kind, part):
        return gather_copy(block_place(full), peers, gather_sems, kind, part)

    def step_body(step, carry):
        kind, part, block, mine = block_at(step, peers, gathers)

        if gathers:
            @pl.when(kind == 0)
            def _():
                gather(1, part).wait_recv()

            @pl.when(kind == 1)
            def _():
                gather(0, part).wait_recv()
                gather(2, part).start()

            @pl.when(kind == 2)
            def _():
                gather(2, part).wait_recv()

        share = partial(block, step)

        def scatter(kind):
            return scatter_copy(peers, buffers, scatter_sems, kind, part)

        @pl.when(mine == 1)
        def _():
            own[part] = share

        @pl.when(kind == 0)
        def _():
            buffers[2][part] = share.astype(BF16)
            scatter(1).start()

        @pl.when(kind == 1)
        def _():
            kept[...] = share

        @pl.when(kind == 2)
        def _():
            buffers[0][part] = share.astype(BF16)
            scatter(0).start()
            scatter(0).wait_recv()
            buffers[4][part] = (kept[...] + buffers[1][part].astype(F32)).astype(BF16)
            scatter(2).start()

        if ring is not None:
            pl.when(step % 3 == 2)(lambda: ring.advance(step // 3, 4))
        return carry

    lax.fori_loop(0, 8, step_body, 0)


def scattered(peers, scatter_sems, buffers, own, part):
    for kind in (1, 2):
        scatter_copy(peers, buffers, scatter_sems, kind, part).wait_recv()
    return own[part] + buffers[3][part].astype(F32) + buffers[5][part].astype(F32)


def drain_gather(peers, full, gather_sems):
    for part in range(2):
        for kind in range(3):
            gather_copy(block_place(full), peers, gather_sems, kind, part).wait_send()


def drain_scatter(peers, scatter_sems, buffers):
    for part in range(2):
        for kind in range(3):
            scatter_copy(peers, buffers, scatter_sems, kind, part).wait_send()


def feed_kernel(gain_at, follows, io, token_gated, x_ref, gains_ref, out_weight, up_columns,
                down_weight, *refs):
    refs = list(refs)
    weight_ref, up_in = (refs.pop(0), refs.pop(0)) if follows else (None, None)
    mid_ref, full, next_ref, units, gelus, slopes = refs[:6]
    refs = refs[6:]
    if follows:
        next_full, project_ref, next_up = refs[:3]
        *refs, next_send, next_recv = refs[3:]
    up_weight, kept, own, *rest = refs
    buffers, sems = rest[:6], rest[6:]
    gather_send, gather_recv, scatter_send, scatter_recv = sems
    gather_sems, scatter_sems = (gather_send, gather_recv), (scatter_send, scatter_recv)
    peers = chan_peers()
    me, mate, across, _ = peers
    width, tokens = x_ref.shape
    half = tokens // 2
    hidden = down_weight.shape[1]
    greet((mate, across))
    io.ready(0, 1, 2, 3)
    for part in range(2):
        columns = slice(part * half, (part + 1) * half)
        mid = x_ref[:, columns] + matmul(out_weight[...], token_gated[:, columns])
        mid_ref[:, columns] = mid
        normal, _ = norm_columns(mid)
        gain = gains_ref[:, gain_at : gain_at + 1]
        bias = gains_ref[:, gain_at + 1 : gain_at + 2]
        full[me * 2 + part] = (normal * gain + bias).astype(BF16)
        for kind in range(2):
            gather_copy(block_place(full), peers, gather_sems, kind, part).start()
    io.flush(0)
    io.ready(4, 5)
    transpose_columns(up_weight, up_columns, 256)

    def partial(block, step):
        normed = full[block]
        tile = 256
        for n in range(hidden // tile):
            gate = matmul(up_weight[n * tile : (n + 1) * tile], normed)
            up = matmul(up_weight[hidden + n * tile : hidden + (n + 1) * tile], normed)
            rows = slice(n * tile, (n + 1) * tile)
            cdf = 0.5 * (1.0 + lax.erf(gate * math.sqrt(0.5)))
            density = jnp.exp(-0.5 * gate * gate) * (1.0 / math.sqrt(2.0 * math.pi))
            gelu = gate * cdf
            units[block, rows] = (gelu * up).astype(BF16)
            gelus[block, rows] = gelu.astype(BF16)
            slopes[block, rows] = (up * (cdf + gate * density)).astype(BF16)
        return matmul(down_weight[...], units[block])

    run_blocks(peers, full, gather_sems, scatter_sems, buffers, partial, kept, own)
    for number in (1, 3, 4, 5):
        io.flush(number)
    if follows:
        io.ready(6, 7)
    place = block_place(next_full) if follows else None
    for part in range(2):
        if follows:
            cuts = width // 64
            lax.fori_loop(
                cuts * part // 2, cuts * (part + 1) // 2, split_rows(next_up, up_in, 64, True), 0
            )
        columns = slice(part * half, (part + 1) * half)
        value = mid_ref[:, columns] + scattered(peers, scatter_sems, buffers, own, part)
        next_ref[:, columns] = value.astype(next_ref.dtype)
        if follows:
            normal, _ = norm_columns(value)
            gain = gains_ref[:, gain_at + 2 : gain_at + 3]
            bias = gains_ref[:, gain_at + 3 : gain_at + 4]
            next_full[me * 2 + part] = (normal * gain + bias).astype(BF16)
            for kind in range(2):
                gather_copy(place, peers, (next_send, next_recv), kind, part).start()
    io.flush(2)
    if follows:
        io.flush(8)
    drain_gather(peers, full, gather_sems)
    drain_scatter(peers, scatter_sems, buffers)
    if follows:
        project_blocks(io, peers, next_full, (next_send, next_recv), weight_ref, project_ref, 6, 7)


def project_blocks(io, peers, full, sems, weight_ref, project_ref, full_out, project_out):
    me, mate, across, diag = peers
    half = full.shape[2]

    def gather(kind, part):
        return gather_copy(block_place(full), peers, sems, kind, part)

    order = [(me, 0), (me, 1), (mate, 0), (mate, 1)]
    order += [(across, 0), (diag, 0), (across, 1), (diag, 1)]
    for step, (owner, part) in enumerate(order):
        if 2 <= step < 4:
            gather(1, part).wait_recv()
        elif step >= 4 and step % 2 == 0:
            gather(0, part).wait_recv()
            gather(2, part).start()
        elif step >= 4:
            gather(2, part).wait_recv()
        block = owner * 2 + part
        io.flush(full_out, step, block)
        columns = span(block, half)
        project_ref[:, columns] = matmul(weight_ref[...], full[block])
        io.flush(project_out, step, (slice(None), columns))
    for kind in range(3):
        for part in range(2):
            gather(kind, part).wait_send()


def feed_forward(token_gated, values, gains, out_weight, up_columns, down_weight, following, gain_at,
                 collective):
    width, tokens = values.shape
    half = tokens // 2
    follows = list(following)
    block = ((8, width, half), BF16)
    outs = [((width, tokens), F32), block]
    outs.append(((width, tokens), F32 if follows else BF16))
    hidden = down_weight[0].shape[2]
    outs += [((8, hidden, half), BF16)] * 3
    parts = [1] * 6
    extra = []
    if follows:
        outs += [block, ((follows[0][0].shape[1], 4 * tokens), F32)]
        outs.append(((width, 2 * hidden), BF16))
        parts += [8, 8, 1]
        extra = [pltpu.SemaphoreType.DMA((3, 2))] * 2
    return fused_call(
        lambda *refs: feed_kernel(gain_at, bool(follows), *refs),
        [token_gated, values, gains, out_weight, up_columns, down_weight] + follows,
        outs,
        [
            pltpu.VMEM((2 * hidden, width), BF16),
            pltpu.VMEM((width, half), F32),
            pltpu.VMEM((2, width, half), F32),
        ]
        + scatter_buffers(width, half)
        + [pltpu.SemaphoreType.DMA((3, 2))] * 4
        + extra,
        collective,
        "feed_forward",
        parts,
    )


def weight_grad(store, rows, columns, left, right, blocks, row_tile, column_tile):
    across = columns // column_tile

    def one(n, carry):
        row, column = span(n // across, row_tile), span(n % across, column_tile)
        total = matmul_nt(left(0, row), right(0, column))
        for block in range(1, blocks):
            total = total + matmul_nt(left(block, row), right(block, column))
        store(n // across, column, total)
        return carry

    lax.fori_loop(0, rows // row_tile * across, one, 0)


def feed_back_kernel(gain_at, gathered, tracks, io, grad_ref, down_weight, gelus, slopes, up_columns,
                     out_weight, mid_ref, gains_ref, token_gated, units, normed, *refs):
    refs = list(refs)
    rings = len(tracks)
    inputs = len(ring_operands(tracks))
    ring_in, refs = refs[:inputs], refs[inputs:]
    state_ref, gated_ref, feed_grads, out_grad, sums_ref = refs[:5]
    large, refs = refs[5 : 5 + rings], refs[5 + rings :]
    ring = None
    if rings:
        sources = [io.source[11 + n] for n in range(inputs)]
        ring = Ring(tracks, ring_in, large, refs[-rings - 2 :], sources)
        refs = refs[: -rings - 2]
    full = grad_ref if gathered else refs.pop(0)
    mixer_low, kept, own, turned, *rest, load_sems = refs
    gated_low = full
    buffers, sems = rest[:6], rest[6:]
    send, recv, gather_send, gather_recv, scatter_send, scatter_recv = sems
    gather_sems, scatter_sems = (gather_send, gather_recv), (scatter_send, scatter_recv)
    if gathered:
        gather_sems = None
    peers = chan_peers()
    me, mate, across, diag = peers
    width, tokens = mid_ref.shape
    half = tokens // 2
    shard = gated_ref.shape[0]
    hidden = down_weight.shape[1]
    tile = 256
    saved = ((io.source[2], gelus), (io.source[3], slopes))
    if gathered:
        saved += ((io.source[0], full),)

    def loads(step, block):
        return [
            pltpu.make_async_copy(source.at[block], target.at[block], load_sems.at[n, step])
            for n, (source, target) in enumerate(saved)
        ]

    for step in range(8):
        for copy in loads(step, block_at(step, peers, not gathered)[2]):
            copy.start()
    greet(peers[1:], ring.toward if rings else ())
    if not gathered:
        io.ready(0)
        for part in range(2):
            full[me * 2 + part] = grad_ref[:, part * half : (part + 1) * half].astype(BF16)
            for kind in range(2):
                gather_copy(block_place(full), peers, gather_sems, kind, part).start()
    if rings:
        ring.start()
    io.ready(1)
    down_rows, out_rows = turned.at[:hidden], turned.at[:width]
    transpose_into(down_rows, down_weight, tile)
    io.ready(4)
    if rings:
        io.ready(*range(11, 11 + rings))

    def partial(block, step):
        for copy in loads(step, block):
            copy.wait()
        grad = full[block]
        for n in range(hidden // tile):
            rows = slice(n * tile, (n + 1) * tile)
            unit_grad = matmul(down_rows[rows], grad)
            slopes[block, rows] = (unit_grad * slopes[block, rows].astype(F32)).astype(BF16)
            gelus[block, rows] = (unit_grad * gelus[block, rows].astype(F32)).astype(BF16)
        return matmul(up_columns[:, :hidden], slopes[block]) + matmul(
            up_columns[:, hidden:], gelus[block]
        )

    run_blocks(peers, full, gather_sems, scatter_sems, buffers, partial, kept, own, ring)
    io.ready(5, 6, 7, 8, 9, 10)
    transpose_into(out_rows, out_weight, tile)
    if not gathered:
        drain_gather(peers, full, gather_sems)

    def a2a(part, n):
        peer = (across, diag, mate)[n]
        return send_to(
            peer,
            gated_low.at[part, span(peer, shard, 32), :],
            gated_ref.at[:, span(me * 2 + part, half)],
            send.at[part, n],
            recv.at[part, n],
        )

    chunk_rows = feed_grads.shape[1] // 3
    row_tile = 384

    def store_grad(kind):
        def store(index, column, total):
            chunks = row_tile // chunk_rows
            for n in range(chunks):
                feed_grads[
                    index * chunks + n, kind * chunk_rows : (kind + 1) * chunk_rows, column
                ] = total[n * chunk_rows : (n + 1) * chunk_rows].astype(BF16)

        return store

    def feed_grad(kind):
        if kind == 0:
            left, right = lambda b, r: full[b, r], lambda b, c: units[b, c]
        else:
            def left(b, r):
                return normed[b, r]

            def right(b, c):
                return (slopes, gelus)[kind - 1][b, c]

        weight_grad(store_grad(kind), width, hidden, left, right, 8, row_tile, tile)

    def store_out(index, column, total):
        out_grad[span(index, tile), column] = total.astype(BF16)

    gain = gains_ref[:, gain_at : gain_at + 1]
    for part in range(2):
        feed_grad(part)
        if rings:
            ring.advance(2 + part, 4)
        columns = slice(part * half, (part + 1) * half)
        grad = scattered(peers, scatter_sems, buffers, own, part)
        change, product = norm_pullback(grad, mid_ref[:, columns], gain)
        before = full[me * 2 + part].astype(F32) if gathered else grad_ref[:, columns]
        state = before + change
        state_ref[:, columns] = state
        mixer_low[:, columns] = state.astype(BF16)
        gated_low[part] = matmul(out_rows[...], mixer_low[:, columns]).astype(BF16)
        for n in range(3):
            a2a(part, n).start()
        if part == 0:
            sums_ref[:, 0:1] = lane_sums(product)
            sums_ref[:, 1:2] = lane_sums(grad)
        else:
            sums_ref[:, 0:1] = sums_ref[:, 0:1] + lane_sums(product)
            sums_ref[:, 1:2] = sums_ref[:, 1:2] + lane_sums(grad)
    io.flush(0)
    feed_grad(2)
    io.flush(2)
    io.flush(4)
    for part in range(2):
        gated_ref[:, span(me * 2 + part, half)] = gated_low[part, span(me, shard, 32), :]
    weight_grad(
        store_out, width, width,
        lambda b, r: mixer_low[r, :], lambda b, c: token_gated[c, :], 1, tile, tile,
    )
    io.flush(3)
    if rings:
        ring.finish()
        for n in range(rings):
            io.flush(5 + n)
    for part in range(2):
        for n in range(3):
            a2a(part, n).wait()
    io.flush(1)
    drain_scatter(peers, scatter_sems, buffers)


def feed_back(grad, mid, gains, normed, up_columns, down_weight, out_weight, token_gated, saved,
              tracks, gain_at, count, collective):
    width, tokens = mid.shape
    half = tokens // 2
    hidden = down_weight[0].shape[2]
    gathered = grad.ndim == 3
    units, gelus, slopes = saved
    own_loads = tuple(range(11, 11 + len(tracks)))
    carries = tuple(range(11 + len(tracks), 11 + len(ring_operands(tracks))))
    manual = (2, 3) + ((0,) if gathered else ()) + carries
    return fused_call(
        lambda *refs: feed_back_kernel(gain_at, gathered, tracks, *refs),
        [grad, down_weight, gelus, slopes, up_columns, out_weight, mid, gains, token_gated, units]
        + [normed]
        + ring_operands(tracks),
        [
            ((width, tokens), F32),
            ((width // 4, 4 * tokens), BF16),
            ((count, 3 * width // count, hidden), BF16),
            ((width, width), BF16),
            ((width, 8), F32),
        ]
        + [one.out() for one in tracks],
        [pltpu.VMEM((8, width, half), BF16)] * (not gathered)
        + [
            pltpu.VMEM((width, tokens), BF16),
            pltpu.VMEM((width, half), F32),
            pltpu.VMEM((2, width, half), F32),
            pltpu.VMEM((max(hidden, width), width), BF16),
        ]
        + scatter_buffers(width, half)
        + [pltpu.SemaphoreType.DMA((2, 3))] * 2
        + [pltpu.SemaphoreType.DMA((3, 2))] * 4
        + [pltpu.SemaphoreType.DMA((3, 8))]
        + ring_scratch(tracks),
        collective,
        "feed_back",
        [1] * (5 + len(tracks)),
        manual=manual,
        order=((0,) if not gathered else ()) + (1, 4) + own_loads,
    )


def project_back_kernel(gain_at, each, tracks, in_track, io, project_grad, weight_ref, square_ref, normed,
                        state_ref, x_ref, gains_ref, *refs):
    inputs = len(ring_operands(tracks))
    ring_in, refs = refs[:inputs], refs[inputs:]
    next_ref, in_grad, sums_ref = refs[:3]
    large, refs = refs[3 : 3 + len(tracks)], refs[3 + len(tracks) :]
    in_held, *refs = refs
    kept, own, weight_rows, in_full, *rest = refs
    buffers, (scatter_send, scatter_recv, *ring_rest) = rest[:6], rest[6:]
    *ring_rest, in_slots, in_send, in_recv = ring_rest
    in_ring = Ring([in_track], [in_grad], [in_held], [in_slots, in_send, in_recv], [in_grad])
    scatter_sems = (scatter_send, scatter_recv)
    peers = chan_peers()
    me, mate, across, diag = peers
    sources = [io.source[7 + n] for n in range(inputs)]
    ring = Ring(tracks, ring_in, large, ring_rest, sources)
    width, tokens = x_ref.shape
    half = tokens // 2
    rows = weight_ref.shape[0]
    shard = rows // 3
    greet((mate, across), ring.toward)
    ring.start()
    io.ready(1)
    for first, size in ((0, 512), (512, rows - 512)):
        weight_rows[:, first : first + size] = weight_ref[first : first + size].T
    io.ready(0)

    def share(owner, part):
        return matmul(weight_rows[...], project_grad[:, span(owner * 2 + part, half)])

    for part in range(2):
        buffers[0][part] = share(diag, part).astype(BF16)
        scatter_copy(peers, buffers, scatter_sems, 0, part).start()
        kept[...] = share(across, part)
        scatter_copy(peers, buffers, scatter_sems, 0, part).wait_recv()
        buffers[4][part] = (kept[...] + buffers[1][part].astype(F32)).astype(BF16)
        scatter_copy(peers, buffers, scatter_sems, 2, part).start()
    for part in range(2):
        buffers[2][part] = share(mate, part).astype(BF16)
        scatter_copy(peers, buffers, scatter_sems, 1, part).start()
        own[part] = share(me, part)
    io.ready(2, 3)
    if in_full.shape[1] > 4 * each:
        in_full[...] = jnp.zeros_like(in_full)
    for chunk in range(shard // each):
        in_full[chunk, 3 * each : 4 * each] = square_ref[chunk * each : (chunk + 1) * each]
    tile = 256
    for stream in range(3):
        def column_tile(n, carry):
            column = span(n, tile)
            total = None
            for block in range(8):
                left = project_grad[
                    stream * shard : (stream + 1) * shard, block * half : (block + 1) * half
                ]
                value = matmul_nt(left, normed[block, column])
                total = value if total is None else total + value
            for chunk in range(shard // each):
                in_full[chunk, stream * each : (stream + 1) * each, column] = total[
                    chunk * each : (chunk + 1) * each
                ]
            return carry

        lax.fori_loop(0, width // tile, column_tile, 0)
    in_grad[...] = in_full[...].astype(BF16)
    in_ring.start()
    io.flush(1)
    io.ready(*range(7, 7 + len(tracks)))
    ring.advance(0, 2)
    io.ready(4, 5, 6)
    gain = gains_ref[:, gain_at : gain_at + 1]
    for part in range(2):
        columns = slice(part * half, (part + 1) * half)
        grad = scattered(peers, scatter_sems, buffers, own, part)
        change, product = norm_pullback(grad, x_ref[:, columns], gain)
        next_ref[:, columns] = state_ref[:, columns] + change
        if part == 0:
            sums_ref[:, 0:1] = lane_sums(product)
            sums_ref[:, 1:2] = lane_sums(grad)
            ring.advance(1, 2)
            in_ring.advance(0, 1)
        else:
            sums_ref[:, 0:1] = sums_ref[:, 0:1] + lane_sums(product)
            sums_ref[:, 1:2] = sums_ref[:, 1:2] + lane_sums(grad)
    io.flush(0)
    io.flush(2)
    ring.finish()
    for n in range(len(tracks)):
        io.flush(3 + n)
    in_ring.finish()
    io.flush(3 + len(tracks))
    drain_scatter(peers, scatter_sems, buffers)


def project_back(project_grad, state, values, gains, normed, weight, square, tracks, gain_at,
                 collective):
    width, tokens = values.shape
    half = tokens // 2
    rows = project_grad.shape[0]
    count = tracks[0].count
    each = rows // 3 // count
    packed = (count, ring_rows(4 * each), width)
    in_track = Track(jax.ShapeDtypeStruct(packed, BF16), 0, count // 4)
    return fused_call(
        lambda *refs: project_back_kernel(gain_at, each, tracks, in_track, *refs),
        [project_grad, weight, square, normed, state, values, gains] + ring_operands(tracks),
        [((width, tokens), F32), (packed, BF16), ((width, 8), F32)]
        + [one.out() for one in tracks + [in_track]],
        [
            pltpu.VMEM((width, half), F32),
            pltpu.VMEM((2, width, half), F32),
            pltpu.VMEM((width, rows), BF16),
            pltpu.VMEM(packed, F32),
        ]
        + scatter_buffers(width, half)
        + [pltpu.SemaphoreType.DMA((3, 2))] * 2
        + ring_scratch(tracks)
        + ring_scratch([in_track]),
        collective,
        "project_back",
        [1] * (4 + len(tracks)),
        manual=tuple(range(7 + len(tracks), 7 + len(ring_operands(tracks)))),
        order=(1, 0) + tuple(range(7, 7 + len(tracks))),
    )


def mask_heads(values, keep, blocks):
    length = values.shape[1] // blocks
    pieces = []
    for j in range(blocks):
        start = j * length
        pieces.append(values[:, start : start + 128] * keep[:, start : start + 128])
        pieces.append(values[:, start + 128 : start + length])
    return jnp.concatenate(pieces, axis=1)


def eight(rows):
    if isinstance(rows, int):
        return pl.ds(rows, 8)
    return pl.ds(pl.multiple_of(rows, 8), 8)


def sixteen(rows):
    if isinstance(rows, int):
        return pl.ds(rows, 16)
    return pl.ds(pl.multiple_of(rows, 16), 16)


def stream_rows(project_ref, columns_ref, keep_ref, rows, shard, stream, blocks):
    values = project_ref[eight(stream * shard + rows), :]
    total = values * columns_ref[eight(rows), stream : stream + 1]
    for offset in (1, 2):
        moved = mask_heads(pltpu.roll(values, offset, 1), keep_ref[offset - 1 : offset, :], blocks)
        column = 3 * offset + stream
        total = total + moved * columns_ref[eight(rows), column : column + 1]
    return total


def sequence_factor(power, cond, facts, blocks):
    energy = []
    for i in range(blocks):
        total = 0.0
        for j in range(blocks):
            total = total + power[j] * facts.same[i][j]
        energy.append(total * facts.inverse)
    logs = [jnp.log(1.0 + value) for value in energy]
    factor = [
        (1.0 + cond * value) * facts.same[i][i] for i, value in enumerate(logs)
    ]
    return energy, logs, factor


def block_sums(values, blocks):
    length = values.shape[1] // blocks
    return [lane_sums(values[:, i * length : (i + 1) * length]) for i in range(blocks)]


def spread_blocks(columns, length):
    return jnp.concatenate(
        [jnp.broadcast_to(column, (column.shape[0], length)) for column in columns], axis=1
    )


def plain_bins(spectrum_ref, rows, shard, blocks):
    half = spectrum_ref.shape[1] // 2
    bins = []
    for k in range(blocks):
        here = spectrum_ref[eight(k * shard + rows), :]
        bins.append((here[:, :half], here[:, half:]))
    return bins


def filter_bins(spectrum_ref, sign, rows, shard, blocks):
    plain = plain_bins(spectrum_ref, rows, shard, blocks)
    bins = [plain[0]]
    for k in range(1, blocks):
        (real, imag), (before_real, before_imag) = plain[k], plain[k - 1]
        bins.append((real - sign * before_imag, imag + sign * before_real))
    return bins


def store_blocks(target, values, rows, shard, blocks):
    length = values.shape[1] // blocks
    for j in range(blocks):
        target[sixteen(j * shard + rows), :] = values[:, j * length : (j + 1) * length]


def join(halves):
    return jnp.concatenate(halves, axis=0).astype(BF16)


def channel_cuts(shard, streams):
    size = shard // LOADS
    return [(s * shard + n * size, size) for n in range(LOADS) for s in range(streams)]


def channel_order(numbers, streams=3):
    order = []
    for n in range(LOADS):
        for number in numbers:
            each = streams if number == 1 else 1
            order += [(number, n * each + i) for i in range(each)]
    return tuple(order)


def run_groups(prepare, transform, combine, invert, finish, after):
    prepare(0)
    for i in range(LOADS + 1):
        if i < LOADS:
            transform(i)
        if i + 1 < LOADS:
            prepare(i + 1)
        if i:
            invert(i - 1)
        if i < LOADS:
            combine(i)
        if i:
            finish(i - 1)
            after(i - 1)


def conv_forward_kernel(blocks, carries, io, filter_ref, project_ref, columns_ref, keep_ref,
                        sign_ref, table_ref, seq_ref, carried_in, back_ref, token_gated, conv_ref,
                        carried, gated, factor_ref, *refs):
    signal_low, filter_low, signal_bins, filter_spectrum, out_low, convolved = (
        refs[2 * n : 2 * n + 2] for n in range(6)
    )
    send, recv, *sems = refs[12:]
    shard, slots = gated.shape
    length = slots // blocks
    scale = 1.0 / length
    size = shard // LOADS
    peers = chan_peers()
    me = peers[0]
    tokens = slots // 4
    parts = carried.shape[0]
    facts = Facts(seq_ref, blocks, length)
    greet(peers[1:])

    def gather(kind, part):
        return gather_copy(
            lambda owner, part: carried.at[part, span(owner, shard, 32), :],
            peers, sems, kind, part,
        )

    def forward(first, last):
        for part in range(parts * first // LOADS, parts * last // LOADS):
            gather(0, part).wait_recv()
            gather(2, part).start()

    io.ready(7)
    for part in range(parts):
        if carries == 1:
            carried[part, span(me, shard, 32), :] = carried_in[part]
        else:
            lanes = carried.shape[2]
            carried[part, span(me, shard, 32), :] = carried_in[:, part * lanes : (part + 1) * lanes]
        for kind in range(2):
            gather(kind, part).start()
    io.ready(2, 3, 4)

    def prepare(group):
        base, place = group * size, group % 2
        if group < 2:
            cuts = slice(0, 1) if group == 0 else slice(1, LOADS)
            io.ready(0, cuts=cuts)
            io.ready(1, cuts=slice(3 * cuts.start, 3 * cuts.stop))
        for n in range(size // 16):
            rows = base + n * 16
            signals = []
            for part in range(2):
                here = rows + 8 * part
                one, two = (
                    stream_rows(project_ref, columns_ref, keep_ref, here, shard, stream, blocks)
                    for stream in (1, 2)
                )
                signals.append(one * two)
                cond = columns_ref[eight(here), 9:10]
                _, _, factor = sequence_factor(block_sums(two * two, blocks), cond, facts, blocks)
                for j in range(blocks):
                    factor_ref[eight(here), j : j + 1] = factor[j]
            store_blocks(signal_low[place], join(signals), n * 16, size, blocks)
            kernel = filter_ref[sixteen(rows), :].astype(BF16)
            store_blocks(filter_low[place], kernel, n * 16, size, blocks)

    def transform(group):
        place = group % 2
        if group == 0:
            io.ready(5, 8)
        signal_bins[place][...] = matmul(signal_low[place][...], table_ref[...])
        filter_spectrum[place][...] = matmul(filter_low[place][...], table_ref[...])

    def combine(group):
        place = group % 2
        for n in range(size // 16):
            joined = [[] for _ in range(blocks)]
            for part in range(2):
                here = n * 16 + 8 * part
                window = filter_bins(filter_spectrum[place], sign_ref[0:1, :], here, size, blocks)
                signal = plain_bins(signal_bins[place], here, size, blocks)
                for i in range(blocks):
                    real = imag = None
                    for j in range(i, -1, -1):
                        fr, fi = window[i - j]
                        sr, si = signal[j]
                        more_real, more_imag = fr * sr - fi * si, fr * si + fi * sr
                        if j == i:
                            real, imag = more_real, more_imag
                        else:
                            factor = facts.same[i][j]
                            real, imag = real + more_real * factor, imag + more_imag * factor
                    joined[i].append(jnp.concatenate([real, imag], axis=1))
            for i in range(blocks):
                out_low[place][sixteen(i * size + n * 16), :] = join(joined[i])

    def invert(group):
        place = group % 2
        convolved[place][...] = matmul(out_low[place][...], back_ref[...]) * scale

    def finish(group):
        base, place = group * size, group % 2
        for n in range(size // 16):
            rows = base + n * 16
            results = []
            for part in range(2):
                here = rows + 8 * part
                zero = stream_rows(project_ref, columns_ref, keep_ref, here, shard, 0, blocks)
                pieces = []
                for j in range(blocks):
                    source = convolved[place][eight(j * size + n * 16 + 8 * part), :]
                    columns = slice(j * length, (j + 1) * length)
                    conv_ref[eight(here), columns] = source
                    pieces.append(zero[:, columns] * (source * factor_ref[eight(here), j : j + 1]))
                results.append(jnp.concatenate(pieces, axis=1))
            gated[sixteen(rows), :] = join(results)

    copies = []

    def after(group):
        base = group * size
        mine = pl.ds(pl.multiple_of(me * shard + base, 16), size)
        copies.extend(
            exchange(
                peers, lambda peer: gated.at[pl.ds(base, size), span(peer, tokens)],
                lambda: token_gated.at[mine], send.at[group], recv.at[group],
            )
        )
        token_gated[mine, :] = gated[base : base + size, span(me, tokens)]
        io.flush(1, group, pl.ds(base, size))
        forward(group, group + 1)

    run_groups(prepare, transform, combine, invert, finish, after)
    for part in range(parts):
        for kind in (1, 2):
            gather(kind, part).wait_recv()
        io.flush(2, part, part)
    for copy in copies:
        copy.wait()
    io.flush(0)
    for part in range(parts):
        for kind in range(3):
            gather(kind, part).wait_send()


def conv_forward(project, filter_rows, columns, keep, sign, table, seq_table, back, carried,
                 carries, blocks, collective):
    shard, slots = filter_rows[0].shape[1:]
    width = 4 * shard
    length = slots // blocks
    rows = blocks * (shard // LOADS)
    low = pltpu.VMEM((rows, length), BF16)
    bins = pltpu.VMEM((rows, 2 * length), F32)
    if carries == 1:
        out = ((carried.shape[0], width, width), BF16)
    else:
        out = ((8, width, slots // 8), BF16)
    return fused_call(
        lambda *refs: conv_forward_kernel(blocks, carries, *refs),
        [filter_rows, project, columns, keep, sign, table, seq_table, carried, back],
        [((width, slots // 4), BF16), ((shard, slots), F32), out],
        [
            pltpu.VMEM((shard, slots), BF16),
            pltpu.VMEM((shard, 128), F32),
        ]
        + [low] * 4
        + [bins] * 4
        + [pltpu.VMEM((rows, 2 * length), BF16)] * 2
        + [pltpu.VMEM((rows, length), F32)] * 2
        + [pltpu.SemaphoreType.DMA((LOADS, 3))] * 2
        + [pltpu.SemaphoreType.DMA((3, out[0][0]))] * 2,
        collective,
        "conv_forward",
        [1, LOADS, out[0][0]],
        6,
        (7, 2, 3, 4) + channel_order((1, 0)) + (5, 8),
        {0: channel_cuts(shard, 1), 1: channel_cuts(shard, 3)},
    )


def conv_backward_kernel(blocks, tracks, with_outputs, io, grad_ref, project_ref, conv_ref,
                         filter_ref, columns_ref, keep_ref, sign_ref, table_ref, seq_ref,
                         square_ref, *refs):
    refs = list(refs)
    back_ref = refs.pop(len(ring_operands(tracks)) + with_outputs)
    rings = len(tracks)
    inputs = len(ring_operands(tracks))
    ring_in, refs = refs[:inputs], refs[inputs:]
    if with_outputs:
        residual_ref = refs.pop(0)
    project_grad, filter_pack, square_sum, sums_ref = refs[:4]
    large, refs = refs[4 : 4 + rings], refs[4 + rings :]
    if with_outputs:
        outputs_ref = refs.pop(0)
        *refs, out_land, out_send, out_recv = refs
    sources = [io.source[10 + n] for n in range(inputs)]
    ring = Ring(tracks, ring_in, large, refs[-rings - 2 :], sources)
    refs = refs[: -rings - 2]
    mixed, energy_ref, square_land, square_send, square_recv, *pairs = refs
    signal_low, filter_low, grad_low, signal_bins, filter_spectrum, grad_bins = (
        pairs[2 * n : 2 * n + 2] for n in range(6)
    )
    signal_out, filter_out, signal_grad, filter_grad = (
        pairs[2 * n : 2 * n + 2] for n in range(6, 10)
    )
    peers = chan_peers()
    greet(peers[1:], ring.toward)
    ring.start()
    copies = exchange(
        peers, lambda peer: io.source[9].at[peer], lambda: square_land.at[peers[0]],
        square_send, square_recv,
    )
    if with_outputs:
        copies += to_channels(
            peers, io.source[10 + inputs], out_land, out_send, out_recv
        )
    io.ready(4, 5, 6)
    shard, slots = grad_ref.shape
    length = slots // blocks
    scale = 1.0 / length
    steps = shard // 16
    facts = Facts(seq_ref, blocks, length)

    size = shard // LOADS

    def prepare(group):
        base, place = group * size, group % 2
        if group < 2:
            cuts = slice(0, 1) if group == 0 else slice(1, LOADS)
            for number, each in ((0, 1), (1, 3), (2, 1), (3, 1)):
                io.ready(number, cuts=slice(each * cuts.start, each * cuts.stop))
        for n in range(size // 16):
            rows = base + n * 16
            signals, scaled = [], []
            grads = grad_ref[sixteen(rows), :].astype(F32)
            for part in range(2):
                here = rows + 8 * part
                zero, one, two = (
                    stream_rows(project_ref, columns_ref, keep_ref, here, shard, stream, blocks)
                    for stream in range(3)
                )
                mixed[0, eight(here), :] = one
                mixed[1, eight(here), :] = two
                signals.append(one * two)
                cond = columns_ref[eight(here), 9:10]
                power = block_sums(two * two, blocks)
                energy, logs, factor = sequence_factor(power, cond, facts, blocks)
                conv_grad = grads[8 * part : 8 * part + 8] * zero
                factor_grad = block_sums(conv_grad * conv_ref[eight(here), :], blocks)
                cond_grad = 0.0
                for j in range(blocks):
                    cond_grad = cond_grad + factor_grad[j] * logs[j]
                sums_ref[eight(here), 9:10] = cond_grad
                for i in range(blocks):
                    total = 0.0
                    for j in range(blocks):
                        total = total + factor_grad[j] * facts.same[i][j]
                    energy_ref[eight(here), i : i + 1] = (
                        total * cond / (1.0 + energy[i]) * (2.0 * facts.inverse)
                    )
                    energy_ref[eight(here), blocks + i : blocks + i + 1] = factor[i]
                scaled.append(
                    conv_grad * spread_blocks([value * scale for value in factor], length)
                )
            store_blocks(signal_low[place], join(signals), n * 16, size, blocks)
            store_blocks(grad_low[place], join(scaled), n * 16, size, blocks)
            kernel = filter_ref[sixteen(rows), :].astype(BF16)
            store_blocks(filter_low[place], kernel, n * 16, size, blocks)

    def transform(group):
        place = group % 2
        if group == 0:
            io.ready(7, 10 + inputs + with_outputs)
        grad_bins[place][...] = matmul(grad_low[place][...], table_ref[...])
        signal_bins[place][...] = matmul(signal_low[place][...], table_ref[...])
        filter_spectrum[place][...] = matmul(filter_low[place][...], table_ref[...])

    def combine(group):
        place = group % 2
        sign = sign_ref[0:1, :]
        for n in range(size // 16):
            joined = [[] for _ in range(blocks)]
            windows = [[] for _ in range(blocks)]
            for part in range(2):
                here = n * 16 + 8 * part
                window = filter_bins(filter_spectrum[place], sign, here, size, blocks)
                signal = plain_bins(signal_bins[place], here, size, blocks)
                grads = plain_bins(grad_bins[place], here, size, blocks)
                for j in range(blocks):
                    for i in range(j, blocks):
                        fr, fi = window[i - j]
                        gr, gi = grads[i]
                        more_real, more_imag = fr * gr + fi * gi, fr * gi - fi * gr
                        if i == j:
                            real, imag = more_real, more_imag
                        else:
                            factor = facts.same[i][j]
                            real, imag = real + more_real * factor, imag + more_imag * factor
                    joined[j].append(jnp.concatenate([real, imag], axis=1))
                after = None
                for k in reversed(range(blocks)):
                    real = imag = None
                    for j in range(blocks - k):
                        sr, si = signal[j]
                        gr, gi = grads[j + k]
                        more_real, more_imag = sr * gr + si * gi, sr * gi - si * gr
                        if k:
                            factor = facts.same[j + k][j]
                            more_real, more_imag = more_real * factor, more_imag * factor
                        real = more_real if real is None else real + more_real
                        imag = more_imag if imag is None else imag + more_imag
                    if after is None:
                        whole = (real, imag)
                    else:
                        whole = (real + sign * after[1], imag - sign * after[0])
                    windows[k].append(jnp.concatenate(whole, axis=1))
                    after = (real, imag)
            for j in range(blocks):
                signal_out[place][sixteen(j * size + n * 16), :] = join(joined[j])
                filter_out[place][sixteen(j * size + n * 16), :] = join(windows[j])

    count, pack_rows, lanes = filter_pack.shape
    each = shard // count
    stack = slots // lanes
    if pack_rows > stack * each:
        filter_pack[...] = jnp.zeros_like(filter_pack)

    def invert(group):
        place = group % 2
        signal_grad[place][...] = matmul(signal_out[place][...], back_ref[...])
        filter_grad[place][...] = matmul(filter_out[place][...], back_ref[...])

    def finish(group):
        base, place = group * size, group % 2
        for chunk in range(size // each):
            lags = [
                filter_grad[place][j * size + chunk * each : j * size + (chunk + 1) * each, :]
                for j in range(blocks)
            ]
            layers = [
                jnp.concatenate(lags[n * blocks // stack : (n + 1) * blocks // stack], axis=1)
                for n in range(stack)
            ]
            value = layers[0] if stack == 1 else jnp.concatenate(layers, axis=0)
            filter_pack[base // each + chunk, : stack * each] = value.astype(BF16)
        for n in range(size // 16):
            rows = base + n * 16
            totals = [[] for _ in range(3)]
            outer = grad_ref[sixteen(rows), :].astype(F32)
            for part in range(2):
                here = rows + 8 * part
                local = eight(here)
                factor = [energy_ref[local, blocks + i : blocks + i + 1] for i in range(blocks)]
                energy = [energy_ref[local, i : i + 1] for i in range(blocks)]
                signal = jnp.concatenate(
                    [
                        signal_grad[place][eight(j * size + n * 16 + 8 * part), :]
                        for j in range(blocks)
                    ],
                    axis=1,
                )
                for stream in range(3):
                    if stream == 0:
                        value = outer[8 * part : 8 * part + 8] * (
                            conv_ref[local, :] * spread_blocks(factor, length)
                        )
                    elif stream == 1:
                        value = signal * mixed[1, local, :]
                    else:
                        value = signal * mixed[0, local, :] + (
                            spread_blocks(energy, length) * mixed[1, local, :]
                        )
                    plain = project_ref[eight(stream * shard + here), :]
                    total = value * columns_ref[local, stream : stream + 1]
                    sums_ref[local, stream : stream + 1] = lane_sums(value * plain)
                    for offset in (1, 2):
                        column = 3 * offset + stream
                        moved = pltpu.roll(
                            mask_heads(value, keep_ref[offset - 1 : offset, :], blocks),
                            slots - offset, 1,
                        )
                        sums_ref[local, column : column + 1] = lane_sums(moved * plain)
                        total = total + moved * columns_ref[local, column : column + 1]
                    totals[stream].append(total)
            for stream in range(3):
                project_grad[sixteen(stream * shard + rows), :] = join(totals[stream])

    def after(group):
        if group == 0:
            io.ready(*range(10, 10 + rings))
        if group < 3:
            ring.advance(group, 3)

    run_groups(prepare, transform, combine, invert, finish, after)
    io.flush(1)
    for stream in range(3):
        io.flush(0, stream, pl.ds(stream * shard, shard))
    for copy in copies:
        copy.wait()
    io.ready(9)
    total = square_ref[peers[0]].astype(F32)
    for peer in peers[1:]:
        total = total + square_land[peer].astype(F32)
    square_sum[...] = total
    io.flush(2)
    if with_outputs:
        io.ready(10 + inputs)
        tokens = residual_ref.shape[1]
        out_land[:, span(peers[0], tokens)] = residual_ref[span(peers[0], shard, 32), :]
        outputs_ref[...] = out_land[...].astype(F32)
        io.flush(4 + rings)
    io.flush(3)
    ring.finish()
    for n in range(rings):
        io.flush(4 + n)


def filter_layout(shard, slots, count):
    each = shard // count
    stack = 2 if each % 8 == 0 else 1
    return count, ring_rows(stack * each), slots // stack


def conv_backward(grad, project, conv, filter_rows, columns, keep, sign, table, seq_table, back, square,
                  tracks, residual, blocks, collective):
    shard, slots = filter_rows[0].shape[1:]
    length = slots // blocks
    rows = blocks * (shard // LOADS)
    low = pltpu.VMEM((rows, length), BF16)
    bins = pltpu.VMEM((rows, 2 * length), F32)
    out = pltpu.VMEM((rows, 2 * length), BF16)
    back_out = pltpu.VMEM((rows, length), F32)
    outs, extra = [], []
    if residual:
        outs = [((shard, slots), F32)]
        extra = [pltpu.VMEM((shard, slots), BF16)] + [pltpu.SemaphoreType.DMA((3,))] * 2
    return fused_call(
        lambda *refs: conv_backward_kernel(blocks, tracks, bool(residual), *refs),
        [grad, project, conv, filter_rows, columns, keep, sign, table, seq_table, square]
        + ring_operands(tracks)
        + list(residual)
        + [back],
        [
            ((3 * shard, slots), BF16),
            (filter_layout(shard, slots, tracks[0].count), BF16),
            ((shard, 4 * shard), F32),
            ((shard, 128), F32),
        ]
        + [one.out() for one in tracks]
        + outs,
        [pltpu.VMEM((2, shard, slots), F32), pltpu.VMEM((shard, 128), F32)]
        + [pltpu.VMEM(square.shape, BF16)]
        + [pltpu.SemaphoreType.DMA((3,))] * 2
        + [low] * 6
        + [bins] * 6
        + [out] * 4
        + [back_out] * 4
        + ring_scratch(tracks)
        + extra,
        collective,
        "conv_backward",
        [3, 1, 1, 1] + [1] * (len(tracks) + len(outs)),
        8,
        (4, 5, 6) + channel_order((0, 1, 2, 3)) + (7,),
        {0: channel_cuts(shard, 1), 1: channel_cuts(shard, 3), 2: channel_cuts(shard, 1)}
        | {3: channel_cuts(shard, 1)},
        tuple(range(10 + len(tracks), 10 + len(ring_operands(tracks)))),
    )


def last_kernel(layers, tracks, io, state_ref, *refs):
    refs = list(refs)
    gain_sums, refs = refs[: 2 * layers], refs[2 * layers :]
    row_sums, refs = refs[:layers], refs[layers:]
    rings, inputs = len(tracks), len(ring_operands(tracks))
    ring_in, refs = refs[:inputs], refs[inputs:]
    input_grad, small_out = refs[:2]
    large, refs = refs[2 : 2 + rings], refs[2 + rings :]
    state_low, landing, sums, turn, gains, gains_land, small_own, small_land, *refs = refs
    chan_send, chan_recv, small_send, small_recv, state_send, state_recv, *refs = refs
    peers = chan_peers()
    me = peers[0]
    dp = lax.axis_index("dp")
    first = 1 + 3 * layers
    ring = Ring(tracks, ring_in, large, refs, [io.source[first + n] for n in range(inputs)])
    count = ring.count
    shard = landing.shape[0]
    greet(peers[1:], [(dp + offset) % count for offset in range(1, count)])
    ring.start()
    io.ready(*range(0, first))
    for layer in range(layers):
        sums[:, 4 * layer : 4 * layer + 2] = gain_sums[2 * layer][:, 0:2]
        sums[:, 4 * layer + 2 : 4 * layer + 4] = gain_sums[2 * layer + 1][:, 0:2]
    turn[...] = jnp.zeros_like(turn)
    for owner in range(4):
        turn[:shard, : 4 * layers] = sums[owner * shard : (owner + 1) * shard, : 4 * layers]
        gains[owner] = turn[...].T[: 4 * layers]
    copies = exchange(
        peers, lambda peer: gains.at[peer], lambda: gains_land.at[me], chan_send, chan_recv
    )
    state_low[...] = state_ref[...].astype(BF16)
    state_copies = to_channels(peers, state_low, landing, state_send, state_recv)
    landing[:, span(me, state_low.shape[1])] = state_low[span(me, shard, 32), :]
    io.ready(*range(first, first + rings))
    ring.advance(0, 6)
    for layer in range(layers):
        turn[:shard, 10 * layer : 10 * layer + 10] = row_sums[layer][:, 0:10]
    small_own[4 * layers :, :] = turn[...].T[: small_own.shape[0] - 4 * layers]
    for copy in copies:
        copy.wait()
    total = gains[me]
    for peer in peers[1:]:
        total = total + gains_land[peer]
    small_own[: 4 * layers, :] = total
    small_copies = []
    for offset in range(1, count):
        copy = pltpu.make_async_remote_copy(
            small_own,
            small_land.at[offset - 1],
            small_send.at[offset - 1],
            small_recv.at[offset - 1],
            device_id={"dp": (dp + offset) % count},
        )
        copy.start()
        small_copies.append(copy)
    for point in range(1, 4):
        ring.advance(point, 6)
    small = small_own[...]
    for copy in small_copies:
        copy.wait()
    for n in range(count - 1):
        small = small + small_land[n]
    small_out[...] = small
    io.flush(1)
    ring.advance(4, 6)
    for copy in state_copies:
        copy.wait()
    input_grad[...] = landing[...].astype(F32)
    io.flush(0)
    ring.advance(5, 6)
    ring.finish()
    for n in range(rings):
        io.flush(2 + n)


def last_sums(state, gain_sums, row_sums, tracks, collective):
    width, tokens = state.shape
    shard = width // 4
    layers = len(row_sums)
    count = tracks[0].count
    small = (-(-14 * layers // 8) * 8, 256)
    return fused_call(
        lambda *refs: last_kernel(layers, tracks, *refs),
        [state] + gain_sums + row_sums + ring_operands(tracks),
        [((shard, 4 * tokens), F32), (small, F32)] + [one.out() for one in tracks],
        [
            pltpu.VMEM((width, tokens), BF16),
            pltpu.VMEM((shard, 4 * tokens), BF16),
            pltpu.VMEM((width, 128), F32),
            pltpu.VMEM((256, 128), F32),
            pltpu.VMEM((4, 4 * layers, 256), F32),
            pltpu.VMEM((4, 4 * layers, 256), F32),
            pltpu.VMEM(small, F32),
            pltpu.VMEM((count - 1,) + small, F32),
            pltpu.SemaphoreType.DMA((3,)),
            pltpu.SemaphoreType.DMA((3,)),
            pltpu.SemaphoreType.DMA((count - 1,)),
            pltpu.SemaphoreType.DMA((count - 1,)),
            pltpu.SemaphoreType.DMA((3,)),
            pltpu.SemaphoreType.DMA((3,)),
        ]
        + ring_scratch(tracks),
        collective,
        "last_sums",
        [1] * (2 + len(tracks)),
        order=tuple(range(1, 1 + 3 * layers)) + (0,),
        manual=tuple(
            range(1 + 3 * layers + len(tracks), 1 + 3 * layers + len(ring_operands(tracks)))
        ),
    )


def collect_kernel(layers, *refs):
    refs = list(refs)
    outputs_in, input_in, small = refs[:3]
    refs = refs[3:]
    feeds, refs = refs[:layers], refs[layers:]
    filters, refs = refs[:layers], refs[layers:]
    packs, refs = refs[:layers], refs[layers:]
    (outputs, input_grad, mix_gain, mix_bias, in_grad, short, filter_grad, cond, out_grad, glu_gain,
     glu_bias, up_grad, down_grad, held, sems) = refs
    pairs = ((outputs_in, outputs), (input_in, input_grad))
    loads = [
        pltpu.make_async_copy(source, held.at[n], sems.at[n]) for n, (source, _) in enumerate(pairs)
    ]
    copies = [
        pltpu.make_async_copy(held.at[n], target, sems.at[2 + n])
        for n, (_, target) in enumerate(pairs)
    ]
    for copy in loads:
        copy.start()
    each = in_grad.shape[1]
    shard = cond.shape[1]
    lanes = filters[0].shape[1]
    for layer in range(layers):
        for kind, out in enumerate((mix_gain, mix_bias, glu_gain, glu_bias)):
            row = 4 * layer + kind
            out[layer : layer + 1, :] = small[row : row + 1, :shard]
        row = 4 * layers + 10 * layer
        for tap in range(3):
            short[layer, tap] = small[row + 3 * tap : row + 3 * tap + 3, :shard]
        cond[layer : layer + 1, :] = small[row + 9 : row + 10, :shard]
        for stream in range(3):
            in_grad[layer, :, stream, :] = packs[layer][stream * each : (stream + 1) * each]
        out_grad[layer] = packs[layer][3 * each : 4 * each]
        for n in range(filter_grad.shape[2] // lanes):
            filter_grad[layer, :, n * lanes : (n + 1) * lanes] = filters[layer][
                n * each : (n + 1) * each
            ]
        rows = down_grad.shape[1]
        down_grad[layer] = feeds[layer][:rows]
        for kind in range(2):
            up_grad[layer, :, kind, :] = feeds[layer][(kind + 1) * rows : (kind + 2) * rows]
        loads[layer].wait()
        copies[layer].start()
    for copy in copies:
        copy.wait()


def collect(outputs, input_grad, small, feeds, filters, packs, each):
    layers = len(feeds)
    shard, slots = outputs.shape
    width = 4 * shard
    rows, hidden = feeds[0].shape[0] // 3, feeds[0].shape[1]
    anywhere = pl.BlockSpec(memory_space=pl.ANY)
    local = pl.BlockSpec(memory_space=pltpu.VMEM)
    operands = [outputs, input_grad, small, *feeds, *filters, *packs]
    small_shape = (layers, shard)
    shapes = [
        (shard, slots), (shard, slots), small_shape, small_shape, (layers, each, 3, width),
        (layers, 3, 3, shard), (layers, each, slots), small_shape, (layers, each, width),
        small_shape, small_shape, (layers, rows, 2, hidden), (layers, rows, hidden),
    ]
    return pl.pallas_call(
        lambda *refs: collect_kernel(layers, *refs),
        out_shape=tuple(jax.ShapeDtypeStruct(shape, F32) for shape in shapes),
        in_specs=[anywhere] * 2 + [local] * (len(operands) - 2),
        out_specs=tuple([anywhere] * 2 + [local] * (len(shapes) - 2)),
        scratch_shapes=[pltpu.VMEM((2, shard, slots), F32), pltpu.SemaphoreType.DMA((4,))],
        compiler_params=pltpu.CompilerParams(vmem_limit_bytes=VMEM_LIMIT),
        name="collect",
    )(*operands)


def body(
    inputs,
    seq_table,
    mix_gain,
    mix_bias,
    in_proj,
    short_conv,
    long_filter,
    cond_weight,
    out_proj,
    glu_gain,
    glu_bias,
    glu_in,
    glu_out,
    cotangent,
):
    shard, slots = inputs.shape
    layers, width = in_proj.shape[0], in_proj.shape[3]
    hidden = glu_out.shape[2]
    blocks = 4
    count = lax.axis_size("dp")
    each = shard // count
    table = jnp.asarray(dft_table(slots // blocks), BF16)
    sign = jnp.asarray(np.tile(1.0 - 2.0 * (np.arange(slots // blocks) % 2), (8, 1)), F32)
    residual, gains, normed, project, in_rows, up_columns, columns, keep = first_project(
        inputs, (mix_gain, mix_bias, glu_gain, glu_bias), in_proj, short_conv, cond_weight,
        (glu_in, 0), seq_table, 1,
    )
    constants = (keep, sign, table, seq_table, jnp.asarray(dft_table(slots // blocks).T, BF16))
    kept, state = [], None
    for l in range(layers):
        token_gated, conv, carried = conv_forward(
            project, (long_filter, l), (columns, l), *constants, cotangent if l else out_proj,
            2 if l else 1, blocks, 10 + l,
        )
        if l:
            state = carried
        else:
            full_out = carried
        middle, normed_glu, after, *rest = feed_forward(
            token_gated, residual, gains, (full_out, l), up_columns, (glu_out, l),
            ((in_rows, l + 1), (glu_in, l + 1)) if l + 1 < layers else (), 4 * l + 2, 20 + l,
        )
        saved, follow = [up_columns] + rest[:3], rest[3:]
        kept.append((residual, normed, project, conv, token_gated, middle, normed_glu, saved))
        residual = after
        if follow:
            normed, project, up_columns = follow
    feeds, filters, packs, gain_sums, row_sums = ([None] * layers for _ in range(5))
    waiting = []
    for l in reversed(range(layers)):
        before, normed, project, conv, token_gated, middle, normed_glu, saved = kept[l]
        top = l == layers - 1
        state, gated_grad, feed_grads, out_grad, glu_sums, *large = feed_back(
            state, middle, gains, normed_glu, saved[0], (glu_out, l), (full_out, l), token_gated,
            saved[1:], waiting, 4 * l + 2, count, 30 + l,
        )
        if waiting:
            filters[l + 1], packs[l + 1], feeds[l + 1] = large
        one, two = (3 * count // 8, 5 * count // 8) if l else (count // 2, count - 1)
        project_low, filter_pack, square, row_sums[l], held, *rest = conv_backward(
            gated_grad, project, conv, (long_filter, l), (columns, l), *constants,
            out_grad.reshape(4, shard, width), [Track(feed_grads, 0, one)],
            (residual,) if top else (), blocks, 40 + l,
        )
        if top:
            outputs = rest[0]
        tracks = [Track(feed_grads, one, two, held), Track(filter_pack, 0, count // 4)]
        state, in_pack, mix_sums, feed_held, held, in_held = project_back(
            project_low, state, before, gains, normed, (in_rows, l), square,
            tracks, 4 * l, 50 + l,
        )
        waiting = [
            Track(filter_pack, count // 4, count - 1, held),
            Track(in_pack, count // 4, count - 1, in_held),
        ]
        if l:
            waiting.append(Track(feed_grads, two, count - 1, feed_held))
        else:
            feeds[0] = feed_held
        gain_sums[l] = [mix_sums, glu_sums]
    input_grad, small, filters[0], packs[0] = last_sums(
        state, [one for pair in gain_sums for one in pair], row_sums, waiting, 60
    )
    return collect(outputs, input_grad, small, feeds, filters, packs, each)


def solution(mesh):
    in_specs = (
        P("chan", "dp"),
        P("dp", None),
        P(None, "chan"),
        P(None, "chan"),
        P(None, "chan", None, None),
        P(None, None, None, "chan"),
        P(None, "chan", None),
        P(None, "chan"),
        P(None, "chan", None),
        P(None, "chan"),
        P(None, "chan"),
        P(None, None, None, "chan"),
        P(None, None, "chan"),
        P("chan", "dp"),
    )
    out_specs = (
        P("chan", "dp"),
        P("chan", "dp"),
        P(None, "chan"),
        P(None, "chan"),
        P(None, ("chan", "dp"), None, None),
        P(None, None, None, "chan"),
        P(None, ("chan", "dp"), None),
        P(None, "chan"),
        P(None, ("chan", "dp"), None),
        P(None, "chan"),
        P(None, "chan"),
        P(None, "dp", None, "chan"),
        P(None, "dp", "chan"),
    )
    return jax.shard_map(body, mesh=mesh, in_specs=in_specs, out_specs=out_specs, check_vma=False)
```

```python
import math

import jax
import jax.numpy as jnp
import numpy as np
from jax import lax
from jax.experimental import pallas as pl
from jax.experimental.pallas import tpu as pltpu
from jax.sharding import PartitionSpec as P

EPSILON = 1e-05
F32 = jnp.float32
BF16 = jnp.bfloat16
VMEM_LIMIT = 63 * 2**20
LOADS = 4


def dft_table(block_len):
    period = 2 * block_len
    position = np.arange(block_len)[:, None]
    phase = ((2 * np.arange(block_len)[None, :] + 1) * position) % (2 * period)
    phase = phase * (math.pi / period)
    return np.concatenate([np.cos(phase), -np.sin(phase)], axis=1)


class Facts:
    def __init__(self, table_ref, blocks, block_len):
        length, count = table_ref[0, 0], table_ref[0, 1]
        used = length * count
        pair = jnp.where(length >= 2 * block_len, 1.0, 0.0)
        four = jnp.where(length >= 4 * block_len, 1.0, 0.0)
        active = [jnp.where(i * block_len < used, 1.0, 0.0) for i in range(blocks)]
        self.same = [[None] * blocks for _ in range(blocks)]
        for i in range(blocks):
            for j in range(blocks):
                if i == j:
                    self.same[i][j] = active[i]
                else:
                    joined = pair if i // 2 == j // 2 else four
                    self.same[i][j] = active[i] * active[j] * joined
        shortest = 1.0 / block_len
        self.inverse = shortest * (1.0 - 0.5 * pair - 0.25 * four)


class Io:
    def __init__(self, source, loads, stores):
        self.source, self.loads, self.stores, self.pending = source, loads, stores, []

    def ready(self, *numbers, cuts=None):
        for number in numbers:
            for copy in self.loads[number] if cuts is None else self.loads[number][cuts]:
                copy.wait()

    def flush(self, number, part=0, at=None):
        source, target, sems = self.stores[number]
        if at is not None:
            source, target = source.at[at], target.at[at]
        copy = pltpu.make_async_copy(source, target, sems.at[part])
        copy.start()
        self.pending.append(copy)

    def finish(self):
        for copy in self.pending:
            copy.wait()


def fused_call(kernel, operands, outs, scratch, collective, name, parts, scalars=-1, order=(),
               cuts=None, manual=()):
    arrays, layers = [], []
    for operand in operands:
        array, layer = operand if isinstance(operand, tuple) else (operand, None)
        arrays.append(array)
        layers.append(layer)
    cuts = cuts or {}
    inputs, results = len(arrays), len(outs)
    buffers, sems = [], []
    for number, (array, layer) in enumerate(zip(arrays, layers)):
        if number != scalars:
            buffers.append(pltpu.VMEM(array.shape if layer is None else array.shape[1:], array.dtype))
            sems.append(pltpu.SemaphoreType.DMA((len(cuts.get(number, (0,))),)))
    for (shape, dtype), count in zip(outs, parts):
        buffers.append(pltpu.VMEM(shape, dtype))
        sems.append(pltpu.SemaphoreType.DMA((count,)))

    def body(*refs):
        extra = list(refs[inputs + results + len(scratch) :])
        places, marks = extra[: len(buffers)], extra[len(buffers) :]
        sources, loads, stores, views, n = {}, {}, {}, [], 0
        for number in range(inputs):
            if number == scalars:
                views.append(refs[number])
                continue
            source = refs[number]
            if layers[number] is not None:
                source = source.at[layers[number]]
            sources[number] = source
            views.append(places[n])
            if number not in manual:
                pairs = [(source, places[n])]
                if number in cuts:
                    rows = [pl.ds(*one) for one in cuts[number]]
                    pairs = [(source.at[one], places[n].at[one]) for one in rows]
                loads[number] = [
                    pltpu.make_async_copy(*pair, marks[n].at[i]) for i, pair in enumerate(pairs)
                ]
            n += 1
        for number in range(results):
            stores[number] = (places[n], refs[inputs + number], marks[n])
            views.append(places[n])
            n += 1
        started = set()
        for one in list(order) + list(loads):
            number, chosen = one if isinstance(one, tuple) else (one, None)
            for i, copy in enumerate(loads[number]):
                if (chosen is None or i == chosen) and (number, i) not in started:
                    started.add((number, i))
                    copy.start()
        io = Io(sources, loads, stores)
        kernel(io, *views, *refs[inputs + results : inputs + results + len(scratch)])
        io.finish()

    anywhere = pl.BlockSpec(memory_space=pl.ANY)
    scalar_spec = pl.BlockSpec(memory_space=pltpu.SMEM)
    params = {}
    if collective is not None:
        params = dict(collective_id=collective, has_side_effects=True)
    return pl.pallas_call(
        body,
        out_shape=tuple(jax.ShapeDtypeStruct(*out) for out in outs),
        in_specs=[scalar_spec if n == scalars else anywhere for n in range(inputs)],
        out_specs=tuple([anywhere] * results),
        scratch_shapes=list(scratch) + buffers + sems,
        compiler_params=pltpu.CompilerParams(vmem_limit_bytes=VMEM_LIMIT, **params),
        name=name,
    )(*arrays)


def ring_position(index, count):
    odd = index % 2
    return (1 - odd) * (index // 2) + odd * (count - 1 - index // 2)


def ring_member(position, count):
    late = position // (count // 2)
    return (1 - late) * 2 * position + late * (2 * (count - 1 - position) + 1)


def chan_peers():
    me = lax.axis_index("chan")
    mate = me + 1 - 2 * (me % 2)
    across = (me + 2) % 4
    return me, mate, across, (mate + 2) % 4


def greet(peers, members=()):
    barrier = pltpu.get_barrier_semaphore()
    for peer in peers:
        pl.semaphore_signal(barrier, inc=1, device_id={"chan": peer})
    for member in members:
        pl.semaphore_signal(barrier, inc=1, device_id={"dp": member})
    pl.semaphore_wait(barrier, len(peers) + len(members))


def send_to(peer, source, target, send, recv):
    return pltpu.make_async_remote_copy(source, target, send, recv, device_id={"chan": peer})


def span(index, size, unit=None):
    if isinstance(index, int):
        return pl.ds(index * size, size)
    return pl.ds(pl.multiple_of(index * size, unit or size), size)


def gather_copy(place, peers, sems, kind, part):
    me, mate, across, _ = peers
    block = place(across if kind == 2 else me, part)
    send, recv = sems
    return send_to(
        across if kind == 0 else mate, block, block, send.at[kind, part], recv.at[kind, part]
    )


def norm_columns(values):
    mean = jnp.mean(values, axis=0, keepdims=True)
    center = values - mean
    inverse = lax.rsqrt(jnp.mean(center * center, axis=0, keepdims=True) + EPSILON)
    return center * inverse, inverse


def norm_pullback(grad, values, gain):
    normal, inverse = norm_columns(values)
    product = grad * normal
    scaled = grad * gain
    first = jnp.mean(scaled, axis=0, keepdims=True)
    second = jnp.mean(product * gain, axis=0, keepdims=True)
    return inverse * (scaled - first - normal * second), product


def lane_sums(values):
    return jnp.sum(values, axis=1, keepdims=True)


def matmul(left, right):
    return jnp.dot(left, right, preferred_element_type=F32)


def matmul_nt(left, right):
    return lax.dot_general(
        left, right, (((1,), (1,)), ((), ())), preferred_element_type=F32
    )


def transpose_into(target, source, tile):
    for n in range(source.shape[0] // tile):
        target[:, n * tile : (n + 1) * tile] = source[n * tile : (n + 1) * tile].T


def transpose_columns(target, source, tile):
    for n in range(source.shape[1] // tile):
        target[n * tile : (n + 1) * tile, :] = source[:, n * tile : (n + 1) * tile].T


def exchange(peers, source, target, send, recv):
    copies = []
    for n, peer in enumerate((peers[2], peers[3], peers[1])):
        copy = send_to(peer, source(peer), target(), send.at[n], recv.at[n])
        copy.start()
        copies.append(copy)
    return copies


def to_channels(peers, low, landing, send, recv):
    shard, tokens = landing.shape[0], low.shape[1]
    me = peers[0]
    mine = span(me, tokens)
    copies = exchange(
        peers, lambda peer: low.at[span(peer, shard, 32), :], lambda: landing.at[:, mine], send, recv
    )
    return copies


class Track:
    def __init__(self, own, first, last, carry=None):
        self.own, self.first, self.last, self.carry = own, first, last, carry
        self.count, self.rows, self.lanes = own.shape

    def out(self):
        if self.last == self.count - 1:
            return ((self.rows, self.lanes), F32)
        return ((2, self.rows, self.lanes // 2), BF16)


def ring_operands(tracks):
    return [one.own for one in tracks] + [one.carry for one in tracks if one.first]


def ring_scratch(tracks):
    slots = [
        pltpu.VMEM((one.last - one.first, 2, one.rows, one.lanes // 2), BF16) for one in tracks
    ]
    if not tracks:
        return []
    longest = max(one.last - one.first for one in tracks)
    return slots + [pltpu.SemaphoreType.DMA((longest, len(tracks), 2))] * 2


class Ring:
    def __init__(self, tracks, operands, outs, scratch, sources):
        self.tracks, self.outs = tracks, outs
        self.count = tracks[0].count
        self.owns = operands[: len(tracks)]
        self.sources = sources[: len(tracks)]
        carries = list(sources[len(tracks) :])
        self.carries = [carries.pop(0) if one.first else None for one in tracks]
        *self.slots, self.send, self.recv = scratch
        self.here = lax.axis_index("dp")
        self.place = ring_position(self.here, self.count)
        after = ring_member((self.place + 1) % self.count, self.count)
        before = ring_member((self.place + self.count - 1) % self.count, self.count)
        self.toward = (after, before)
        self.rounds = max(one.last - one.first for one in tracks) - 1

    def copy(self, track, direction, turn, source):
        return pltpu.make_async_remote_copy(
            source,
            self.slots[track].at[turn, direction],
            self.send.at[turn, track, direction],
            self.recv.at[turn, track, direction],
            device_id={"dp": self.toward[direction]},
        )

    def owner(self, direction, step):
        move = step + 1
        if direction == 0:
            move = self.count - move
        return ring_member((self.place + move) % self.count, self.count)

    def own(self, track, direction, owner, owns=None):
        own = (owns or self.owns)[track]
        half = own.shape[2] // 2
        return own.at[owner, :, pl.ds(direction * half, half)]

    def held(self, track, direction, turn):
        return self.slots[track].at[turn, direction]

    def start(self):
        for track, carry in enumerate(self.carries):
            for direction in range(2):
                if carry is None:
                    source = self.own(track, direction, self.owner(direction, 0), self.sources)
                else:
                    source = carry.at[direction]
                self.copy(track, direction, 0, source).start()

    def round(self, turn, extra):
        for track, info in enumerate(self.tracks):
            def one(track=track, info=info):
                for direction in range(2):
                    held = self.held(track, direction, turn - 1)
                    self.copy(track, direction, turn - 1, held).wait_recv()
                    own = self.own(track, direction, self.owner(direction, info.first + turn))
                    held[...] = (held[...].astype(F32) + own[...].astype(F32)).astype(BF16)
                    self.copy(track, direction, turn, held).start()

            if info.last - info.first - 1 == self.rounds:
                one()
            else:
                pl.when(turn < info.last - info.first)(one)
        return extra

    def advance(self, point, points):
        first, last = self.rounds * point // points, self.rounds * (point + 1) // points
        if isinstance(point, int) and last == first:
            return
        if isinstance(point, int) and last == first + 1:
            self.round(last, 0)
            return
        lax.fori_loop(1 + first, 1 + last, self.round, 0)

    def loop(self, body, steps, point, pieces, points):
        for n in range(pieces):
            lax.fori_loop(steps * n // pieces, steps * (n + 1) // pieces, body, 0)
            self.advance(point + n, points)

    def finish(self):
        for track, (info, out) in enumerate(zip(self.tracks, self.outs)):
            turns = info.last - info.first
            half = info.lanes // 2
            whole = info.last == self.count - 1
            for direction in range(2):
                held = self.held(track, direction, turns - 1)
                self.copy(track, direction, turns - 1, held).wait_recv()
                owner = self.here if whole else self.owner(direction, info.last)
                own = self.own(track, direction, owner)
                total = held[...].astype(F32) + own[...].astype(F32)
                if whole:
                    out[:, pl.ds(direction * half, half)] = total
                else:
                    out[direction] = total.astype(BF16)

        def settle(turn, extra):
            for track, info in enumerate(self.tracks):
                def one(track=track):
                    for direction in range(2):
                        held = self.held(track, direction, turn)
                        self.copy(track, direction, turn, held).wait_send()

                if info.last - info.first == self.rounds + 1:
                    one()
                else:
                    pl.when(turn < info.last - info.first)(one)
            return extra

        lax.fori_loop(0, self.rounds + 1, settle, 0)


def ring_rows(rows):
    return -(-rows // 16) * 16


def split_rows(target, source, unit):
    _, kinds, lanes = source.shape

    def one(n, carry):
        here = span(n, unit)
        for kind in range(kinds):
            target[here, kind * lanes : (kind + 1) * lanes] = source[here, kind, :]
        return carry

    return one


def first_project_kernel(
    io, inputs_ref, mix_gain, mix_bias, glu_gain, glu_bias, weight_ref, short_in, cond_in, up_in,
    seq_ref, x_ref, gains_ref, full, project_ref, up_ref, columns_ref, keep_ref,
    raw, gains_low, gains_land, turn, send, recv, gains_send, gains_recv,
):
    peers = chan_peers()
    me = peers[0]
    shard, slots = inputs_ref.shape
    parts, width, half = raw.shape
    layers = mix_gain.shape[0]
    greet(peers[1:])
    io.ready(0, 1, 2, 3, 4)

    def gather(kind, part):
        return gather_copy(
            lambda owner, part: raw.at[part, span(owner, shard, 32), :],
            peers, (send, recv), kind, part,
        )

    for layer in range(layers):
        for kind, one in enumerate((mix_gain, mix_bias, glu_gain, glu_bias)):
            row = 4 * layer + kind
            gains_low[row : row + 1, :] = one[layer : layer + 1, :]
    gains_land[me] = gains_low[...]
    copies = exchange(
        peers, lambda peer: gains_low, lambda: gains_land.at[me], gains_send, gains_recv
    )
    for part in range(parts):
        raw[part, span(me, shard, 32), :] = inputs_ref[:, part * half : (part + 1) * half]
        for kind in range(2):
            gather(kind, part).start()
    io.ready(6, 7)
    for layer in range(layers):
        turn[...] = jnp.zeros_like(turn)
        for row in range(9):
            turn[row : row + 1, :shard] = short_in[row // 3, row % 3, layer : layer + 1, :]
        turn[9:10, :shard] = cond_in[layer : layer + 1, :]
        columns_ref[layer] = turn[...].T[:shard]
    slot = lax.broadcasted_iota(jnp.int32, keep_ref.shape, 1)
    row = lax.broadcasted_iota(jnp.int32, keep_ref.shape, 0)
    within = slot & (seq_ref[0, 0] - 1)
    keep_ref[...] = jnp.where(within > row, 1.0, 0.0)
    io.flush(5)
    io.flush(6)
    for copy in copies:
        copy.wait()
    turn[...] = jnp.zeros_like(turn)
    for owner in range(4):
        turn[: 4 * layers, :shard] = gains_land[owner]
        gains_ref[owner * shard : (owner + 1) * shard, :] = turn[...].T[:shard]
    io.flush(1)
    io.ready(5, 8)
    gather(0, 0).wait_recv()
    gather(2, 0).start()
    for part in range(parts):
        if part + 1 < parts:
            gather(0, part + 1).wait_recv()
            gather(2, part + 1).start()
        gather(1, part).wait_recv()
        gather(2, part).wait_recv()
        values = raw[part].astype(F32)

        @pl.when(me == part // 2)
        def _():
            x_ref[:, (part % 2) * half : (part % 2 + 1) * half] = values

        normal, _ = norm_columns(values)
        full[part] = (normal * gains_ref[:, 0:1] + gains_ref[:, 1:2]).astype(BF16)
        io.flush(2, part, part)
        columns = slice(part * half, (part + 1) * half)
        project_ref[:, columns] = matmul(weight_ref[...], full[part])
        io.flush(3, part, (slice(None), pl.ds(part * half, half)))
        cuts = width // 64
        lax.fori_loop(
            cuts * part // parts, cuts * (part + 1) // parts, split_rows(up_ref, up_in, 64), 0
        )
    io.flush(0)
    io.flush(4)
    for part in range(parts):
        for kind in range(3):
            gather(kind, part).wait_send()


def first_project(inputs, gain_arrays, weight, short_conv, cond_weight, glu_in, seq_table,
                  collective):
    shard, slots = inputs.shape
    layers = len(gain_arrays[0])
    rows, width = weight[0].shape[1:]
    hidden = glu_in[0].shape[3]
    tokens = slots // 4
    return fused_call(
        first_project_kernel,
        [inputs, *gain_arrays, weight, short_conv, cond_weight, glu_in, seq_table],
        [
            ((width, tokens), F32),
            ((width, 128), F32),
            ((8, width, tokens // 2), BF16),
            ((rows, slots), F32),
            ((width, 2 * hidden), BF16),
            ((layers, shard, 128), F32),
            ((8, slots), F32),
        ],
        [
            pltpu.VMEM((8, width, tokens // 2), BF16),
            pltpu.VMEM((4 * layers, shard), F32),
            pltpu.VMEM((4, 4 * layers, shard), F32),
            pltpu.VMEM((128, 256), F32),
        ]
        + [pltpu.SemaphoreType.DMA((3, 8))] * 2
        + [pltpu.SemaphoreType.DMA((3,))] * 2,
        collective,
        "first_project",
        (1, 1, 8, 8, 1, 1, 1),
        9,
    )


def scatter_copy(peers, buffers, sems, kind, part):
    _, mate, across, _ = peers
    send, recv = sems
    return send_to(
        across if kind == 2 else mate,
        buffers[2 * kind].at[part],
        buffers[2 * kind + 1].at[part],
        send.at[kind, part],
        recv.at[kind, part],
    )


def scatter_buffers(width, half):
    return [pltpu.VMEM((2, width, half), BF16)] * 6


def block_place(full):
    return lambda owner, part: full.at[owner * 2 + part]


def block_at(step, peers, gathers):
    me, mate, across, diag = peers
    if gathers:
        mine = 1 - (step + 6) // 8
        kind = (step + 1) % 3
        part = mine * step + (1 - mine) * ((step - 2) // 3)
        kind = kind - mine * 4
    else:
        near = step // 4
        mine = step // 6
        part = (1 - near) * (step // 2) + near * (step % 2)
        kind = (1 - near) * (1 + step % 2) - mine
    far = kind * (2 - kind) * (across - mate) + kind * (kind - 1) // 2 * (diag - mate)
    return kind, part, ((1 - mine) * (mate + far) + mine * me) * 2 + part, mine


def run_blocks(peers, full, gather_sems, scatter_sems, buffers, partial, kept, own, ring=None):
    me, mate, across, diag = peers
    gathers = gather_sems is not None

    def gather(kind, part):
        return gather_copy(block_place(full), peers, gather_sems, kind, part)

    def step_body(step, carry):
        kind, part, block, mine = block_at(step, peers, gathers)

        if gathers:
            @pl.when(kind == 0)
            def _():
                gather(1, part).wait_recv()

            @pl.when(kind == 1)
            def _():
                gather(0, part).wait_recv()
                gather(2, part).start()

            @pl.when(kind == 2)
            def _():
                gather(2, part).wait_recv()

        share = partial(block, step)

        def scatter(kind):
            return scatter_copy(peers, buffers, scatter_sems, kind, part)

        @pl.when(mine == 1)
        def _():
            own[part] = share

        @pl.when(kind == 0)
        def _():
            buffers[2][part] = share.astype(BF16)
            scatter(1).start()

        @pl.when(kind == 1)
        def _():
            kept[...] = share

        @pl.when(kind == 2)
        def _():
            buffers[0][part] = share.astype(BF16)
            scatter(0).start()
            scatter(0).wait_recv()
            buffers[4][part] = (kept[...] + buffers[1][part].astype(F32)).astype(BF16)
            scatter(2).start()

        if ring is not None:
            pl.when(step % 3 == 2)(lambda: ring.advance(step // 3, 4))
        return carry

    lax.fori_loop(0, 8, step_body, 0)


def scattered(peers, scatter_sems, buffers, own, part):
    for kind in (1, 2):
        scatter_copy(peers, buffers, scatter_sems, kind, part).wait_recv()
    return own[part] + buffers[3][part].astype(F32) + buffers[5][part].astype(F32)


def drain_gather(peers, full, gather_sems):
    for part in range(2):
        for kind in range(3):
            gather_copy(block_place(full), peers, gather_sems, kind, part).wait_send()


def drain_scatter(peers, scatter_sems, buffers):
    for part in range(2):
        for kind in range(3):
            scatter_copy(peers, buffers, scatter_sems, kind, part).wait_send()


def feed_kernel(gain_at, follows, io, token_gated, x_ref, gains_ref, out_weight, up_columns,
                down_weight, *refs):
    refs = list(refs)
    weight_ref, up_in = (refs.pop(0), refs.pop(0)) if follows else (None, None)
    mid_ref, full, next_ref, units, gelus, slopes = refs[:6]
    refs = refs[6:]
    if follows:
        next_full, project_ref, next_up = refs[:3]
        *refs, next_send, next_recv = refs[3:]
    up_weight, kept, own, *rest = refs
    buffers, sems = rest[:6], rest[6:]
    gather_send, gather_recv, scatter_send, scatter_recv = sems
    gather_sems, scatter_sems = (gather_send, gather_recv), (scatter_send, scatter_recv)
    peers = chan_peers()
    me, mate, across, _ = peers
    width, tokens = x_ref.shape
    half = tokens // 2
    hidden = down_weight.shape[1]
    greet((mate, across))
    io.ready(0, 1, 2, 3)
    for part in range(2):
        columns = slice(part * half, (part + 1) * half)
        mid = x_ref[:, columns] + matmul(out_weight[...], token_gated[:, columns])
        mid_ref[:, columns] = mid
        normal, _ = norm_columns(mid)
        gain = gains_ref[:, gain_at : gain_at + 1]
        bias = gains_ref[:, gain_at + 1 : gain_at + 2]
        full[me * 2 + part] = (normal * gain + bias).astype(BF16)
        for kind in range(2):
            gather_copy(block_place(full), peers, gather_sems, kind, part).start()
    io.flush(0)
    io.ready(4, 5)
    transpose_columns(up_weight, up_columns, 256)

    def partial(block, step):
        normed = full[block]
        tile = 256
        gates = matmul(up_weight[:hidden], normed)
        ups = matmul(up_weight[hidden:], normed)
        for n in range(hidden // tile):
            rows = slice(n * tile, (n + 1) * tile)
            gate, up = gates[rows], ups[rows]
            cdf = 0.5 * (1.0 + lax.erf(gate * math.sqrt(0.5)))
            density = jnp.exp(-0.5 * gate * gate) * (1.0 / math.sqrt(2.0 * math.pi))
            gelu = gate * cdf
            units[block, rows] = (gelu * up).astype(BF16)
            gelus[block, rows] = gelu.astype(BF16)
            slopes[block, rows] = (up * (cdf + gate * density)).astype(BF16)
        return matmul(down_weight[...], units[block])

    run_blocks(peers, full, gather_sems, scatter_sems, buffers, partial, kept, own)
    for number in (1, 3, 4, 5):
        io.flush(number)
    if follows:
        io.ready(6, 7)
    place = block_place(next_full) if follows else None
    for part in range(2):
        if follows:
            cuts = width // 64
            lax.fori_loop(
                cuts * part // 2, cuts * (part + 1) // 2, split_rows(next_up, up_in, 64), 0
            )
        columns = slice(part * half, (part + 1) * half)
        value = mid_ref[:, columns] + scattered(peers, scatter_sems, buffers, own, part)
        next_ref[:, columns] = value.astype(next_ref.dtype)
        if follows:
            normal, _ = norm_columns(value)
            gain = gains_ref[:, gain_at + 2 : gain_at + 3]
            bias = gains_ref[:, gain_at + 3 : gain_at + 4]
            next_full[me * 2 + part] = (normal * gain + bias).astype(BF16)
            for kind in range(2):
                gather_copy(place, peers, (next_send, next_recv), kind, part).start()
    io.flush(2)
    if follows:
        io.flush(8)
    drain_gather(peers, full, gather_sems)
    drain_scatter(peers, scatter_sems, buffers)
    if follows:
        project_blocks(io, peers, next_full, (next_send, next_recv), weight_ref, project_ref, 6, 7)


def project_blocks(io, peers, full, sems, weight_ref, project_ref, full_out, project_out):
    me, mate, across, diag = peers
    half = full.shape[2]

    def gather(kind, part):
        return gather_copy(block_place(full), peers, sems, kind, part)

    order = [(me, 0), (me, 1), (mate, 0), (mate, 1)]
    order += [(across, 0), (diag, 0), (across, 1), (diag, 1)]
    for step, (owner, part) in enumerate(order):
        if 2 <= step < 4:
            gather(1, part).wait_recv()
        elif step >= 4 and step % 2 == 0:
            gather(0, part).wait_recv()
            gather(2, part).start()
        elif step >= 4:
            gather(2, part).wait_recv()
        block = owner * 2 + part
        io.flush(full_out, step, block)
        columns = span(block, half)
        project_ref[:, columns] = matmul(weight_ref[...], full[block])
        io.flush(project_out, step, (slice(None), columns))
    for kind in range(3):
        for part in range(2):
            gather(kind, part).wait_send()


def feed_forward(token_gated, values, gains, out_weight, up_columns, down_weight, following, gain_at,
                 collective):
    width, tokens = values.shape
    half = tokens // 2
    follows = list(following)
    block = ((8, width, half), BF16)
    outs = [((width, tokens), F32), block]
    outs.append(((width, tokens), F32 if follows else BF16))
    hidden = down_weight[0].shape[2]
    outs += [((8, hidden, half), BF16)] * 3
    parts = [1] * 6
    extra = []
    if follows:
        outs += [block, ((follows[0][0].shape[1], 4 * tokens), F32)]
        outs.append(((width, 2 * hidden), BF16))
        parts += [8, 8, 1]
        extra = [pltpu.SemaphoreType.DMA((3, 2))] * 2
    return fused_call(
        lambda *refs: feed_kernel(gain_at, bool(follows), *refs),
        [token_gated, values, gains, out_weight, up_columns, down_weight] + follows,
        outs,
        [
            pltpu.VMEM((2 * hidden, width), BF16),
            pltpu.VMEM((width, half), F32),
            pltpu.VMEM((2, width, half), F32),
        ]
        + scatter_buffers(width, half)
        + [pltpu.SemaphoreType.DMA((3, 2))] * 4
        + extra,
        collective,
        "feed_forward",
        parts,
    )


def weight_grad(store, rows, columns, left, right, blocks, row_tile, column_tile):
    across = columns // column_tile

    def one(n, carry):
        row, column = span(n // across, row_tile), span(n % across, column_tile)
        total = matmul_nt(left(0, row), right(0, column))
        for block in range(1, blocks):
            total = total + matmul_nt(left(block, row), right(block, column))
        store(n // across, column, total)
        return carry

    lax.fori_loop(0, rows // row_tile * across, one, 0)


def feed_back_kernel(gain_at, gathered, tracks, io, grad_ref, down_weight, gelus, slopes, up_columns,
                     out_weight, mid_ref, gains_ref, token_gated, units, normed, *refs):
    refs = list(refs)
    rings = len(tracks)
    inputs = len(ring_operands(tracks))
    ring_in, refs = refs[:inputs], refs[inputs:]
    state_ref, gated_ref, feed_grads, out_grad, sums_ref = refs[:5]
    large, refs = refs[5 : 5 + rings], refs[5 + rings :]
    ring = None
    if rings:
        sources = [io.source[11 + n] for n in range(inputs)]
        ring = Ring(tracks, ring_in, large, refs[-rings - 2 :], sources)
        refs = refs[: -rings - 2]
    full = grad_ref if gathered else refs.pop(0)
    mixer_low, kept, own, turned, *rest, load_sems = refs
    gated_low = full
    buffers, sems = rest[:6], rest[6:]
    send, recv, gather_send, gather_recv, scatter_send, scatter_recv = sems
    gather_sems, scatter_sems = (gather_send, gather_recv), (scatter_send, scatter_recv)
    if gathered:
        gather_sems = None
    peers = chan_peers()
    me, mate, across, diag = peers
    width, tokens = mid_ref.shape
    half = tokens // 2
    shard = gated_ref.shape[0]
    hidden = down_weight.shape[1]
    tile = 256
    saved = ((io.source[2], gelus), (io.source[3], slopes))
    if gathered:
        saved += ((io.source[0], full),)

    def loads(step, block):
        return [
            pltpu.make_async_copy(source.at[block], target.at[block], load_sems.at[n, step])
            for n, (source, target) in enumerate(saved)
        ]

    for step in range(8):
        for copy in loads(step, block_at(step, peers, not gathered)[2]):
            copy.start()
    greet(peers[1:], ring.toward if rings else ())
    if not gathered:
        io.ready(0)
        for part in range(2):
            full[me * 2 + part] = grad_ref[:, part * half : (part + 1) * half].astype(BF16)
            for kind in range(2):
                gather_copy(block_place(full), peers, gather_sems, kind, part).start()
    if rings:
        ring.start()
    io.ready(1)
    down_rows, out_rows = turned.at[:hidden], turned.at[:width]
    transpose_into(down_rows, down_weight, tile)
    io.ready(4)
    if rings:
        io.ready(*range(11, 11 + rings))

    def partial(block, step):
        for copy in loads(step, block):
            copy.wait()
        unit_grads = matmul(down_rows[...], full[block])
        for n in range(hidden // tile):
            rows = slice(n * tile, (n + 1) * tile)
            unit_grad = unit_grads[rows]
            slopes[block, rows] = (unit_grad * slopes[block, rows].astype(F32)).astype(BF16)
            gelus[block, rows] = (unit_grad * gelus[block, rows].astype(F32)).astype(BF16)
        return matmul(up_columns[:, :hidden], slopes[block]) + matmul(
            up_columns[:, hidden:], gelus[block]
        )

    run_blocks(peers, full, gather_sems, scatter_sems, buffers, partial, kept, own, ring)
    io.ready(5, 6, 7, 8, 9, 10)
    transpose_into(out_rows, out_weight, tile)
    if not gathered:
        drain_gather(peers, full, gather_sems)

    def a2a(part, n):
        peer = (across, diag, mate)[n]
        return send_to(
            peer,
            gated_low.at[part, span(peer, shard, 32), :],
            gated_ref.at[:, span(me * 2 + part, half)],
            send.at[part, n],
            recv.at[part, n],
        )

    chunk_rows = feed_grads.shape[1] // 3
    row_tile = 384

    def store_grad(kind):
        def store(index, column, total):
            chunks = row_tile // chunk_rows
            for n in range(chunks):
                feed_grads[
                    index * chunks + n, kind * chunk_rows : (kind + 1) * chunk_rows, column
                ] = total[n * chunk_rows : (n + 1) * chunk_rows].astype(BF16)

        return store

    def feed_grad(kind):
        if kind == 0:
            left, right = lambda b, r: full[b, r], lambda b, c: units[b, c]
        else:
            def left(b, r):
                return normed[b, r]

            def right(b, c):
                return (slopes, gelus)[kind - 1][b, c]

        weight_grad(store_grad(kind), width, hidden, left, right, 8, row_tile, tile)

    def store_out(index, column, total):
        out_grad[span(index, tile), column] = total.astype(BF16)

    gain = gains_ref[:, gain_at : gain_at + 1]
    for part in range(2):
        feed_grad(part)
        if rings:
            ring.advance(2 + part, 4)
        columns = slice(part * half, (part + 1) * half)
        grad = scattered(peers, scatter_sems, buffers, own, part)
        change, product = norm_pullback(grad, mid_ref[:, columns], gain)
        before = full[me * 2 + part].astype(F32) if gathered else grad_ref[:, columns]
        state = before + change
        state_ref[:, columns] = state
        mixer_low[:, columns] = state.astype(BF16)
        gated_low[part] = matmul(out_rows[...], mixer_low[:, columns]).astype(BF16)
        for n in range(3):
            a2a(part, n).start()
        if part == 0:
            sums_ref[:, 0:1] = lane_sums(product)
            sums_ref[:, 1:2] = lane_sums(grad)
        else:
            sums_ref[:, 0:1] = sums_ref[:, 0:1] + lane_sums(product)
            sums_ref[:, 1:2] = sums_ref[:, 1:2] + lane_sums(grad)
    io.flush(0)
    feed_grad(2)
    io.flush(2)
    io.flush(4)
    for part in range(2):
        gated_ref[:, span(me * 2 + part, half)] = gated_low[part, span(me, shard, 32), :]
    weight_grad(
        store_out, width, width,
        lambda b, r: mixer_low[r, :], lambda b, c: token_gated[c, :], 1, tile, tile,
    )
    io.flush(3)
    if rings:
        ring.finish()
        for n in range(rings):
            io.flush(5 + n)
    for part in range(2):
        for n in range(3):
            a2a(part, n).wait()
    io.flush(1)
    drain_scatter(peers, scatter_sems, buffers)


def feed_back(grad, mid, gains, normed, up_columns, down_weight, out_weight, token_gated, saved,
              tracks, gain_at, count, collective):
    width, tokens = mid.shape
    half = tokens // 2
    hidden = down_weight[0].shape[2]
    gathered = grad.ndim == 3
    units, gelus, slopes = saved
    own_loads = tuple(range(11, 11 + len(tracks)))
    carries = tuple(range(11 + len(tracks), 11 + len(ring_operands(tracks))))
    manual = (2, 3) + ((0,) if gathered else ()) + carries
    return fused_call(
        lambda *refs: feed_back_kernel(gain_at, gathered, tracks, *refs),
        [grad, down_weight, gelus, slopes, up_columns, out_weight, mid, gains, token_gated, units]
        + [normed]
        + ring_operands(tracks),
        [
            ((width, tokens), F32),
            ((width // 4, 4 * tokens), BF16),
            ((count, 3 * width // count, hidden), BF16),
            ((width, width), BF16),
            ((width, 8), F32),
        ]
        + [one.out() for one in tracks],
        [pltpu.VMEM((8, width, half), BF16)] * (not gathered)
        + [
            pltpu.VMEM((width, tokens), BF16),
            pltpu.VMEM((width, half), F32),
            pltpu.VMEM((2, width, half), F32),
            pltpu.VMEM((max(hidden, width), width), BF16),
        ]
        + scatter_buffers(width, half)
        + [pltpu.SemaphoreType.DMA((2, 3))] * 2
        + [pltpu.SemaphoreType.DMA((3, 2))] * 4
        + [pltpu.SemaphoreType.DMA((3, 8))]
        + ring_scratch(tracks),
        collective,
        "feed_back",
        [1] * (5 + len(tracks)),
        manual=manual,
        order=((0,) if not gathered else ()) + (1, 4) + own_loads,
    )


def project_back_kernel(gain_at, each, tracks, in_track, io, project_grad, weight_ref, square_ref, normed,
                        state_ref, x_ref, gains_ref, *refs):
    inputs = len(ring_operands(tracks))
    ring_in, refs = refs[:inputs], refs[inputs:]
    next_ref, in_grad, sums_ref = refs[:3]
    large, refs = refs[3 : 3 + len(tracks)], refs[3 + len(tracks) :]
    in_held, *refs = refs
    kept, own, weight_rows, in_full, *rest = refs
    buffers, (scatter_send, scatter_recv, *ring_rest) = rest[:6], rest[6:]
    *ring_rest, in_slots, in_send, in_recv = ring_rest
    in_ring = Ring([in_track], [in_grad], [in_held], [in_slots, in_send, in_recv], [in_grad])
    scatter_sems = (scatter_send, scatter_recv)
    peers = chan_peers()
    me, mate, across, diag = peers
    sources = [io.source[7 + n] for n in range(inputs)]
    ring = Ring(tracks, ring_in, large, ring_rest, sources)
    width, tokens = x_ref.shape
    half = tokens // 2
    rows = weight_ref.shape[0]
    shard = rows // 3
    greet((mate, across), ring.toward)
    ring.start()
    io.ready(1)
    for first, size in ((0, 512), (512, rows - 512)):
        weight_rows[:, first : first + size] = weight_ref[first : first + size].T
    io.ready(0)

    def share(owner, part):
        return matmul(weight_rows[...], project_grad[:, span(owner * 2 + part, half)])

    for part in range(2):
        buffers[0][part] = share(diag, part).astype(BF16)
        scatter_copy(peers, buffers, scatter_sems, 0, part).start()
        kept[...] = share(across, part)
        scatter_copy(peers, buffers, scatter_sems, 0, part).wait_recv()
        buffers[4][part] = (kept[...] + buffers[1][part].astype(F32)).astype(BF16)
        scatter_copy(peers, buffers, scatter_sems, 2, part).start()
    for part in range(2):
        buffers[2][part] = share(mate, part).astype(BF16)
        scatter_copy(peers, buffers, scatter_sems, 1, part).start()
        own[part] = share(me, part)
    io.ready(2, 3)
    if in_full.shape[1] > 4 * each:
        in_full[...] = jnp.zeros_like(in_full)
    for chunk in range(shard // each):
        in_full[chunk, 3 * each : 4 * each] = square_ref[chunk * each : (chunk + 1) * each]
    tile = 256
    for stream in range(3):
        def column_tile(n, carry):
            column = span(n, tile)
            total = None
            for block in range(8):
                left = project_grad[
                    stream * shard : (stream + 1) * shard, block * half : (block + 1) * half
                ]
                value = matmul_nt(left, normed[block, column])
                total = value if total is None else total + value
            for chunk in range(shard // each):
                in_full[chunk, stream * each : (stream + 1) * each, column] = total[
                    chunk * each : (chunk + 1) * each
                ]
            return carry

        lax.fori_loop(0, width // tile, column_tile, 0)
    in_grad[...] = in_full[...].astype(BF16)
    in_ring.start()
    io.flush(1)
    io.ready(*range(7, 7 + len(tracks)))
    ring.advance(0, 2)
    io.ready(4, 5, 6)
    gain = gains_ref[:, gain_at : gain_at + 1]
    for part in range(2):
        columns = slice(part * half, (part + 1) * half)
        grad = scattered(peers, scatter_sems, buffers, own, part)
        change, product = norm_pullback(grad, x_ref[:, columns], gain)
        next_ref[:, columns] = state_ref[:, columns] + change
        if part == 0:
            sums_ref[:, 0:1] = lane_sums(product)
            sums_ref[:, 1:2] = lane_sums(grad)
            ring.advance(1, 2)
            in_ring.advance(0, 1)
        else:
            sums_ref[:, 0:1] = sums_ref[:, 0:1] + lane_sums(product)
            sums_ref[:, 1:2] = sums_ref[:, 1:2] + lane_sums(grad)
    io.flush(0)
    io.flush(2)
    ring.finish()
    for n in range(len(tracks)):
        io.flush(3 + n)
    in_ring.finish()
    io.flush(3 + len(tracks))
    drain_scatter(peers, scatter_sems, buffers)


def project_back(project_grad, state, values, gains, normed, weight, square, tracks, gain_at,
                 collective):
    width, tokens = values.shape
    half = tokens // 2
    rows = project_grad.shape[0]
    count = tracks[0].count
    each = rows // 3 // count
    packed = (count, ring_rows(4 * each), width)
    in_track = Track(jax.ShapeDtypeStruct(packed, BF16), 0, count // 4)
    return fused_call(
        lambda *refs: project_back_kernel(gain_at, each, tracks, in_track, *refs),
        [project_grad, weight, square, normed, state, values, gains] + ring_operands(tracks),
        [((width, tokens), F32), (packed, BF16), ((width, 8), F32)]
        + [one.out() for one in tracks + [in_track]],
        [
            pltpu.VMEM((width, half), F32),
            pltpu.VMEM((2, width, half), F32),
            pltpu.VMEM((width, rows), BF16),
            pltpu.VMEM(packed, F32),
        ]
        + scatter_buffers(width, half)
        + [pltpu.SemaphoreType.DMA((3, 2))] * 2
        + ring_scratch(tracks)
        + ring_scratch([in_track]),
        collective,
        "project_back",
        [1] * (4 + len(tracks)),
        manual=tuple(range(7 + len(tracks), 7 + len(ring_operands(tracks)))),
        order=(1, 0) + tuple(range(7, 7 + len(tracks))),
    )


def mask_heads(values, keep, blocks):
    length = values.shape[1] // blocks
    pieces = []
    for j in range(blocks):
        start = j * length
        pieces.append(values[:, start : start + 128] * keep[:, start : start + 128])
        pieces.append(values[:, start + 128 : start + length])
    return jnp.concatenate(pieces, axis=1)


def eight(rows):
    if isinstance(rows, int):
        return pl.ds(rows, 8)
    return pl.ds(pl.multiple_of(rows, 8), 8)


def sixteen(rows):
    if isinstance(rows, int):
        return pl.ds(rows, 16)
    return pl.ds(pl.multiple_of(rows, 16), 16)


def stream_rows(project_ref, columns_ref, keep_ref, rows, shard, stream, blocks):
    values = project_ref[eight(stream * shard + rows), :]
    total = values * columns_ref[eight(rows), stream : stream + 1]
    for offset in (1, 2):
        moved = mask_heads(pltpu.roll(values, offset, 1), keep_ref[offset - 1 : offset, :], blocks)
        column = 3 * offset + stream
        total = total + moved * columns_ref[eight(rows), column : column + 1]
    return total


def sequence_factor(power, cond, facts, blocks):
    energy = []
    for i in range(blocks):
        total = 0.0
        for j in range(blocks):
            total = total + power[j] * facts.same[i][j]
        energy.append(total * facts.inverse)
    logs = [jnp.log(1.0 + value) for value in energy]
    factor = [
        (1.0 + cond * value) * facts.same[i][i] for i, value in enumerate(logs)
    ]
    return energy, logs, factor


def block_sums(values, blocks):
    length = values.shape[1] // blocks
    return [lane_sums(values[:, i * length : (i + 1) * length]) for i in range(blocks)]


def spread_blocks(columns, length):
    return jnp.concatenate(
        [jnp.broadcast_to(column, (column.shape[0], length)) for column in columns], axis=1
    )


def plain_bins(spectrum_ref, rows, shard, blocks):
    half = spectrum_ref.shape[1] // 2
    bins = []
    for k in range(blocks):
        here = spectrum_ref[eight(k * shard + rows), :]
        bins.append((here[:, :half], here[:, half:]))
    return bins


def filter_bins(spectrum_ref, sign, rows, shard, blocks):
    plain = plain_bins(spectrum_ref, rows, shard, blocks)
    bins = [plain[0]]
    for k in range(1, blocks):
        (real, imag), (before_real, before_imag) = plain[k], plain[k - 1]
        bins.append((real - sign * before_imag, imag + sign * before_real))
    return bins


def store_blocks(target, values, rows, shard, blocks):
    length = values.shape[1] // blocks
    for j in range(blocks):
        target[sixteen(j * shard + rows), :] = values[:, j * length : (j + 1) * length]


def join(halves):
    return jnp.concatenate(halves, axis=0).astype(BF16)


def channel_cuts(shard, streams):
    size = shard // LOADS
    return [(s * shard + n * size, size) for n in range(LOADS) for s in range(streams)]


def channel_order(numbers, streams=3):
    order = []
    for n in range(LOADS):
        for number in numbers:
            each = streams if number == 1 else 1
            order += [(number, n * each + i) for i in range(each)]
    return tuple(order)


def run_groups(prepare, transform, combine, invert, finish, after):
    prepare(0)
    for i in range(LOADS + 1):
        if i < LOADS:
            transform(i)
        if i + 1 < LOADS:
            prepare(i + 1)
        if i:
            invert(i - 1)
        if i < LOADS:
            combine(i)
        if i:
            finish(i - 1)
            after(i - 1)


def conv_forward_kernel(blocks, carries, io, filter_ref, project_ref, columns_ref, keep_ref,
                        sign_ref, table_ref, seq_ref, carried_in, back_ref, token_gated, conv_ref,
                        carried, gated, factor_ref, *refs):
    signal_low, filter_low, signal_bins, filter_spectrum, out_low, convolved = (
        refs[2 * n : 2 * n + 2] for n in range(6)
    )
    send, recv, *sems = refs[12:]
    shard, slots = gated.shape
    length = slots // blocks
    scale = 1.0 / length
    size = shard // LOADS
    peers = chan_peers()
    me = peers[0]
    tokens = slots // 4
    parts = carried.shape[0]
    facts = Facts(seq_ref, blocks, length)
    greet(peers[1:])

    def gather(kind, part):
        return gather_copy(
            lambda owner, part: carried.at[part, span(owner, shard, 32), :],
            peers, sems, kind, part,
        )

    def forward(first, last):
        for part in range(parts * first // LOADS, parts * last // LOADS):
            gather(0, part).wait_recv()
            gather(2, part).start()

    io.ready(7)
    for part in range(parts):
        if carries == 1:
            carried[part, span(me, shard, 32), :] = carried_in[part]
        else:
            lanes = carried.shape[2]
            carried[part, span(me, shard, 32), :] = carried_in[:, part * lanes : (part + 1) * lanes]
        for kind in range(2):
            gather(kind, part).start()
    io.ready(2, 3, 4)

    def prepare(group):
        base, place = group * size, group % 2
        if group < 2:
            cuts = slice(0, 1) if group == 0 else slice(1, LOADS)
            io.ready(0, cuts=cuts)
            io.ready(1, cuts=slice(3 * cuts.start, 3 * cuts.stop))
        for n in range(size // 16):
            rows = base + n * 16
            signals = []
            for part in range(2):
                here = rows + 8 * part
                one, two = (
                    stream_rows(project_ref, columns_ref, keep_ref, here, shard, stream, blocks)
                    for stream in (1, 2)
                )
                signals.append(one * two)
                cond = columns_ref[eight(here), 9:10]
                _, _, factor = sequence_factor(block_sums(two * two, blocks), cond, facts, blocks)
                for j in range(blocks):
                    factor_ref[eight(here), j : j + 1] = factor[j]
            store_blocks(signal_low[place], join(signals), n * 16, size, blocks)
            kernel = filter_ref[sixteen(rows), :].astype(BF16)
            store_blocks(filter_low[place], kernel, n * 16, size, blocks)

    def transform(group):
        place = group % 2
        if group == 0:
            io.ready(5, 8)
        signal_bins[place][...] = matmul(signal_low[place][...], table_ref[...])
        filter_spectrum[place][...] = matmul(filter_low[place][...], table_ref[...])

    def combine(group):
        place = group % 2
        for n in range(size // 16):
            joined = [[] for _ in range(blocks)]
            for part in range(2):
                here = n * 16 + 8 * part
                window = filter_bins(filter_spectrum[place], sign_ref[0:1, :], here, size, blocks)
                signal = plain_bins(signal_bins[place], here, size, blocks)
                for i in range(blocks):
                    real = imag = None
                    for j in range(i, -1, -1):
                        fr, fi = window[i - j]
                        sr, si = signal[j]
                        more_real, more_imag = fr * sr - fi * si, fr * si + fi * sr
                        if j == i:
                            real, imag = more_real, more_imag
                        else:
                            factor = facts.same[i][j]
                            real, imag = real + more_real * factor, imag + more_imag * factor
                    joined[i].append(jnp.concatenate([real, imag], axis=1))
            for i in range(blocks):
                out_low[place][sixteen(i * size + n * 16), :] = join(joined[i])

    def invert(group):
        place = group % 2
        convolved[place][...] = matmul(out_low[place][...], back_ref[...]) * scale

    def finish(group):
        base, place = group * size, group % 2
        for n in range(size // 16):
            rows = base + n * 16
            results = []
            for part in range(2):
                here = rows + 8 * part
                zero = stream_rows(project_ref, columns_ref, keep_ref, here, shard, 0, blocks)
                pieces = []
                for j in range(blocks):
                    source = convolved[place][eight(j * size + n * 16 + 8 * part), :]
                    columns = slice(j * length, (j + 1) * length)
                    conv_ref[eight(here), columns] = source
                    pieces.append(zero[:, columns] * (source * factor_ref[eight(here), j : j + 1]))
                results.append(jnp.concatenate(pieces, axis=1))
            gated[sixteen(rows), :] = join(results)

    copies = []

    def after(group):
        base = group * size
        mine = pl.ds(pl.multiple_of(me * shard + base, 16), size)
        copies.extend(
            exchange(
                peers, lambda peer: gated.at[pl.ds(base, size), span(peer, tokens)],
                lambda: token_gated.at[mine], send.at[group], recv.at[group],
            )
        )
        token_gated[mine, :] = gated[base : base + size, span(me, tokens)]
        io.flush(1, group, pl.ds(base, size))
        forward(group, group + 1)

    run_groups(prepare, transform, combine, invert, finish, after)
    for part in range(parts):
        for kind in (1, 2):
            gather(kind, part).wait_recv()
        io.flush(2, part, part)
    for copy in copies:
        copy.wait()
    io.flush(0)
    for part in range(parts):
        for kind in range(3):
            gather(kind, part).wait_send()


def conv_forward(project, filter_rows, columns, keep, sign, table, seq_table, back, carried,
                 carries, blocks, collective):
    shard, slots = filter_rows[0].shape[1:]
    width = 4 * shard
    length = slots // blocks
    rows = blocks * (shard // LOADS)
    low = pltpu.VMEM((rows, length), BF16)
    bins = pltpu.VMEM((rows, 2 * length), F32)
    if carries == 1:
        out = ((carried.shape[0], width, width), BF16)
    else:
        out = ((8, width, slots // 8), BF16)
    return fused_call(
        lambda *refs: conv_forward_kernel(blocks, carries, *refs),
        [filter_rows, project, columns, keep, sign, table, seq_table, carried, back],
        [((width, slots // 4), BF16), ((shard, slots), F32), out],
        [
            pltpu.VMEM((shard, slots), BF16),
            pltpu.VMEM((shard, 128), F32),
        ]
        + [low] * 4
        + [bins] * 4
        + [pltpu.VMEM((rows, 2 * length), BF16)] * 2
        + [pltpu.VMEM((rows, length), F32)] * 2
        + [pltpu.SemaphoreType.DMA((LOADS, 3))] * 2
        + [pltpu.SemaphoreType.DMA((3, out[0][0]))] * 2,
        collective,
        "conv_forward",
        [1, LOADS, out[0][0]],
        6,
        (7, 2, 3, 4) + channel_order((1, 0)) + (5, 8),
        {0: channel_cuts(shard, 1), 1: channel_cuts(shard, 3)},
    )


def conv_backward_kernel(blocks, tracks, with_outputs, io, grad_ref, project_ref, conv_ref,
                         filter_ref, columns_ref, keep_ref, sign_ref, table_ref, seq_ref,
                         square_ref, *refs):
    refs = list(refs)
    back_ref = refs.pop(len(ring_operands(tracks)) + with_outputs)
    rings = len(tracks)
    inputs = len(ring_operands(tracks))
    ring_in, refs = refs[:inputs], refs[inputs:]
    if with_outputs:
        residual_ref = refs.pop(0)
    project_grad, filter_pack, square_sum, sums_ref = refs[:4]
    large, refs = refs[4 : 4 + rings], refs[4 + rings :]
    if with_outputs:
        outputs_ref = refs.pop(0)
        *refs, out_land, out_send, out_recv = refs
    sources = [io.source[10 + n] for n in range(inputs)]
    ring = Ring(tracks, ring_in, large, refs[-rings - 2 :], sources)
    refs = refs[: -rings - 2]
    mixed, energy_ref, square_land, square_send, square_recv, *pairs = refs
    signal_low, filter_low, grad_low, signal_bins, filter_spectrum, grad_bins = (
        pairs[2 * n : 2 * n + 2] for n in range(6)
    )
    signal_out, filter_out, signal_grad, filter_grad = (
        pairs[2 * n : 2 * n + 2] for n in range(6, 10)
    )
    peers = chan_peers()
    greet(peers[1:], ring.toward)
    ring.start()
    copies = exchange(
        peers, lambda peer: io.source[9].at[peer], lambda: square_land.at[peers[0]],
        square_send, square_recv,
    )
    if with_outputs:
        copies += to_channels(
            peers, io.source[10 + inputs], out_land, out_send, out_recv
        )
    io.ready(4, 5, 6)
    shard, slots = grad_ref.shape
    length = slots // blocks
    scale = 1.0 / length
    steps = shard // 16
    facts = Facts(seq_ref, blocks, length)

    size = shard // LOADS

    def prepare(group):
        base, place = group * size, group % 2
        if group < 2:
            cuts = slice(0, 1) if group == 0 else slice(1, LOADS)
            for number, each in ((0, 1), (1, 3), (2, 1), (3, 1)):
                io.ready(number, cuts=slice(each * cuts.start, each * cuts.stop))
        for n in range(size // 16):
            rows = base + n * 16
            signals, scaled = [], []
            grads = grad_ref[sixteen(rows), :].astype(F32)
            for part in range(2):
                here = rows + 8 * part
                zero, one, two = (
                    stream_rows(project_ref, columns_ref, keep_ref, here, shard, stream, blocks)
                    for stream in range(3)
                )
                mixed[0, eight(here), :] = one
                mixed[1, eight(here), :] = two
                signals.append(one * two)
                cond = columns_ref[eight(here), 9:10]
                power = block_sums(two * two, blocks)
                energy, logs, factor = sequence_factor(power, cond, facts, blocks)
                conv_grad = grads[8 * part : 8 * part + 8] * zero
                factor_grad = block_sums(conv_grad * conv_ref[eight(here), :], blocks)
                cond_grad = 0.0
                for j in range(blocks):
                    cond_grad = cond_grad + factor_grad[j] * logs[j]
                sums_ref[eight(here), 9:10] = cond_grad
                for i in range(blocks):
                    total = 0.0
                    for j in range(blocks):
                        total = total + factor_grad[j] * facts.same[i][j]
                    energy_ref[eight(here), i : i + 1] = (
                        total * cond / (1.0 + energy[i]) * (2.0 * facts.inverse)
                    )
                    energy_ref[eight(here), blocks + i : blocks + i + 1] = factor[i]
                scaled.append(
                    conv_grad * spread_blocks([value * scale for value in factor], length)
                )
            store_blocks(signal_low[place], join(signals), n * 16, size, blocks)
            store_blocks(grad_low[place], join(scaled), n * 16, size, blocks)
            kernel = filter_ref[sixteen(rows), :].astype(BF16)
            store_blocks(filter_low[place], kernel, n * 16, size, blocks)

    def transform(group):
        place = group % 2
        if group == 0:
            io.ready(7, 10 + inputs + with_outputs)
        grad_bins[place][...] = matmul(grad_low[place][...], table_ref[...])
        signal_bins[place][...] = matmul(signal_low[place][...], table_ref[...])
        filter_spectrum[place][...] = matmul(filter_low[place][...], table_ref[...])

    def combine(group):
        place = group % 2
        sign = sign_ref[0:1, :]
        for n in range(size // 16):
            joined = [[] for _ in range(blocks)]
            windows = [[] for _ in range(blocks)]
            for part in range(2):
                here = n * 16 + 8 * part
                window = filter_bins(filter_spectrum[place], sign, here, size, blocks)
                signal = plain_bins(signal_bins[place], here, size, blocks)
                grads = plain_bins(grad_bins[place], here, size, blocks)
                for j in range(blocks):
                    for i in range(j, blocks):
                        fr, fi = window[i - j]
                        gr, gi = grads[i]
                        more_real, more_imag = fr * gr + fi * gi, fr * gi - fi * gr
                        if i == j:
                            real, imag = more_real, more_imag
                        else:
                            factor = facts.same[i][j]
                            real, imag = real + more_real * factor, imag + more_imag * factor
                    joined[j].append(jnp.concatenate([real, imag], axis=1))
                after = None
                for k in reversed(range(blocks)):
                    real = imag = None
                    for j in range(blocks - k):
                        sr, si = signal[j]
                        gr, gi = grads[j + k]
                        more_real, more_imag = sr * gr + si * gi, sr * gi - si * gr
                        if k:
                            factor = facts.same[j + k][j]
                            more_real, more_imag = more_real * factor, more_imag * factor
                        real = more_real if real is None else real + more_real
                        imag = more_imag if imag is None else imag + more_imag
                    if after is None:
                        whole = (real, imag)
                    else:
                        whole = (real + sign * after[1], imag - sign * after[0])
                    windows[k].append(jnp.concatenate(whole, axis=1))
                    after = (real, imag)
            for j in range(blocks):
                signal_out[place][sixteen(j * size + n * 16), :] = join(joined[j])
                filter_out[place][sixteen(j * size + n * 16), :] = join(windows[j])

    count, pack_rows, lanes = filter_pack.shape
    each = shard // count
    stack = slots // lanes
    if pack_rows > stack * each:
        filter_pack[...] = jnp.zeros_like(filter_pack)

    def invert(group):
        place = group % 2
        signal_grad[place][...] = matmul(signal_out[place][...], back_ref[...])
        filter_grad[place][...] = matmul(filter_out[place][...], back_ref[...])

    def finish(group):
        base, place = group * size, group % 2
        for chunk in range(size // each):
            lags = [
                filter_grad[place][j * size + chunk * each : j * size + (chunk + 1) * each, :]
                for j in range(blocks)
            ]
            layers = [
                jnp.concatenate(lags[n * blocks // stack : (n + 1) * blocks // stack], axis=1)
                for n in range(stack)
            ]
            value = layers[0] if stack == 1 else jnp.concatenate(layers, axis=0)
            filter_pack[base // each + chunk, : stack * each] = value.astype(BF16)
        for n in range(size // 16):
            rows = base + n * 16
            totals = [[] for _ in range(3)]
            outer = grad_ref[sixteen(rows), :].astype(F32)
            for part in range(2):
                here = rows + 8 * part
                local = eight(here)
                factor = [energy_ref[local, blocks + i : blocks + i + 1] for i in range(blocks)]
                energy = [energy_ref[local, i : i + 1] for i in range(blocks)]
                signal = jnp.concatenate(
                    [
                        signal_grad[place][eight(j * size + n * 16 + 8 * part), :]
                        for j in range(blocks)
                    ],
                    axis=1,
                )
                for stream in range(3):
                    if stream == 0:
                        value = outer[8 * part : 8 * part + 8] * (
                            conv_ref[local, :] * spread_blocks(factor, length)
                        )
                    elif stream == 1:
                        value = signal * mixed[1, local, :]
                    else:
                        value = signal * mixed[0, local, :] + (
                            spread_blocks(energy, length) * mixed[1, local, :]
                        )
                    plain = project_ref[eight(stream * shard + here), :]
                    total = value * columns_ref[local, stream : stream + 1]
                    sums_ref[local, stream : stream + 1] = lane_sums(value * plain)
                    for offset in (1, 2):
                        column = 3 * offset + stream
                        moved = pltpu.roll(
                            mask_heads(value, keep_ref[offset - 1 : offset, :], blocks),
                            slots - offset, 1,
                        )
                        sums_ref[local, column : column + 1] = lane_sums(moved * plain)
                        total = total + moved * columns_ref[local, column : column + 1]
                    totals[stream].append(total)
            for stream in range(3):
                project_grad[sixteen(stream * shard + rows), :] = join(totals[stream])

    def after(group):
        if group == 0:
            io.ready(*range(10, 10 + rings))
        if group < 3:
            ring.advance(group, 3)

    run_groups(prepare, transform, combine, invert, finish, after)
    io.flush(1)
    for stream in range(3):
        io.flush(0, stream, pl.ds(stream * shard, shard))
    for copy in copies:
        copy.wait()
    io.ready(9)
    total = square_ref[peers[0]].astype(F32)
    for peer in peers[1:]:
        total = total + square_land[peer].astype(F32)
    square_sum[...] = total
    io.flush(2)
    if with_outputs:
        io.ready(10 + inputs)
        tokens = residual_ref.shape[1]
        out_land[:, span(peers[0], tokens)] = residual_ref[span(peers[0], shard, 32), :]
        outputs_ref[...] = out_land[...].astype(F32)
        io.flush(4 + rings)
    io.flush(3)
    ring.finish()
    for n in range(rings):
        io.flush(4 + n)


def filter_layout(shard, slots, count):
    each = shard // count
    stack = 2 if each % 8 == 0 else 1
    return count, ring_rows(stack * each), slots // stack


def conv_backward(grad, project, conv, filter_rows, columns, keep, sign, table, seq_table, back, square,
                  tracks, residual, blocks, collective):
    shard, slots = filter_rows[0].shape[1:]
    length = slots // blocks
    rows = blocks * (shard // LOADS)
    low = pltpu.VMEM((rows, length), BF16)
    bins = pltpu.VMEM((rows, 2 * length), F32)
    out = pltpu.VMEM((rows, 2 * length), BF16)
    back_out = pltpu.VMEM((rows, length), F32)
    outs, extra = [], []
    if residual:
        outs = [((shard, slots), F32)]
        extra = [pltpu.VMEM((shard, slots), BF16)] + [pltpu.SemaphoreType.DMA((3,))] * 2
    return fused_call(
        lambda *refs: conv_backward_kernel(blocks, tracks, bool(residual), *refs),
        [grad, project, conv, filter_rows, columns, keep, sign, table, seq_table, square]
        + ring_operands(tracks)
        + list(residual)
        + [back],
        [
            ((3 * shard, slots), BF16),
            (filter_layout(shard, slots, tracks[0].count), BF16),
            ((shard, 4 * shard), F32),
            ((shard, 128), F32),
        ]
        + [one.out() for one in tracks]
        + outs,
        [pltpu.VMEM((2, shard, slots), F32), pltpu.VMEM((shard, 128), F32)]
        + [pltpu.VMEM(square.shape, BF16)]
        + [pltpu.SemaphoreType.DMA((3,))] * 2
        + [low] * 6
        + [bins] * 6
        + [out] * 4
        + [back_out] * 4
        + ring_scratch(tracks)
        + extra,
        collective,
        "conv_backward",
        [3, 1, 1, 1] + [1] * (len(tracks) + len(outs)),
        8,
        (4, 5, 6) + channel_order((0, 1, 2, 3)) + (7,),
        {0: channel_cuts(shard, 1), 1: channel_cuts(shard, 3), 2: channel_cuts(shard, 1)}
        | {3: channel_cuts(shard, 1)},
        tuple(range(10 + len(tracks), 10 + len(ring_operands(tracks)))),
    )


def last_kernel(layers, tracks, io, state_ref, *refs):
    refs = list(refs)
    gain_sums, refs = refs[: 2 * layers], refs[2 * layers :]
    row_sums, refs = refs[:layers], refs[layers:]
    rings, inputs = len(tracks), len(ring_operands(tracks))
    ring_in, refs = refs[:inputs], refs[inputs:]
    input_grad, small_out = refs[:2]
    large, refs = refs[2 : 2 + rings], refs[2 + rings :]
    state_low, landing, sums, turn, gains, gains_land, small_own, small_land, *refs = refs
    chan_send, chan_recv, small_send, small_recv, state_send, state_recv, *refs = refs
    peers = chan_peers()
    me = peers[0]
    dp = lax.axis_index("dp")
    first = 1 + 3 * layers
    ring = Ring(tracks, ring_in, large, refs, [io.source[first + n] for n in range(inputs)])
    count = ring.count
    shard = landing.shape[0]
    greet(peers[1:], [(dp + offset) % count for offset in range(1, count)])
    ring.start()
    io.ready(*range(0, first))
    for layer in range(layers):
        sums[:, 4 * layer : 4 * layer + 2] = gain_sums[2 * layer][:, 0:2]
        sums[:, 4 * layer + 2 : 4 * layer + 4] = gain_sums[2 * layer + 1][:, 0:2]
    turn[...] = jnp.zeros_like(turn)
    for owner in range(4):
        turn[:shard, : 4 * layers] = sums[owner * shard : (owner + 1) * shard, : 4 * layers]
        gains[owner] = turn[...].T[: 4 * layers]
    copies = exchange(
        peers, lambda peer: gains.at[peer], lambda: gains_land.at[me], chan_send, chan_recv
    )
    state_low[...] = state_ref[...].astype(BF16)
    state_copies = to_channels(peers, state_low, landing, state_send, state_recv)
    landing[:, span(me, state_low.shape[1])] = state_low[span(me, shard, 32), :]
    io.ready(*range(first, first + rings))
    ring.advance(0, 6)
    for layer in range(layers):
        turn[:shard, 10 * layer : 10 * layer + 10] = row_sums[layer][:, 0:10]
    small_own[4 * layers :, :] = turn[...].T[: small_own.shape[0] - 4 * layers]
    for copy in copies:
        copy.wait()
    total = gains[me]
    for peer in peers[1:]:
        total = total + gains_land[peer]
    small_own[: 4 * layers, :] = total
    small_copies = []
    for offset in range(1, count):
        copy = pltpu.make_async_remote_copy(
            small_own,
            small_land.at[offset - 1],
            small_send.at[offset - 1],
            small_recv.at[offset - 1],
            device_id={"dp": (dp + offset) % count},
        )
        copy.start()
        small_copies.append(copy)
    for point in range(1, 4):
        ring.advance(point, 6)
    small = small_own[...]
    for copy in small_copies:
        copy.wait()
    for n in range(count - 1):
        small = small + small_land[n]
    small_out[...] = small
    io.flush(1)
    ring.advance(4, 6)
    for copy in state_copies:
        copy.wait()
    input_grad[...] = landing[...].astype(F32)
    io.flush(0)
    ring.advance(5, 6)
    ring.finish()
    for n in range(rings):
        io.flush(2 + n)


def last_sums(state, gain_sums, row_sums, tracks, collective):
    width, tokens = state.shape
    shard = width // 4
    layers = len(row_sums)
    count = tracks[0].count
    small = (-(-14 * layers // 8) * 8, 256)
    return fused_call(
        lambda *refs: last_kernel(layers, tracks, *refs),
        [state] + gain_sums + row_sums + ring_operands(tracks),
        [((shard, 4 * tokens), F32), (small, F32)] + [one.out() for one in tracks],
        [
            pltpu.VMEM((width, tokens), BF16),
            pltpu.VMEM((shard, 4 * tokens), BF16),
            pltpu.VMEM((width, 128), F32),
            pltpu.VMEM((256, 128), F32),
            pltpu.VMEM((4, 4 * layers, 256), F32),
            pltpu.VMEM((4, 4 * layers, 256), F32),
            pltpu.VMEM(small, F32),
            pltpu.VMEM((count - 1,) + small, F32),
            pltpu.SemaphoreType.DMA((3,)),
            pltpu.SemaphoreType.DMA((3,)),
            pltpu.SemaphoreType.DMA((count - 1,)),
            pltpu.SemaphoreType.DMA((count - 1,)),
            pltpu.SemaphoreType.DMA((3,)),
            pltpu.SemaphoreType.DMA((3,)),
        ]
        + ring_scratch(tracks),
        collective,
        "last_sums",
        [1] * (2 + len(tracks)),
        order=tuple(range(1, 1 + 3 * layers)) + (0,),
        manual=tuple(
            range(1 + 3 * layers + len(tracks), 1 + 3 * layers + len(ring_operands(tracks)))
        ),
    )


def collect_kernel(layers, *refs):
    refs = list(refs)
    outputs_in, input_in, small = refs[:3]
    refs = refs[3:]
    feeds, refs = refs[:layers], refs[layers:]
    filters, refs = refs[:layers], refs[layers:]
    packs, refs = refs[:layers], refs[layers:]
    (outputs, input_grad, mix_gain, mix_bias, in_grad, short, filter_grad, cond, out_grad, glu_gain,
     glu_bias, up_grad, down_grad, held, sems) = refs
    pairs = ((outputs_in, outputs), (input_in, input_grad))
    loads = [
        pltpu.make_async_copy(source, held.at[n], sems.at[n]) for n, (source, _) in enumerate(pairs)
    ]
    copies = [
        pltpu.make_async_copy(held.at[n], target, sems.at[2 + n])
        for n, (_, target) in enumerate(pairs)
    ]
    for copy in loads:
        copy.start()
    each = in_grad.shape[2]
    shard = cond.shape[1]
    lanes = filters[0].shape[1]
    for layer in range(layers):
        for kind, out in enumerate((mix_gain, mix_bias, glu_gain, glu_bias)):
            row = 4 * layer + kind
            out[layer : layer + 1, :] = small[row : row + 1, :shard]
        row = 4 * layers + 10 * layer
        for n in range(9):
            short[n // 3, n % 3, layer : layer + 1, :] = small[row + n : row + n + 1, :shard]
        cond[layer : layer + 1, :] = small[row + 9 : row + 10, :shard]
        for stream in range(3):
            in_grad[layer, stream] = packs[layer][stream * each : (stream + 1) * each]
        out_grad[layer] = packs[layer][3 * each : 4 * each]
        for n in range(filter_grad.shape[2] // lanes):
            filter_grad[layer, :, n * lanes : (n + 1) * lanes] = filters[layer][
                n * each : (n + 1) * each
            ]
        rows = down_grad.shape[1]
        down_grad[layer] = feeds[layer][:rows]
        for kind in range(2):
            up_grad[layer, :, kind, :] = feeds[layer][(kind + 1) * rows : (kind + 2) * rows]
        loads[layer].wait()
        copies[layer].start()
    for copy in copies:
        copy.wait()


def collect(outputs, input_grad, small, feeds, filters, packs, each):
    layers = len(feeds)
    shard, slots = outputs.shape
    width = 4 * shard
    rows, hidden = feeds[0].shape[0] // 3, feeds[0].shape[1]
    anywhere = pl.BlockSpec(memory_space=pl.ANY)
    local = pl.BlockSpec(memory_space=pltpu.VMEM)
    operands = [outputs, input_grad, small, *feeds, *filters, *packs]
    small_shape = (layers, shard)
    shapes = [
        (shard, slots), (shard, slots), small_shape, small_shape, (layers, 3, each, width),
        (3, 3, layers, shard), (layers, each, slots), small_shape, (layers, each, width),
        small_shape, small_shape, (layers, rows, 2, hidden), (layers, rows, hidden),
    ]
    return pl.pallas_call(
        lambda *refs: collect_kernel(layers, *refs),
        out_shape=tuple(jax.ShapeDtypeStruct(shape, F32) for shape in shapes),
        in_specs=[anywhere] * 2 + [local] * (len(operands) - 2),
        out_specs=tuple([anywhere] * 2 + [local] * (len(shapes) - 2)),
        scratch_shapes=[pltpu.VMEM((2, shard, slots), F32), pltpu.SemaphoreType.DMA((4,))],
        compiler_params=pltpu.CompilerParams(vmem_limit_bytes=VMEM_LIMIT),
        name="collect",
    )(*operands)


def body(
    inputs,
    seq_table,
    mix_gain,
    mix_bias,
    in_proj,
    short_conv,
    long_filter,
    cond_weight,
    out_proj,
    glu_gain,
    glu_bias,
    glu_in,
    glu_out,
    cotangent,
):
    shard, slots = inputs.shape
    layers, width = in_proj.shape[0], in_proj.shape[3]
    hidden = glu_out.shape[2]
    blocks = 4
    count = lax.axis_size("dp")
    each = shard // count
    table = jnp.asarray(dft_table(slots // blocks), BF16)
    sign = jnp.asarray(np.tile(1.0 - 2.0 * (np.arange(slots // blocks) % 2), (8, 1)), F32)
    in_rows = in_proj.transpose(0, 2, 1, 3).reshape(layers, 3 * shard, width)
    taps = short_conv.transpose(1, 2, 0, 3)
    residual, gains, normed, project, up_columns, columns, keep = first_project(
        inputs, (mix_gain, mix_bias, glu_gain, glu_bias), (in_rows, 0), taps, cond_weight,
        (glu_in, 0), seq_table, 1,
    )
    constants = (keep, sign, table, seq_table, jnp.asarray(dft_table(slots // blocks).T, BF16))
    kept, state = [], None
    for l in range(layers):
        token_gated, conv, carried = conv_forward(
            project, (long_filter, l), (columns, l), *constants, cotangent if l else out_proj,
            2 if l else 1, blocks, 10 + l,
        )
        if l:
            state = carried
        else:
            full_out = carried
        middle, normed_glu, after, *rest = feed_forward(
            token_gated, residual, gains, (full_out, l), up_columns, (glu_out, l),
            ((in_rows, l + 1), (glu_in, l + 1)) if l + 1 < layers else (), 4 * l + 2, 20 + l,
        )
        saved, follow = [up_columns] + rest[:3], rest[3:]
        kept.append((residual, normed, project, conv, token_gated, middle, normed_glu, saved))
        residual = after
        if follow:
            normed, project, up_columns = follow
    feeds, filters, packs, gain_sums, row_sums = ([None] * layers for _ in range(5))
    waiting = []
    for l in reversed(range(layers)):
        before, normed, project, conv, token_gated, middle, normed_glu, saved = kept[l]
        top = l == layers - 1
        state, gated_grad, feed_grads, out_grad, glu_sums, *large = feed_back(
            state, middle, gains, normed_glu, saved[0], (glu_out, l), (full_out, l), token_gated,
            saved[1:], waiting, 4 * l + 2, count, 30 + l,
        )
        if waiting:
            filters[l + 1], packs[l + 1], feeds[l + 1] = large
        one, two = (3 * count // 8, 5 * count // 8) if l else (count // 2, count - 1)
        project_low, filter_pack, square, row_sums[l], held, *rest = conv_backward(
            gated_grad, project, conv, (long_filter, l), (columns, l), *constants,
            out_grad.reshape(4, shard, width), [Track(feed_grads, 0, one)],
            (residual,) if top else (), blocks, 40 + l,
        )
        if top:
            outputs = rest[0]
        tracks = [Track(feed_grads, one, two, held), Track(filter_pack, 0, count // 4)]
        state, in_pack, mix_sums, feed_held, held, in_held = project_back(
            project_low, state, before, gains, normed, (in_rows, l), square,
            tracks, 4 * l, 50 + l,
        )
        waiting = [
            Track(filter_pack, count // 4, count - 1, held),
            Track(in_pack, count // 4, count - 1, in_held),
        ]
        if l:
            waiting.append(Track(feed_grads, two, count - 1, feed_held))
        else:
            feeds[0] = feed_held
        gain_sums[l] = [mix_sums, glu_sums]
    input_grad, small, filters[0], packs[0] = last_sums(
        state, [one for pair in gain_sums for one in pair], row_sums, waiting, 60
    )
    results = list(collect(outputs, input_grad, small, feeds, filters, packs, each))
    results[4] = results[4].transpose(0, 2, 1, 3)
    results[5] = results[5].transpose(2, 0, 1, 3)
    return tuple(results)


def solution(mesh):
    in_specs = (
        P("chan", "dp"),
        P("dp", None),
        P(None, "chan"),
        P(None, "chan"),
        P(None, "chan", None, None),
        P(None, None, None, "chan"),
        P(None, "chan", None),
        P(None, "chan"),
        P(None, "chan", None),
        P(None, "chan"),
        P(None, "chan"),
        P(None, None, None, "chan"),
        P(None, None, "chan"),
        P("chan", "dp"),
    )
    out_specs = (
        P("chan", "dp"),
        P("chan", "dp"),
        P(None, "chan"),
        P(None, "chan"),
        P(None, ("chan", "dp"), None, None),
        P(None, None, None, "chan"),
        P(None, ("chan", "dp"), None),
        P(None, "chan"),
        P(None, ("chan", "dp"), None),
        P(None, "chan"),
        P(None, "chan"),
        P(None, "dp", None, "chan"),
        P(None, "dp", "chan"),
    )
    return jax.shard_map(body, mesh=mesh, in_specs=in_specs, out_specs=out_specs, check_vma=False)
```

```python
import math

import jax
import jax.numpy as jnp
import numpy as np
from jax import lax
from jax.experimental import pallas as pl
from jax.experimental.pallas import tpu as pltpu
from jax.sharding import PartitionSpec as P

EPSILON = 1e-05
F32 = jnp.float32
BF16 = jnp.bfloat16
VMEM_LIMIT = 63 * 2**20
LOADS = 4


def dft_table(block_len):
    period = 2 * block_len
    position = np.arange(block_len)[:, None]
    phase = ((2 * np.arange(block_len)[None, :] + 1) * position) % (2 * period)
    phase = phase * (math.pi / period)
    return np.concatenate([np.cos(phase), -np.sin(phase)], axis=1)


class Facts:
    def __init__(self, table_ref, blocks, block_len):
        length, count = table_ref[0, 0], table_ref[0, 1]
        used = length * count
        pair = jnp.where(length >= 2 * block_len, 1.0, 0.0)
        four = jnp.where(length >= 4 * block_len, 1.0, 0.0)
        active = [jnp.where(i * block_len < used, 1.0, 0.0) for i in range(blocks)]
        self.same = [[None] * blocks for _ in range(blocks)]
        for i in range(blocks):
            for j in range(blocks):
                if i == j:
                    self.same[i][j] = active[i]
                else:
                    joined = pair if i // 2 == j // 2 else four
                    self.same[i][j] = active[i] * active[j] * joined
        shortest = 1.0 / block_len
        self.inverse = shortest * (1.0 - 0.5 * pair - 0.25 * four)


class Io:
    def __init__(self, source, loads, stores):
        self.source, self.loads, self.stores, self.pending = source, loads, stores, []

    def ready(self, *numbers, cuts=None):
        for number in numbers:
            for copy in self.loads[number] if cuts is None else self.loads[number][cuts]:
                copy.wait()

    def flush(self, number, part=0, at=None):
        source, target, sems = self.stores[number]
        if at is not None:
            source, target = source.at[at], target.at[at]
        copy = pltpu.make_async_copy(source, target, sems.at[part])
        copy.start()
        self.pending.append(copy)

    def finish(self):
        for copy in self.pending:
            copy.wait()


def fused_call(kernel, operands, outs, scratch, collective, name, parts, scalars=-1, order=(),
               cuts=None, manual=()):
    arrays, layers = [], []
    for operand in operands:
        array, layer = operand if isinstance(operand, tuple) else (operand, None)
        arrays.append(array)
        layers.append(layer)
    cuts = cuts or {}
    inputs, results = len(arrays), len(outs)
    buffers, sems = [], []
    for number, (array, layer) in enumerate(zip(arrays, layers)):
        if number != scalars:
            buffers.append(pltpu.VMEM(array.shape if layer is None else array.shape[1:], array.dtype))
            sems.append(pltpu.SemaphoreType.DMA((len(cuts.get(number, (0,))),)))
    for (shape, dtype), count in zip(outs, parts):
        buffers.append(pltpu.VMEM(shape, dtype))
        sems.append(pltpu.SemaphoreType.DMA((count,)))

    def body(*refs):
        extra = list(refs[inputs + results + len(scratch) :])
        places, marks = extra[: len(buffers)], extra[len(buffers) :]
        sources, loads, stores, views, n = {}, {}, {}, [], 0
        for number in range(inputs):
            if number == scalars:
                views.append(refs[number])
                continue
            source = refs[number]
            if layers[number] is not None:
                source = source.at[layers[number]]
            sources[number] = source
            views.append(places[n])
            if number not in manual:
                pairs = [(source, places[n])]
                if number in cuts:
                    rows = [pl.ds(*one) for one in cuts[number]]
                    pairs = [(source.at[one], places[n].at[one]) for one in rows]
                loads[number] = [
                    pltpu.make_async_copy(*pair, marks[n].at[i]) for i, pair in enumerate(pairs)
                ]
            n += 1
        for number in range(results):
            stores[number] = (places[n], refs[inputs + number], marks[n])
            views.append(places[n])
            n += 1
        started = set()
        for one in list(order) + list(loads):
            number, chosen = one if isinstance(one, tuple) else (one, None)
            for i, copy in enumerate(loads[number]):
                if (chosen is None or i == chosen) and (number, i) not in started:
                    started.add((number, i))
                    copy.start()
        io = Io(sources, loads, stores)
        kernel(io, *views, *refs[inputs + results : inputs + results + len(scratch)])
        io.finish()

    anywhere = pl.BlockSpec(memory_space=pl.ANY)
    scalar_spec = pl.BlockSpec(memory_space=pltpu.SMEM)
    params = {}
    if collective is not None:
        params = dict(collective_id=collective, has_side_effects=True)
    return pl.pallas_call(
        body,
        out_shape=tuple(jax.ShapeDtypeStruct(*out) for out in outs),
        in_specs=[scalar_spec if n == scalars else anywhere for n in range(inputs)],
        out_specs=tuple([anywhere] * results),
        scratch_shapes=list(scratch) + buffers + sems,
        compiler_params=pltpu.CompilerParams(vmem_limit_bytes=VMEM_LIMIT, **params),
        name=name,
    )(*arrays)


def ring_position(index, count):
    odd = index % 2
    return (1 - odd) * (index // 2) + odd * (count - 1 - index // 2)


def ring_member(position, count):
    late = position // (count // 2)
    return (1 - late) * 2 * position + late * (2 * (count - 1 - position) + 1)


def chan_peers():
    me = lax.axis_index("chan")
    mate = me + 1 - 2 * (me % 2)
    across = (me + 2) % 4
    return me, mate, across, (mate + 2) % 4


def greet(peers, members=()):
    barrier = pltpu.get_barrier_semaphore()
    for peer in peers:
        pl.semaphore_signal(barrier, inc=1, device_id={"chan": peer})
    for member in members:
        pl.semaphore_signal(barrier, inc=1, device_id={"dp": member})
    pl.semaphore_wait(barrier, len(peers) + len(members))


def send_to(peer, source, target, send, recv):
    return pltpu.make_async_remote_copy(source, target, send, recv, device_id={"chan": peer})


def span(index, size, unit=None):
    if isinstance(index, int):
        return pl.ds(index * size, size)
    return pl.ds(pl.multiple_of(index * size, unit or size), size)


def gather_copy(place, peers, sems, kind, part):
    me, mate, across, _ = peers
    block = place(across if kind == 2 else me, part)
    send, recv = sems
    return send_to(
        across if kind == 0 else mate, block, block, send.at[kind, part], recv.at[kind, part]
    )


def norm_columns(values):
    mean = jnp.mean(values, axis=0, keepdims=True)
    center = values - mean
    inverse = lax.rsqrt(jnp.mean(center * center, axis=0, keepdims=True) + EPSILON)
    return center * inverse, inverse


def norm_pullback(grad, values, gain):
    normal, inverse = norm_columns(values)
    product = grad * normal
    scaled = grad * gain
    first = jnp.mean(scaled, axis=0, keepdims=True)
    second = jnp.mean(product * gain, axis=0, keepdims=True)
    return inverse * (scaled - first - normal * second), product


def lane_sums(values):
    return jnp.sum(values, axis=1, keepdims=True)


def matmul(left, right):
    return jnp.dot(left, right, preferred_element_type=F32)


def matmul_nt(left, right):
    return lax.dot_general(
        left, right, (((1,), (1,)), ((), ())), preferred_element_type=F32
    )


def transpose_into(target, source, tile):
    for n in range(source.shape[0] // tile):
        target[:, n * tile : (n + 1) * tile] = source[n * tile : (n + 1) * tile].T


def transpose_columns(target, source, tile):
    for n in range(source.shape[1] // tile):
        target[n * tile : (n + 1) * tile, :] = source[:, n * tile : (n + 1) * tile].T


def exchange(peers, source, target, send, recv):
    copies = []
    for n, peer in enumerate((peers[2], peers[3], peers[1])):
        copy = send_to(peer, source(peer), target(), send.at[n], recv.at[n])
        copy.start()
        copies.append(copy)
    return copies


def to_channels(peers, low, landing, send, recv):
    shard, tokens = landing.shape[0], low.shape[1]
    me = peers[0]
    mine = span(me, tokens)
    copies = exchange(
        peers, lambda peer: low.at[span(peer, shard, 32), :], lambda: landing.at[:, mine], send, recv
    )
    return copies


class Track:
    def __init__(self, own, first, last, carry=None):
        self.own, self.first, self.last, self.carry = own, first, last, carry
        self.count, self.rows, self.lanes = own.shape

    def out(self):
        if self.last == self.count - 1:
            return ((self.rows, self.lanes), F32)
        return ((2, self.rows, self.lanes // 2), BF16)


def ring_operands(tracks):
    return [one.own for one in tracks] + [one.carry for one in tracks if one.first]


def ring_scratch(tracks):
    slots = [
        pltpu.VMEM((one.last - one.first, 2, one.rows, one.lanes // 2), BF16) for one in tracks
    ]
    if not tracks:
        return []
    longest = max(one.last - one.first for one in tracks)
    return slots + [pltpu.SemaphoreType.DMA((longest, len(tracks), 2))] * 2


class Ring:
    def __init__(self, tracks, operands, outs, scratch, sources):
        self.tracks, self.outs = tracks, outs
        self.count = tracks[0].count
        self.owns = operands[: len(tracks)]
        self.sources = sources[: len(tracks)]
        carries = list(sources[len(tracks) :])
        self.carries = [carries.pop(0) if one.first else None for one in tracks]
        *self.slots, self.send, self.recv = scratch
        self.here = lax.axis_index("dp")
        self.place = ring_position(self.here, self.count)
        after = ring_member((self.place + 1) % self.count, self.count)
        before = ring_member((self.place + self.count - 1) % self.count, self.count)
        self.toward = (after, before)
        self.rounds = max(one.last - one.first for one in tracks) - 1

    def copy(self, track, direction, turn, source):
        return pltpu.make_async_remote_copy(
            source,
            self.slots[track].at[turn, direction],
            self.send.at[turn, track, direction],
            self.recv.at[turn, track, direction],
            device_id={"dp": self.toward[direction]},
        )

    def owner(self, direction, step):
        move = step + 1
        if direction == 0:
            move = self.count - move
        return ring_member((self.place + move) % self.count, self.count)

    def own(self, track, direction, owner, owns=None):
        own = (owns or self.owns)[track]
        half = own.shape[2] // 2
        return own.at[owner, :, pl.ds(direction * half, half)]

    def held(self, track, direction, turn):
        return self.slots[track].at[turn, direction]

    def start(self):
        for track, carry in enumerate(self.carries):
            for direction in range(2):
                if carry is None:
                    source = self.own(track, direction, self.owner(direction, 0), self.sources)
                else:
                    source = carry.at[direction]
                self.copy(track, direction, 0, source).start()

    def round(self, turn, extra):
        for track, info in enumerate(self.tracks):
            def one(track=track, info=info):
                for direction in range(2):
                    held = self.held(track, direction, turn - 1)
                    self.copy(track, direction, turn - 1, held).wait_recv()
                    own = self.own(track, direction, self.owner(direction, info.first + turn))
                    held[...] = (held[...].astype(F32) + own[...].astype(F32)).astype(BF16)
                    self.copy(track, direction, turn, held).start()

            if info.last - info.first - 1 == self.rounds:
                one()
            else:
                pl.when(turn < info.last - info.first)(one)
        return extra

    def advance(self, point, points):
        first, last = self.rounds * point // points, self.rounds * (point + 1) // points
        if isinstance(point, int) and last == first:
            return
        if isinstance(point, int) and last == first + 1:
            self.round(last, 0)
            return
        lax.fori_loop(1 + first, 1 + last, self.round, 0)

    def loop(self, body, steps, point, pieces, points):
        for n in range(pieces):
            lax.fori_loop(steps * n // pieces, steps * (n + 1) // pieces, body, 0)
            self.advance(point + n, points)

    def finish(self):
        for track, (info, out) in enumerate(zip(self.tracks, self.outs)):
            turns = info.last - info.first
            half = info.lanes // 2
            whole = info.last == self.count - 1
            for direction in range(2):
                held = self.held(track, direction, turns - 1)
                self.copy(track, direction, turns - 1, held).wait_recv()
                owner = self.here if whole else self.owner(direction, info.last)
                own = self.own(track, direction, owner)
                total = held[...].astype(F32) + own[...].astype(F32)
                if whole:
                    out[:, pl.ds(direction * half, half)] = total
                else:
                    out[direction] = total.astype(BF16)

        def settle(turn, extra):
            for track, info in enumerate(self.tracks):
                def one(track=track):
                    for direction in range(2):
                        held = self.held(track, direction, turn)
                        self.copy(track, direction, turn, held).wait_send()

                if info.last - info.first == self.rounds + 1:
                    one()
                else:
                    pl.when(turn < info.last - info.first)(one)
            return extra

        lax.fori_loop(0, self.rounds + 1, settle, 0)


def ring_rows(rows):
    return -(-rows // 16) * 16


def split_rows(target, source, unit):
    _, kinds, lanes = source.shape

    def one(n, carry):
        here = span(n, unit)
        for kind in range(kinds):
            target[here, kind * lanes : (kind + 1) * lanes] = source[here, kind, :]
        return carry

    return one


def first_project_kernel(
    io, inputs_ref, mix_gain, mix_bias, glu_gain, glu_bias, weight_ref, short_in, cond_in, up_in,
    seq_ref, x_ref, gains_ref, full, project_ref, up_ref, columns_ref, keep_ref,
    raw, gains_low, gains_land, turn, send, recv, gains_send, gains_recv,
):
    peers = chan_peers()
    me = peers[0]
    shard, slots = inputs_ref.shape
    parts, width, half = raw.shape
    layers = mix_gain.shape[0]
    greet(peers[1:])
    io.ready(0, 1, 2, 3, 4)

    def gather(kind, part):
        return gather_copy(
            lambda owner, part: raw.at[part, span(owner, shard, 32), :],
            peers, (send, recv), kind, part,
        )

    for layer in range(layers):
        for kind, one in enumerate((mix_gain, mix_bias, glu_gain, glu_bias)):
            row = 4 * layer + kind
            gains_low[row : row + 1, :] = one[layer : layer + 1, :]
    gains_land[me] = gains_low[...]
    copies = exchange(
        peers, lambda peer: gains_low, lambda: gains_land.at[me], gains_send, gains_recv
    )
    for part in range(parts):
        raw[part, span(me, shard, 32), :] = inputs_ref[:, part * half : (part + 1) * half]
        for kind in range(2):
            gather(kind, part).start()
    io.ready(6, 7)
    for layer in range(layers):
        turn[...] = jnp.zeros_like(turn)
        for row in range(9):
            turn[row : row + 1, :shard] = short_in[row // 3, row % 3, layer : layer + 1, :]
        turn[9:10, :shard] = cond_in[layer : layer + 1, :]
        columns_ref[layer] = turn[...].T[:shard]
    slot = lax.broadcasted_iota(jnp.int32, keep_ref.shape, 1)
    row = lax.broadcasted_iota(jnp.int32, keep_ref.shape, 0)
    within = slot & (seq_ref[0, 0] - 1)
    keep_ref[...] = jnp.where(within > row, 1.0, 0.0)
    io.flush(5)
    io.flush(6)
    for copy in copies:
        copy.wait()
    turn[...] = jnp.zeros_like(turn)
    for owner in range(4):
        turn[: 4 * layers, :shard] = gains_land[owner]
        gains_ref[owner * shard : (owner + 1) * shard, :] = turn[...].T[:shard]
    io.flush(1)
    io.ready(5, 8)
    gather(0, 0).wait_recv()
    gather(2, 0).start()
    for part in range(parts):
        if part + 1 < parts:
            gather(0, part + 1).wait_recv()
            gather(2, part + 1).start()
        gather(1, part).wait_recv()
        gather(2, part).wait_recv()
        values = raw[part].astype(F32)

        @pl.when(me == part // 2)
        def _():
            x_ref[:, (part % 2) * half : (part % 2 + 1) * half] = values

        normal, _ = norm_columns(values)
        full[part] = (normal * gains_ref[:, 0:1] + gains_ref[:, 1:2]).astype(BF16)
        io.flush(2, part, part)
        columns = slice(part * half, (part + 1) * half)
        project_ref[:, columns] = matmul(weight_ref[...], full[part])
        io.flush(3, part, (slice(None), pl.ds(part * half, half)))
        cuts = width // 64
        lax.fori_loop(
            cuts * part // parts, cuts * (part + 1) // parts, split_rows(up_ref, up_in, 64), 0
        )
    io.flush(0)
    io.flush(4)
    for part in range(parts):
        for kind in range(3):
            gather(kind, part).wait_send()


def first_project(inputs, gain_arrays, weight, short_conv, cond_weight, glu_in, seq_table,
                  collective):
    shard, slots = inputs.shape
    layers = len(gain_arrays[0])
    rows, width = weight[0].shape[1:]
    hidden = glu_in[0].shape[3]
    tokens = slots // 4
    return fused_call(
        first_project_kernel,
        [inputs, *gain_arrays, weight, short_conv, cond_weight, glu_in, seq_table],
        [
            ((width, tokens), F32),
            ((width, 128), F32),
            ((8, width, tokens // 2), BF16),
            ((rows, slots), F32),
            ((width, 2 * hidden), BF16),
            ((layers, shard, 128), F32),
            ((8, slots), F32),
        ],
        [
            pltpu.VMEM((8, width, tokens // 2), BF16),
            pltpu.VMEM((4 * layers, shard), F32),
            pltpu.VMEM((4, 4 * layers, shard), F32),
            pltpu.VMEM((128, 256), F32),
        ]
        + [pltpu.SemaphoreType.DMA((3, 8))] * 2
        + [pltpu.SemaphoreType.DMA((3,))] * 2,
        collective,
        "first_project",
        (1, 1, 8, 8, 1, 1, 1),
        9,
    )


def scatter_copy(peers, buffers, sems, kind, part):
    _, mate, across, _ = peers
    send, recv = sems
    return send_to(
        across if kind == 2 else mate,
        buffers[2 * kind].at[part],
        buffers[2 * kind + 1].at[part],
        send.at[kind, part],
        recv.at[kind, part],
    )


def scatter_buffers(width, half):
    return [pltpu.VMEM((2, width, half), BF16)] * 6


def block_place(full):
    return lambda owner, part: full.at[owner * 2 + part]


def block_at(step, peers, gathers):
    me, mate, across, diag = peers
    if gathers:
        mine = 1 - (step + 6) // 8
        kind = (step + 1) % 3
        part = mine * step + (1 - mine) * ((step - 2) // 3)
        kind = kind - mine * 4
    else:
        near = step // 4
        mine = step // 6
        part = (1 - near) * (step // 2) + near * (step % 2)
        kind = (1 - near) * (1 + step % 2) - mine
    far = kind * (2 - kind) * (across - mate) + kind * (kind - 1) // 2 * (diag - mate)
    return kind, part, ((1 - mine) * (mate + far) + mine * me) * 2 + part, mine


def run_blocks(peers, full, gather_sems, scatter_sems, buffers, partial, kept, own, ring=None):
    me, mate, across, diag = peers
    gathers = gather_sems is not None

    def gather(kind, part):
        return gather_copy(block_place(full), peers, gather_sems, kind, part)

    def step_body(step, carry):
        kind, part, block, mine = block_at(step, peers, gathers)

        if gathers:
            @pl.when(kind == 0)
            def _():
                gather(1, part).wait_recv()

            @pl.when(kind == 1)
            def _():
                gather(0, part).wait_recv()
                gather(2, part).start()

            @pl.when(kind == 2)
            def _():
                gather(2, part).wait_recv()

        share = partial(block, step)

        def scatter(kind):
            return scatter_copy(peers, buffers, scatter_sems, kind, part)

        @pl.when(mine == 1)
        def _():
            own[part] = share

        @pl.when(kind == 0)
        def _():
            buffers[2][part] = share.astype(BF16)
            scatter(1).start()

        @pl.when(kind == 1)
        def _():
            kept[...] = share

        @pl.when(kind == 2)
        def _():
            buffers[0][part] = share.astype(BF16)
            scatter(0).start()
            scatter(0).wait_recv()
            buffers[4][part] = (kept[...] + buffers[1][part].astype(F32)).astype(BF16)
            scatter(2).start()

        if ring is not None:
            pl.when(step % 3 == 2)(lambda: ring.advance(step // 3, 4))
        return carry

    lax.fori_loop(0, 8, step_body, 0)


def scattered(peers, scatter_sems, buffers, own, part):
    for kind in (1, 2):
        scatter_copy(peers, buffers, scatter_sems, kind, part).wait_recv()
    return own[part] + buffers[3][part].astype(F32) + buffers[5][part].astype(F32)


def drain_gather(peers, full, gather_sems):
    for part in range(2):
        for kind in range(3):
            gather_copy(block_place(full), peers, gather_sems, kind, part).wait_send()


def drain_scatter(peers, scatter_sems, buffers):
    for part in range(2):
        for kind in range(3):
            scatter_copy(peers, buffers, scatter_sems, kind, part).wait_send()


def feed_kernel(gain_at, follows, io, token_gated, x_ref, gains_ref, out_weight, up_columns,
                down_weight, *refs):
    refs = list(refs)
    weight_ref, up_in = (refs.pop(0), refs.pop(0)) if follows else (None, None)
    mid_ref, full, next_ref, units, gelus, slopes = refs[:6]
    refs = refs[6:]
    if follows:
        next_full, project_ref, next_up = refs[:3]
        *refs, next_send, next_recv = refs[3:]
    up_weight, kept, own, *rest = refs
    buffers, sems = rest[:6], rest[6:]
    gather_send, gather_recv, scatter_send, scatter_recv = sems
    gather_sems, scatter_sems = (gather_send, gather_recv), (scatter_send, scatter_recv)
    peers = chan_peers()
    me, mate, across, _ = peers
    width, tokens = x_ref.shape
    half = tokens // 2
    hidden = down_weight.shape[1]
    greet((mate, across))
    io.ready(0, 1, 2, 3)
    for part in range(2):
        columns = slice(part * half, (part + 1) * half)
        mid = x_ref[:, columns] + matmul(out_weight[...], token_gated[:, columns])
        mid_ref[:, columns] = mid
        normal, _ = norm_columns(mid)
        gain = gains_ref[:, gain_at : gain_at + 1]
        bias = gains_ref[:, gain_at + 1 : gain_at + 2]
        full[me * 2 + part] = (normal * gain + bias).astype(BF16)
        for kind in range(2):
            gather_copy(block_place(full), peers, gather_sems, kind, part).start()
    io.flush(0)
    io.ready(4, 5)
    transpose_columns(up_weight, up_columns, 256)

    def partial(block, step):
        normed = full[block]
        tile = 256
        gates = matmul(up_weight[:hidden], normed)
        ups = matmul(up_weight[hidden:], normed)
        for n in range(hidden // tile):
            rows = slice(n * tile, (n + 1) * tile)
            gate, up = gates[rows], ups[rows]
            cdf = 0.5 * (1.0 + lax.erf(gate * math.sqrt(0.5)))
            density = jnp.exp(-0.5 * gate * gate) * (1.0 / math.sqrt(2.0 * math.pi))
            gelu = gate * cdf
            units[block, rows] = (gelu * up).astype(BF16)
            gelus[block, rows] = gelu.astype(BF16)
            slopes[block, rows] = (up * (cdf + gate * density)).astype(BF16)
        return matmul(down_weight[...], units[block])

    run_blocks(peers, full, gather_sems, scatter_sems, buffers, partial, kept, own)
    for number in (1, 3, 4, 5):
        io.flush(number)
    if follows:
        io.ready(6, 7)
    place = block_place(next_full) if follows else None
    for part in range(2):
        if follows:
            cuts = width // 64
            lax.fori_loop(
                cuts * part // 2, cuts * (part + 1) // 2, split_rows(next_up, up_in, 64), 0
            )
        columns = slice(part * half, (part + 1) * half)
        value = mid_ref[:, columns] + scattered(peers, scatter_sems, buffers, own, part)
        next_ref[:, columns] = value.astype(next_ref.dtype)
        if follows:
            normal, _ = norm_columns(value)
            gain = gains_ref[:, gain_at + 2 : gain_at + 3]
            bias = gains_ref[:, gain_at + 3 : gain_at + 4]
            next_full[me * 2 + part] = (normal * gain + bias).astype(BF16)
            for kind in range(2):
                gather_copy(place, peers, (next_send, next_recv), kind, part).start()
    io.flush(2)
    if follows:
        io.flush(8)
    drain_gather(peers, full, gather_sems)
    drain_scatter(peers, scatter_sems, buffers)
    if follows:
        project_blocks(io, peers, next_full, (next_send, next_recv), weight_ref, project_ref, 6, 7)


def project_blocks(io, peers, full, sems, weight_ref, project_ref, full_out, project_out):
    me, mate, across, diag = peers
    half = full.shape[2]

    def gather(kind, part):
        return gather_copy(block_place(full), peers, sems, kind, part)

    order = [(me, 0), (me, 1), (mate, 0), (mate, 1)]
    order += [(across, 0), (diag, 0), (across, 1), (diag, 1)]
    for step, (owner, part) in enumerate(order):
        if 2 <= step < 4:
            gather(1, part).wait_recv()
        elif step >= 4 and step % 2 == 0:
            gather(0, part).wait_recv()
            gather(2, part).start()
        elif step >= 4:
            gather(2, part).wait_recv()
        block = owner * 2 + part
        io.flush(full_out, step, block)
        columns = span(block, half)
        project_ref[:, columns] = matmul(weight_ref[...], full[block])
        io.flush(project_out, step, (slice(None), columns))
    for kind in range(3):
        for part in range(2):
            gather(kind, part).wait_send()


def feed_forward(token_gated, values, gains, out_weight, up_columns, down_weight, following, gain_at,
                 collective):
    width, tokens = values.shape
    half = tokens // 2
    follows = list(following)
    block = ((8, width, half), BF16)
    outs = [((width, tokens), F32), block]
    outs.append(((width, tokens), F32 if follows else BF16))
    hidden = down_weight[0].shape[2]
    outs += [((8, hidden, half), BF16)] * 3
    parts = [1] * 6
    extra = []
    if follows:
        outs += [block, ((follows[0][0].shape[1], 4 * tokens), F32)]
        outs.append(((width, 2 * hidden), BF16))
        parts += [8, 8, 1]
        extra = [pltpu.SemaphoreType.DMA((3, 2))] * 2
    return fused_call(
        lambda *refs: feed_kernel(gain_at, bool(follows), *refs),
        [token_gated, values, gains, out_weight, up_columns, down_weight] + follows,
        outs,
        [
            pltpu.VMEM((2 * hidden, width), BF16),
            pltpu.VMEM((width, half), F32),
            pltpu.VMEM((2, width, half), F32),
        ]
        + scatter_buffers(width, half)
        + [pltpu.SemaphoreType.DMA((3, 2))] * 4
        + extra,
        collective,
        "feed_forward",
        parts,
    )


def weight_grad(store, rows, columns, left, right, blocks, row_tile, column_tile):
    across = columns // column_tile

    def one(n, carry):
        row, column = span(n // across, row_tile), span(n % across, column_tile)
        total = matmul_nt(left(0, row), right(0, column))
        for block in range(1, blocks):
            total = total + matmul_nt(left(block, row), right(block, column))
        store(n // across, column, total)
        return carry

    lax.fori_loop(0, rows // row_tile * across, one, 0)


def feed_back_kernel(gain_at, gathered, tracks, io, grad_ref, down_weight, gelus, slopes, up_columns,
                     out_weight, mid_ref, gains_ref, token_gated, units, normed, *refs):
    refs = list(refs)
    rings = len(tracks)
    inputs = len(ring_operands(tracks))
    ring_in, refs = refs[:inputs], refs[inputs:]
    state_ref, gated_ref, feed_grads, out_grad, sums_ref = refs[:5]
    large, refs = refs[5 : 5 + rings], refs[5 + rings :]
    ring = None
    if rings:
        sources = [io.source[11 + n] for n in range(inputs)]
        ring = Ring(tracks, ring_in, large, refs[-rings - 2 :], sources)
        refs = refs[: -rings - 2]
    full = grad_ref if gathered else refs.pop(0)
    mixer_low, kept, own, turned, *rest, load_sems = refs
    gated_low = full
    buffers, sems = rest[:6], rest[6:]
    send, recv, gather_send, gather_recv, scatter_send, scatter_recv = sems
    gather_sems, scatter_sems = (gather_send, gather_recv), (scatter_send, scatter_recv)
    if gathered:
        gather_sems = None
    peers = chan_peers()
    me, mate, across, diag = peers
    width, tokens = mid_ref.shape
    half = tokens // 2
    shard = gated_ref.shape[0]
    hidden = down_weight.shape[1]
    tile = 256
    saved = ((io.source[2], gelus), (io.source[3], slopes))
    if gathered:
        saved += ((io.source[0], full),)

    def loads(step, block):
        return [
            pltpu.make_async_copy(source.at[block], target.at[block], load_sems.at[n, step])
            for n, (source, target) in enumerate(saved)
        ]

    for step in range(8):
        for copy in loads(step, block_at(step, peers, not gathered)[2]):
            copy.start()
    greet(peers[1:], ring.toward if rings else ())
    if not gathered:
        io.ready(0)
        for part in range(2):
            full[me * 2 + part] = grad_ref[:, part * half : (part + 1) * half].astype(BF16)
            for kind in range(2):
                gather_copy(block_place(full), peers, gather_sems, kind, part).start()
    if rings:
        ring.start()
    io.ready(1)
    down_rows, out_rows = turned.at[:hidden], turned.at[:width]
    transpose_into(down_rows, down_weight, tile)
    io.ready(4)
    if rings:
        io.ready(*range(11, 11 + rings))

    def partial(block, step):
        for copy in loads(step, block):
            copy.wait()
        grad = full[block]
        for n in range(hidden // tile):
            rows = slice(n * tile, (n + 1) * tile)
            unit_grad = matmul(down_rows[rows], grad)
            slopes[block, rows] = (unit_grad * slopes[block, rows].astype(F32)).astype(BF16)
            gelus[block, rows] = (unit_grad * gelus[block, rows].astype(F32)).astype(BF16)
        return matmul(up_columns[:, :hidden], slopes[block]) + matmul(
            up_columns[:, hidden:], gelus[block]
        )

    run_blocks(peers, full, gather_sems, scatter_sems, buffers, partial, kept, own, ring)
    io.ready(5, 6, 7, 8, 9, 10)
    transpose_into(out_rows, out_weight, tile)
    if not gathered:
        drain_gather(peers, full, gather_sems)

    def a2a(part, n):
        peer = (across, diag, mate)[n]
        return send_to(
            peer,
            gated_low.at[part, span(peer, shard, 32), :],
            gated_ref.at[:, span(me * 2 + part, half)],
            send.at[part, n],
            recv.at[part, n],
        )

    chunk_rows = feed_grads.shape[1] // 3
    row_tile = 384

    def store_grad(kind):
        def store(index, column, total):
            chunks = row_tile // chunk_rows
            for n in range(chunks):
                feed_grads[
                    index * chunks + n, kind * chunk_rows : (kind + 1) * chunk_rows, column
                ] = total[n * chunk_rows : (n + 1) * chunk_rows].astype(BF16)

        return store

    def feed_grad(kind):
        if kind == 0:
            left, right = lambda b, r: full[b, r], lambda b, c: units[b, c]
        else:
            def left(b, r):
                return normed[b, r]

            def right(b, c):
                return (slopes, gelus)[kind - 1][b, c]

        weight_grad(store_grad(kind), width, hidden, left, right, 8, row_tile, tile)

    def store_out(index, column, total):
        out_grad[span(index, tile), column] = total.astype(BF16)

    gain = gains_ref[:, gain_at : gain_at + 1]
    for part in range(2):
        feed_grad(part)
        if rings:
            ring.advance(2 + part, 4)
        columns = slice(part * half, (part + 1) * half)
        grad = scattered(peers, scatter_sems, buffers, own, part)
        change, product = norm_pullback(grad, mid_ref[:, columns], gain)
        before = full[me * 2 + part].astype(F32) if gathered else grad_ref[:, columns]
        state = before + change
        state_ref[:, columns] = state
        mixer_low[:, columns] = state.astype(BF16)
        gated_low[part] = matmul(out_rows[...], mixer_low[:, columns]).astype(BF16)
        for n in range(3):
            a2a(part, n).start()
        if part == 0:
            sums_ref[:, 0:1] = lane_sums(product)
            sums_ref[:, 1:2] = lane_sums(grad)
        else:
            sums_ref[:, 0:1] = sums_ref[:, 0:1] + lane_sums(product)
            sums_ref[:, 1:2] = sums_ref[:, 1:2] + lane_sums(grad)
    io.flush(0)
    feed_grad(2)
    io.flush(2)
    io.flush(4)
    for part in range(2):
        gated_ref[:, span(me * 2 + part, half)] = gated_low[part, span(me, shard, 32), :]
    weight_grad(
        store_out, width, width,
        lambda b, r: mixer_low[r, :], lambda b, c: token_gated[c, :], 1, tile, tile,
    )
    io.flush(3)
    if rings:
        ring.finish()
        for n in range(rings):
            io.flush(5 + n)
    for part in range(2):
        for n in range(3):
            a2a(part, n).wait()
    io.flush(1)
    drain_scatter(peers, scatter_sems, buffers)


def feed_back(grad, mid, gains, normed, up_columns, down_weight, out_weight, token_gated, saved,
              tracks, gain_at, count, collective):
    width, tokens = mid.shape
    half = tokens // 2
    hidden = down_weight[0].shape[2]
    gathered = grad.ndim == 3
    units, gelus, slopes = saved
    own_loads = tuple(range(11, 11 + len(tracks)))
    carries = tuple(range(11 + len(tracks), 11 + len(ring_operands(tracks))))
    manual = (2, 3) + ((0,) if gathered else ()) + carries
    return fused_call(
        lambda *refs: feed_back_kernel(gain_at, gathered, tracks, *refs),
        [grad, down_weight, gelus, slopes, up_columns, out_weight, mid, gains, token_gated, units]
        + [normed]
        + ring_operands(tracks),
        [
            ((width, tokens), F32),
            ((width // 4, 4 * tokens), BF16),
            ((count, 3 * width // count, hidden), BF16),
            ((width, width), BF16),
            ((width, 8), F32),
        ]
        + [one.out() for one in tracks],
        [pltpu.VMEM((8, width, half), BF16)] * (not gathered)
        + [
            pltpu.VMEM((width, tokens), BF16),
            pltpu.VMEM((width, half), F32),
            pltpu.VMEM((2, width, half), F32),
            pltpu.VMEM((max(hidden, width), width), BF16),
        ]
        + scatter_buffers(width, half)
        + [pltpu.SemaphoreType.DMA((2, 3))] * 2
        + [pltpu.SemaphoreType.DMA((3, 2))] * 4
        + [pltpu.SemaphoreType.DMA((3, 8))]
        + ring_scratch(tracks),
        collective,
        "feed_back",
        [1] * (5 + len(tracks)),
        manual=manual,
        order=((0,) if not gathered else ()) + (1, 4) + own_loads,
    )


def project_back_kernel(gain_at, each, tracks, in_track, io, project_grad, weight_ref, square_ref, normed,
                        state_ref, x_ref, gains_ref, *refs):
    inputs = len(ring_operands(tracks))
    ring_in, refs = refs[:inputs], refs[inputs:]
    next_ref, in_grad, sums_ref = refs[:3]
    large, refs = refs[3 : 3 + len(tracks)], refs[3 + len(tracks) :]
    in_held, *refs = refs
    kept, own, weight_rows, in_full, *rest = refs
    buffers, (scatter_send, scatter_recv, *ring_rest) = rest[:6], rest[6:]
    *ring_rest, in_slots, in_send, in_recv = ring_rest
    in_ring = Ring([in_track], [in_grad], [in_held], [in_slots, in_send, in_recv], [in_grad])
    scatter_sems = (scatter_send, scatter_recv)
    peers = chan_peers()
    me, mate, across, diag = peers
    sources = [io.source[7 + n] for n in range(inputs)]
    ring = Ring(tracks, ring_in, large, ring_rest, sources)
    width, tokens = x_ref.shape
    half = tokens // 2
    rows = weight_ref.shape[0]
    shard = rows // 3
    greet((mate, across), ring.toward)
    ring.start()
    io.ready(1)
    for first, size in ((0, 512), (512, rows - 512)):
        weight_rows[:, first : first + size] = weight_ref[first : first + size].T
    io.ready(0)

    def share(owner, part):
        return matmul(weight_rows[...], project_grad[:, span(owner * 2 + part, half)])

    for part in range(2):
        buffers[0][part] = share(diag, part).astype(BF16)
        scatter_copy(peers, buffers, scatter_sems, 0, part).start()
        kept[...] = share(across, part)
        scatter_copy(peers, buffers, scatter_sems, 0, part).wait_recv()
        buffers[4][part] = (kept[...] + buffers[1][part].astype(F32)).astype(BF16)
        scatter_copy(peers, buffers, scatter_sems, 2, part).start()
    for part in range(2):
        buffers[2][part] = share(mate, part).astype(BF16)
        scatter_copy(peers, buffers, scatter_sems, 1, part).start()
        own[part] = share(me, part)
    io.ready(2, 3)
    if in_full.shape[1] > 4 * each:
        in_full[...] = jnp.zeros_like(in_full)
    for chunk in range(shard // each):
        in_full[chunk, 3 * each : 4 * each] = square_ref[chunk * each : (chunk + 1) * each]
    tile = 256
    for stream in range(3):
        def column_tile(n, carry):
            column = span(n, tile)
            total = None
            for block in range(8):
                left = project_grad[
                    stream * shard : (stream + 1) * shard, block * half : (block + 1) * half
                ]
                value = matmul_nt(left, normed[block, column])
                total = value if total is None else total + value
            for chunk in range(shard // each):
                in_full[chunk, stream * each : (stream + 1) * each, column] = total[
                    chunk * each : (chunk + 1) * each
                ]
            return carry

        lax.fori_loop(0, width // tile, column_tile, 0)
    in_grad[...] = in_full[...].astype(BF16)
    in_ring.start()
    io.flush(1)
    io.ready(*range(7, 7 + len(tracks)))
    ring.advance(0, 2)
    io.ready(4, 5, 6)
    gain = gains_ref[:, gain_at : gain_at + 1]
    for part in range(2):
        columns = slice(part * half, (part + 1) * half)
        grad = scattered(peers, scatter_sems, buffers, own, part)
        change, product = norm_pullback(grad, x_ref[:, columns], gain)
        next_ref[:, columns] = state_ref[:, columns] + change
        if part == 0:
            sums_ref[:, 0:1] = lane_sums(product)
            sums_ref[:, 1:2] = lane_sums(grad)
            ring.advance(1, 2)
            in_ring.advance(0, 1)
        else:
            sums_ref[:, 0:1] = sums_ref[:, 0:1] + lane_sums(product)
            sums_ref[:, 1:2] = sums_ref[:, 1:2] + lane_sums(grad)
    io.flush(0)
    io.flush(2)
    ring.finish()
    for n in range(len(tracks)):
        io.flush(3 + n)
    in_ring.finish()
    io.flush(3 + len(tracks))
    drain_scatter(peers, scatter_sems, buffers)


def project_back(project_grad, state, values, gains, normed, weight, square, tracks, gain_at,
                 collective):
    width, tokens = values.shape
    half = tokens // 2
    rows = project_grad.shape[0]
    count = tracks[0].count
    each = rows // 3 // count
    packed = (count, ring_rows(4 * each), width)
    in_track = Track(jax.ShapeDtypeStruct(packed, BF16), 0, count // 4)
    return fused_call(
        lambda *refs: project_back_kernel(gain_at, each, tracks, in_track, *refs),
        [project_grad, weight, square, normed, state, values, gains] + ring_operands(tracks),
        [((width, tokens), F32), (packed, BF16), ((width, 8), F32)]
        + [one.out() for one in tracks + [in_track]],
        [
            pltpu.VMEM((width, half), F32),
            pltpu.VMEM((2, width, half), F32),
            pltpu.VMEM((width, rows), BF16),
            pltpu.VMEM(packed, F32),
        ]
        + scatter_buffers(width, half)
        + [pltpu.SemaphoreType.DMA((3, 2))] * 2
        + ring_scratch(tracks)
        + ring_scratch([in_track]),
        collective,
        "project_back",
        [1] * (4 + len(tracks)),
        manual=tuple(range(7 + len(tracks), 7 + len(ring_operands(tracks)))),
        order=(1, 0) + tuple(range(7, 7 + len(tracks))),
    )


def mask_heads(values, keep, blocks):
    length = values.shape[1] // blocks
    pieces = []
    for j in range(blocks):
        start = j * length
        pieces.append(values[:, start : start + 128] * keep[:, start : start + 128])
        pieces.append(values[:, start + 128 : start + length])
    return jnp.concatenate(pieces, axis=1)


def eight(rows):
    if isinstance(rows, int):
        return pl.ds(rows, 8)
    return pl.ds(pl.multiple_of(rows, 8), 8)


def sixteen(rows):
    if isinstance(rows, int):
        return pl.ds(rows, 16)
    return pl.ds(pl.multiple_of(rows, 16), 16)


def stream_rows(project_ref, columns_ref, keep_ref, rows, shard, stream, blocks):
    values = project_ref[eight(stream * shard + rows), :]
    total = values * columns_ref[eight(rows), stream : stream + 1]
    for offset in (1, 2):
        moved = mask_heads(pltpu.roll(values, offset, 1), keep_ref[offset - 1 : offset, :], blocks)
        column = 3 * offset + stream
        total = total + moved * columns_ref[eight(rows), column : column + 1]
    return total


def sequence_factor(power, cond, facts, blocks):
    energy = []
    for i in range(blocks):
        total = 0.0
        for j in range(blocks):
            total = total + power[j] * facts.same[i][j]
        energy.append(total * facts.inverse)
    logs = [jnp.log(1.0 + value) for value in energy]
    factor = [
        (1.0 + cond * value) * facts.same[i][i] for i, value in enumerate(logs)
    ]
    return energy, logs, factor


def block_sums(values, blocks):
    length = values.shape[1] // blocks
    return [lane_sums(values[:, i * length : (i + 1) * length]) for i in range(blocks)]


def spread_blocks(columns, length):
    return jnp.concatenate(
        [jnp.broadcast_to(column, (column.shape[0], length)) for column in columns], axis=1
    )


def plain_bins(spectrum_ref, rows, shard, blocks):
    half = spectrum_ref.shape[1] // 2
    bins = []
    for k in range(blocks):
        here = spectrum_ref[eight(k * shard + rows), :]
        bins.append((here[:, :half], here[:, half:]))
    return bins


def filter_bins(spectrum_ref, sign, rows, shard, blocks):
    plain = plain_bins(spectrum_ref, rows, shard, blocks)
    bins = [plain[0]]
    for k in range(1, blocks):
        (real, imag), (before_real, before_imag) = plain[k], plain[k - 1]
        bins.append((real - sign * before_imag, imag + sign * before_real))
    return bins


def store_blocks(target, values, rows, shard, blocks):
    length = values.shape[1] // blocks
    for j in range(blocks):
        target[sixteen(j * shard + rows), :] = values[:, j * length : (j + 1) * length]


def join(halves):
    return jnp.concatenate(halves, axis=0).astype(BF16)


def channel_cuts(shard, streams):
    size = shard // LOADS
    return [(s * shard + n * size, size) for n in range(LOADS) for s in range(streams)]


def channel_order(numbers, streams=3):
    order = []
    for n in range(LOADS):
        for number in numbers:
            each = streams if number == 1 else 1
            order += [(number, n * each + i) for i in range(each)]
    return tuple(order)


def run_groups(prepare, transform, combine, invert, finish, after):
    prepare(0)
    for i in range(LOADS + 1):
        if i < LOADS:
            transform(i)
        if i + 1 < LOADS:
            prepare(i + 1)
        if i:
            invert(i - 1)
        if i < LOADS:
            combine(i)
        if i:
            finish(i - 1)
            after(i - 1)


def conv_forward_kernel(blocks, carries, io, filter_ref, project_ref, columns_ref, keep_ref,
                        sign_ref, table_ref, seq_ref, carried_in, back_ref, token_gated, conv_ref,
                        carried, gated, factor_ref, *refs):
    signal_low, filter_low, signal_bins, filter_spectrum, out_low, convolved = (
        refs[2 * n : 2 * n + 2] for n in range(6)
    )
    send, recv, *sems = refs[12:]
    shard, slots = gated.shape
    length = slots // blocks
    scale = 1.0 / length
    size = shard // LOADS
    peers = chan_peers()
    me = peers[0]
    tokens = slots // 4
    parts = carried.shape[0]
    facts = Facts(seq_ref, blocks, length)
    greet(peers[1:])

    def gather(kind, part):
        return gather_copy(
            lambda owner, part: carried.at[part, span(owner, shard, 32), :],
            peers, sems, kind, part,
        )

    def forward(first, last):
        for part in range(parts * first // LOADS, parts * last // LOADS):
            gather(0, part).wait_recv()
            gather(2, part).start()

    io.ready(7)
    for part in range(parts):
        if carries == 1:
            carried[part, span(me, shard, 32), :] = carried_in[part]
        else:
            lanes = carried.shape[2]
            carried[part, span(me, shard, 32), :] = carried_in[:, part * lanes : (part + 1) * lanes]
        for kind in range(2):
            gather(kind, part).start()
    io.ready(2, 3, 4)

    def prepare(group):
        base, place = group * size, group % 2
        if group < 2:
            cuts = slice(0, 1) if group == 0 else slice(1, LOADS)
            io.ready(0, cuts=cuts)
            io.ready(1, cuts=slice(3 * cuts.start, 3 * cuts.stop))
        for n in range(size // 16):
            rows = base + n * 16
            signals = []
            for part in range(2):
                here = rows + 8 * part
                one, two = (
                    stream_rows(project_ref, columns_ref, keep_ref, here, shard, stream, blocks)
                    for stream in (1, 2)
                )
                signals.append(one * two)
                cond = columns_ref[eight(here), 9:10]
                _, _, factor = sequence_factor(block_sums(two * two, blocks), cond, facts, blocks)
                for j in range(blocks):
                    factor_ref[eight(here), j : j + 1] = factor[j]
            store_blocks(signal_low[place], join(signals), n * 16, size, blocks)
            kernel = filter_ref[sixteen(rows), :].astype(BF16)
            store_blocks(filter_low[place], kernel, n * 16, size, blocks)

    def transform(group):
        place = group % 2
        if group == 0:
            io.ready(5, 8)
        signal_bins[place][...] = matmul(signal_low[place][...], table_ref[...])
        filter_spectrum[place][...] = matmul(filter_low[place][...], table_ref[...])

    def combine(group):
        place = group % 2
        for n in range(size // 16):
            joined = [[] for _ in range(blocks)]
            for part in range(2):
                here = n * 16 + 8 * part
                window = filter_bins(filter_spectrum[place], sign_ref[0:1, :], here, size, blocks)
                signal = plain_bins(signal_bins[place], here, size, blocks)
                for i in range(blocks):
                    real = imag = None
                    for j in range(i, -1, -1):
                        fr, fi = window[i - j]
                        sr, si = signal[j]
                        more_real, more_imag = fr * sr - fi * si, fr * si + fi * sr
                        if j == i:
                            real, imag = more_real, more_imag
                        else:
                            factor = facts.same[i][j]
                            real, imag = real + more_real * factor, imag + more_imag * factor
                    joined[i].append(jnp.concatenate([real, imag], axis=1))
            for i in range(blocks):
                out_low[place][sixteen(i * size + n * 16), :] = join(joined[i])

    def invert(group):
        place = group % 2
        convolved[place][...] = matmul(out_low[place][...], back_ref[...]) * scale

    def finish(group):
        base, place = group * size, group % 2
        for n in range(size // 16):
            rows = base + n * 16
            results = []
            for part in range(2):
                here = rows + 8 * part
                zero = stream_rows(project_ref, columns_ref, keep_ref, here, shard, 0, blocks)
                pieces = []
                for j in range(blocks):
                    source = convolved[place][eight(j * size + n * 16 + 8 * part), :]
                    columns = slice(j * length, (j + 1) * length)
                    conv_ref[eight(here), columns] = source
                    pieces.append(zero[:, columns] * (source * factor_ref[eight(here), j : j + 1]))
                results.append(jnp.concatenate(pieces, axis=1))
            gated[sixteen(rows), :] = join(results)

    copies = []

    def after(group):
        base = group * size
        mine = pl.ds(pl.multiple_of(me * shard + base, 16), size)
        copies.extend(
            exchange(
                peers, lambda peer: gated.at[pl.ds(base, size), span(peer, tokens)],
                lambda: token_gated.at[mine], send.at[group], recv.at[group],
            )
        )
        token_gated[mine, :] = gated[base : base + size, span(me, tokens)]
        io.flush(1, group, pl.ds(base, size))
        forward(group, group + 1)

    run_groups(prepare, transform, combine, invert, finish, after)
    for part in range(parts):
        for kind in (1, 2):
            gather(kind, part).wait_recv()
        io.flush(2, part, part)
    for copy in copies:
        copy.wait()
    io.flush(0)
    for part in range(parts):
        for kind in range(3):
            gather(kind, part).wait_send()


def conv_forward(project, filter_rows, columns, keep, sign, table, seq_table, back, carried,
                 carries, blocks, collective):
    shard, slots = filter_rows[0].shape[1:]
    width = 4 * shard
    length = slots // blocks
    rows = blocks * (shard // LOADS)
    low = pltpu.VMEM((rows, length), BF16)
    bins = pltpu.VMEM((rows, 2 * length), F32)
    if carries == 1:
        out = ((carried.shape[0], width, width), BF16)
    else:
        out = ((8, width, slots // 8), BF16)
    return fused_call(
        lambda *refs: conv_forward_kernel(blocks, carries, *refs),
        [filter_rows, project, columns, keep, sign, table, seq_table, carried, back],
        [((width, slots // 4), BF16), ((shard, slots), F32), out],
        [
            pltpu.VMEM((shard, slots), BF16),
            pltpu.VMEM((shard, 128), F32),
        ]
        + [low] * 4
        + [bins] * 4
        + [pltpu.VMEM((rows, 2 * length), BF16)] * 2
        + [pltpu.VMEM((rows, length), F32)] * 2
        + [pltpu.SemaphoreType.DMA((LOADS, 3))] * 2
        + [pltpu.SemaphoreType.DMA((3, out[0][0]))] * 2,
        collective,
        "conv_forward",
        [1, LOADS, out[0][0]],
        6,
        (7, 2, 3, 4) + channel_order((1, 0)) + (5, 8),
        {0: channel_cuts(shard, 1), 1: channel_cuts(shard, 3)},
    )


def conv_backward_kernel(blocks, tracks, with_outputs, io, grad_ref, project_ref, conv_ref,
                         filter_ref, columns_ref, keep_ref, sign_ref, table_ref, seq_ref,
                         square_ref, *refs):
    refs = list(refs)
    back_ref = refs.pop(len(ring_operands(tracks)) + with_outputs)
    rings = len(tracks)
    inputs = len(ring_operands(tracks))
    ring_in, refs = refs[:inputs], refs[inputs:]
    if with_outputs:
        residual_ref = refs.pop(0)
    project_grad, filter_pack, square_sum, sums_ref = refs[:4]
    large, refs = refs[4 : 4 + rings], refs[4 + rings :]
    if with_outputs:
        outputs_ref = refs.pop(0)
        *refs, out_land, out_send, out_recv = refs
    sources = [io.source[10 + n] for n in range(inputs)]
    ring = Ring(tracks, ring_in, large, refs[-rings - 2 :], sources)
    refs = refs[: -rings - 2]
    mixed, energy_ref, square_land, square_send, square_recv, *pairs = refs
    signal_low, filter_low, grad_low, signal_bins, filter_spectrum, grad_bins = (
        pairs[2 * n : 2 * n + 2] for n in range(6)
    )
    signal_out, filter_out, signal_grad, filter_grad = (
        pairs[2 * n : 2 * n + 2] for n in range(6, 10)
    )
    peers = chan_peers()
    greet(peers[1:], ring.toward)
    ring.start()
    copies = exchange(
        peers, lambda peer: io.source[9].at[peer], lambda: square_land.at[peers[0]],
        square_send, square_recv,
    )
    if with_outputs:
        copies += to_channels(
            peers, io.source[10 + inputs], out_land, out_send, out_recv
        )
    io.ready(4, 5, 6)
    shard, slots = grad_ref.shape
    length = slots // blocks
    scale = 1.0 / length
    steps = shard // 16
    facts = Facts(seq_ref, blocks, length)

    size = shard // LOADS

    def prepare(group):
        base, place = group * size, group % 2
        if group < 2:
            cuts = slice(0, 1) if group == 0 else slice(1, LOADS)
            for number, each in ((0, 1), (1, 3), (2, 1), (3, 1)):
                io.ready(number, cuts=slice(each * cuts.start, each * cuts.stop))
        for n in range(size // 16):
            rows = base + n * 16
            signals, scaled = [], []
            grads = grad_ref[sixteen(rows), :].astype(F32)
            for part in range(2):
                here = rows + 8 * part
                zero, one, two = (
                    stream_rows(project_ref, columns_ref, keep_ref, here, shard, stream, blocks)
                    for stream in range(3)
                )
                mixed[0, eight(here), :] = one
                mixed[1, eight(here), :] = two
                signals.append(one * two)
                cond = columns_ref[eight(here), 9:10]
                power = block_sums(two * two, blocks)
                energy, logs, factor = sequence_factor(power, cond, facts, blocks)
                conv_grad = grads[8 * part : 8 * part + 8] * zero
                factor_grad = block_sums(conv_grad * conv_ref[eight(here), :], blocks)
                cond_grad = 0.0
                for j in range(blocks):
                    cond_grad = cond_grad + factor_grad[j] * logs[j]
                sums_ref[eight(here), 9:10] = cond_grad
                for i in range(blocks):
                    total = 0.0
                    for j in range(blocks):
                        total = total + factor_grad[j] * facts.same[i][j]
                    energy_ref[eight(here), i : i + 1] = (
                        total * cond / (1.0 + energy[i]) * (2.0 * facts.inverse)
                    )
                    energy_ref[eight(here), blocks + i : blocks + i + 1] = factor[i]
                scaled.append(
                    conv_grad * spread_blocks([value * scale for value in factor], length)
                )
            store_blocks(signal_low[place], join(signals), n * 16, size, blocks)
            store_blocks(grad_low[place], join(scaled), n * 16, size, blocks)
            kernel = filter_ref[sixteen(rows), :].astype(BF16)
            store_blocks(filter_low[place], kernel, n * 16, size, blocks)

    def transform(group):
        place = group % 2
        if group == 0:
            io.ready(7, 10 + inputs + with_outputs)
        grad_bins[place][...] = matmul(grad_low[place][...], table_ref[...])
        signal_bins[place][...] = matmul(signal_low[place][...], table_ref[...])
        filter_spectrum[place][...] = matmul(filter_low[place][...], table_ref[...])

    def combine(group):
        place = group % 2
        sign = sign_ref[0:1, :]
        for n in range(size // 16):
            joined = [[] for _ in range(blocks)]
            windows = [[] for _ in range(blocks)]
            for part in range(2):
                here = n * 16 + 8 * part
                window = filter_bins(filter_spectrum[place], sign, here, size, blocks)
                signal = plain_bins(signal_bins[place], here, size, blocks)
                grads = plain_bins(grad_bins[place], here, size, blocks)
                for j in range(blocks):
                    for i in range(j, blocks):
                        fr, fi = window[i - j]
                        gr, gi = grads[i]
                        more_real, more_imag = fr * gr + fi * gi, fr * gi - fi * gr
                        if i == j:
                            real, imag = more_real, more_imag
                        else:
                            factor = facts.same[i][j]
                            real, imag = real + more_real * factor, imag + more_imag * factor
                    joined[j].append(jnp.concatenate([real, imag], axis=1))
                after = None
                for k in reversed(range(blocks)):
                    real = imag = None
                    for j in range(blocks - k):
                        sr, si = signal[j]
                        gr, gi = grads[j + k]
                        more_real, more_imag = sr * gr + si * gi, sr * gi - si * gr
                        if k:
                            factor = facts.same[j + k][j]
                            more_real, more_imag = more_real * factor, more_imag * factor
                        real = more_real if real is None else real + more_real
                        imag = more_imag if imag is None else imag + more_imag
                    if after is None:
                        whole = (real, imag)
                    else:
                        whole = (real + sign * after[1], imag - sign * after[0])
                    windows[k].append(jnp.concatenate(whole, axis=1))
                    after = (real, imag)
            for j in range(blocks):
                signal_out[place][sixteen(j * size + n * 16), :] = join(joined[j])
                filter_out[place][sixteen(j * size + n * 16), :] = join(windows[j])

    count, pack_rows, lanes = filter_pack.shape
    each = shard // count
    stack = slots // lanes
    if pack_rows > stack * each:
        filter_pack[...] = jnp.zeros_like(filter_pack)

    def invert(group):
        place = group % 2
        signal_grad[place][...] = matmul(signal_out[place][...], back_ref[...])
        filter_grad[place][...] = matmul(filter_out[place][...], back_ref[...])

    def finish(group):
        base, place = group * size, group % 2
        for chunk in range(size // each):
            lags = [
                filter_grad[place][j * size + chunk * each : j * size + (chunk + 1) * each, :]
                for j in range(blocks)
            ]
            layers = [
                jnp.concatenate(lags[n * blocks // stack : (n + 1) * blocks // stack], axis=1)
                for n in range(stack)
            ]
            value = layers[0] if stack == 1 else jnp.concatenate(layers, axis=0)
            filter_pack[base // each + chunk, : stack * each] = value.astype(BF16)
        for n in range(size // 16):
            rows = base + n * 16
            totals = [[] for _ in range(3)]
            outer = grad_ref[sixteen(rows), :].astype(F32)
            for part in range(2):
                here = rows + 8 * part
                local = eight(here)
                factor = [energy_ref[local, blocks + i : blocks + i + 1] for i in range(blocks)]
                energy = [energy_ref[local, i : i + 1] for i in range(blocks)]
                signal = jnp.concatenate(
                    [
                        signal_grad[place][eight(j * size + n * 16 + 8 * part), :]
                        for j in range(blocks)
                    ],
                    axis=1,
                )
                for stream in range(3):
                    if stream == 0:
                        value = outer[8 * part : 8 * part + 8] * (
                            conv_ref[local, :] * spread_blocks(factor, length)
                        )
                    elif stream == 1:
                        value = signal * mixed[1, local, :]
                    else:
                        value = signal * mixed[0, local, :] + (
                            spread_blocks(energy, length) * mixed[1, local, :]
                        )
                    plain = project_ref[eight(stream * shard + here), :]
                    total = value * columns_ref[local, stream : stream + 1]
                    sums_ref[local, stream : stream + 1] = lane_sums(value * plain)
                    for offset in (1, 2):
                        column = 3 * offset + stream
                        moved = pltpu.roll(
                            mask_heads(value, keep_ref[offset - 1 : offset, :], blocks),
                            slots - offset, 1,
                        )
                        sums_ref[local, column : column + 1] = lane_sums(moved * plain)
                        total = total + moved * columns_ref[local, column : column + 1]
                    totals[stream].append(total)
            for stream in range(3):
                project_grad[sixteen(stream * shard + rows), :] = join(totals[stream])

    def after(group):
        if group == 0:
            io.ready(*range(10, 10 + rings))
        if group < 3:
            ring.advance(group, 3)

    run_groups(prepare, transform, combine, invert, finish, after)
    io.flush(1)
    for stream in range(3):
        io.flush(0, stream, pl.ds(stream * shard, shard))
    for copy in copies:
        copy.wait()
    io.ready(9)
    total = square_ref[peers[0]].astype(F32)
    for peer in peers[1:]:
        total = total + square_land[peer].astype(F32)
    square_sum[...] = total
    io.flush(2)
    if with_outputs:
        io.ready(10 + inputs)
        tokens = residual_ref.shape[1]
        out_land[:, span(peers[0], tokens)] = residual_ref[span(peers[0], shard, 32), :]
        outputs_ref[...] = out_land[...].astype(F32)
        io.flush(4 + rings)
    io.flush(3)
    ring.finish()
    for n in range(rings):
        io.flush(4 + n)


def filter_layout(shard, slots, count):
    each = shard // count
    stack = 2 if each % 8 == 0 else 1
    return count, ring_rows(stack * each), slots // stack


def conv_backward(grad, project, conv, filter_rows, columns, keep, sign, table, seq_table, back, square,
                  tracks, residual, blocks, collective):
    shard, slots = filter_rows[0].shape[1:]
    length = slots // blocks
    rows = blocks * (shard // LOADS)
    low = pltpu.VMEM((rows, length), BF16)
    bins = pltpu.VMEM((rows, 2 * length), F32)
    out = pltpu.VMEM((rows, 2 * length), BF16)
    back_out = pltpu.VMEM((rows, length), F32)
    outs, extra = [], []
    if residual:
        outs = [((shard, slots), F32)]
        extra = [pltpu.VMEM((shard, slots), BF16)] + [pltpu.SemaphoreType.DMA((3,))] * 2
    return fused_call(
        lambda *refs: conv_backward_kernel(blocks, tracks, bool(residual), *refs),
        [grad, project, conv, filter_rows, columns, keep, sign, table, seq_table, square]
        + ring_operands(tracks)
        + list(residual)
        + [back],
        [
            ((3 * shard, slots), BF16),
            (filter_layout(shard, slots, tracks[0].count), BF16),
            ((shard, 4 * shard), F32),
            ((shard, 128), F32),
        ]
        + [one.out() for one in tracks]
        + outs,
        [pltpu.VMEM((2, shard, slots), F32), pltpu.VMEM((shard, 128), F32)]
        + [pltpu.VMEM(square.shape, BF16)]
        + [pltpu.SemaphoreType.DMA((3,))] * 2
        + [low] * 6
        + [bins] * 6
        + [out] * 4
        + [back_out] * 4
        + ring_scratch(tracks)
        + extra,
        collective,
        "conv_backward",
        [3, 1, 1, 1] + [1] * (len(tracks) + len(outs)),
        8,
        (4, 5, 6) + channel_order((0, 1, 2, 3)) + (7,),
        {0: channel_cuts(shard, 1), 1: channel_cuts(shard, 3), 2: channel_cuts(shard, 1)}
        | {3: channel_cuts(shard, 1)},
        tuple(range(10 + len(tracks), 10 + len(ring_operands(tracks)))),
    )


def last_kernel(layers, tracks, io, state_ref, *refs):
    refs = list(refs)
    gain_sums, refs = refs[: 2 * layers], refs[2 * layers :]
    row_sums, refs = refs[:layers], refs[layers:]
    rings, inputs = len(tracks), len(ring_operands(tracks))
    ring_in, refs = refs[:inputs], refs[inputs:]
    input_grad, small_out = refs[:2]
    large, refs = refs[2 : 2 + rings], refs[2 + rings :]
    state_low, landing, sums, turn, gains, gains_land, small_own, small_land, *refs = refs
    chan_send, chan_recv, small_send, small_recv, state_send, state_recv, *refs = refs
    peers = chan_peers()
    me = peers[0]
    dp = lax.axis_index("dp")
    first = 1 + 3 * layers
    ring = Ring(tracks, ring_in, large, refs, [io.source[first + n] for n in range(inputs)])
    count = ring.count
    shard = landing.shape[0]
    greet(peers[1:], [(dp + offset) % count for offset in range(1, count)])
    ring.start()
    io.ready(*range(0, first))
    for layer in range(layers):
        sums[:, 4 * layer : 4 * layer + 2] = gain_sums[2 * layer][:, 0:2]
        sums[:, 4 * layer + 2 : 4 * layer + 4] = gain_sums[2 * layer + 1][:, 0:2]
    turn[...] = jnp.zeros_like(turn)
    for owner in range(4):
        turn[:shard, : 4 * layers] = sums[owner * shard : (owner + 1) * shard, : 4 * layers]
        gains[owner] = turn[...].T[: 4 * layers]
    copies = exchange(
        peers, lambda peer: gains.at[peer], lambda: gains_land.at[me], chan_send, chan_recv
    )
    state_low[...] = state_ref[...].astype(BF16)
    state_copies = to_channels(peers, state_low, landing, state_send, state_recv)
    landing[:, span(me, state_low.shape[1])] = state_low[span(me, shard, 32), :]
    io.ready(*range(first, first + rings))
    ring.advance(0, 6)
    for layer in range(layers):
        turn[:shard, 10 * layer : 10 * layer + 10] = row_sums[layer][:, 0:10]
    small_own[4 * layers :, :] = turn[...].T[: small_own.shape[0] - 4 * layers]
    for copy in copies:
        copy.wait()
    total = gains[me]
    for peer in peers[1:]:
        total = total + gains_land[peer]
    small_own[: 4 * layers, :] = total
    small_copies = []
    for offset in range(1, count):
        copy = pltpu.make_async_remote_copy(
            small_own,
            small_land.at[offset - 1],
            small_send.at[offset - 1],
            small_recv.at[offset - 1],
            device_id={"dp": (dp + offset) % count},
        )
        copy.start()
        small_copies.append(copy)
    for point in range(1, 4):
        ring.advance(point, 6)
    small = small_own[...]
    for copy in small_copies:
        copy.wait()
    for n in range(count - 1):
        small = small + small_land[n]
    small_out[...] = small
    io.flush(1)
    ring.advance(4, 6)
    for copy in state_copies:
        copy.wait()
    input_grad[...] = landing[...].astype(F32)
    io.flush(0)
    ring.advance(5, 6)
    ring.finish()
    for n in range(rings):
        io.flush(2 + n)


def last_sums(state, gain_sums, row_sums, tracks, collective):
    width, tokens = state.shape
    shard = width // 4
    layers = len(row_sums)
    count = tracks[0].count
    small = (-(-14 * layers // 8) * 8, 256)
    return fused_call(
        lambda *refs: last_kernel(layers, tracks, *refs),
        [state] + gain_sums + row_sums + ring_operands(tracks),
        [((shard, 4 * tokens), F32), (small, F32)] + [one.out() for one in tracks],
        [
            pltpu.VMEM((width, tokens), BF16),
            pltpu.VMEM((shard, 4 * tokens), BF16),
            pltpu.VMEM((width, 128), F32),
            pltpu.VMEM((256, 128), F32),
            pltpu.VMEM((4, 4 * layers, 256), F32),
            pltpu.VMEM((4, 4 * layers, 256), F32),
            pltpu.VMEM(small, F32),
            pltpu.VMEM((count - 1,) + small, F32),
            pltpu.SemaphoreType.DMA((3,)),
            pltpu.SemaphoreType.DMA((3,)),
            pltpu.SemaphoreType.DMA((count - 1,)),
            pltpu.SemaphoreType.DMA((count - 1,)),
            pltpu.SemaphoreType.DMA((3,)),
            pltpu.SemaphoreType.DMA((3,)),
        ]
        + ring_scratch(tracks),
        collective,
        "last_sums",
        [1] * (2 + len(tracks)),
        order=tuple(range(1, 1 + 3 * layers)) + (0,),
        manual=tuple(
            range(1 + 3 * layers + len(tracks), 1 + 3 * layers + len(ring_operands(tracks)))
        ),
    )


def collect_kernel(layers, *refs):
    refs = list(refs)
    outputs_in, input_in, small = refs[:3]
    refs = refs[3:]
    feeds, refs = refs[:layers], refs[layers:]
    filters, refs = refs[:layers], refs[layers:]
    packs, refs = refs[:layers], refs[layers:]
    (outputs, input_grad, mix_gain, mix_bias, in_grad, short, filter_grad, cond, out_grad, glu_gain,
     glu_bias, up_grad, down_grad, held, sems) = refs
    pairs = ((outputs_in, outputs), (input_in, input_grad))
    loads = [
        pltpu.make_async_copy(source, held.at[n], sems.at[n]) for n, (source, _) in enumerate(pairs)
    ]
    copies = [
        pltpu.make_async_copy(held.at[n], target, sems.at[2 + n])
        for n, (_, target) in enumerate(pairs)
    ]
    for copy in loads:
        copy.start()
    each = in_grad.shape[2]
    shard = cond.shape[1]
    lanes = filters[0].shape[1]
    for layer in range(layers):
        for kind, out in enumerate((mix_gain, mix_bias, glu_gain, glu_bias)):
            row = 4 * layer + kind
            out[layer : layer + 1, :] = small[row : row + 1, :shard]
        row = 4 * layers + 10 * layer
        for n in range(9):
            short[n // 3, n % 3, layer : layer + 1, :] = small[row + n : row + n + 1, :shard]
        cond[layer : layer + 1, :] = small[row + 9 : row + 10, :shard]
        for stream in range(3):
            in_grad[layer, stream] = packs[layer][stream * each : (stream + 1) * each]
        out_grad[layer] = packs[layer][3 * each : 4 * each]
        for n in range(filter_grad.shape[2] // lanes):
            filter_grad[layer, :, n * lanes : (n + 1) * lanes] = filters[layer][
                n * each : (n + 1) * each
            ]
        rows = down_grad.shape[1]
        down_grad[layer] = feeds[layer][:rows]
        for kind in range(2):
            up_grad[layer, :, kind, :] = feeds[layer][(kind + 1) * rows : (kind + 2) * rows]
        loads[layer].wait()
        copies[layer].start()
    for copy in copies:
        copy.wait()


def collect(outputs, input_grad, small, feeds, filters, packs, each):
    layers = len(feeds)
    shard, slots = outputs.shape
    width = 4 * shard
    rows, hidden = feeds[0].shape[0] // 3, feeds[0].shape[1]
    anywhere = pl.BlockSpec(memory_space=pl.ANY)
    local = pl.BlockSpec(memory_space=pltpu.VMEM)
    operands = [outputs, input_grad, small, *feeds, *filters, *packs]
    small_shape = (layers, shard)
    shapes = [
        (shard, slots), (shard, slots), small_shape, small_shape, (layers, 3, each, width),
        (3, 3, layers, shard), (layers, each, slots), small_shape, (layers, each, width),
        small_shape, small_shape, (layers, rows, 2, hidden), (layers, rows, hidden),
    ]
    return pl.pallas_call(
        lambda *refs: collect_kernel(layers, *refs),
        out_shape=tuple(jax.ShapeDtypeStruct(shape, F32) for shape in shapes),
        in_specs=[anywhere] * 2 + [local] * (len(operands) - 2),
        out_specs=tuple([anywhere] * 2 + [local] * (len(shapes) - 2)),
        scratch_shapes=[pltpu.VMEM((2, shard, slots), F32), pltpu.SemaphoreType.DMA((4,))],
        compiler_params=pltpu.CompilerParams(vmem_limit_bytes=VMEM_LIMIT),
        name="collect",
    )(*operands)


def body(
    inputs,
    seq_table,
    mix_gain,
    mix_bias,
    in_proj,
    short_conv,
    long_filter,
    cond_weight,
    out_proj,
    glu_gain,
    glu_bias,
    glu_in,
    glu_out,
    cotangent,
):
    shard, slots = inputs.shape
    layers, width = in_proj.shape[0], in_proj.shape[3]
    hidden = glu_out.shape[2]
    blocks = 4
    count = lax.axis_size("dp")
    each = shard // count
    table = jnp.asarray(dft_table(slots // blocks), BF16)
    sign = jnp.asarray(np.tile(1.0 - 2.0 * (np.arange(slots // blocks) % 2), (8, 1)), F32)
    in_rows = in_proj.transpose(0, 2, 1, 3).reshape(layers, 3 * shard, width)
    taps = short_conv.transpose(1, 2, 0, 3)
    residual, gains, normed, project, up_columns, columns, keep = first_project(
        inputs, (mix_gain, mix_bias, glu_gain, glu_bias), (in_rows, 0), taps, cond_weight,
        (glu_in, 0), seq_table, 1,
    )
    constants = (keep, sign, table, seq_table, jnp.asarray(dft_table(slots // blocks).T, BF16))
    kept, state = [], None
    for l in range(layers):
        token_gated, conv, carried = conv_forward(
            project, (long_filter, l), (columns, l), *constants, cotangent if l else out_proj,
            2 if l else 1, blocks, 10 + l,
        )
        if l:
            state = carried
        else:
            full_out = carried
        middle, normed_glu, after, *rest = feed_forward(
            token_gated, residual, gains, (full_out, l), up_columns, (glu_out, l),
            ((in_rows, l + 1), (glu_in, l + 1)) if l + 1 < layers else (), 4 * l + 2, 20 + l,
        )
        saved, follow = [up_columns] + rest[:3], rest[3:]
        kept.append((residual, normed, project, conv, token_gated, middle, normed_glu, saved))
        residual = after
        if follow:
            normed, project, up_columns = follow
    feeds, filters, packs, gain_sums, row_sums = ([None] * layers for _ in range(5))
    waiting = []
    for l in reversed(range(layers)):
        before, normed, project, conv, token_gated, middle, normed_glu, saved = kept[l]
        top = l == layers - 1
        state, gated_grad, feed_grads, out_grad, glu_sums, *large = feed_back(
            state, middle, gains, normed_glu, saved[0], (glu_out, l), (full_out, l), token_gated,
            saved[1:], waiting, 4 * l + 2, count, 30 + l,
        )
        if waiting:
            filters[l + 1], packs[l + 1], feeds[l + 1] = large
        one, two = (3 * count // 8, 5 * count // 8) if l else (count // 2, count - 1)
        project_low, filter_pack, square, row_sums[l], held, *rest = conv_backward(
            gated_grad, project, conv, (long_filter, l), (columns, l), *constants,
            out_grad.reshape(4, shard, width), [Track(feed_grads, 0, one)],
            (residual,) if top else (), blocks, 40 + l,
        )
        if top:
            outputs = rest[0]
        tracks = [Track(feed_grads, one, two, held), Track(filter_pack, 0, count // 4)]
        state, in_pack, mix_sums, feed_held, held, in_held = project_back(
            project_low, state, before, gains, normed, (in_rows, l), square,
            tracks, 4 * l, 50 + l,
        )
        waiting = [
            Track(filter_pack, count // 4, count - 1, held),
            Track(in_pack, count // 4, count - 1, in_held),
        ]
        if l:
            waiting.append(Track(feed_grads, two, count - 1, feed_held))
        else:
            feeds[0] = feed_held
        gain_sums[l] = [mix_sums, glu_sums]
    input_grad, small, filters[0], packs[0] = last_sums(
        state, [one for pair in gain_sums for one in pair], row_sums, waiting, 60
    )
    results = list(collect(outputs, input_grad, small, feeds, filters, packs, each))
    results[4] = results[4].transpose(0, 2, 1, 3)
    results[5] = results[5].transpose(2, 0, 1, 3)
    return tuple(results)


def solution(mesh):
    in_specs = (
        P("chan", "dp"),
        P("dp", None),
        P(None, "chan"),
        P(None, "chan"),
        P(None, "chan", None, None),
        P(None, None, None, "chan"),
        P(None, "chan", None),
        P(None, "chan"),
        P(None, "chan", None),
        P(None, "chan"),
        P(None, "chan"),
        P(None, None, None, "chan"),
        P(None, None, "chan"),
        P("chan", "dp"),
    )
    out_specs = (
        P("chan", "dp"),
        P("chan", "dp"),
        P(None, "chan"),
        P(None, "chan"),
        P(None, ("chan", "dp"), None, None),
        P(None, None, None, "chan"),
        P(None, ("chan", "dp"), None),
        P(None, "chan"),
        P(None, ("chan", "dp"), None),
        P(None, "chan"),
        P(None, "chan"),
        P(None, "dp", None, "chan"),
        P(None, "dp", "chan"),
    )
    return jax.shard_map(body, mesh=mesh, in_specs=in_specs, out_specs=out_specs, check_vma=False)
```
